32 devices in a mesh: seq: 8 (over y, x, core), head: 4 (over z).
Axes of the slice: x: 2, y: 2, z: 4, core: 2. Of those that a mesh axis runs over, the one named last changes fastest.
Arguments:
- tokens: bfloat16 [1, 4096, 1536], P(None, 'seq', 'head'), may hold values from -6 to 6
- decay_codes: int32 [1, 4096, 48], P(None, 'seq', 'head'), may hold values from 0 to 524288, as said below
- norm_gain: bfloat16 [1536], P('head'), may hold values from 0.25 to 1.75
- gate_weight: bfloat16 [1536, 3072], P(None, 'head'), may hold values from -0.15625 to 0.15625
- value_weight: bfloat16 [1536, 3072], P(None, 'head'), may hold values from -0.15625 to 0.15625
- state_weight: bfloat16 [1536, 256], replicated, may hold values from -0.15625 to 0.15625
- value_kernel: bfloat16 [4, 3072], P(None, 'head'), may hold values from -3 to 3
- value_bias: bfloat16 [3072], P('head'), may hold values from -3 to 3
- state_kernel: bfloat16 [4, 256], replicated, may hold values from -3 to 3
- state_bias: bfloat16 [256], replicated, may hold values from -3 to 3
- skip_scale: float32 [48], P('head'), may hold values from 0.5 to 1.5
- gated_gain: bfloat16 [3072], P('head'), may hold values from 0.25 to 1.75
- output_weight: bfloat16 [3072, 1536], P('head'), may hold values from -0.109375 to 0.109375
- cotangent: bfloat16 [1, 4096, 1536], P(None, 'seq', 'head'), may hold values from -6 to 6
Outputs:
- block_out: bfloat16 [1, 4096, 1536], P(None, 'seq', 'head')
- tokens_gradient: bfloat16 [1, 4096, 1536], P(None, 'seq', 'head')
- norm_gain_gradient: float32 [1536], P('head')
- gate_weight_gradient: float32 [1536, 3072], P(None, 'head')
- value_weight_gradient: float32 [1536, 3072], P(None, 'head')
- state_weight_gradient: float32 [1536, 256], replicated
- value_kernel_gradient: float32 [4, 3072], P(None, 'head')
- value_bias_gradient: float32 [3072], P('head')
- state_kernel_gradient: float32 [4, 256], replicated
- state_bias_gradient: float32 [256], replicated
- skip_scale_gradient: float32 [48], P('head')
- gated_gain_gradient: float32 [3072], P('head')
- output_weight_gradient: float32 [3072, 1536], P('head')
The draws below stay inside these ranges and needn't reach their ends.
Inputs may be any that keep to these rules, and one draw needn't show every extreme that they name: `decay_codes`: decay factors are exp(-code / 1048576).
All inputs are finite; a program needn't handle non-finite values.
Results may differ from the reference program's by a relative error of at most 0.012.
The reference program's roundings to bfloat16 on the way count: a program that leaves them out, or rounds other values in their place, can miss the bound.
Values may be sent and summed in bfloat16 or wider, within the bound.
No kernel may reach another device: no remote copies, remote signals or barrier semaphores. Data moves between devices by JAX's collectives and lax.ppermute only.
A program may use at most 128 MiB of HBM per device.

```python
from functools import partial
import jax
import jax.numpy as jnp
from jax import lax

D = 1536
MIXER_HEADS = 48
HEAD_DIM = 64
NSTATE = 128
KERNEL = 4
GROUP = 256
SEQUENCE_COUNT = 1
INNER = 3072
SEQUENCE_LENGTH = 4096


def draw_decay_codes(key, part):
    key = jax.random.fold_in(key, 7)
    variety_key, quick_key, gradual_key, surge_key = jax.random.split(key, 4)
    array_shape = (SEQUENCE_COUNT, SEQUENCE_LENGTH, MIXER_HEADS)
    fast_heads = jax.random.randint(variety_key, (SEQUENCE_COUNT, 1, MIXER_HEADS), 0, 2)
    fast_codes = jax.random.randint(quick_key, array_shape, 30000, 80001)
    slow_codes = jax.random.randint(gradual_key, array_shape, 0, 1 + 1048576 // SEQUENCE_LENGTH)
    selected = jnp.where(fast_heads == 1, fast_codes, slow_codes)
    locations = jax.random.randint(surge_key, (SEQUENCE_COUNT, 3, MIXER_HEADS), 0, SEQUENCE_LENGTH)
    token_positions = jnp.arange(SEQUENCE_LENGTH)[None, :, None, None]
    surges = jnp.any(token_positions == locations[:, None, :, :], axis=2)
    return jnp.where(surges, 524288, selected).astype(jnp.int32)


def steps_of(own_key, dims, cuts, low, largest):
    factor_of = 1.0
    for position, blocks in cuts:
        heights = jax.random.uniform(jax.random.fold_in(jax.random.fold_in(own_key, 6), position), (blocks,), jnp.float32, low / len(cuts), largest / len(cuts))
        factor_of = factor_of * jnp.repeat(jnp.exp(heights), dims[position] // blocks).reshape((-1,) + (1,) * (len(dims) - 1 - position))
    return factor_of


def centred(own_key, extent, scale, most, cuts=(), kind=jnp.bfloat16):
    entries = scale * jax.random.normal(own_key, extent, jnp.float32)
    if cuts:
        entries = entries * steps_of(own_key, extent, cuts, -0.22, 0.18)
    return jnp.clip(entries, -most, most).astype(kind)


def setup_inputs(seed: int = 0) -> dict:
    seeds = jax.random.split(jax.random.key(seed), 15)
    tokens = centred(seeds[0], (SEQUENCE_COUNT, SEQUENCE_LENGTH, D), 1.0, 6.0, ((1, 8), (2, 4)))
    decay_codes = draw_decay_codes(jax.random.fold_in(seeds[14], 71), 0)
    norm_gain = jnp.clip(1.0 + 0.15 * jax.random.normal(seeds[2], (D,), jnp.float32), 0.25, 1.75).astype(jnp.bfloat16)
    gate_weight = centred(seeds[3], (D, INNER), D ** -0.5, 0.15625, ((1, 4),))
    value_weight = centred(seeds[4], (D, INNER), D ** -0.5, 0.15625, ((1, 4),))
    state_weight = centred(seeds[5], (D, 2 * NSTATE), D ** -0.5, 0.15625)
    value_kernel = centred(seeds[6], (KERNEL, INNER), KERNEL ** -0.5, 3.0, ((1, 4),))
    value_bias = centred(seeds[7], (INNER,), 0.5, 3.0, ((0, 4),))
    state_kernel = centred(seeds[8], (KERNEL, 2 * NSTATE), KERNEL ** -0.5, 3.0)
    state_bias = centred(seeds[9], (2 * NSTATE,), 0.5, 3.0)
    skip_scale = jnp.clip(0.5 + 1.0 * jax.random.uniform(seeds[10], (MIXER_HEADS,), jnp.float32) ** steps_of(seeds[10], (MIXER_HEADS,), ((0, 4),), -0.2, 0.2), 0.5, 1.5)
    gated_gain = jnp.clip(1.0 + 0.15 * jax.random.normal(seeds[11], (INNER,), jnp.float32), 0.25, 1.75).astype(jnp.bfloat16)
    output_weight = centred(seeds[12], (INNER, D), INNER ** -0.5, 0.109375, ((0, 4),))
    cotangent = centred(seeds[13], (SEQUENCE_COUNT, SEQUENCE_LENGTH, D), 1.0, 6.0, ((1, 8), (2, 4)))
    return {"tokens": tokens, "decay_codes": decay_codes, "norm_gain": norm_gain, "gate_weight": gate_weight, "value_weight": value_weight, "state_weight": state_weight, "value_kernel": value_kernel, "value_bias": value_bias, "state_kernel": state_kernel, "state_bias": state_bias, "skip_scale": skip_scale, "gated_gain": gated_gain, "output_weight": output_weight, "cotangent": cotangent}


DECAY_STEP = 1.0 / 1048576.0
EPSILON = 1e-05
HIGHEST = lax.Precision.HIGHEST

@jax.custom_vjp
def low(v):
    return lax.optimization_barrier(v.astype(jnp.bfloat16)).astype(jnp.float32)

@jax.custom_vjp
def low_back(v):
    return v

def low_keep(v):
    return (low(v), None)

def low_pass(kept, grad):
    return (grad,)

def back_keep(v):
    return (v, None)

def back_low(kept, grad):
    return (low(grad),)
low.defvjp(low_keep, low_pass)
low_back.defvjp(back_keep, back_low)

def causal_conv(values, kernel, shift_bias):
    length = values.shape[1]
    padded = jnp.concatenate([jnp.zeros((values.shape[0], KERNEL - 1, values.shape[2]), jnp.float32), values], axis=1)
    summed = shift_bias
    for offset in range(KERNEL):
        summed = summed + kernel[offset] * padded[:, offset:offset + length]
    return summed

def decay_factors(cumulative, lower_mask):
    heads_first = jnp.swapaxes(cumulative, 1, 2)
    spread = heads_first[:, :, :, None] - heads_first[:, :, None, :]
    return jnp.where(lower_mask, jnp.exp(jnp.where(lower_mask, spread, 0.0)), 0.0)

def block_step(carry_state, pieces):
    weighted, decay_part, input_map, output_map = pieces
    block_len = decay_part.shape[1]
    lower_mask = jnp.arange(block_len)[:, None] >= jnp.arange(block_len)[None, :]
    cumulative = jnp.cumsum(decay_part, axis=1)
    factors = decay_factors(cumulative, lower_mask)
    scores = jnp.einsum('btn,bsn->bts', output_map, input_map, precision=HIGHEST)
    intra = jnp.einsum('bhts,bshp->bthp', factors * scores[:, None], weighted, precision=HIGHEST)
    inter = jnp.einsum('btn,bhpn->bthp', output_map, carry_state, precision=HIGHEST) * jnp.exp(cumulative)[..., None]
    last_sum = cumulative[:, -1]
    fading = jnp.exp(last_sum[:, None, :] - cumulative)
    new_state = jnp.exp(last_sum)[:, :, None, None] * carry_state + jnp.einsum('bshp,bsn->bhpn', fading[..., None] * weighted, input_map, precision=HIGHEST)
    return (new_state, intra + inter)

def forward(inputs, norm_gain, gate_weight, value_weight, state_weight, value_kernel, value_bias, state_kernel, state_bias, skip_scale, gated_gain, output_weight, decay_log, input_weight):
    num_seqs, length = (inputs.shape[0], inputs.shape[1])
    scale_in = lax.rsqrt(lax.optimization_barrier(jnp.mean(inputs * inputs, axis=-1, keepdims=True)) + EPSILON)
    normed = low(inputs * scale_in * norm_gain)
    gate_pre = low_back(jnp.einsum('bld,de->ble', normed, gate_weight, precision=HIGHEST))
    value_raw = low_back(low(jnp.einsum('bld,de->ble', normed, value_weight, precision=HIGHEST)))
    state_raw = low_back(low(jnp.einsum('bld,de->ble', normed, state_weight, precision=HIGHEST)))
    value_conv = low(jax.nn.silu(causal_conv(value_raw, value_kernel, value_bias)))
    state_conv = low(jax.nn.silu(causal_conv(state_raw, state_kernel, state_bias)))
    value_heads = value_conv.reshape(num_seqs, length, MIXER_HEADS, HEAD_DIM)
    weighted = value_heads * input_weight[..., None]
    input_map = state_conv[..., :NSTATE]
    output_map = state_conv[..., NSTATE:]
    num_blocks = length // GROUP

    def blocks(values):
        return jnp.moveaxis(values.reshape((num_seqs, num_blocks, GROUP) + values.shape[2:]), 1, 0)
    initial = jnp.zeros((num_seqs, MIXER_HEADS, HEAD_DIM, NSTATE), jnp.float32)
    _, outputs = lax.scan(jax.checkpoint(block_step), initial, (blocks(weighted), blocks(decay_log), blocks(input_map), blocks(output_map)))
    ssd_out = jnp.moveaxis(outputs, 0, 1).reshape(num_seqs, length, MIXER_HEADS, HEAD_DIM)
    mixer_out = ssd_out + skip_scale[:, None] * value_heads
    gated_out = mixer_out.reshape(num_seqs, length, INNER) * jax.nn.silu(gate_pre)
    scale_gate = lax.rsqrt(lax.optimization_barrier(jnp.mean(gated_out * gated_out, axis=-1, keepdims=True)) + EPSILON)
    mixed = low(gated_out * scale_gate * gated_gain)
    return inputs + jnp.einsum('ble,ed->bld', mixed, output_weight, precision=HIGHEST)

def reference(tokens, decay_codes, norm_gain, gate_weight, value_weight, state_weight, value_kernel, value_bias, state_kernel, state_bias, skip_scale, gated_gain, output_weight, cotangent):
    decay_log = -decay_codes.astype(jnp.float32) * DECAY_STEP
    input_weight = jnp.sqrt(-jnp.expm1(2.0 * decay_log))
    params = jax.tree.map(lambda values: values.astype(jnp.float32), (tokens, norm_gain, gate_weight, value_weight, state_weight, value_kernel, value_bias, state_kernel, state_bias, skip_scale, gated_gain, output_weight))
    block_out, pullback = jax.vjp(partial(forward, decay_log=decay_log, input_weight=input_weight), *params)
    gradients = pullback(cotangent.astype(jnp.float32))
    return (block_out.astype(jnp.bfloat16), gradients[0].astype(jnp.bfloat16), gradients[1], gradients[2], gradients[3], gradients[4], gradients[5], gradients[6], gradients[7], gradients[8], gradients[9], gradients[10], gradients[11])
```

```python
import jax
import jax.numpy as jnp
from jax import lax
from jax.sharding import PartitionSpec as P

HEAD_DIM = 64
NSTATE = 128
KERNEL = 4
GROUP = 256


DECAY_STEP = 1.0 / 1048576.0
EPSILON = 1e-05


def from_behind(value, axis, by):
    size = lax.axis_size(axis)
    pairs = [(i, i + by) for i in range(size) if 0 <= i + by < size]
    return lax.ppermute(value, axis, pairs)


def spans(decays, level, mine):
    index = jnp.arange(decays.shape[0])[:, None]
    group = index >> level
    own = mine >> level
    pick = lambda mask: jnp.sum(jnp.where(mask, decays, 0.0), axis=0)
    return (
        pick(group == own),
        pick(group == (own ^ 1)),
        pick((group == own) & (index < mine)),
        pick((group == own) & (index > mine)),
    )


def exchange(value, axis, bits):
    return lax.ppermute(value, axis, [(i, i ^ bits) for i in range(lax.axis_size(axis))])


def entering(total, decays, axis, backward):
    count, mine = lax.axis_size(axis), lax.axis_index(axis)
    prefix = jnp.zeros_like(total)
    level = 0
    while (1 << level) < count:
        own, other, below, above = spans(decays, level, mine)
        passed = above if backward else below
        upper = ((mine >> level) & 1) == 1
        receives = jnp.logical_not(upper) if backward else upper
        arrived = exchange(total, axis, 1 << level)
        grown = lambda logs, state: jnp.exp(logs)[:, None, None] * state
        prefix = jnp.where(receives, grown(passed, arrived) + prefix, prefix)
        total = jnp.where(receives, grown(own, arrived) + total, grown(other, total) + arrived)
        level += 1
    return prefix


def turn(value, axis, by):
    size = lax.axis_size(axis)
    return lax.ppermute(value, axis, [(i, (i + by) % size) for i in range(size)])


def gather_all(value, axis):
    size, mine = lax.axis_size(axis), lax.axis_index(axis)
    out = jnp.zeros((size,) + value.shape, value.dtype)
    out = lax.dynamic_update_slice_in_dim(out, value[None], mine, 0)
    for by in range(1, size):
        out = lax.dynamic_update_slice_in_dim(
            out, turn(value, axis, by)[None], (mine + size - by) % size, 0
        )
    return out


def total_over(value, axis):
    summed = value
    for by in range(1, lax.axis_size(axis)):
        summed = summed + turn(value, axis, by)
    return summed


def scatter_columns(value, axis):
    size, mine = lax.axis_size(axis), lax.axis_index(axis)
    width = value.shape[-1] // size
    part = lambda owner: lax.dynamic_slice_in_dim(value, owner * width, width, value.ndim - 1)
    summed = part(mine)
    for by in range(1, size):
        piece = part((mine + by) % size).astype(jnp.bfloat16)
        summed = summed + turn(piece, axis, by).astype(jnp.float32)
    return summed


def seq_scatter(value, axis):
    size, mine = lax.axis_size(axis), lax.axis_index(axis)
    rows = value.shape[0] // 2
    core, chip, chips = mine & 1, mine >> 1, size // 2
    low = value.astype(jnp.bfloat16)
    given = lax.dynamic_slice_in_dim(low, (1 - core) * rows, rows, 0)
    kept = lax.dynamic_slice_in_dim(value, core * rows, rows, 0).astype(jnp.float32)
    half = kept + exchange(given, axis, 1).astype(jnp.float32)
    low_half = half.astype(jnp.bfloat16)
    rows = rows // chips
    summed = lax.dynamic_slice_in_dim(half, chip * rows, rows, 0)
    for other in range(1, chips):
        piece = lax.dynamic_slice_in_dim(low_half, (chip ^ other) * rows, rows, 0)
        summed = summed + exchange(piece, axis, 2 * other).astype(jnp.float32)
    return summed


def seq_collect(piece, axis):
    size, mine = lax.axis_size(axis), lax.axis_index(axis)
    core, chip, chips = mine & 1, mine >> 1, size // 2
    low = piece.astype(jnp.bfloat16)
    rows = piece.shape[0]
    half = jnp.zeros((chips * rows,) + piece.shape[1:], jnp.bfloat16)
    half = lax.dynamic_update_slice_in_dim(half, low, chip * rows, 0)
    for other in range(1, chips):
        half = lax.dynamic_update_slice_in_dim(
            half, exchange(low, axis, 2 * other), (chip ^ other) * rows, 0
        )
    partner = exchange(half, axis, 1)
    first = jnp.where(core == 0, half, partner)
    second = jnp.where(core == 0, partner, half)
    return jnp.concatenate([first, second], axis=0).astype(jnp.float32)


def silu_slope(values):
    sigmoid = jax.nn.sigmoid(values)
    return sigmoid * (1.0 + values * (1.0 - sigmoid))


def causal_conv(current, before, kernel, shift_bias):
    padded = jnp.concatenate([before, current], axis=1).astype(jnp.float32)
    length = current.shape[1]
    summed = shift_bias.astype(jnp.float32)
    for offset in range(kernel.shape[0]):
        summed = summed + kernel[offset].astype(jnp.float32) * padded[:, offset : offset + length]
    return summed


def conv_back(slopes, after, kernel):
    padded = jnp.concatenate([slopes, after], axis=1)
    length = slopes.shape[1]
    kernel_size = kernel.shape[0]
    summed = jnp.zeros_like(slopes)
    for offset in range(kernel_size):
        begin = kernel_size - 1 - offset
        summed = summed + kernel[offset].astype(jnp.float32) * padded[:, begin : begin + length]
    return summed


def kernel_grads(slopes, current, before, kernel_size):
    padded = jnp.concatenate([before, current], axis=1).astype(jnp.float32)
    length = current.shape[1]
    taps_list = [
        jnp.sum(slopes * padded[:, offset : offset + length], axis=(0, 1))
        for offset in range(kernel_size)
    ]
    return (jnp.stack(taps_list, axis=0), jnp.sum(slopes, axis=(0, 1)))


def decay_factors(cumulative):
    block_len = cumulative.shape[1]
    lower_mask = jnp.arange(block_len)[:, None] >= jnp.arange(block_len)[None, :]
    heads_first = jnp.swapaxes(cumulative, 1, 2)
    spread = heads_first[:, :, :, None] - heads_first[:, :, None, :]
    return jnp.where(lower_mask, jnp.exp(jnp.where(lower_mask, spread, 0.0)), 0.0)


def low_einsum(names, left, right):
    return jnp.einsum(
        names,
        left.astype(jnp.bfloat16),
        right.astype(jnp.bfloat16),
        preferred_element_type=jnp.float32,
    )


def full_einsum(names, left, right):
    return jnp.einsum(names, left, right, precision=lax.Precision.HIGHEST)


def map_scores(output_map, input_map):
    return jnp.einsum(
        "btn,bsn->bts",
        output_map.astype(jnp.bfloat16),
        input_map.astype(jnp.bfloat16),
        preferred_element_type=jnp.float32,
    )


def local_block(carry_state, pieces):
    weighted, decay_part, input_map, output_map = pieces
    cumulative = jnp.cumsum(decay_part, axis=1)
    factors = decay_factors(cumulative)
    scores = map_scores(output_map, input_map)
    intra = low_einsum("bhts,bshp->bthp", factors * scores[:, None], weighted)
    inter = (
        full_einsum("btn,bhpn->bthp", output_map, carry_state)
        * jnp.exp(cumulative)[..., None]
    )
    last_sum = cumulative[:, -1]
    fading = jnp.exp(last_sum[:, None, :] - cumulative)
    new_state = jnp.exp(last_sum)[:, :, None, None] * carry_state + low_einsum(
        "bshp,bsn->bhpn", fading[..., None] * weighted, input_map
    )
    return (new_state, (intra + inter, carry_state))


def backward_block(later_grad, pieces):
    weighted, decay_part, input_map, output_map, out_grad, start_state = pieces
    cumulative = jnp.cumsum(decay_part, axis=1)
    factors = decay_factors(cumulative)
    scores = map_scores(output_map, input_map)
    last_sum = cumulative[:, -1]
    fading = jnp.exp(last_sum[:, None, :] - cumulative)
    growth = jnp.exp(cumulative)
    weighted_grad = low_einsum(
        "bhts,bthp->bshp", factors * scores[:, None], out_grad
    )
    weighted_grad = weighted_grad + fading[..., None] * full_einsum("bhpn,bsn->bshp", later_grad, input_map
    )
    score_grad = jnp.sum(
        low_einsum(
        "bthp,bshp->bhts", out_grad, weighted) * factors, axis=1
    )
    grown_grad = growth[..., None] * out_grad
    output_grad = low_einsum(
        "bts,bsn->btn", score_grad, input_map) + full_einsum("bthp,bhpn->btn", grown_grad, start_state
    )
    input_grad = low_einsum(
        "bts,btn->bsn", score_grad, output_map) + full_einsum("bshp,bhpn->bsn", fading[..., None] * weighted, later_grad
    )
    start_grad = jnp.exp(last_sum)[:, :, None, None] * later_grad + full_einsum("bthp,btn->bhpn", grown_grad, output_map
    )
    return (start_grad, (weighted_grad, input_grad, output_grad))


def per_device(
    tokens,
    decay_codes,
    norm_gain,
    gate_weight,
    value_weight,
    state_weight,
    value_kernel,
    value_bias,
    state_kernel,
    state_bias,
    skip_scale,
    gated_gain,
    output_weight,
    cotangent,
):
    num_seqs, tok_count, own_width = tokens.shape
    local_heads = skip_scale.shape[0]
    inner_width = local_heads * HEAD_DIM
    margin = KERNEL - 1
    num_blocks = tok_count // GROUP

    def blocks(values):
        return jnp.moveaxis(values.reshape((num_seqs, num_blocks, GROUP) + values.shape[2:]), 1, 0)

    def unblock(values):
        return jnp.moveaxis(values, 0, 1).reshape((num_seqs, tok_count) + values.shape[3:])

    packed = jnp.concatenate(
        [tokens[0], jnp.broadcast_to(norm_gain[None], (16, own_width))], axis=0
    )
    gathered = jnp.concatenate(list(gather_all(packed, "head")), axis=1)
    full_tokens, full_gain = gathered[None, :tok_count], gathered[tok_count]
    full_cotangent = lax.all_gather(cotangent, "head", axis=2, tiled=True)
    inputs = full_tokens.astype(jnp.float32)
    scale_in = lax.rsqrt(jnp.mean(inputs * inputs, axis=2, keepdims=True) + EPSILON)
    gain_full = full_gain.astype(jnp.float32)
    normed = (inputs * scale_in * gain_full).astype(jnp.bfloat16)
    gate_pre = jnp.einsum("btd,de->bte", normed, gate_weight, preferred_element_type=jnp.float32)
    value_raw = jnp.einsum(
        "btd,de->bte", normed, value_weight, preferred_element_type=jnp.float32
    ).astype(jnp.bfloat16)
    state_raw = jnp.einsum(
        "btd,de->bte", normed, state_weight, preferred_element_type=jnp.float32
    ).astype(jnp.bfloat16)
    value_before, state_before = from_behind(
        (value_raw[:, -margin:], state_raw[:, -margin:]), "seq", 1
    )
    value_pre = causal_conv(value_raw, value_before, value_kernel, value_bias)
    value_conv = jax.nn.silu(value_pre).astype(jnp.bfloat16)
    state_pre = causal_conv(state_raw, state_before, state_kernel, state_bias)
    state_conv = jax.nn.silu(state_pre).astype(jnp.bfloat16)
    decay_log = -decay_codes.astype(jnp.float32) * DECAY_STEP
    input_weight = jnp.sqrt(-jnp.expm1(2.0 * decay_log))
    value_heads = value_conv.astype(jnp.float32).reshape(num_seqs, tok_count, local_heads, HEAD_DIM)
    weighted = value_heads * input_weight[..., None]
    input_map = state_conv[:, :, :NSTATE].astype(jnp.float32)
    output_map = state_conv[:, :, NSTATE:].astype(jnp.float32)
    zero_state = jnp.zeros((num_seqs, local_heads, HEAD_DIM, NSTATE), jnp.float32)
    state, outs, starts = zero_state, [], []
    pieces = (blocks(weighted), blocks(decay_log), blocks(input_map), blocks(output_map))
    for block in range(num_blocks):
        state, (out, start) = local_block(state, tuple(piece[block] for piece in pieces))
        outs.append(out)
        starts.append(start)
    local_end = state
    running = jnp.cumsum(decay_log, axis=1)
    device_decay = running[:, -1]
    decays = lax.all_gather(device_decay[0], "seq")
    state_in = entering(local_end[0], decays, "seq", False)[None]
    growth = jnp.exp(running)
    ssd_out = jnp.concatenate(outs, axis=1) + growth[..., None] * full_einsum("btn,bhpn->bthp", output_map, state_in
    )
    mixer_out = ssd_out + skip_scale[:, None] * value_heads
    mixer_flat = mixer_out.reshape(num_seqs, tok_count, inner_width)
    gate_silu = jax.nn.silu(gate_pre)
    gated_out = mixer_flat * gate_silu
    gain_gate = gated_gain.astype(jnp.float32)
    mixed_grad = jnp.einsum(
        "btd,ed->bte", full_cotangent, output_weight, preferred_element_type=jnp.float32
    )
    scaled_grad = mixed_grad * gain_gate
    inner_total = inner_width * lax.axis_size("head")
    sums = jnp.concatenate(
        [jnp.sum(gated_out * gated_out, axis=2), jnp.sum(gated_out * scaled_grad, axis=2)], axis=0
    )
    sums = total_over(sums, "head")
    square_sum, cross_gate = sums[:num_seqs], sums[num_seqs:]
    scale_gate = lax.rsqrt(square_sum / inner_total + EPSILON)[..., None]
    mixed = (gated_out * scale_gate * gain_gate).astype(jnp.bfloat16)
    output_weight_gradient = jnp.einsum(
        "bte,btd->ed", mixed, full_cotangent, preferred_element_type=jnp.float32
    )
    output_weight_gradient = lax.psum(output_weight_gradient.astype(jnp.bfloat16), "seq").astype(
        jnp.float32
    )
    partial_out = jnp.einsum(
        "bte,ed->btd", mixed, output_weight, preferred_element_type=jnp.float32
    )
    branch = lax.psum_scatter(
        partial_out.astype(jnp.bfloat16), "head", scatter_dimension=2, tiled=True
    ).astype(jnp.float32)
    own_inputs = tokens.astype(jnp.float32)
    block_out = (own_inputs + branch).astype(jnp.bfloat16)
    gated_gain_gradient = jnp.sum(mixed_grad * gated_out * scale_gate, axis=(0, 1))
    gated_grad = (
        scale_gate * scaled_grad - gated_out * scale_gate**3 * (cross_gate / inner_total)[..., None]
    )
    mixer_grad = (gated_grad * gate_silu).reshape(num_seqs, tok_count, local_heads, HEAD_DIM)
    gate_grad = (gated_grad * mixer_flat * silu_slope(gate_pre)).astype(jnp.bfloat16)
    gate_weight_gradient = jnp.einsum(
        "btd,bte->de", normed, gate_grad, preferred_element_type=jnp.float32
    )
    gate_weight_gradient = lax.psum(gate_weight_gradient.astype(jnp.bfloat16), "seq").astype(
        jnp.float32
    )
    skip_scale_gradient = jnp.sum(mixer_grad * value_heads, axis=(0, 1, 3))
    grad_pieces, later, results = blocks(mixer_grad), zero_state, [None] * num_blocks
    for block in reversed(range(num_blocks)):
        later, results[block] = backward_block(
            later, tuple(piece[block] for piece in pieces) + (grad_pieces[block], starts[block])
        )
    weighted_grad, input_grad, output_grad = (
        jnp.concatenate(parts, axis=1) for parts in zip(*results)
    )
    grad_after = entering(later[0], decays, "seq", True)[None]
    fading = jnp.exp(device_decay[:, None] - running)
    weighted_grad = weighted_grad + fading[..., None] * full_einsum("bhpn,btn->bthp", grad_after, input_map
    )
    input_grad = input_grad + full_einsum("bthp,bhpn->btn", fading[..., None] * weighted, grad_after
    )
    output_grad = output_grad + full_einsum("bthp,bhpn->btn", growth[..., None] * mixer_grad, state_in
    )
    conv_grad = weighted_grad * input_weight[..., None] + mixer_grad * skip_scale[:, None]
    value_slope = conv_grad.reshape(num_seqs, tok_count, inner_width) * silu_slope(value_pre)
    map_part = jnp.concatenate([input_grad, output_grad], axis=2)
    state_slope = map_part * silu_slope(state_pre)
    value_after, state_after = from_behind(
        (value_slope[:, :margin], state_slope[:, :margin]), "seq", -1
    )
    value_raw_grad = conv_back(value_slope, value_after, value_kernel).astype(jnp.bfloat16)
    state_raw_grad = conv_back(state_slope, state_after, state_kernel).astype(jnp.bfloat16)
    value_kernel_gradient, value_bias_gradient = kernel_grads(
        value_slope, value_raw, value_before, KERNEL
    )
    state_kernel_gradient, state_bias_gradient = kernel_grads(
        state_slope, state_raw, state_before, KERNEL
    )
    normed_part = (
        jnp.einsum("bte,de->btd", gate_grad, gate_weight, preferred_element_type=jnp.float32)
        + jnp.einsum(
            "bte,de->btd", value_raw_grad, value_weight, preferred_element_type=jnp.float32
        )
        + jnp.einsum(
            "bte,de->btd", state_raw_grad, state_weight, preferred_element_type=jnp.float32
        )
    )
    weighted_inputs = inputs * gain_full
    cross_part = jnp.sum(weighted_inputs * normed_part, axis=2)
    norm_gain_part = jnp.sum(normed_part * inputs * scale_in, axis=(0, 1))
    normed_grad = scatter_columns(normed_part, "head")
    cross_sum = total_over(cross_part, "head")
    value_weight_gradient = jnp.einsum(
        "btd,bte->de", normed, value_raw_grad, preferred_element_type=jnp.float32
    )
    state_weight_gradient = jnp.einsum(
        "btd,bte->de", normed, state_raw_grad, preferred_element_type=jnp.float32
    )
    value_weight_gradient = seq_collect(seq_scatter(value_weight_gradient, "seq"), "seq")
    state_weight_gradient = seq_collect(
        total_over(seq_scatter(state_weight_gradient, "seq"), "head"), "seq"
    )
    own_gain = norm_gain.astype(jnp.float32)
    full_width = inputs.shape[2]
    tokens_gradient = (
        scale_in * own_gain * normed_grad
        - own_inputs * scale_in**3 * (cross_sum / full_width)[..., None]
        + cotangent.astype(jnp.float32)
    ).astype(jnp.bfloat16)
    shared = jnp.concatenate(
        [norm_gain_part, state_kernel_gradient.reshape(-1), state_bias_gradient]
    )
    shared = total_over(shared, "head")
    own = jnp.concatenate(
        [
            value_kernel_gradient.reshape(-1),
            value_bias_gradient,
            gated_gain_gradient,
            skip_scale_gradient,
        ]
    )
    small = jnp.concatenate([shared, own])
    bits = 1
    while bits < lax.axis_size("seq"):
        small = small + exchange(small, "seq", bits)
        bits *= 2
    shapes = [
        (full_width,),
        state_kernel_gradient.shape,
        state_bias_gradient.shape,
        value_kernel_gradient.shape,
        value_bias_gradient.shape,
        gated_gain_gradient.shape,
        skip_scale_gradient.shape,
    ]
    cut, begin = [], 0
    for shape in shapes:
        length = 1
        for extent in shape:
            length *= extent
        cut.append(small[begin : begin + length].reshape(shape))
        begin += length
    (
        norm_gain_gradient,
        state_kernel_gradient,
        state_bias_gradient,
        value_kernel_gradient,
        value_bias_gradient,
        gated_gain_gradient,
        skip_scale_gradient,
    ) = cut
    norm_gain_gradient = lax.dynamic_slice_in_dim(
        norm_gain_gradient, lax.axis_index("head") * own_width, own_width, 0
    )
    return (
        block_out,
        tokens_gradient,
        norm_gain_gradient,
        gate_weight_gradient,
        value_weight_gradient,
        state_weight_gradient,
        value_kernel_gradient,
        value_bias_gradient,
        state_kernel_gradient,
        state_bias_gradient,
        skip_scale_gradient,
        gated_gain_gradient,
        output_weight_gradient,
    )


def solution(mesh):
    in_specs = (
        P(None, "seq", "head"),
        P(None, "seq", "head"),
        P("head"),
        P(None, "head"),
        P(None, "head"),
        P(),
        P(None, "head"),
        P("head"),
        P(),
        P(),
        P("head"),
        P("head"),
        P("head", None),
        P(None, "seq", "head"),
    )
    out_specs = (
        P(None, "seq", "head"),
        P(None, "seq", "head"),
        P("head"),
        P(None, "head"),
        P(None, "head"),
        P(),
        P(None, "head"),
        P("head"),
        P(),
        P(),
        P("head"),
        P("head"),
        P("head", None),
    )
    return jax.shard_map(
        per_device, mesh=mesh, in_specs=in_specs, out_specs=out_specs, check_vma=False
    )
```

```python
import functools

import jax
import jax.numpy as jnp
from jax import lax
from jax.experimental import pallas as pl
from jax.experimental.pallas import tpu as pltpu
from jax.sharding import Mesh
from jax.sharding import PartitionSpec as P

HEAD_DIM = 64
NSTATE = 128
KERNEL = 4
CHUNK = 128
BLOCK = 384
VMEM_LIMIT = 20 * 1024 * 1024
HALO = 16


DECAY_STEP = 1.0 / 1048576.0
EPSILON = 1e-05
BF16 = jnp.bfloat16
F32 = jnp.float32


def tie(value, other):
    return lax.optimization_barrier((value, other))[0]


def from_behind(value, by):
    axis = ("chip", "core")
    size = lax.axis_size("chip") * 2
    pairs = [(i, i + by) for i in range(size) if 0 <= i + by < size]
    return lax.ppermute(value, axis, pairs)


def beside(value):
    return lax.ppermute(value, "core", [(0, 1), (1, 0)])


def deal(parts, axis):
    return lax.all_to_all(parts, axis, 0, 0)


def gather_all(value, axis):
    size = lax.axis_size(axis)
    return deal(jnp.broadcast_to(value[None], (size,) + value.shape), axis)


def decay_weights(logs, backward):
    chips, mine = lax.axis_size("chip"), lax.axis_index("chip")
    source = jnp.arange(chips)[:, None]
    middle = jnp.arange(chips)[None, :]
    if backward:
        between, passes = (middle < source) & (middle > mine), source > mine
    else:
        between, passes = (middle > source) & (middle < mine), source < mine
    spans = jnp.sum(jnp.where(between[:, :, None], logs[None], 0.0), axis=1)
    return jnp.where(passes, jnp.exp(spans), 0.0)


def entering(total, own_decay, other_decay, weights, backward):
    core = lax.axis_index("core")
    receives = core == (0 if backward else 1)
    half = total.shape[0] // 2
    partner = beside(total)
    part = lambda value: lax.dynamic_slice_in_dim(value, core * half, half, 0)
    pair = jnp.where(
        receives,
        own_decay * part(partner) + part(total),
        other_decay * part(total) + part(partner),
    )
    arrived = gather_all(pair, "chip")
    prefix = jnp.sum(arrived * weights[:, None, :], axis=0)
    other = beside(prefix)
    whole = jnp.where(
        core == 0,
        jnp.concatenate([prefix, other], axis=0),
        jnp.concatenate([other, prefix], axis=0),
    )
    return jnp.where(receives, other_decay * whole + partner, whole)


def chip_sums(kept, given):
    return (kept.astype(F32) + beside(given).astype(F32)).astype(BF16)


def seq_sums(halves):
    summed = jnp.sum(deal(halves, "chip").astype(F32), axis=0).astype(BF16)
    return gather_all(summed, "chip")


def dot(left, right):
    return jnp.dot(left, right, preferred_element_type=F32)


def dot_nt(left, right):
    return lax.dot_general(left, right, (((1,), (1,)), ((), ())), preferred_element_type=F32)


def dot_tn(left, right):
    return lax.dot_general(left, right, (((0,), (0,)), ((), ())), preferred_element_type=F32)


def split(values):
    high = values.astype(BF16)
    return high, (values - high.astype(F32)).astype(BF16)


def lower_mask():
    row = lax.broadcasted_iota(jnp.int32, (CHUNK, CHUNK), 0)
    column = lax.broadcasted_iota(jnp.int32, (CHUNK, CHUNK), 1)
    return row >= column


def decay_kernel(codes_ref, weight_ref, e_ref, f_ref, k_ref):
    heads, channels = codes_ref.shape[1], e_ref.shape[1]
    row = lax.broadcasted_iota(jnp.int32, (heads, channels), 0)
    column = lax.broadcasted_iota(jnp.int32, (heads, channels), 1)
    first = row * HEAD_DIM
    spread = jnp.where((column >= first) & (column < first + HEAD_DIM), 1.0, 0.0).astype(BF16)

    def expand(values):
        high, low = split(values)
        return dot(high, spread) + dot(low, spread)

    lower = jnp.where(lower_mask(), 1.0, 0.0).astype(F32)
    count = codes_ref.shape[0] // CHUNK
    line = lax.broadcasted_iota(jnp.int32, (8, heads), 0)
    marks = jnp.zeros((8, heads), F32)
    total = jnp.zeros((1, heads), F32)
    for chunk in range(count):
        rows = pl.ds(chunk * CHUNK, CHUNK)
        logs = codes_ref[rows, :].astype(F32) * (-DECAY_STEP)
        cumulative = jnp.dot(
            lower, logs, precision=lax.Precision.HIGHEST, preferred_element_type=F32
        )
        last = cumulative[CHUNK - 1 :]
        middle = 0.5 * last
        e_ref[rows, :] = expand(jnp.exp(cumulative - middle))
        f_ref[rows, :] = expand(weight_ref[rows, :] * jnp.exp(middle - cumulative))
        marks = jnp.where(line == chunk, jnp.exp(middle), marks)
        total = total + last
    marks = jnp.where(line == 7, total, marks)
    high, low = split(marks)
    lowest = (marks - high.astype(F32) - low.astype(F32)).astype(BF16)
    k_ref[...] = dot(high, spread) + dot(low, spread) + dot(lowest, spread)


def taps(window, kernel, bias, begin):
    summed = bias
    for offset in range(KERNEL):
        summed = summed + kernel[offset : offset + 1] * window[begin + offset : begin + offset + CHUNK]
    return summed


def silu_parts(values):
    sigmoid = jax.nn.sigmoid(values)
    return values * sigmoid, sigmoid * (1.0 + values * (1.0 - sigmoid))


def conv_kernel(
    value_ref, state_ref, value_kernel_ref, value_bias_ref, state_kernel_ref, state_bias_ref,
    f_ref, k_ref, conv_ref, weighted_ref, value_slope_ref, maps_ref, state_slope_ref, total_ref,
):
    count = conv_ref.shape[0] // CHUNK
    value_kernel, value_bias = value_kernel_ref[...].astype(F32), value_bias_ref[...].astype(F32)
    state_kernel, state_bias = state_kernel_ref[...].astype(F32), state_bias_ref[...].astype(F32)
    state = jnp.zeros((NSTATE, conv_ref.shape[1]), F32)
    for chunk in range(count):
        rows = pl.ds(chunk * CHUNK, CHUNK)
        around = pl.ds(chunk * CHUNK, CHUNK + HALO)
        pre = taps(state_ref[around, :].astype(F32), state_kernel, state_bias, HALO - KERNEL + 1)
        conv, slope = silu_parts(pre)
        maps = conv.astype(BF16)
        maps_ref[rows, :] = maps
        state_slope_ref[rows, :] = slope
        pre = taps(value_ref[around, :].astype(F32), value_kernel, value_bias, HALO - KERNEL + 1)
        conv, slope = silu_parts(pre)
        conv = conv.astype(BF16)
        conv_ref[rows, :] = conv
        value_slope_ref[rows, :] = slope
        weighted = (conv.astype(F32) * f_ref[rows, :]).astype(BF16)
        weighted_ref[rows, :] = weighted
        factor = k_ref[chunk : chunk + 1, :]
        state = factor * (factor * state + dot_tn(maps[:, :NSTATE], weighted))
    total_ref[...] = state


def mixer_kernel(
    state_ref, maps_ref, weighted_ref, conv_ref, e_ref, k_ref, skip_ref, gate_ref, grad_ref, gain_ref,
    mixer_ref, stats_ref, high_ref, low_ref,
):
    count = conv_ref.shape[0] // CHUNK
    mask = lower_mask()
    lane = lax.broadcasted_iota(jnp.int32, (CHUNK, CHUNK), 1)
    state = state_ref[...]
    skip, gain = skip_ref[...], gain_ref[...].astype(F32)
    for chunk in range(count):
        rows = pl.ds(chunk * CHUNK, CHUNK)
        factor = k_ref[chunk : chunk + 1, :]
        input_map, output_map = maps_ref[rows, :NSTATE], maps_ref[rows, NSTATE:]
        weighted = weighted_ref[rows, :]
        scaled = factor * state
        high, low = split(scaled)
        high_ref[chunk], low_ref[chunk] = high, low
        scores = jnp.where(mask, dot_nt(output_map, input_map), 0.0).astype(BF16)
        mixed = dot(
            jnp.concatenate([scores, output_map], axis=1), jnp.concatenate([weighted, high], axis=0)
        )
        mixed = mixed + dot(output_map, low)
        mixer = e_ref[rows, :] * mixed + skip * conv_ref[rows, :].astype(F32)
        mixer_ref[rows, :] = mixer
        gate = gate_ref[rows, :]
        gated = mixer * (gate * jax.nn.sigmoid(gate))
        squares = jnp.sum(gated * gated, axis=1, keepdims=True)
        products = jnp.sum(gated * (grad_ref[rows, :] * gain), axis=1, keepdims=True)
        sums = jnp.where(lane == 0, squares, jnp.where(lane == 1, products, 0.0))
        stats_ref[:, chunk * CHUNK : (chunk + 1) * CHUNK] = sums.T[:8]
        state = factor * (scaled + dot_tn(input_map, weighted))


def gate_kernel(
    inner, stats_ref, mixer_ref, gate_ref, grad_ref, gain_ref, conv_ref, e_ref, k_ref, maps_ref,
    mixed_ref, gate_grad_ref, mixer_grad_ref, small_ref, total_ref,
):
    count, channels = conv_ref.shape[0] // CHUNK, conv_ref.shape[1]
    gain = gain_ref[...].astype(F32)
    state = jnp.zeros((NSTATE, channels), F32)
    gain_sum = jnp.zeros((1, channels), F32)
    skip_sum = jnp.zeros((1, channels), F32)
    for chunk in reversed(range(count)):
        rows = pl.ds(chunk * CHUNK, CHUNK)
        stats = stats_ref[:, chunk * CHUNK : (chunk + 1) * CHUNK]
        stats = jnp.concatenate([stats, jnp.zeros((CHUNK - 8, CHUNK), F32)], axis=0).T
        scale = lax.rsqrt(stats[:, 0:1] / inner + EPSILON)
        cross = stats[:, 1:2] * (scale * scale * scale) / inner
        gate = gate_ref[rows, :]
        silu, slope = silu_parts(gate)
        mixer = mixer_ref[rows, :]
        gated = mixer * silu
        normed = gated * scale
        mixed_ref[rows, :] = (normed * gain).astype(BF16)
        grad = grad_ref[rows, :]
        gain_sum = gain_sum + jnp.sum(grad * normed, axis=0, keepdims=True)
        gated_grad = scale * (grad * gain) - gated * cross
        gate_grad_ref[rows, :] = (gated_grad * mixer * slope).astype(BF16)
        mixer_grad = gated_grad * silu
        mixer_grad_ref[rows, :] = mixer_grad
        skip_sum = skip_sum + jnp.sum(mixer_grad * conv_ref[rows, :].astype(F32), axis=0, keepdims=True)
        high, low = split(e_ref[rows, :] * mixer_grad)
        output_map = maps_ref[rows, NSTATE:]
        factor = k_ref[chunk : chunk + 1, :]
        state = factor * (factor * state + (dot_tn(output_map, high) + dot_tn(output_map, low)))
    line = lax.broadcasted_iota(jnp.int32, (8, channels), 0)
    small_ref[...] = jnp.where(line == 0, gain_sum, jnp.where(line == 1, skip_sum, 0.0))
    total_ref[...] = state


def back_kernel(
    state_ref, mixer_grad_ref, e_ref, f_ref, k_ref, weighted_ref, high_ref, low_ref, maps_ref,
    value_slope_ref, state_slope_ref, skip_ref,
    value_ref, map_ref,
):
    count = weighted_ref.shape[0] // CHUNK
    lower = lower_mask()
    upper = jnp.logical_not(lower) | (
        lax.broadcasted_iota(jnp.int32, (CHUNK, CHUNK), 0)
        == lax.broadcasted_iota(jnp.int32, (CHUNK, CHUNK), 1)
    )
    state = state_ref[...]
    skip = skip_ref[...]
    for chunk in reversed(range(count)):
        rows = pl.ds(chunk * CHUNK, CHUNK)
        factor = k_ref[chunk : chunk + 1, :]
        input_map, output_map = maps_ref[rows, :NSTATE], maps_ref[rows, NSTATE:]
        weighted = weighted_ref[rows, :]
        mixer_grad = mixer_grad_ref[rows, :]
        high, low = split(e_ref[rows, :] * mixer_grad)
        scaled = factor * state
        state_high, state_low = split(scaled)
        both = jnp.concatenate([weighted, high_ref[chunk]], axis=0)
        sums = dot_nt(high, both) + dot_nt(low, both)
        score_grad = jnp.where(lower, sums[:, :CHUNK], 0.0).astype(BF16)
        output_grad = sums[:, CHUNK:] + dot_nt(high, low_ref[chunk]) + dot(score_grad, input_map)
        sums = dot_nt(weighted, jnp.concatenate([state_high, state_low], axis=0))
        input_grad = sums[:, :NSTATE] + sums[:, NSTATE:] + dot_tn(score_grad, output_map)
        scores = jnp.where(upper, dot_nt(input_map, output_map), 0.0).astype(BF16)
        grads = dot(
            jnp.concatenate([scores, input_map], axis=1), jnp.concatenate([high, state_high], axis=0)
        )
        value_ref[rows, :] = (f_ref[rows, :] * grads + skip * mixer_grad) * value_slope_ref[rows, :]
        slope = state_slope_ref[rows, :]
        map_ref[rows, :NSTATE] = input_grad * slope[:, :NSTATE]
        map_ref[rows, NSTATE:] = output_grad * slope[:, NSTATE:]
        state = factor * (scaled + (dot_tn(output_map, high) + dot_tn(output_map, low)))


def conv_back_kernel(
    value_ref, value_after_ref, state_ref, state_after_ref, value_raw_ref, state_raw_ref,
    value_kernel_ref, state_kernel_ref,
    value_grad_ref, state_grad_ref, value_small_ref, state_small_ref,
):
    def back(slope_ref, after_ref, raw_ref, kernel_ref, grad_ref, small_ref):
        count, channels = slope_ref.shape[0] // CHUNK, slope_ref.shape[1]
        kernel = kernel_ref[...].astype(F32)
        sums = [jnp.zeros((1, channels), F32) for _ in range(KERNEL + 1)]
        for chunk in range(count):
            rows = pl.ds(chunk * CHUNK, CHUNK)
            slope = slope_ref[rows, :]
            if chunk + 1 < count:
                after = slope_ref[pl.ds((chunk + 1) * CHUNK, 8), :]
            else:
                after = after_ref[...]
            window = jnp.concatenate([slope, after], axis=0)
            raw = raw_ref[pl.ds(chunk * CHUNK, CHUNK + HALO), :].astype(F32)
            grad = jnp.zeros_like(slope)
            for offset in range(KERNEL):
                back_by = KERNEL - 1 - offset
                grad = grad + kernel[offset : offset + 1] * window[back_by : back_by + CHUNK]
                begin = HALO - KERNEL + 1 + offset
                sums[offset] = sums[offset] + jnp.sum(
                    slope * raw[begin : begin + CHUNK], axis=0, keepdims=True
                )
            sums[KERNEL] = sums[KERNEL] + jnp.sum(slope, axis=0, keepdims=True)
            grad_ref[rows, :] = grad.astype(BF16)
        line = lax.broadcasted_iota(jnp.int32, (8, channels), 0)
        small = jnp.zeros((8, channels), F32)
        for place, value in enumerate(sums):
            small = jnp.where(line == place, value, small)
        small_ref[...] = small

    back(state_ref, state_after_ref, state_raw_ref, state_kernel_ref, state_grad_ref, state_small_ref)
    back(value_ref, value_after_ref, value_raw_ref, value_kernel_ref, value_grad_ref, value_small_ref)


def store_piece(core_ref, kept_ref, given_ref, place, piece):
    chips = kept_ref.shape[0]
    core, chip = divmod(place, chips)
    piece = piece.astype(BF16)

    @pl.when(core_ref[0] == core)
    def _():
        kept_ref[chip] = piece

    @pl.when(core_ref[0] != core)
    def _():
        given_ref[chip] = piece


def early_kernel(core_ref, normed_ref, gate_ref, mixed_ref, grad_ref, kept_ref, given_ref, held_ref):
    chips, rows, channels = kept_ref.shape
    width = normed_ref.shape[1]
    pieces = 2 * chips
    step = width // pieces
    out_rows = channels // pieces
    for begin in range(0, channels, BLOCK):
        held_ref[begin : begin + BLOCK, :] = dot_tn(mixed_ref[:, begin : begin + BLOCK], grad_ref[...])
    for begin in range(0, width, BLOCK):
        block = dot_tn(normed_ref[:, begin : begin + BLOCK], gate_ref[...])
        for place in range(begin // step, (begin + BLOCK) // step):
            own = held_ref[place * out_rows : (place + 1) * out_rows, :]
            parts = [block[place * step - begin : (place + 1) * step - begin]]
            parts += [own[:, i : i + channels] for i in range(0, width, channels)]
            store_piece(core_ref, kept_ref, given_ref, place, jnp.concatenate(parts, axis=0))


def late_kernel(core_ref, normed_ref, value_ref, kept_ref, given_ref):
    chips = kept_ref.shape[0]
    width = normed_ref.shape[1]
    step = width // (2 * chips)
    for begin in range(0, width, BLOCK):
        block = dot_tn(normed_ref[:, begin : begin + BLOCK], value_ref[...])
        for place in range(begin // step, (begin + BLOCK) // step):
            piece = block[place * step - begin : (place + 1) * step - begin]
            store_piece(core_ref, kept_ref, given_ref, place, piece)


def early_out_kernel(core_ref, own_ref, other_ref, gate_ref, output_ref):
    chips, rows, channels = own_ref.shape
    width = gate_ref.shape[0]
    step = width // (2 * chips)
    out_rows = channels // (2 * chips)

    def write(core, source_ref):
        for chip in range(chips):
            place = core * chips + chip
            piece = source_ref[chip].astype(F32)
            gate_ref[place * step : (place + 1) * step, :] = piece[:step]
            output_ref[place * out_rows : (place + 1) * out_rows, :] = jnp.concatenate(
                [
                    piece[step + i * out_rows : step + (i + 1) * out_rows]
                    for i in range(width // channels)
                ],
                axis=1,
            )

    for core in range(2):
        pl.when(core_ref[0] == core)(functools.partial(write, core, own_ref))
        pl.when(core_ref[0] != core)(functools.partial(write, core, other_ref))


def late_out_kernel(core_ref, own_ref, other_ref, value_ref):
    chips, step, _ = own_ref.shape

    def write(core, source_ref):
        for chip in range(chips):
            place = core * chips + chip
            value_ref[place * step : (place + 1) * step, :] = source_ref[chip].astype(F32)

    for core in range(2):
        pl.when(core_ref[0] == core)(functools.partial(write, core, own_ref))
        pl.when(core_ref[0] != core)(functools.partial(write, core, other_ref))


def shared_kernel(
    head_ref, normed_ref, state_ref, gain_ref, map_small_ref, value_small_ref, gate_small_ref, out_ref
):
    width, channels, lanes = normed_ref.shape[1], value_small_ref.shape[1], out_ref.shape[1]
    for begin in range(0, width, BLOCK):
        out_ref[begin : begin + BLOCK, :] = dot_tn(normed_ref[:, begin : begin + BLOCK], state_ref[...])
    out_ref[width:, :] = jnp.zeros((out_ref.shape[0] - width, lanes), F32)
    out_ref[width : width + 8, :] = map_small_ref[...]
    begin = width + 8
    for i in range(0, width, lanes):
        out_ref[begin + i // lanes : begin + i // lanes + 1, :] = gain_ref[:, i : i + lanes]
    begin = begin + 8
    span = own_rows(channels)
    for head in range((out_ref.shape[0] - begin) // span):

        @pl.when(head_ref[0] == head)
        def _():
            for i in range(0, channels, 128):
                row = begin + head * span + (i // lanes) * 16
                column = i % lanes
                out_ref[row : row + 8, column : column + 128] = value_small_ref[:, i : i + 128]
                out_ref[row + 8 : row + 16, column : column + 128] = gate_small_ref[:, i : i + 128]


def own_rows(channels):
    return -(-channels // (2 * NSTATE)) * 16


def run(kernel, outs, args, name, flops, scalars=0, scratch=()):
    shapes = [jax.ShapeDtypeStruct(shape, kind) for shape, kind in outs]
    moved = sum(a.size * a.dtype.itemsize for a in args) + sum(
        s.size * s.dtype.itemsize for s in shapes
    )
    return pl.pallas_call(
        kernel,
        out_shape=shapes,
        in_specs=[pl.BlockSpec(memory_space=pltpu.SMEM)] * scalars
        + [pl.BlockSpec(memory_space=pltpu.VMEM)] * (len(args) - scalars),
        out_specs=[pl.BlockSpec(memory_space=pltpu.VMEM)] * len(outs),
        scratch_shapes=list(scratch),
        compiler_params=pltpu.CompilerParams(vmem_limit_bytes=VMEM_LIMIT),
        cost_estimate=pl.CostEstimate(flops=flops, bytes_accessed=moved, transcendentals=0),
        name=name,
    )(*args)


def per_device(
    tokens, decay_codes, norm_gain, gate_weight, value_weight, state_weight, value_kernel, value_bias,
    state_kernel, state_bias, skip_scale, gated_gain, output_weight, cotangent,
):
    tokens, decay_codes, cotangent = tokens[0], decay_codes[0], cotangent[0]
    count, own_width = tokens.shape
    heads = skip_scale.shape[0]
    channels = heads * HEAD_DIM
    head_size, chips = lax.axis_size("head"), lax.axis_size("chip")
    core, mine = lax.axis_index("core"), lax.axis_index("head")
    seq_size = 2 * chips
    width = own_width * head_size
    maps_width = 2 * NSTATE
    chunks = count // CHUNK
    core_index, head_index = core.astype(jnp.int32)[None], mine.astype(jnp.int32)[None]

    gathered = gather_all(tokens, "head")
    before = from_behind(tokens[-HALO:], 1)
    margin = gather_all(
        jnp.concatenate([before, jnp.broadcast_to(norm_gain[None], (HALO, own_width))], axis=0),
        "head",
    )
    logs = decay_codes.astype(F32) * (-DECAY_STEP)
    input_weight = jnp.sqrt(-jnp.expm1(2.0 * logs))
    e_full, f_full, factors = run(
        decay_kernel,
        [((count, channels), F32), ((count, channels), F32), ((8, channels), F32)],
        (decay_codes, input_weight),
        "decays",
        count * channels * 200,
    )
    all_logs = lax.all_to_all(
        jnp.broadcast_to(factors[None], (seq_size, 8, channels)), ("chip", "core"), 0, 0
    )[:, 7].reshape(chips, 2, channels)
    pair_logs = jnp.sum(all_logs, axis=1)
    own_logs = lax.dynamic_index_in_dim(all_logs, lax.axis_index("chip"), 0, keepdims=False)
    own_decay = jnp.exp(lax.dynamic_index_in_dim(own_logs, core, 0))
    other_decay = jnp.exp(lax.dynamic_index_in_dim(own_logs, 1 - core, 0))
    before_weights = decay_weights(pair_logs, False)
    after_weights = decay_weights(pair_logs, True)
    skip_full = jnp.repeat(skip_scale, HEAD_DIM)[None]

    margin_full = jnp.concatenate([margin[i] for i in range(head_size)], axis=1)
    full = jnp.concatenate([gathered[i] for i in range(head_size)], axis=1)
    full_cotangent = lax.all_gather(tie(cotangent, full), "head", axis=1, tiled=True)
    gain_full = margin_full[HALO].astype(F32)
    inputs_all = jnp.concatenate([margin_full[:HALO], full], axis=0).astype(F32)
    scale_all = lax.rsqrt(jnp.mean(inputs_all * inputs_all, axis=1, keepdims=True) + EPSILON)
    normed_all = (inputs_all * scale_all * gain_full).astype(BF16)
    normed, scale_in = normed_all[HALO:], scale_all[HALO:]
    value_raw = dot(normed_all, value_weight).astype(BF16)
    state_raw = dot(normed_all, state_weight).astype(BF16)
    conv, weighted, value_slope, maps, map_slope, local_end = run(
        conv_kernel,
        [
            ((count, channels), BF16),
            ((count, channels), BF16),
            ((count, channels), F32),
            ((count, maps_width), BF16),
            ((count, maps_width), F32),
            ((NSTATE, channels), F32),
        ],
        (
            value_raw, state_raw, value_kernel, value_bias[None], state_kernel, state_bias[None],
            f_full, factors,
        ),
        "conv",
        count * channels * 400,
    )
    state_in = entering(local_end, own_decay, other_decay, before_weights, False)
    gate_pre = dot(normed, gate_weight)
    mixed_grad = dot_nt(full_cotangent, output_weight)
    state_in = tie(state_in, gate_pre)
    mixer, stats, high, low = run(
        mixer_kernel,
        [
            ((count, channels), F32),
            ((8, count), F32),
            ((chunks, NSTATE, channels), BF16),
            ((chunks, NSTATE, channels), BF16),
        ],
        (
            state_in, maps, weighted, conv, e_full, factors, skip_full, gate_pre, mixed_grad,
            gated_gain[None],
        ),
        "mixer",
        count * channels * 1000,
    )
    stats = jnp.sum(gather_all(stats, "head"), axis=0)
    mixed, gate_grad, mixer_grad, gate_small, start_grad = run(
        functools.partial(gate_kernel, float(channels * head_size)),
        [
            ((count, channels), BF16),
            ((count, channels), BF16),
            ((count, channels), F32),
            ((8, channels), F32),
            ((NSTATE, channels), F32),
        ],
        (stats, mixer, gate_pre, mixed_grad, gated_gain[None], conv, e_full, factors, maps),
        "gate",
        count * channels * 600,
    )
    grad_after = entering(start_grad, own_decay, other_decay, after_weights, True)

    step, out_rows = width // seq_size, channels // seq_size
    rows = step + out_rows * (width // channels)
    early_kept, early_given = run(
        early_kernel,
        [((chips, rows, channels), BF16), ((chips, rows, channels), BF16)],
        (core_index, normed, gate_grad, mixed, full_cotangent),
        "early",
        4 * count * channels * width,
        scalars=1,
        scratch=[pltpu.VMEM((channels, width), F32)],
    )
    early_halves = chip_sums(early_kept, early_given)
    partial_out = dot(mixed, output_weight).astype(BF16)
    partial_out = jnp.stack(
        [partial_out[:, i * own_width : (i + 1) * own_width] for i in range(head_size)]
    )
    branch = jnp.sum(deal(partial_out, "head").astype(F32), axis=0)
    block_out = (tokens.astype(F32) + branch).astype(BF16)
    early = seq_sums(early_halves)

    value_grads, map_grads = run(
        back_kernel,
        [((count, channels), F32), ((count, maps_width), F32)],
        (
            tie(grad_after, (early_given, partial_out)), mixer_grad, e_full, f_full, factors,
            weighted, high, low, maps, value_slope, map_slope, skip_full,
        ),
        "back",
        count * channels * 2000,
    )
    after = from_behind(jnp.concatenate([value_grads[:8], map_grads[:8]], axis=1), -1)
    after = tie(after, early_halves)
    value_raw_grad, state_raw_grad, value_small, state_small = run(
        conv_back_kernel,
        [
            ((count, channels), BF16),
            ((count, maps_width), BF16),
            ((8, channels), F32),
            ((8, maps_width), F32),
        ],
        (
            value_grads, after[:, :channels], map_grads, after[:, channels:], value_raw, state_raw,
            value_kernel, state_kernel,
        ),
        "conv_back",
        count * channels * 100,
    )
    late_kept, late_given = run(
        late_kernel,
        [((chips, step, channels), BF16), ((chips, step, channels), BF16)],
        (core_index, normed, value_raw_grad),
        "late",
        2 * count * channels * width,
        scalars=1,
    )
    late_halves = chip_sums(late_kept, late_given)
    normed_part = (
        dot_nt(gate_grad, gate_weight)
        + dot_nt(value_raw_grad, value_weight)
        + dot_nt(state_raw_grad, state_weight)
    )
    inputs = full.astype(F32)
    cross_part = jnp.sum(inputs * gain_full * normed_part, axis=1)
    gain_part = jnp.sum(normed_part * inputs * scale_in, axis=0)
    normed_low = normed_part.astype(BF16)
    normed_low = jnp.stack(
        [normed_low[:, i * own_width : (i + 1) * own_width] for i in range(head_size)]
    )
    normed_grad = jnp.sum(deal(normed_low, "head").astype(F32), axis=0)
    cross_sum = jnp.sum(
        gather_all(jnp.broadcast_to(cross_part[None], (8, count)), "head")[:, 0], axis=0
    )
    late = seq_sums(late_halves)
    span = own_rows(channels)
    shared_rows = width + 16 + head_size * span
    shared = run(
        shared_kernel,
        [((shared_rows, maps_width), F32)],
        (
            head_index, normed, state_raw_grad, gain_part[None], state_small, value_small, gate_small
        ),
        "shared",
        2 * count * maps_width * width,
        scalars=1,
    )[0]
    shared = lax.psum(shared, ("chip", "core", "head"))
    early_other = beside(early)
    gate_weight_gradient, output_weight_gradient = run(
        early_out_kernel,
        [((width, channels), F32), ((channels, width), F32)],
        (core_index, early, early_other),
        "early_out",
        4 * channels * width,
        scalars=1,
    )
    value_weight_gradient = run(
        late_out_kernel,
        [((width, channels), F32)],
        (core_index, late, beside(late)),
        "late_out",
        2 * channels * width,
        scalars=1,
    )[0]
    state_weight_gradient = shared[:width]
    map_small = shared[width : width + 8]
    state_kernel_gradient, state_bias_gradient = map_small[:KERNEL], map_small[KERNEL]
    norm_gain_gradient = lax.dynamic_slice_in_dim(
        shared[width + 8 : width + 8 + width // maps_width].reshape(width), mine * own_width,
        own_width, 0,
    )
    own_small = lax.dynamic_slice_in_dim(shared, width + 16 + mine * span, span, 0)
    own_small = own_small.reshape(span // 16, 16, maps_width)
    own_small = jnp.moveaxis(own_small, 0, 1).reshape(16, -1)[:, :channels]
    value_kernel_gradient, value_bias_gradient = own_small[:KERNEL], own_small[KERNEL]
    gated_gain_gradient = own_small[8]
    skip_scale_gradient = jnp.sum(own_small[9].reshape(heads, HEAD_DIM), axis=1)

    tokens_gradient = (
        scale_in * norm_gain.astype(F32) * normed_grad
        - tokens.astype(F32) * scale_in**3 * (cross_sum / width)[:, None]
        + cotangent.astype(F32)
    ).astype(BF16)
    return (
        block_out[None],
        tokens_gradient[None],
        norm_gain_gradient,
        gate_weight_gradient,
        value_weight_gradient,
        state_weight_gradient,
        value_kernel_gradient,
        value_bias_gradient,
        state_kernel_gradient,
        state_bias_gradient,
        skip_scale_gradient,
        gated_gain_gradient,
        output_weight_gradient,
    )


def solution(mesh):
    seq_size, head_size = mesh.shape["seq"], mesh.shape["head"]
    mesh = Mesh(mesh.devices.reshape(seq_size // 2, 2, head_size), ("chip", "core", "head"))
    seq = ("chip", "core")
    in_specs = (
        P(None, seq, "head"),
        P(None, seq, "head"),
        P("head"),
        P(None, "head"),
        P(None, "head"),
        P(),
        P(None, "head"),
        P("head"),
        P(),
        P(),
        P("head"),
        P("head"),
        P("head", None),
        P(None, seq, "head"),
    )
    out_specs = (
        P(None, seq, "head"),
        P(None, seq, "head"),
        P("head"),
        P(None, "head"),
        P(None, "head"),
        P(),
        P(None, "head"),
        P("head"),
        P(),
        P(),
        P("head"),
        P("head"),
        P("head", None),
    )
    return jax.shard_map(
        per_device, mesh=mesh, in_specs=in_specs, out_specs=out_specs, check_vma=False
    )
```

```python
import functools

import jax
import jax.numpy as jnp
from jax import lax
from jax.experimental import pallas as pl
from jax.experimental.pallas import tpu as pltpu
from jax.sharding import Mesh
from jax.sharding import PartitionSpec as P

HEAD_DIM = 64
NSTATE = 128
KERNEL = 4
CHUNK = 128
BLOCK = 384
VMEM_LIMIT = 20 * 1024 * 1024
HALO = 16


DECAY_STEP = 1.0 / 1048576.0
EPSILON = 1e-05
BF16 = jnp.bfloat16
F32 = jnp.float32


def from_behind(value, by):
    axis = ("chip", "core")
    size = lax.axis_size("chip") * 2
    pairs = [(i, i + by) for i in range(size) if 0 <= i + by < size]
    return lax.ppermute(value, axis, pairs)


def beside(value):
    return lax.ppermute(value, "core", [(0, 1), (1, 0)])


def turn(value, axis, by):
    size = lax.axis_size(axis)
    return lax.ppermute(value, axis, [(i, (i + by) % size) for i in range(size)])


def turn_all(value, axis):
    return [value] + [turn(value, axis, by) for by in range(1, lax.axis_size(axis))]


def cross(value, bits):
    return lax.ppermute(value, "chip", [(i, i ^ bits) for i in range(lax.axis_size("chip"))])


def cross_all(value):
    return [value] + [cross(value, bits) for bits in range(1, lax.axis_size("chip"))]


def butterfly(value, axis):
    bits = 1
    while bits < lax.axis_size(axis):
        size = lax.axis_size(axis)
        value = value + lax.ppermute(value, axis, [(i, i ^ bits) for i in range(size)])
        bits *= 2
    return value


def decay_weights(logs, backward):
    chips, mine = lax.axis_size("chip"), lax.axis_index("chip")
    place = jnp.arange(chips) ^ mine
    source, middle = place[:, None], place[None, :]
    if backward:
        between, passes = (middle < source) & (middle > mine), source > mine
    else:
        between, passes = (middle > source) & (middle < mine), source < mine
    spans = jnp.sum(jnp.where(between[:, :, None], logs[None], 0.0), axis=1)
    return jnp.where(passes, jnp.exp(spans), 0.0)


def entering(total, own_decay, other_decay, weights, backward):
    core = lax.axis_index("core")
    receives = core == (0 if backward else 1)
    half = total.shape[0] // 2
    partner = beside(total)
    part = lambda value: lax.dynamic_slice_in_dim(value, core * half, half, 0)
    pair = jnp.where(
        receives,
        own_decay * part(partner) + part(total),
        other_decay * part(total) + part(partner),
    )
    prefix = jnp.zeros_like(pair)
    for bits in range(1, lax.axis_size("chip")):
        prefix = prefix + cross(pair, bits) * weights[bits : bits + 1]
    other = beside(prefix)
    whole = jnp.where(
        core == 0,
        jnp.concatenate([prefix, other], axis=0),
        jnp.concatenate([other, prefix], axis=0),
    )
    return jnp.where(receives, other_decay * whole + partner, whole), pair


def dot(left, right):
    return jnp.dot(left, right, preferred_element_type=F32)


def dot_nt(left, right):
    return lax.dot_general(left, right, (((1,), (1,)), ((), ())), preferred_element_type=F32)


def dot_tn(left, right):
    return lax.dot_general(left, right, (((0,), (0,)), ((), ())), preferred_element_type=F32)


def split(values):
    high = values.astype(BF16)
    return high, (values - high.astype(F32)).astype(BF16)


def lower_mask():
    row = lax.broadcasted_iota(jnp.int32, (CHUNK, CHUNK), 0)
    column = lax.broadcasted_iota(jnp.int32, (CHUNK, CHUNK), 1)
    return row >= column


def decay_kernel(codes_ref, weight_ref, e_ref, f_ref, k_ref):
    heads, channels = codes_ref.shape[1], e_ref.shape[1]
    row = lax.broadcasted_iota(jnp.int32, (heads, channels), 0)
    column = lax.broadcasted_iota(jnp.int32, (heads, channels), 1)
    first = row * HEAD_DIM
    spread = jnp.where((column >= first) & (column < first + HEAD_DIM), 1.0, 0.0).astype(BF16)

    def expand(values):
        high, low = split(values)
        return dot(high, spread) + dot(low, spread)

    lower = jnp.where(lower_mask(), 1.0, 0.0).astype(F32)
    count = codes_ref.shape[0] // CHUNK
    line = lax.broadcasted_iota(jnp.int32, (8, heads), 0)
    marks = jnp.zeros((8, heads), F32)
    total = jnp.zeros((1, heads), F32)
    for chunk in range(count):
        rows = pl.ds(chunk * CHUNK, CHUNK)
        logs = codes_ref[rows, :].astype(F32) * (-DECAY_STEP)
        cumulative = jnp.dot(
            lower, logs, precision=lax.Precision.HIGHEST, preferred_element_type=F32
        )
        last = cumulative[CHUNK - 1 :]
        middle = 0.5 * last
        e_ref[rows, :] = expand(jnp.exp(cumulative - middle))
        f_ref[rows, :] = expand(weight_ref[rows, :] * jnp.exp(middle - cumulative))
        marks = jnp.where(line == chunk, jnp.exp(middle), marks)
        total = total + last
    marks = jnp.where(line == 7, total, marks)
    high, low = split(marks)
    lowest = (marks - high.astype(F32) - low.astype(F32)).astype(BF16)
    k_ref[...] = dot(high, spread) + dot(low, spread) + dot(lowest, spread)


def taps(window, kernel, bias, begin):
    summed = bias
    for offset in range(KERNEL):
        summed = summed + kernel[offset : offset + 1] * window[begin + offset : begin + offset + CHUNK]
    return summed


def silu_parts(values):
    sigmoid = jax.nn.sigmoid(values)
    return values * sigmoid, sigmoid * (1.0 + values * (1.0 - sigmoid))


def first_step(action):
    pl.when(pl.program_id(0) == 0)(action)


def clear(*refs):
    def action():
        for ref in refs:
            ref[...] = jnp.zeros_like(ref)

    first_step(action)


def place_parts(mine, parts, target, width, value):
    size = len(parts)
    if width % 128 == 0:
        for i in range(size):
            owner = lax.rem(mine + size - i, size)
            target[:, pl.ds(pl.multiple_of(owner * width, 128), width)] = value(i)
        return

    def write(me):
        for i in range(size):
            owner = (me + size - i) % size
            target[:, owner * width : (owner + 1) * width] = value(i)

    for me in range(size):
        pl.when(mine == me)(functools.partial(write, me))


def norm_kernel(size, head_ref, *refs):
    parts, margins, (own_ref,) = refs[:size], refs[size : 2 * size], refs[2 * size : 2 * size + 1]
    normed_ref, full_ref, gain_ref, scale_ref, copy_ref = refs[2 * size + 1 : 2 * size + 6]
    head_normed, = refs[2 * size + 6 :]
    width = parts[0].shape[1]
    mine = head_ref[0]

    def scale_of(refs, rows):
        squares = sum(jnp.sum(ref[:rows].astype(F32) ** 2, axis=1, keepdims=True) for ref in refs)
        return lax.rsqrt(squares / (size * width) + EPSILON)

    scale = scale_of(parts, parts[0].shape[0])
    scale_ref[...] = jnp.broadcast_to(scale, scale_ref.shape)
    ahead = scale_of(margins, HALO)
    gain = lambda i: margins[i][HALO : HALO + 1, :].astype(F32)
    place_parts(
        mine, margins, head_normed, width,
        lambda i: (margins[i][:HALO].astype(F32) * ahead * gain(i)).astype(BF16),
    )
    place_parts(
        mine, parts, normed_ref.at[HALO:], width,
        lambda i: (parts[i][...].astype(F32) * scale_ref[:, 0:1] * gain(i)).astype(BF16),
    )
    normed_ref[:HALO, :] = head_normed[...]
    place_parts(mine, parts, full_ref, width, lambda i: parts[i][...])
    place_parts(
        mine, margins, gain_ref, width, lambda i: jnp.broadcast_to(gain(i), (8, width))
    )
    copy_ref[...] = own_ref[...]


def place_kernel(head_ref, *refs):
    parts, target = refs[:-1], refs[-1]
    place_parts(head_ref[0], parts, target, parts[0].shape[1], lambda i: parts[i][...])


def conv_kernel(
    value_ref, state_ref, value_kernel_ref, value_bias_ref, state_kernel_ref, state_bias_ref,
    f_ref, k_ref, conv_ref, weighted_ref, value_slope_ref, maps_ref, state_slope_ref, total_ref,
):
    chunk = pl.program_id(0)
    clear(total_ref)
    around = pl.ds(pl.multiple_of(chunk * CHUNK, CHUNK), CHUNK + HALO)
    pre = taps(
        state_ref[around, :].astype(F32), state_kernel_ref[...].astype(F32),
        state_bias_ref[...].astype(F32), HALO - KERNEL + 1,
    )
    conv, slope = silu_parts(pre)
    maps = conv.astype(BF16)
    maps_ref[...] = maps
    state_slope_ref[...] = slope
    pre = taps(
        value_ref[around, :].astype(F32), value_kernel_ref[...].astype(F32),
        value_bias_ref[...].astype(F32), HALO - KERNEL + 1,
    )
    conv, slope = silu_parts(pre)
    conv = conv.astype(BF16)
    conv_ref[...] = conv
    value_slope_ref[...] = slope
    weighted = (conv.astype(F32) * f_ref[...]).astype(BF16)
    weighted_ref[...] = weighted
    factor = k_ref[pl.ds(chunk, 1), :]
    total_ref[...] = factor * (factor * total_ref[...] + dot_tn(maps[:, :NSTATE], weighted))


def mixer_kernel(
    state_in_ref, maps_ref, weighted_ref, conv_ref, e_ref, k_ref, skip_ref, gate_ref, grad_ref, gain_ref,
    mixer_ref, stats_ref, high_ref, low_ref, state_ref,
):
    chunk = pl.program_id(0)

    def start():
        state_ref[...] = state_in_ref[...]

    first_step(start)
    lane = lax.broadcasted_iota(jnp.int32, (CHUNK, CHUNK), 1)
    factor = k_ref[pl.ds(chunk, 1), :]
    input_map, output_map = maps_ref[:, :NSTATE], maps_ref[:, NSTATE:]
    weighted = weighted_ref[...]
    scaled = factor * state_ref[...]
    high, low = split(scaled)
    high_ref[0], low_ref[0] = high, low
    scores = jnp.where(lower_mask(), dot_nt(output_map, input_map), 0.0).astype(BF16)
    mixed = dot(
        jnp.concatenate([scores, output_map], axis=1), jnp.concatenate([weighted, high], axis=0)
    )
    mixed = mixed + dot(output_map, low)
    mixer = e_ref[...] * mixed + skip_ref[...] * conv_ref[...].astype(F32)
    mixer_ref[...] = mixer
    gate = gate_ref[...]
    gated = mixer * (gate * jax.nn.sigmoid(gate))
    squares = jnp.sum(gated * gated, axis=1, keepdims=True)
    products = jnp.sum(gated * (grad_ref[...] * gain_ref[...].astype(F32)), axis=1, keepdims=True)
    sums = jnp.where(lane == 0, squares, jnp.where(lane == 1, products, 0.0))
    stats_ref[...] = sums.T[:8]
    state_ref[...] = factor * (scaled + dot_tn(input_map, weighted))


def column(row_block):
    rest = jnp.zeros((CHUNK - row_block.shape[0], CHUNK), F32)
    return jnp.concatenate([row_block, rest], axis=0).T


def gate_kernel(
    inner, chunks, size, *refs
):
    stats_refs = refs[:size]
    (
        mixer_ref, gate_ref, grad_ref, gain_ref, conv_ref, e_ref, k_ref, maps_ref,
        mixed_ref, gate_grad_ref, mixer_grad_ref, small_ref, total_ref,
    ) = refs[size:]
    chunk = chunks - 1 - pl.program_id(0)
    clear(small_ref, total_ref)
    gain = gain_ref[...].astype(F32)
    stats = column(sum(ref[...] for ref in stats_refs))
    scale = lax.rsqrt(stats[:, 0:1] / inner + EPSILON)
    cross_term = stats[:, 1:2] * (scale * scale * scale) / inner
    silu, slope = silu_parts(gate_ref[...])
    mixer = mixer_ref[...]
    gated = mixer * silu
    normed = gated * scale
    mixed_ref[...] = (normed * gain).astype(BF16)
    grad = grad_ref[...]
    gated_grad = scale * (grad * gain) - gated * cross_term
    gate_grad_ref[...] = (gated_grad * mixer * slope).astype(BF16)
    mixer_grad = gated_grad * silu
    mixer_grad_ref[...] = mixer_grad
    small_ref[0:1, :] += jnp.sum(grad * normed, axis=0, keepdims=True)
    small_ref[1:2, :] += jnp.sum(mixer_grad * conv_ref[...].astype(F32), axis=0, keepdims=True)
    high, low = split(e_ref[...] * mixer_grad)
    output_map = maps_ref[:, NSTATE:]
    factor = k_ref[pl.ds(chunk, 1), :]
    total_ref[...] = factor * (
        factor * total_ref[...] + (dot_tn(output_map, high) + dot_tn(output_map, low))
    )


def back_kernel(
    chunks, after_ref, state_in_ref, mixer_grad_ref, e_ref, f_ref, k_ref, weighted_ref, high_ref, low_ref,
    maps_ref, value_slope_ref, state_slope_ref, skip_ref,
    value_ref, map_ref, state_ref,
):
    chunk = chunks - 1 - pl.program_id(0)

    def start():
        state_ref[...] = state_in_ref[...]

    first_step(start)
    lower = lower_mask()
    row = lax.broadcasted_iota(jnp.int32, (CHUNK, CHUNK), 0)
    upper = row <= lax.broadcasted_iota(jnp.int32, (CHUNK, CHUNK), 1)
    factor = k_ref[pl.ds(chunk, 1), :]
    input_map, output_map = maps_ref[:, :NSTATE], maps_ref[:, NSTATE:]
    weighted = weighted_ref[...]
    mixer_grad = mixer_grad_ref[...]
    high, low = split(e_ref[...] * mixer_grad)
    scaled = factor * state_ref[...]
    state_high, state_low = split(scaled)
    both = jnp.concatenate([weighted, high_ref[0]], axis=0)
    sums = dot_nt(high, both) + dot_nt(low, both)
    score_grad = jnp.where(lower, sums[:, :CHUNK], 0.0).astype(BF16)
    output_grad = sums[:, CHUNK:] + dot_nt(high, low_ref[0]) + dot(score_grad, input_map)
    sums = dot_nt(weighted, jnp.concatenate([state_high, state_low], axis=0))
    input_grad = sums[:, :NSTATE] + sums[:, NSTATE:] + dot_tn(score_grad, output_map)
    scores = jnp.where(upper, dot_nt(input_map, output_map), 0.0).astype(BF16)
    grads = dot(
        jnp.concatenate([scores, input_map], axis=1), jnp.concatenate([high, state_high], axis=0)
    )
    value_ref[...] = (f_ref[...] * grads + skip_ref[...] * mixer_grad) * value_slope_ref[...]
    slope = state_slope_ref[...]
    map_ref[:, :NSTATE] = input_grad * slope[:, :NSTATE]
    map_ref[:, NSTATE:] = output_grad * slope[:, NSTATE:]
    state_ref[...] = factor * (scaled + (dot_tn(output_map, high) + dot_tn(output_map, low)))


def conv_back_kernel(
    chunks, other_ref, value_ref, map_ref, after_ref, value_raw_ref, state_raw_ref, value_kernel_ref,
    state_kernel_ref,
    value_grad_ref, state_grad_ref, value_small_ref, state_small_ref, value_next_ref, state_next_ref,
):
    chunk = chunks - 1 - pl.program_id(0)
    channels = value_ref.shape[1]
    clear(value_small_ref, state_small_ref)

    def start():
        value_next_ref[...] = after_ref[:, :channels]
        state_next_ref[...] = after_ref[:, channels:]

    first_step(start)

    def back(slope_ref, next_ref, raw_ref, kernel_ref, grad_ref, small_ref):
        kernel = kernel_ref[...].astype(F32)
        slope = slope_ref[...]
        window = jnp.concatenate([slope, next_ref[...]], axis=0)
        around = pl.ds(pl.multiple_of(chunk * CHUNK, CHUNK), CHUNK + HALO)
        raw = raw_ref[around, :].astype(F32)
        grad = jnp.zeros_like(slope)
        for offset in range(KERNEL):
            back_by = KERNEL - 1 - offset
            grad = grad + kernel[offset : offset + 1] * window[back_by : back_by + CHUNK]
            begin = HALO - KERNEL + 1 + offset
            small_ref[offset : offset + 1, :] += jnp.sum(
                slope * raw[begin : begin + CHUNK], axis=0, keepdims=True
            )
        small_ref[KERNEL : KERNEL + 1, :] += jnp.sum(slope, axis=0, keepdims=True)
        grad_ref[...] = grad.astype(BF16)
        next_ref[...] = slope[:8]

    back(map_ref, state_next_ref, state_raw_ref, state_kernel_ref, state_grad_ref, state_small_ref)
    back(value_ref, value_next_ref, value_raw_ref, value_kernel_ref, value_grad_ref, value_small_ref)


def store_part(mine, outs, owner, value):
    size = len(outs)
    for i in range(size):

        @pl.when(lax.rem(owner - mine + size, size) == i)
        def _(i=i):
            outs[i][...] = value


def out_kernel(size, pair_ref, head_ref, mixed_ref, weight_ref, *outs):
    width = outs[0].shape[1]
    for owner in range(size):
        value = dot(mixed_ref[...], weight_ref[:, owner * width : (owner + 1) * width])
        store_part(head_ref[0], outs, owner, value.astype(BF16))


def normed_kernel(
    size, head_ref, gate_grad_ref, value_grad_ref, state_grad_ref, gate_weight_ref, value_weight_ref,
    state_weight_ref, full_ref, gain_ref, scale_ref, *refs
):
    outs, gain_part_ref, cross_ref = refs[:size], refs[size], refs[size + 1]
    count, width = full_ref.shape[0], full_ref.shape[1] // size
    scale = scale_ref[:, 0:1]
    crossed = jnp.zeros((count, 1), F32)
    for owner in range(size):
        own = slice(owner * width, (owner + 1) * width)
        value = (
            dot_nt(gate_grad_ref[...], gate_weight_ref[own, :])
            + dot_nt(value_grad_ref[...], value_weight_ref[own, :])
            + dot_nt(state_grad_ref[...], state_weight_ref[own, :])
        )
        weighed = value * full_ref[:, own].astype(F32)
        crossed = crossed + jnp.sum(weighed * gain_ref[0:1, own], axis=1, keepdims=True)
        gain_part_ref[0:1, own] = jnp.sum(weighed * scale, axis=0, keepdims=True)
        value = value.astype(BF16)
        for i in range(size):

            @pl.when(lax.rem(owner - head_ref[0] + size, size) == i)
            def _(i=i, value=value):
                outs[i][:count, :] = value

    chunks = count // CHUNK
    line = lax.broadcasted_iota(jnp.int32, (HALO, CHUNK), 0)
    lane = lax.broadcasted_iota(jnp.int32, (CHUNK, CHUNK), 1)
    packed = jnp.zeros((HALO, CHUNK), F32)
    for chunk in range(chunks):
        sums = crossed[chunk * CHUNK : (chunk + 1) * CHUNK]
        row = jnp.where(lane == 0, sums, 0.0).T[0:1]
        high = row.astype(BF16).astype(F32)
        packed = jnp.where(line == chunk, high, packed)
        packed = jnp.where(line == chunks + chunk, row - high, packed)
    for i in range(size):
        outs[i][count:, :] = jnp.zeros_like(outs[i][count:, :])
        outs[i][count:, :CHUNK] = packed.astype(BF16)


def last_kernel(size, full_width, *refs):
    parts, (tokens_ref, scale_ref, gain_ref, cotangent_ref, out_ref) = refs[:size], refs[size:]
    count = tokens_ref.shape[0]
    chunks = count // CHUNK
    crossed = sum(ref[count:, :CHUNK].astype(F32) for ref in parts)
    crossed = crossed[:chunks] + crossed[chunks : 2 * chunks]
    for chunk in range(chunks):
        rows = slice(chunk * CHUNK, (chunk + 1) * CHUNK)
        normed_grad = sum(ref[rows, :].astype(F32) for ref in parts)
        scale = scale_ref[rows, 0:1]
        total = column(jnp.broadcast_to(crossed[chunk : chunk + 1], (8, CHUNK)))[:, 0:1]
        out_ref[rows, :] = (
            scale * gain_ref[...].astype(F32) * normed_grad
            - tokens_ref[rows, :].astype(F32) * (scale * scale * scale * total / full_width)
            + cotangent_ref[rows, :].astype(F32)
        ).astype(BF16)


def store_piece(core_ref, kept_ref, given_ref, place, piece):
    chips = kept_ref.shape[0]
    core, chip = divmod(place, chips)
    piece = piece.astype(BF16)

    @pl.when(core_ref[0] == core)
    def _():
        kept_ref[chip] = piece

    @pl.when(core_ref[0] != core)
    def _():
        given_ref[chip] = piece


def early_kernel(
    pair_ref, core_ref, normed_ref, gate_ref, mixed_ref, grad_ref, kept_ref, given_ref, held_ref
):
    chips, rows, channels = kept_ref.shape
    width = normed_ref.shape[1]
    pieces = 2 * chips
    step = width // pieces
    out_rows = channels // pieces
    for begin in range(0, channels, BLOCK):
        held_ref[begin : begin + BLOCK, :] = dot_tn(mixed_ref[:, begin : begin + BLOCK], grad_ref[...])
    for begin in range(0, width, BLOCK):
        block = dot_tn(normed_ref[HALO:, begin : begin + BLOCK], gate_ref[...])
        for place in range(begin // step, (begin + BLOCK) // step):
            own = held_ref[place * out_rows : (place + 1) * out_rows, :]
            parts = [block[place * step - begin : (place + 1) * step - begin]]
            parts += [own[:, i : i + channels] for i in range(0, width, channels)]
            store_piece(core_ref, kept_ref, given_ref, place, jnp.concatenate(parts, axis=0))


def late_kernel(
    core_ref, normed_ref, value_ref, state_ref, value_small_ref, gate_small_ref, gain_ref,
    state_small_ref, kept_ref, given_ref, own_ref, shared_ref,
):
    chips, rows, channels = kept_ref.shape
    width, maps_width = normed_ref.shape[1], state_ref.shape[1]
    pieces = 2 * chips
    step = width // pieces
    lanes = channels // 128
    own_ref[...] = jnp.zeros_like(own_ref)
    own_ref[: KERNEL + 1, :] = value_small_ref[: KERNEL + 1, :]
    own_ref[KERNEL + 1 : KERNEL + 3, :] = gate_small_ref[:2, :]
    shared_ref[...] = jnp.zeros_like(shared_ref)
    for i in range(width // channels):
        shared_ref[i : i + 1, :] = gain_ref[0:1, i * channels : (i + 1) * channels]
    begin = width // channels
    for i in range(0, (KERNEL + 1) * maps_width, 128):
        tap, column_from = divmod(i, maps_width)
        row, column_to = divmod(i, channels)
        shared_ref[begin + row : begin + row + 1, column_to : column_to + 128] = state_small_ref[
            tap : tap + 1, column_from : column_from + 128
        ]
    line = lax.broadcasted_iota(jnp.int32, (HALO, channels), 0)
    for begin in range(0, width, BLOCK):
        columns = normed_ref[HALO:, begin : begin + BLOCK]
        value = dot_tn(columns, value_ref[...])
        state = dot_tn(columns, state_ref[...])
        for place in range(begin // step, (begin + BLOCK) // step):
            piece = slice(place * step - begin, (place + 1) * step - begin)
            stacked = jnp.concatenate([state[piece, :128], state[piece, 128:]], axis=0)
            part = 2 * step // lanes
            stacked = jnp.concatenate(
                [stacked[i * part : (i + 1) * part] for i in range(lanes)], axis=1
            )
            own, shared = own_ref[place : place + 1, :], shared_ref[place : place + 1, :]
            own_high, shared_high = (v.astype(BF16).astype(F32) for v in (own, shared))
            small = jnp.zeros((HALO, channels), F32)
            for at, line_value in enumerate((own_high, own - own_high, shared_high, shared - shared_high)):
                small = jnp.where(line == at, line_value, small)
            store_piece(
                core_ref, kept_ref, given_ref, place,
                jnp.concatenate([value[piece], stacked, small], axis=0),
            )


def merge_pairs(block):
    tail = block[-HALO:]
    line = lax.broadcasted_iota(jnp.int32, tail.shape, 0)
    own, shared = tail[0:1] + tail[1:2], tail[2:3] + tail[3:4]
    own_high, shared_high = own.astype(BF16).astype(F32), shared.astype(BF16).astype(F32)
    new = jnp.zeros_like(tail)
    for at, value in enumerate((own_high, own - own_high, shared_high, shared - shared_high)):
        new = jnp.where(line == at, value, new)
    return jnp.concatenate([block[:-HALO], new], axis=0)


def half_kernel(paired, chips, chip_ref, kept_ref, arrived_ref, *outs):
    for bits in range(chips):
        place = lax.bitwise_xor(chip_ref[0], bits)
        value = kept_ref[place].astype(F32) + arrived_ref[place].astype(F32)
        if paired:
            value = merge_pairs(value)
        outs[bits][...] = value.astype(outs[bits].dtype)


def piece_kernel(parts, value_rows, *refs):
    total = sum(ref[...].astype(F32) for ref in refs[:parts])
    outs = refs[parts:]
    outs[0][...] = total[:value_rows].astype(BF16)
    if len(outs) > 1:
        outs[1][...] = merge_pairs(total[value_rows:])


def early_out_kernel(core_ref, chip_ref, own_ref, other_ref, gate_ref, output_ref):
    chips, rows, channels = own_ref.shape
    width = gate_ref.shape[0]
    step = width // (2 * chips)
    out_rows = channels // (2 * chips)
    for which, source_ref in enumerate((own_ref, other_ref)):
        for bits in range(chips):
            core = core_ref[0] if which == 0 else 1 - core_ref[0]
            place = core * chips + lax.bitwise_xor(chip_ref[0], bits)
            piece = source_ref[bits].astype(F32)
            gate_ref[pl.ds(pl.multiple_of(place * step, 8), step), :] = piece[:step]
            output_ref[pl.ds(pl.multiple_of(place * out_rows, 8), out_rows), :] = jnp.concatenate(
                [
                    piece[step + i * out_rows : step + (i + 1) * out_rows]
                    for i in range(width // channels)
                ],
                axis=1,
            )


def late_out_kernel(core_ref, chip_ref, own_ref, other_ref, value_ref):
    chips, step, _ = own_ref.shape
    for which, source_ref in enumerate((own_ref, other_ref)):
        for bits in range(chips):
            core = core_ref[0] if which == 0 else 1 - core_ref[0]
            place = core * chips + lax.bitwise_xor(chip_ref[0], bits)
            value_ref[pl.ds(pl.multiple_of(place * step, 8), step), :] = source_ref[bits].astype(F32)


def shared_out_kernel(step, core_ref, chip_ref, own_ref, other_ref, state_ref, small_ref, shared_ref):
    chips, rows, channels = own_ref.shape
    lanes = channels // 128
    part = 2 * step // lanes
    for which, source_ref in enumerate((own_ref, other_ref)):
        for bits in range(chips):
            core = core_ref[0] if which == 0 else 1 - core_ref[0]
            place = core * chips + lax.bitwise_xor(chip_ref[0], bits)
            piece = source_ref[bits].astype(F32)
            stacked = jnp.concatenate(
                [piece[:part, i * 128 : (i + 1) * 128] for i in range(lanes)], axis=0
            )
            state_ref[pl.ds(pl.multiple_of(place * step, 8), step), :] = jnp.concatenate(
                [stacked[:step], stacked[step:]], axis=1
            )
            small_ref[pl.ds(place, 1), :] = piece[part : part + 1] + piece[part + 1 : part + 2]
            shared_ref[pl.ds(place, 1), :] = piece[part + 2 : part + 3] + piece[part + 3 : part + 4]


SCALAR = "scalar"
WHOLE = "whole"
BLOCKED = "blocked"
LANES = "lanes"
LEADING = "leading"
LOOSE = "loose"


def run(kernel, name, flops, args, outs, steps=None, backward=False, scratch=()):
    at = (lambda i: steps - 1 - i) if backward else (lambda i: i)

    def spec(kind, shape):
        if kind == SCALAR:
            return pl.BlockSpec(memory_space=pltpu.SMEM)
        if kind == LOOSE:
            return pl.BlockSpec(memory_space=pl.ANY)
        if steps is None:
            return pl.BlockSpec(memory_space=pltpu.VMEM)
        if kind == BLOCKED:
            return pl.BlockSpec((CHUNK, shape[1]), lambda i: (at(i), 0))
        if kind == LANES:
            return pl.BlockSpec((shape[0], CHUNK), lambda i: (0, at(i)))
        if kind == LEADING:
            return pl.BlockSpec((1,) + shape[1:], lambda i: (at(i),) + (0,) * (len(shape) - 1))
        return pl.BlockSpec(shape, lambda i: (0,) * len(shape))

    moved = sum(a.size * a.dtype.itemsize for kind, a in args if kind != LOOSE)
    shapes = [jax.ShapeDtypeStruct(shape, dtype) for _, shape, dtype in outs]
    moved += sum(a.size * a.dtype.itemsize for a in shapes)
    return pl.pallas_call(
        kernel,
        out_shape=shapes,
        in_specs=[spec(kind, a.shape) for kind, a in args],
        out_specs=[spec(kind, shape) for kind, shape, _ in outs],
        scratch_shapes=list(scratch),
        compiler_params=pltpu.CompilerParams(vmem_limit_bytes=VMEM_LIMIT),
        cost_estimate=pl.CostEstimate(flops=flops, bytes_accessed=moved, transcendentals=0),
        name=name,
        **({} if steps is None else {"grid": (steps,)}),
    )(*(a for _, a in args))


def per_device(
    tokens, decay_codes, norm_gain, gate_weight, value_weight, state_weight, value_kernel, value_bias,
    state_kernel, state_bias, skip_scale, gated_gain, output_weight, cotangent,
):
    tokens, decay_codes, cotangent = tokens[0], decay_codes[0], cotangent[0]
    count, own_width = tokens.shape
    heads = skip_scale.shape[0]
    channels = heads * HEAD_DIM
    head_size, chips = lax.axis_size("head"), lax.axis_size("chip")
    seq_size = 2 * chips
    width = own_width * head_size
    maps_width = 2 * NSTATE
    chunks = count // CHUNK
    core = (SCALAR, lax.axis_index("core").astype(jnp.int32)[None])
    chip = (SCALAR, lax.axis_index("chip").astype(jnp.int32)[None])
    head = (SCALAR, lax.axis_index("head").astype(jnp.int32)[None])

    parts = turn_all(tokens, "head")
    before = from_behind(tokens[-HALO:], 1)
    margins = turn_all(
        jnp.concatenate([before, jnp.broadcast_to(norm_gain[None], (HALO, own_width))], axis=0),
        "head",
    )
    logs = decay_codes.astype(F32) * (-DECAY_STEP)
    input_weight = jnp.sqrt(-jnp.expm1(2.0 * logs))
    e_full, f_full, factors = run(
        decay_kernel, "decays", count * channels * 200,
        [(WHOLE, decay_codes), (WHOLE, input_weight)],
        [
            (WHOLE, (count, channels), F32),
            (WHOLE, (count, channels), F32),
            (WHOLE, (8, channels), F32),
        ],
    )
    other_factors = beside(factors)
    own_decay, other_decay = jnp.exp(factors[7:8]), jnp.exp(other_factors[7:8])
    pair_logs = jnp.concatenate(
        [part[7:8] for part in cross_all(factors + other_factors)], axis=0
    )
    before_weights = decay_weights(pair_logs, False)
    after_weights = decay_weights(pair_logs, True)
    skip_full = jnp.repeat(skip_scale, HEAD_DIM)[None]

    normed, full, gain_full, scale_in, cotangent_copy = run(
        functools.partial(norm_kernel, head_size), "norm", count * width * 10,
        [head] + [(WHOLE, a) for a in parts + margins + [cotangent]],
        [
            (WHOLE, (HALO + count, width), BF16),
            (WHOLE, (count, width), BF16),
            (WHOLE, (8, width), F32),
            (WHOLE, (count, 128), F32),
            (WHOLE, (count, own_width), BF16),
        ],
        scratch=[pltpu.VMEM((HALO, width), BF16)],
    )
    cotangent_parts = turn_all(cotangent_copy, "head")
    value_raw = dot(normed, value_weight).astype(BF16)
    state_raw = dot(normed, state_weight).astype(BF16)
    conv, weighted, value_slope, maps, map_slope, local_end = run(
        conv_kernel, "conv", count * channels * 400,
        [
            (WHOLE, value_raw), (WHOLE, state_raw), (WHOLE, value_kernel), (WHOLE, value_bias[None]),
            (WHOLE, state_kernel), (WHOLE, state_bias[None]), (BLOCKED, f_full), (WHOLE, factors),
        ],
        [
            (BLOCKED, (count, channels), BF16),
            (BLOCKED, (count, channels), BF16),
            (BLOCKED, (count, channels), F32),
            (BLOCKED, (count, maps_width), BF16),
            (BLOCKED, (count, maps_width), F32),
            (WHOLE, (NSTATE, channels), F32),
        ],
        steps=chunks,
    )
    state_in, _ = entering(local_end, own_decay, other_decay, before_weights, False)
    gate_pre = dot(normed[HALO:], gate_weight)
    full_cotangent = run(
        place_kernel, "place", count * width, [head] + [(WHOLE, a) for a in cotangent_parts],
        [(WHOLE, (count, width), BF16)],
    )[0]
    mixed_grad = dot_nt(full_cotangent, output_weight)
    mixer, stats, high, low = run(
        mixer_kernel, "mixer", count * channels * 1000,
        [
            (WHOLE, state_in), (BLOCKED, maps), (BLOCKED, weighted), (BLOCKED, conv),
            (BLOCKED, e_full), (WHOLE, factors), (WHOLE, skip_full), (BLOCKED, gate_pre),
            (BLOCKED, mixed_grad), (WHOLE, gated_gain[None]),
        ],
        [
            (BLOCKED, (count, channels), F32),
            (LANES, (8, count), F32),
            (LEADING, (chunks, NSTATE, channels), BF16),
            (LEADING, (chunks, NSTATE, channels), BF16),
        ],
        steps=chunks,
        scratch=[pltpu.VMEM((NSTATE, channels), F32)],
    )
    mixed, gate_grad, mixer_grad, gate_small, start_grad = run(
        functools.partial(gate_kernel, float(channels * head_size), chunks, head_size),
        "gate", count * channels * 600,
        [(LANES, part) for part in turn_all(stats, "head")]
        + [
            (BLOCKED, mixer), (BLOCKED, gate_pre), (BLOCKED, mixed_grad), (WHOLE, gated_gain[None]),
            (BLOCKED, conv), (BLOCKED, e_full), (WHOLE, factors), (BLOCKED, maps),
        ],
        [
            (BLOCKED, (count, channels), BF16),
            (BLOCKED, (count, channels), BF16),
            (BLOCKED, (count, channels), F32),
            (WHOLE, (8, channels), F32),
            (WHOLE, (NSTATE, channels), F32),
        ],
        steps=chunks,
        backward=True,
    )
    grad_after, pair = entering(start_grad, own_decay, other_decay, after_weights, True)

    out_parts = run(
        functools.partial(out_kernel, head_size), "out", 2 * count * channels * width,
        [(LOOSE, start_grad), head, (WHOLE, mixed), (WHOLE, output_weight)],
        [(WHOLE, (count, own_width), BF16)] * head_size,
    )
    step, out_rows = width // seq_size, channels // seq_size
    rows = step + out_rows * (width // channels)
    early_kept, early_given = run(
        early_kernel, "early", 4 * count * channels * width,
        [
            (LOOSE, pair), core, (WHOLE, normed), (WHOLE, gate_grad), (WHOLE, mixed),
            (WHOLE, full_cotangent),
        ],
        [(WHOLE, (chips, rows, channels), BF16)] * 2,
        scratch=[pltpu.VMEM((channels, width), F32)],
    )
    early_halves = run(
        functools.partial(half_kernel, False, chips), "early_half", chips * rows * channels,
        [chip, (WHOLE, early_kept), (WHOLE, beside(early_given))],
        [(WHOLE, (rows, channels), F32)] + [(WHOLE, (rows, channels), BF16)] * (chips - 1),
    )
    early_piece = run(
        functools.partial(piece_kernel, chips, rows), "early_piece", chips * rows * channels,
        [(WHOLE, early_halves[0])]
        + [(WHOLE, cross(early_halves[bits], bits)) for bits in range(1, chips)],
        [(WHOLE, (rows, channels), BF16)],
    )[0]
    branch = out_parts[0].astype(F32)
    for by in range(1, head_size):
        branch = branch + turn(out_parts[by], "head", by).astype(F32)
    block_out = (tokens.astype(F32) + branch).astype(BF16)

    value_grads, map_grads = run(
        functools.partial(back_kernel, chunks), "back", count * channels * 2000,
        [
            (LOOSE, early_given), (WHOLE, grad_after), (BLOCKED, mixer_grad), (BLOCKED, e_full),
            (BLOCKED, f_full), (WHOLE, factors), (BLOCKED, weighted), (LEADING, high),
            (LEADING, low), (BLOCKED, maps), (BLOCKED, value_slope), (BLOCKED, map_slope),
            (WHOLE, skip_full),
        ],
        [(BLOCKED, (count, channels), F32), (BLOCKED, (count, maps_width), F32)],
        steps=chunks,
        backward=True,
        scratch=[pltpu.VMEM((NSTATE, channels), F32)],
    )
    after = from_behind(jnp.concatenate([value_grads[:8], map_grads[:8]], axis=1), -1)
    value_raw_grad, state_raw_grad, value_small, state_small = run(
        functools.partial(conv_back_kernel, chunks), "conv_back", count * channels * 100,
        [
            (LOOSE, early_halves[0]), (BLOCKED, value_grads), (BLOCKED, map_grads), (WHOLE, after),
            (WHOLE, value_raw), (WHOLE, state_raw), (WHOLE, value_kernel), (WHOLE, state_kernel),
        ],
        [
            (BLOCKED, (count, channels), BF16),
            (BLOCKED, (count, maps_width), BF16),
            (WHOLE, (8, channels), F32),
            (WHOLE, (8, maps_width), F32),
        ],
        steps=chunks,
        backward=True,
        scratch=[pltpu.VMEM((8, channels), F32), pltpu.VMEM((8, maps_width), F32)],
    )
    *normed_parts, gain_part, _ = run(
        functools.partial(normed_kernel, head_size), "normed", 4 * count * channels * width,
        [
            head, (WHOLE, gate_grad), (WHOLE, value_raw_grad), (WHOLE, state_raw_grad),
            (WHOLE, gate_weight), (WHOLE, value_weight), (WHOLE, state_weight), (WHOLE, full),
            (WHOLE, gain_full), (WHOLE, scale_in),
        ],
        [(WHOLE, (count + HALO, own_width), BF16)] * head_size
        + [(WHOLE, (1, width), F32), (WHOLE, (8, 128), F32)],
    )
    lanes = channels // 128
    state_rows = 2 * step // lanes
    late_rows = step + state_rows + HALO
    late_kept, late_given = run(
        late_kernel, "late", 3 * count * channels * width,
        [
            core, (WHOLE, normed), (WHOLE, value_raw_grad), (WHOLE, state_raw_grad),
            (WHOLE, value_small), (WHOLE, gate_small), (WHOLE, gain_part), (WHOLE, state_small),
        ],
        [(WHOLE, (chips, late_rows, channels), BF16)] * 2,
        scratch=[pltpu.VMEM((HALO, channels), F32), pltpu.VMEM((HALO, channels), F32)],
    )
    late_halves = run(
        functools.partial(half_kernel, True, chips), "late_half", chips * late_rows * channels,
        [chip, (WHOLE, late_kept), (WHOLE, beside(late_given))],
        [(WHOLE, (late_rows, channels), F32)] + [(WHOLE, (late_rows, channels), BF16)] * (chips - 1),
    )
    late_piece, shared_piece = run(
        functools.partial(piece_kernel, chips, step), "late_piece", chips * late_rows * channels,
        [(WHOLE, late_halves[0])]
        + [(WHOLE, cross(late_halves[bits], bits)) for bits in range(1, chips)],
        [(WHOLE, (step, channels), BF16), (WHOLE, (late_rows - step, channels), F32)],
    )
    summed = butterfly(shared_piece, "head")
    line = jnp.arange(late_rows - step)[:, None]
    own_line = (line >= state_rows) & (line < state_rows + 2)
    tail = summed[state_rows + 2 : state_rows + 3] + summed[state_rows + 3 : state_rows + 4]
    tail_high = tail.astype(BF16).astype(F32)
    summed = jnp.where(
        line == state_rows + 2, tail_high, jnp.where(line == state_rows + 3, tail - tail_high, summed)
    )
    shared_piece = jnp.where(own_line, shared_piece, summed).astype(BF16)

    late = jnp.stack(cross_all(late_piece))
    early = jnp.stack(cross_all(early_piece))
    shared = jnp.stack(cross_all(shared_piece))
    gate_weight_gradient, output_weight_gradient = run(
        early_out_kernel, "early_out", 4 * channels * width,
        [core, chip, (WHOLE, early), (WHOLE, beside(early))],
        [(WHOLE, (width, channels), F32), (WHOLE, (channels, width), F32)],
    )
    value_weight_gradient = run(
        late_out_kernel, "late_out", 2 * channels * width,
        [core, chip, (WHOLE, late), (WHOLE, beside(late))],
        [(WHOLE, (width, channels), F32)],
    )[0]
    state_weight_gradient, own_small, shared_small = run(
        functools.partial(shared_out_kernel, step), "shared_out", 2 * maps_width * width,
        [core, chip, (WHOLE, shared), (WHOLE, beside(shared))],
        [
            (WHOLE, (width, maps_width), F32),
            (WHOLE, (HALO, channels), F32),
            (WHOLE, (HALO, channels), F32),
        ],
    )
    value_kernel_gradient, value_bias_gradient = own_small[:KERNEL], own_small[KERNEL]
    gated_gain_gradient = own_small[KERNEL + 1]
    skip_scale_gradient = jnp.sum(own_small[KERNEL + 2].reshape(heads, HEAD_DIM), axis=1)
    gain_rows = width // channels
    norm_gain_gradient = lax.dynamic_slice_in_dim(
        shared_small[:gain_rows].reshape(width), lax.axis_index("head") * own_width, own_width, 0
    )
    map_rows = -(-(KERNEL + 1) * maps_width // channels)
    map_small = shared_small[gain_rows : gain_rows + map_rows].reshape(-1)
    map_small = map_small[: (KERNEL + 1) * maps_width].reshape(KERNEL + 1, maps_width)
    state_kernel_gradient, state_bias_gradient = map_small[:KERNEL], map_small[KERNEL]

    tokens_gradient = run(
        functools.partial(last_kernel, head_size, float(width)), "last", count * own_width * 20,
        [(WHOLE, normed_parts[0])]
        + [(WHOLE, turn(normed_parts[by], "head", by)) for by in range(1, head_size)]
        + [(WHOLE, tokens), (WHOLE, scale_in), (WHOLE, norm_gain[None]), (WHOLE, cotangent)],
        [(WHOLE, (count, own_width), BF16)],
    )[0]
    return (
        block_out[None],
        tokens_gradient[None],
        norm_gain_gradient,
        gate_weight_gradient,
        value_weight_gradient,
        state_weight_gradient,
        value_kernel_gradient,
        value_bias_gradient,
        state_kernel_gradient,
        state_bias_gradient,
        skip_scale_gradient,
        gated_gain_gradient,
        output_weight_gradient,
    )


def solution(mesh):
    seq_size, head_size = mesh.shape["seq"], mesh.shape["head"]
    mesh = Mesh(mesh.devices.reshape(seq_size // 2, 2, head_size), ("chip", "core", "head"))
    seq = ("chip", "core")
    in_specs = (
        P(None, seq, "head"),
        P(None, seq, "head"),
        P("head"),
        P(None, "head"),
        P(None, "head"),
        P(),
        P(None, "head"),
        P("head"),
        P(),
        P(),
        P("head"),
        P("head"),
        P("head", None),
        P(None, seq, "head"),
    )
    out_specs = (
        P(None, seq, "head"),
        P(None, seq, "head"),
        P("head"),
        P(None, "head"),
        P(None, "head"),
        P(),
        P(None, "head"),
        P("head"),
        P(),
        P(),
        P("head"),
        P("head"),
        P("head", None),
    )
    return jax.shard_map(
        per_device, mesh=mesh, in_specs=in_specs, out_specs=out_specs, check_vma=False
    )
```

```python
import functools

import jax
import jax.numpy as jnp
from jax import lax
from jax.experimental import pallas as pl
from jax.experimental.pallas import tpu as pltpu
from jax.sharding import Mesh
from jax.sharding import PartitionSpec as P

HEAD_DIM = 64
NSTATE = 128
KERNEL = 4
CHUNK = 128
BLOCK = 384
VMEM_LIMIT = 20 * 1024 * 1024
HALO = 16


DECAY_STEP = 1.0 / 1048576.0
EPSILON = 1e-05
BF16 = jnp.bfloat16
F32 = jnp.float32


def from_behind(value, by):
    axis = ("chip", "core")
    size = lax.axis_size("chip") * 2
    pairs = [(i, i + by) for i in range(size) if 0 <= i + by < size]
    return lax.ppermute(value, axis, pairs)


def beside(value):
    return lax.ppermute(value, "core", [(0, 1), (1, 0)])


def turn(value, axis, by):
    size = lax.axis_size(axis)
    return lax.ppermute(value, axis, [(i, (i + by) % size) for i in range(size)])


def turn_all(value, axis):
    return [value] + [turn(value, axis, by) for by in range(1, lax.axis_size(axis))]


def line_parts(value, axis):
    if lax.axis_size(axis) != 4:
        return turn_all(value, axis), value
    two = turn(value, axis, 2)
    one = lax.ppermute(value, axis, [(0, 1), (1, 2), (2, 3)])
    three = lax.ppermute(value, axis, [(1, 0), (2, 1), (3, 2)])
    passed = lax.ppermute(two, axis, [(2, 3), (1, 0)])
    return [value, one, two, three], passed


def deal(parts, axis):
    return lax.all_to_all(parts, axis, 0, 0)


def cross(value, bits):
    return lax.ppermute(value, "chip", [(i, i ^ bits) for i in range(lax.axis_size("chip"))])


def cross_all(value):
    return [value] + [cross(value, bits) for bits in range(1, lax.axis_size("chip"))]


def butterfly(value, axis):
    bits = 1
    while bits < lax.axis_size(axis):
        size = lax.axis_size(axis)
        value = value + lax.ppermute(value, axis, [(i, i ^ bits) for i in range(size)])
        bits *= 2
    return value


def decay_weights(logs, backward):
    chips, mine = lax.axis_size("chip"), lax.axis_index("chip")
    source = (jnp.arange(chips) ^ mine)[:, None]
    middle = jnp.arange(chips)[None, :]
    if backward:
        between, passes = (middle < source) & (middle > mine), source > mine
    else:
        between, passes = (middle > source) & (middle < mine), source < mine
    spans = jnp.sum(jnp.where(between[:, :, None], logs[None], 0.0), axis=1)
    return jnp.where(passes, jnp.exp(spans), 0.0)


def entering(total, own_decay, other_decay, weights, backward):
    core = lax.axis_index("core")
    receives = core == (0 if backward else 1)
    half = total.shape[0] // 2
    partner = beside(total)
    part = lambda value: lax.dynamic_slice_in_dim(value, core * half, half, 0)
    pair = jnp.where(
        receives,
        own_decay * part(partner) + part(total),
        other_decay * part(total) + part(partner),
    )
    prefix = jnp.zeros_like(pair)
    for bits in range(1, lax.axis_size("chip")):
        prefix = prefix + cross(pair, bits) * weights[bits : bits + 1]
    other = beside(prefix)
    whole = jnp.where(
        core == 0,
        jnp.concatenate([prefix, other], axis=0),
        jnp.concatenate([other, prefix], axis=0),
    )
    return jnp.where(receives, other_decay * whole + partner, whole), pair


def sum_pieces(chip, kept, given, cut, paired, name):
    chips, rows, channels = kept.shape
    arrived = beside(given)
    rest = rows - cut
    size = chips * rows * channels
    if chips != 4:
        halves = run(
            functools.partial(half_kernel, paired, chips), name + "_half", size,
            [chip, (WHOLE, kept), (WHOLE, arrived)],
            [(WHOLE, (rows, channels), F32)] + [(WHOLE, (rows, channels), BF16)] * (chips - 1),
        )
        parts = [halves[0]] + [cross(halves[bits], bits) for bits in range(1, chips)]
        first, last = run(
            functools.partial(piece_kernel, chips, paired, cut), name + "_piece", size,
            [(WHOLE, part) for part in parts],
            [(WHOLE, (cut, channels), BF16), (WHOLE, (rest, channels), F32 if paired else BF16)],
        )
        return first, last, halves[0]
    first, first_give, last, last_give = run(
        functools.partial(square_half_kernel, paired), name + "_half", size,
        [chip, (WHOLE, kept), (WHOLE, arrived)],
        [
            (WHOLE, (2, cut, channels), F32), (WHOLE, (2, cut, channels), BF16),
            (WHOLE, (2, rest, channels), F32), (WHOLE, (2, rest, channels), BF16),
        ],
    )
    mark = first
    first, first_give, last, last_give = run(
        functools.partial(square_next_kernel, paired), name + "_next", size,
        [
            (WHOLE, first), (WHOLE, cross(first_give, 1)),
            (WHOLE, last), (WHOLE, cross(last_give, 2)),
        ],
        [
            (WHOLE, (cut, channels), F32), (WHOLE, (cut, channels), BF16),
            (WHOLE, (rest, channels), F32), (WHOLE, (rest, channels), BF16),
        ],
    )
    first, last = run(
        functools.partial(square_last_kernel, paired), name + "_piece", size,
        [
            (WHOLE, first), (WHOLE, cross(first_give, 2)),
            (WHOLE, last), (WHOLE, cross(last_give, 1)),
        ],
        [(WHOLE, (cut, channels), BF16), (WHOLE, (rest, channels), F32 if paired else BF16)],
    )
    return first, last, mark


def collect(piece, order):
    chips = lax.axis_size("chip")
    if chips != 4:
        found = [(value[None], (bits,)) for bits, value in enumerate(cross_all(piece))]
    else:
        near, far = order
        both = jnp.stack([piece, cross(piece, near)])
        found = [(both, (0, near)), (cross(both, far), (far, far ^ near))]
    return [(value, beside(value), bits) for value, bits in found]


def dot(left, right):
    return jnp.dot(left, right, preferred_element_type=F32)


def dot_nt(left, right):
    return lax.dot_general(left, right, (((1,), (1,)), ((), ())), preferred_element_type=F32)


def dot_tn(left, right):
    return lax.dot_general(left, right, (((0,), (0,)), ((), ())), preferred_element_type=F32)


def split(values):
    high = values.astype(BF16)
    return high, (values - high.astype(F32)).astype(BF16)


def lower_mask():
    row = lax.broadcasted_iota(jnp.int32, (CHUNK, CHUNK), 0)
    column = lax.broadcasted_iota(jnp.int32, (CHUNK, CHUNK), 1)
    return row >= column


def decay_kernel(codes_ref, weight_ref, e_ref, f_ref, k_ref):
    heads, channels = codes_ref.shape[1], e_ref.shape[1]
    row = lax.broadcasted_iota(jnp.int32, (heads, channels), 0)
    column = lax.broadcasted_iota(jnp.int32, (heads, channels), 1)
    first = row * HEAD_DIM
    spread = jnp.where((column >= first) & (column < first + HEAD_DIM), 1.0, 0.0).astype(BF16)

    def expand(values):
        high, low = split(values)
        return dot(high, spread) + dot(low, spread)

    lower = jnp.where(lower_mask(), 1.0, 0.0).astype(F32)
    count = codes_ref.shape[0] // CHUNK
    line = lax.broadcasted_iota(jnp.int32, (8, heads), 0)
    marks = jnp.zeros((8, heads), F32)
    total = jnp.zeros((1, heads), F32)
    for chunk in range(count):
        rows = pl.ds(chunk * CHUNK, CHUNK)
        logs = codes_ref[rows, :].astype(F32) * (-DECAY_STEP)
        cumulative = jnp.dot(
            lower, logs, precision=lax.Precision.HIGHEST, preferred_element_type=F32
        )
        last = cumulative[CHUNK - 1 :]
        middle = 0.5 * last
        e_ref[rows, :] = expand(jnp.exp(cumulative - middle))
        f_ref[rows, :] = expand(weight_ref[rows, :] * jnp.exp(middle - cumulative))
        marks = jnp.where(line == chunk, jnp.exp(middle), marks)
        total = total + last
    marks = jnp.where(line == 7, total, marks)
    high, low = split(marks)
    lowest = (marks - high.astype(F32) - low.astype(F32)).astype(BF16)
    k_ref[...] = dot(high, spread) + dot(low, spread) + dot(lowest, spread)


def taps(window, kernel, bias, begin):
    summed = bias
    for offset in range(KERNEL):
        summed = summed + kernel[offset : offset + 1] * window[begin + offset : begin + offset + CHUNK]
    return summed


def silu_parts(values):
    sigmoid = jax.nn.sigmoid(values)
    return values * sigmoid, sigmoid * (1.0 + values * (1.0 - sigmoid))


def first_step(action):
    pl.when(pl.program_id(0) == 0)(action)


def clear(*refs):
    def action():
        for ref in refs:
            ref[...] = jnp.zeros_like(ref)

    first_step(action)


def place_parts(mine, parts, target, width, value):
    size = len(parts)
    if width % 128 == 0:
        for i in range(size):
            owner = lax.rem(mine + size - i, size)
            target[:, pl.ds(pl.multiple_of(owner * width, 128), width)] = value(i)
        return

    def write(me):
        for i in range(size):
            owner = (me + size - i) % size
            target[:, owner * width : (owner + 1) * width] = value(i)

    for me in range(size):
        pl.when(mine == me)(functools.partial(write, me))


def norm_kernel(size, head_ref, passed_ref, *refs):
    parts, margins, (own_ref,) = refs[:size], refs[size : 2 * size], refs[2 * size : 2 * size + 1]
    normed_ref, full_ref, gain_ref, scale_ref, copy_ref = refs[2 * size + 1 : 2 * size + 6]
    head_normed, = refs[2 * size + 6 :]
    width = parts[0].shape[1]
    mine = head_ref[0]

    def part(i):
        if size == 4 and i == 1:
            return jnp.where(mine == 0, passed_ref[...], parts[i][...])
        if size == 4 and i == 3:
            return jnp.where(mine == 3, passed_ref[...], parts[i][...])
        return parts[i][...]

    def scale_of(values):
        squares = sum(jnp.sum(value.astype(F32) ** 2, axis=1, keepdims=True) for value in values)
        return lax.rsqrt(squares / (size * width) + EPSILON)

    scale = scale_of(part(i) for i in range(size))
    scale_ref[...] = jnp.broadcast_to(scale, scale_ref.shape)
    ahead = scale_of(ref[:HALO] for ref in margins)
    gain = lambda i: margins[i][HALO : HALO + 1, :].astype(F32)
    place_parts(
        mine, margins, head_normed, width,
        lambda i: (margins[i][:HALO].astype(F32) * ahead * gain(i)).astype(BF16),
    )
    place_parts(
        mine, parts, normed_ref.at[HALO:], width,
        lambda i: (part(i).astype(F32) * scale_ref[:, 0:1] * gain(i)).astype(BF16),
    )
    normed_ref[:HALO, :] = head_normed[...]
    place_parts(mine, parts, full_ref, width, part)
    place_parts(
        mine, margins, gain_ref, width, lambda i: jnp.broadcast_to(gain(i), (8, width))
    )
    for i in range(size):
        copy_ref[i] = own_ref[...]


def place_kernel(parts_ref, target):
    width = parts_ref.shape[2]
    for i in range(parts_ref.shape[0]):
        target[:, i * width : (i + 1) * width] = parts_ref[i]


def conv_kernel(
    value_ref, state_ref, value_kernel_ref, value_bias_ref, state_kernel_ref, state_bias_ref,
    f_ref, k_ref, conv_ref, weighted_ref, value_slope_ref, maps_ref, state_slope_ref, total_ref,
):
    chunk = pl.program_id(0)
    clear(total_ref)
    around = pl.ds(pl.multiple_of(chunk * CHUNK, CHUNK), CHUNK + HALO)
    pre = taps(
        state_ref[around, :].astype(F32), state_kernel_ref[...].astype(F32),
        state_bias_ref[...].astype(F32), HALO - KERNEL + 1,
    )
    conv, slope = silu_parts(pre)
    maps = conv.astype(BF16)
    maps_ref[...] = maps
    state_slope_ref[...] = slope
    pre = taps(
        value_ref[around, :].astype(F32), value_kernel_ref[...].astype(F32),
        value_bias_ref[...].astype(F32), HALO - KERNEL + 1,
    )
    conv, slope = silu_parts(pre)
    conv = conv.astype(BF16)
    conv_ref[...] = conv
    value_slope_ref[...] = slope
    weighted = (conv.astype(F32) * f_ref[...]).astype(BF16)
    weighted_ref[...] = weighted
    factor = k_ref[pl.ds(chunk, 1), :]
    total_ref[...] = factor * (factor * total_ref[...] + dot_tn(maps[:, :NSTATE], weighted))


def mixer_kernel(
    state_in_ref, maps_ref, weighted_ref, conv_ref, e_ref, k_ref, skip_ref, gate_ref, grad_ref, gain_ref,
    mixer_ref, stats_ref, high_ref, low_ref, state_ref,
):
    chunk = pl.program_id(0)

    def start():
        state_ref[...] = state_in_ref[...]

    first_step(start)
    lane = lax.broadcasted_iota(jnp.int32, (CHUNK, CHUNK), 1)
    factor = k_ref[pl.ds(chunk, 1), :]
    input_map, output_map = maps_ref[:, :NSTATE], maps_ref[:, NSTATE:]
    weighted = weighted_ref[...]
    scaled = factor * state_ref[...]
    high, low = split(scaled)
    high_ref[0], low_ref[0] = high, low
    scores = jnp.where(lower_mask(), dot_nt(output_map, input_map), 0.0).astype(BF16)
    mixed = dot(
        jnp.concatenate([scores, output_map], axis=1), jnp.concatenate([weighted, high], axis=0)
    )
    mixed = mixed + dot(output_map, low)
    mixer = e_ref[...] * mixed + skip_ref[...] * conv_ref[...].astype(F32)
    mixer_ref[...] = mixer
    gate = gate_ref[...]
    gated = mixer * (gate * jax.nn.sigmoid(gate))
    squares = jnp.sum(gated * gated, axis=1, keepdims=True)
    products = jnp.sum(gated * (grad_ref[...] * gain_ref[...].astype(F32)), axis=1, keepdims=True)
    sums = jnp.where(lane == 0, squares, jnp.where(lane == 1, products, 0.0))
    stats_ref[...] = sums.T[:8]
    state_ref[...] = factor * (scaled + dot_tn(input_map, weighted))


def column(row_block):
    rest = jnp.zeros((CHUNK - row_block.shape[0], CHUNK), F32)
    return jnp.concatenate([row_block, rest], axis=0).T


def gate_kernel(
    inner, chunks, size, *refs
):
    stats_refs = refs[:size]
    (
        mixer_ref, gate_ref, grad_ref, gain_ref, conv_ref, e_ref, k_ref, maps_ref,
        mixed_ref, gate_grad_ref, mixer_grad_ref, small_ref, total_ref,
    ) = refs[size:]
    chunk = chunks - 1 - pl.program_id(0)
    clear(small_ref, total_ref)
    gain = gain_ref[...].astype(F32)
    stats = column(sum(ref[...] for ref in stats_refs))
    scale = lax.rsqrt(stats[:, 0:1] / inner + EPSILON)
    cross_term = stats[:, 1:2] * (scale * scale * scale) / inner
    silu, slope = silu_parts(gate_ref[...])
    mixer = mixer_ref[...]
    gated = mixer * silu
    normed = gated * scale
    mixed_ref[...] = (normed * gain).astype(BF16)
    grad = grad_ref[...]
    gated_grad = scale * (grad * gain) - gated * cross_term
    gate_grad_ref[...] = (gated_grad * mixer * slope).astype(BF16)
    mixer_grad = gated_grad * silu
    mixer_grad_ref[...] = mixer_grad
    small_ref[0:1, :] += jnp.sum(grad * normed, axis=0, keepdims=True)
    small_ref[1:2, :] += jnp.sum(mixer_grad * conv_ref[...].astype(F32), axis=0, keepdims=True)
    high, low = split(e_ref[...] * mixer_grad)
    output_map = maps_ref[:, NSTATE:]
    factor = k_ref[pl.ds(chunk, 1), :]
    total_ref[...] = factor * (
        factor * total_ref[...] + (dot_tn(output_map, high) + dot_tn(output_map, low))
    )


def back_kernel(
    chunks, early_ref, out_ref, state_in_ref, mixer_grad_ref, e_ref, f_ref, k_ref, weighted_ref, high_ref, low_ref,
    maps_ref, value_slope_ref, state_slope_ref, skip_ref,
    value_ref, map_ref, state_ref,
):
    chunk = chunks - 1 - pl.program_id(0)

    def start():
        state_ref[...] = state_in_ref[...]

    first_step(start)
    lower = lower_mask()
    row = lax.broadcasted_iota(jnp.int32, (CHUNK, CHUNK), 0)
    upper = row <= lax.broadcasted_iota(jnp.int32, (CHUNK, CHUNK), 1)
    factor = k_ref[pl.ds(chunk, 1), :]
    input_map, output_map = maps_ref[:, :NSTATE], maps_ref[:, NSTATE:]
    weighted = weighted_ref[...]
    mixer_grad = mixer_grad_ref[...]
    high, low = split(e_ref[...] * mixer_grad)
    scaled = factor * state_ref[...]
    state_high, state_low = split(scaled)
    both = jnp.concatenate([weighted, high_ref[0]], axis=0)
    sums = dot_nt(high, both) + dot_nt(low, both)
    score_grad = jnp.where(lower, sums[:, :CHUNK], 0.0).astype(BF16)
    output_grad = sums[:, CHUNK:] + dot_nt(high, low_ref[0]) + dot(score_grad, input_map)
    sums = dot_nt(weighted, jnp.concatenate([state_high, state_low], axis=0))
    input_grad = sums[:, :NSTATE] + sums[:, NSTATE:] + dot_tn(score_grad, output_map)
    scores = jnp.where(upper, dot_nt(input_map, output_map), 0.0).astype(BF16)
    grads = dot(
        jnp.concatenate([scores, input_map], axis=1), jnp.concatenate([high, state_high], axis=0)
    )
    value_ref[...] = (f_ref[...] * grads + skip_ref[...] * mixer_grad) * value_slope_ref[...]
    slope = state_slope_ref[...]
    map_ref[:, :NSTATE] = input_grad * slope[:, :NSTATE]
    map_ref[:, NSTATE:] = output_grad * slope[:, NSTATE:]
    state_ref[...] = factor * (scaled + (dot_tn(output_map, high) + dot_tn(output_map, low)))


def conv_back_kernel(
    chunks, other_ref, value_ref, map_ref, after_ref, value_raw_ref, state_raw_ref, value_kernel_ref,
    state_kernel_ref,
    value_grad_ref, state_grad_ref, value_small_ref, state_small_ref, value_next_ref, state_next_ref,
):
    chunk = chunks - 1 - pl.program_id(0)
    channels = value_ref.shape[1]
    clear(value_small_ref, state_small_ref)

    def start():
        value_next_ref[...] = after_ref[:, :channels]
        state_next_ref[...] = after_ref[:, channels:]

    first_step(start)

    def back(slope_ref, next_ref, raw_ref, kernel_ref, grad_ref, small_ref):
        kernel = kernel_ref[...].astype(F32)
        slope = slope_ref[...]
        window = jnp.concatenate([slope, next_ref[...]], axis=0)
        around = pl.ds(pl.multiple_of(chunk * CHUNK, CHUNK), CHUNK + HALO)
        raw = raw_ref[around, :].astype(F32)
        grad = jnp.zeros_like(slope)
        for offset in range(KERNEL):
            back_by = KERNEL - 1 - offset
            grad = grad + kernel[offset : offset + 1] * window[back_by : back_by + CHUNK]
            begin = HALO - KERNEL + 1 + offset
            small_ref[offset : offset + 1, :] += jnp.sum(
                slope * raw[begin : begin + CHUNK], axis=0, keepdims=True
            )
        small_ref[KERNEL : KERNEL + 1, :] += jnp.sum(slope, axis=0, keepdims=True)
        grad_ref[...] = grad.astype(BF16)
        next_ref[...] = slope[:8]

    back(map_ref, state_next_ref, state_raw_ref, state_kernel_ref, state_grad_ref, state_small_ref)
    back(value_ref, value_next_ref, value_raw_ref, value_kernel_ref, value_grad_ref, value_small_ref)


def out_kernel(pair_ref, mixed_ref, weight_ref, out_ref):
    width = out_ref.shape[2]
    for owner in range(out_ref.shape[0]):
        value = dot(mixed_ref[...], weight_ref[:, owner * width : (owner + 1) * width])
        out_ref[owner] = value.astype(BF16)


def normed_kernel(
    late_ref, gate_grad_ref, value_grad_ref, state_grad_ref, gate_weight_ref, value_weight_ref,
    state_weight_ref, full_ref, gain_ref, out_ref
):
    size, _, width = out_ref.shape
    count = full_ref.shape[0]
    crossed = jnp.zeros((count, 1), F32)
    for owner in range(size):
        own = slice(owner * width, (owner + 1) * width)
        value = (
            dot_nt(gate_grad_ref[...], gate_weight_ref[own, :])
            + dot_nt(value_grad_ref[...], value_weight_ref[own, :])
            + dot_nt(state_grad_ref[...], state_weight_ref[own, :])
        )
        weighed = value * full_ref[:, own].astype(F32) * gain_ref[0:1, own]
        crossed = crossed + jnp.sum(weighed, axis=1, keepdims=True)
        out_ref[owner, :count, :] = value.astype(BF16)

    chunks = count // CHUNK
    line = lax.broadcasted_iota(jnp.int32, (HALO, CHUNK), 0)
    lane = lax.broadcasted_iota(jnp.int32, (CHUNK, CHUNK), 1)
    packed = jnp.zeros((HALO, CHUNK), F32)
    for chunk in range(chunks):
        sums = crossed[chunk * CHUNK : (chunk + 1) * CHUNK]
        row = jnp.where(lane == 0, sums, 0.0).T[0:1]
        high = row.astype(BF16).astype(F32)
        packed = jnp.where(line == chunk, high, packed)
        packed = jnp.where(line == chunks + chunk, row - high, packed)
    for owner in range(size):
        out_ref[owner, count:, :] = jnp.zeros((HALO, width), BF16)
        out_ref[owner, count:, :CHUNK] = packed.astype(BF16)


def last_kernel(full_width, loose_ref, parts_ref, tokens_ref, scale_ref, gain_ref, cotangent_ref, out_ref):
    count = tokens_ref.shape[0]
    chunks = count // CHUNK
    size = parts_ref.shape[0]
    crossed = sum(parts_ref[i, count:, :CHUNK].astype(F32) for i in range(size))
    crossed = crossed[:chunks] + crossed[chunks : 2 * chunks]
    for chunk in range(chunks):
        rows = slice(chunk * CHUNK, (chunk + 1) * CHUNK)
        normed_grad = sum(parts_ref[i, rows, :].astype(F32) for i in range(size))
        scale = scale_ref[rows, 0:1]
        total = column(jnp.broadcast_to(crossed[chunk : chunk + 1], (8, CHUNK)))[:, 0:1]
        out_ref[rows, :] = (
            scale * gain_ref[...].astype(F32) * normed_grad
            - tokens_ref[rows, :].astype(F32) * (scale * scale * scale * total / full_width)
            + cotangent_ref[rows, :].astype(F32)
        ).astype(BF16)


def store_piece(core_ref, kept_ref, given_ref, place, piece):
    chips = kept_ref.shape[0]
    core, chip = divmod(place, chips)
    piece = piece.astype(BF16)

    @pl.when(core_ref[0] == core)
    def _():
        kept_ref[chip] = piece

    @pl.when(core_ref[0] != core)
    def _():
        given_ref[chip] = piece


def gain_row(weight, block):
    sums = jnp.sum(weight.astype(F32) * block, axis=1, keepdims=True)
    lane = lax.broadcasted_iota(jnp.int32, (CHUNK, CHUNK), 1)
    rows = [
        jnp.where(lane == 0, sums[i : i + CHUNK], 0.0).T[0:1] for i in range(0, BLOCK, CHUNK)
    ]
    return jnp.concatenate(rows, axis=1)


def early_kernel(
    pair_ref, core_ref, normed_ref, gate_ref, mixed_ref, grad_ref, weight_ref,
    kept_ref, given_ref, gain_ref, held_ref
):
    chips, rows, channels = kept_ref.shape
    width = normed_ref.shape[1]
    pieces = 2 * chips
    step = width // pieces
    out_rows = channels // pieces
    for begin in range(0, channels, BLOCK):
        held_ref[begin : begin + BLOCK, :] = dot_tn(mixed_ref[:, begin : begin + BLOCK], grad_ref[...])
    for begin in range(0, width, BLOCK):
        block = dot_tn(normed_ref[HALO:, begin : begin + BLOCK], gate_ref[...])
        gain_ref[0:1, begin : begin + BLOCK] = gain_row(weight_ref[begin : begin + BLOCK, :], block)
        for place in range(begin // step, (begin + BLOCK) // step):
            own = held_ref[place * out_rows : (place + 1) * out_rows, :]
            parts = [block[place * step - begin : (place + 1) * step - begin]]
            parts += [own[:, i : i + channels] for i in range(0, width, channels)]
            store_piece(core_ref, kept_ref, given_ref, place, jnp.concatenate(parts, axis=0))


def late_kernel(
    core_ref, normed_ref, value_ref, state_ref, value_small_ref, gate_small_ref, gain_ref,
    state_small_ref, value_weight_ref, state_weight_ref, gain_full_ref,
    kept_ref, given_ref, own_ref, shared_ref, gains_ref, blocks_ref,
):
    chips, rows, channels = kept_ref.shape
    width, maps_width = normed_ref.shape[1], state_ref.shape[1]
    pieces = 2 * chips
    step = width // pieces
    lanes = channels // 128
    own_ref[...] = jnp.zeros_like(own_ref)
    own_ref[: KERNEL + 1, :] = value_small_ref[: KERNEL + 1, :]
    own_ref[KERNEL + 1 : KERNEL + 3, :] = gate_small_ref[:2, :]
    for begin in range(0, width, BLOCK):
        block = slice(begin, begin + BLOCK)
        columns = normed_ref[HALO:, block]
        value = dot_tn(columns, value_ref[...])
        state = dot_tn(columns, state_ref[...])
        blocks_ref[block, :channels] = value
        blocks_ref[block, channels:] = state
        gains_ref[0:1, block] = (
            gain_ref[0:1, block]
            + gain_row(value_weight_ref[block, :], value)
            + gain_row(state_weight_ref[block, :], state)
        ) / gain_full_ref[0:1, block]
    shared_ref[...] = jnp.zeros_like(shared_ref)
    for i in range(width // channels):
        shared_ref[i : i + 1, :] = gains_ref[0:1, i * channels : (i + 1) * channels]
    begin = width // channels
    for i in range(0, (KERNEL + 1) * maps_width, 128):
        tap, column_from = divmod(i, maps_width)
        row, column_to = divmod(i, channels)
        shared_ref[begin + row : begin + row + 1, column_to : column_to + 128] = state_small_ref[
            tap : tap + 1, column_from : column_from + 128
        ]
    line = lax.broadcasted_iota(jnp.int32, (HALO, channels), 0)
    part = 2 * step // lanes
    for place in range(pieces):
        piece = blocks_ref[place * step : (place + 1) * step, :]
        state = piece[:, channels:]
        stacked = jnp.concatenate([state[:, :128], state[:, 128:]], axis=0)
        stacked = jnp.concatenate(
            [stacked[i * part : (i + 1) * part] for i in range(lanes)], axis=1
        )
        own, shared = own_ref[place : place + 1, :], shared_ref[place : place + 1, :]
        own_high, shared_high = (v.astype(BF16).astype(F32) for v in (own, shared))
        small = jnp.zeros((HALO, channels), F32)
        for at, line_value in enumerate((own_high, own - own_high, shared_high, shared - shared_high)):
            small = jnp.where(line == at, line_value, small)
        store_piece(
            core_ref, kept_ref, given_ref, place,
            jnp.concatenate([piece[:, :channels], stacked, small], axis=0),
        )


def merge_pairs(block):
    tail = block[-HALO:]
    line = lax.broadcasted_iota(jnp.int32, tail.shape, 0)
    own, shared = tail[0:1] + tail[1:2], tail[2:3] + tail[3:4]
    own_high, shared_high = own.astype(BF16).astype(F32), shared.astype(BF16).astype(F32)
    new = jnp.zeros_like(tail)
    for at, value in enumerate((own_high, own - own_high, shared_high, shared - shared_high)):
        new = jnp.where(line == at, value, new)
    return jnp.concatenate([block[:-HALO], new], axis=0)


def half_kernel(paired, chips, chip_ref, kept_ref, arrived_ref, *outs):
    for bits in range(chips):
        place = lax.bitwise_xor(chip_ref[0], bits)
        value = kept_ref[place].astype(F32) + arrived_ref[place].astype(F32)
        if paired:
            value = merge_pairs(value)
        outs[bits][...] = value.astype(outs[bits].dtype)


def piece_kernel(parts, paired, cut, *refs):
    total = sum(ref[...].astype(F32) for ref in refs[:parts])
    first_ref, last_ref = refs[parts:]
    first_ref[...] = total[:cut].astype(BF16)
    last_ref[...] = (merge_pairs(total[cut:]) if paired else total[cut:]).astype(last_ref.dtype)


def square_half_kernel(
    paired, chip_ref, kept_ref, arrived_ref, first_ref, first_give_ref, last_ref, last_give_ref
):
    cut = first_ref.shape[1]
    for bits in range(4):
        place = lax.bitwise_xor(chip_ref[0], bits)
        value = kept_ref[place].astype(F32) + arrived_ref[place].astype(F32)
        first, last = value[:cut], value[cut:]
        if paired:
            last = merge_pairs(last)
        low, high = bits & 1, bits >> 1
        ref = first_give_ref if low else first_ref
        ref[high] = first.astype(ref.dtype)
        ref = last_give_ref if high else last_ref
        ref[low] = last.astype(ref.dtype)


def square_next_kernel(
    paired, first_ref, first_got_ref, last_ref, last_got_ref,
    first_out_ref, first_give_ref, last_out_ref, last_give_ref,
):
    merge = merge_pairs if paired else (lambda value: value)
    first_out_ref[...] = first_ref[0] + first_got_ref[0].astype(F32)
    first_give_ref[...] = (first_ref[1] + first_got_ref[1].astype(F32)).astype(BF16)
    last_out_ref[...] = merge(last_ref[0] + last_got_ref[0].astype(F32))
    last_give_ref[...] = merge(last_ref[1] + last_got_ref[1].astype(F32)).astype(BF16)


def square_last_kernel(
    paired, first_ref, first_got_ref, last_ref, last_got_ref, first_out_ref, last_out_ref
):
    merge = merge_pairs if paired else (lambda value: value)
    first_out_ref[...] = (first_ref[...] + first_got_ref[...].astype(F32)).astype(BF16)
    last_out_ref[...] = merge(last_ref[...] + last_got_ref[...].astype(F32)).astype(last_out_ref.dtype)


def spread_pieces(core_ref, chip_ref, chips, groups, refs, store):
    step = pl.program_id(0)
    core, chip = step // chips, lax.rem(step, chips)
    apart = lax.bitwise_xor(chip, chip_ref[0])
    refs = iter(refs)
    for part, bits_lists in enumerate(groups):
        for bits_list in bits_lists:
            own_ref, other_ref = next(refs), next(refs)
            for at, bits in enumerate(bits_list):

                @pl.when((apart == bits) & (core == core_ref[0]))
                def _(part=part, ref=own_ref, at=at):
                    store(part, ref[at].astype(F32))

                @pl.when((apart == bits) & (core != core_ref[0]))
                def _(part=part, ref=other_ref, at=at):
                    store(part, ref[at].astype(F32))


def early_out_kernel(chips, groups, core_ref, chip_ref, *refs):
    gate_ref, output_ref = refs[-2:]
    out_rows, width = output_ref.shape
    channels = gate_ref.shape[1]

    def store(part, value):
        if part == 0:
            gate_ref[...] = value
        else:
            output_ref[...] = jnp.concatenate(
                [value[i * out_rows : (i + 1) * out_rows] for i in range(width // channels)], axis=1
            )

    spread_pieces(core_ref, chip_ref, chips, groups, refs[:-2], store)


def late_out_kernel(chips, groups, cut, core_ref, chip_ref, *refs):
    value_ref = refs[-1]

    def store(part, value):
        if part == 0:
            value_ref[:cut, :] = value
        else:
            value_ref[cut:, :] = value

    spread_pieces(core_ref, chip_ref, chips, groups, refs[:-1], store)


def shared_out_kernel(chips, groups, core_ref, chip_ref, *refs):
    (
        state_ref, value_kernel_ref, value_bias_ref, state_kernel_ref, state_bias_ref, skip_ref,
        gated_ref, gain_ref, own_ref, shared_ref,
    ) = refs[-10:]
    step, maps_width = state_ref.shape
    channels = own_ref.shape[1]
    lanes = channels // 128
    rows = 2 * step // lanes
    at = pl.program_id(0)

    def store(part, piece):
        stacked = jnp.concatenate(
            [piece[:rows, i * 128 : (i + 1) * 128] for i in range(lanes)], axis=0
        )
        state_ref[...] = jnp.concatenate([stacked[:step], stacked[step:]], axis=1)
        own_ref[pl.ds(at, 1), :] = piece[rows : rows + 1] + piece[rows + 1 : rows + 2]
        shared_ref[pl.ds(at, 1), :] = piece[rows + 2 : rows + 3] + piece[rows + 3 : rows + 4]

    spread_pieces(core_ref, chip_ref, chips, groups, refs[:-10], store)

    @pl.when(at == 2 * chips - 1)
    def _():
        value_kernel_ref[...] = own_ref[:KERNEL, :]
        value_bias_ref[...] = own_ref[KERNEL : KERNEL + 1, :]
        gated_ref[...] = own_ref[KERNEL + 1 : KERNEL + 2, :]
        skip_ref[...] = own_ref[KERNEL + 2 : KERNEL + 3, :]
        gain_rows = gain_ref.shape[1] // channels
        for i in range(gain_rows):
            gain_ref[:, i * channels : (i + 1) * channels] = shared_ref[i : i + 1, :]
        for i in range(0, (KERNEL + 1) * maps_width, 128):
            tap, column_to = divmod(i, maps_width)
            row, column_from = divmod(i, channels)
            value = shared_ref[gain_rows + row : gain_rows + row + 1, column_from : column_from + 128]
            if tap < KERNEL:
                state_kernel_ref[tap : tap + 1, column_to : column_to + 128] = value
            else:
                state_bias_ref[:, column_to : column_to + 128] = value


SCALAR = "scalar"
WHOLE = "whole"
BLOCKED = "blocked"
LANES = "lanes"
LEADING = "leading"
LOOSE = "loose"


def run(kernel, name, flops, args, outs, steps=None, backward=False, scratch=()):
    at = (lambda i: steps - 1 - i) if backward else (lambda i: i)

    def spec(kind, shape):
        if isinstance(kind, int):
            return pl.BlockSpec((kind,) + shape[1:], lambda i: (at(i), 0))
        if kind == SCALAR:
            return pl.BlockSpec(memory_space=pltpu.SMEM)
        if kind == LOOSE:
            return pl.BlockSpec(memory_space=pl.ANY)
        if steps is None:
            return pl.BlockSpec(memory_space=pltpu.VMEM)
        if kind == BLOCKED:
            return pl.BlockSpec((CHUNK, shape[1]), lambda i: (at(i), 0))
        if kind == LANES:
            return pl.BlockSpec((shape[0], CHUNK), lambda i: (0, at(i)))
        if kind == LEADING:
            return pl.BlockSpec((1,) + shape[1:], lambda i: (at(i),) + (0,) * (len(shape) - 1))
        return pl.BlockSpec(shape, lambda i: (0,) * len(shape))

    moved = sum(a.size * a.dtype.itemsize for kind, a in args if kind != LOOSE)
    shapes = [jax.ShapeDtypeStruct(shape, dtype) for _, shape, dtype in outs]
    moved += sum(a.size * a.dtype.itemsize for a in shapes)
    return pl.pallas_call(
        kernel,
        out_shape=shapes,
        in_specs=[spec(kind, a.shape) for kind, a in args],
        out_specs=[spec(kind, shape) for kind, shape, _ in outs],
        scratch_shapes=list(scratch),
        compiler_params=pltpu.CompilerParams(vmem_limit_bytes=VMEM_LIMIT),
        cost_estimate=pl.CostEstimate(flops=flops, bytes_accessed=moved, transcendentals=0),
        name=name,
        **({} if steps is None else {"grid": (steps,)}),
    )(*(a for _, a in args))


def per_device(
    tokens, decay_codes, norm_gain, gate_weight, value_weight, state_weight, value_kernel, value_bias,
    state_kernel, state_bias, skip_scale, gated_gain, output_weight, cotangent,
):
    tokens, decay_codes, cotangent = tokens[0], decay_codes[0], cotangent[0]
    count, own_width = tokens.shape
    heads = skip_scale.shape[0]
    channels = heads * HEAD_DIM
    head_size, chips = lax.axis_size("head"), lax.axis_size("chip")
    seq_size = 2 * chips
    width = own_width * head_size
    maps_width = 2 * NSTATE
    chunks = count // CHUNK
    core = (SCALAR, lax.axis_index("core").astype(jnp.int32)[None])
    chip = (SCALAR, lax.axis_index("chip").astype(jnp.int32)[None])
    head = (SCALAR, lax.axis_index("head").astype(jnp.int32)[None])

    parts, passed = line_parts(tokens, "head")
    before = from_behind(tokens[-HALO:], 1)
    margins = turn_all(
        jnp.concatenate([before, jnp.broadcast_to(norm_gain[None], (HALO, own_width))], axis=0),
        "head",
    )
    logs = decay_codes.astype(F32) * (-DECAY_STEP)
    input_weight = jnp.sqrt(-jnp.expm1(2.0 * logs))
    e_full, f_full, factors = run(
        decay_kernel, "decays", count * channels * 200,
        [(WHOLE, decay_codes), (WHOLE, input_weight)],
        [
            (WHOLE, (count, channels), F32),
            (WHOLE, (count, channels), F32),
            (WHOLE, (8, channels), F32),
        ],
    )
    all_logs = lax.all_to_all(
        jnp.broadcast_to(factors[None], (seq_size, 8, channels)), ("chip", "core"), 0, 0
    )[:, 7].reshape(chips, 2, channels)
    pair_logs = jnp.sum(all_logs, axis=1)
    own_logs = lax.dynamic_index_in_dim(all_logs, lax.axis_index("chip"), 0, keepdims=False)
    own_decay = jnp.exp(lax.dynamic_index_in_dim(own_logs, lax.axis_index("core"), 0))
    other_decay = jnp.exp(lax.dynamic_index_in_dim(own_logs, 1 - lax.axis_index("core"), 0))
    before_weights = decay_weights(pair_logs, False)
    after_weights = decay_weights(pair_logs, True)
    skip_full = jnp.repeat(skip_scale, HEAD_DIM)[None]

    normed, full, gain_full, scale_in, cotangent_copy = run(
        functools.partial(norm_kernel, head_size), "norm", count * width * 10,
        [head] + [(WHOLE, a) for a in [passed] + parts + margins + [cotangent]],
        [
            (WHOLE, (HALO + count, width), BF16),
            (WHOLE, (count, width), BF16),
            (WHOLE, (8, width), F32),
            (WHOLE, (count, 128), F32),
            (WHOLE, (head_size, count, own_width), BF16),
        ],
        scratch=[pltpu.VMEM((HALO, width), BF16)],
    )
    cotangent_parts = deal(cotangent_copy, "head")
    value_raw = dot(normed, value_weight).astype(BF16)
    state_raw = dot(normed, state_weight).astype(BF16)
    conv, weighted, value_slope, maps, map_slope, local_end = run(
        conv_kernel, "conv", count * channels * 400,
        [
            (WHOLE, value_raw), (WHOLE, state_raw), (WHOLE, value_kernel), (WHOLE, value_bias[None]),
            (WHOLE, state_kernel), (WHOLE, state_bias[None]), (BLOCKED, f_full), (WHOLE, factors),
        ],
        [
            (BLOCKED, (count, channels), BF16),
            (BLOCKED, (count, channels), BF16),
            (BLOCKED, (count, channels), F32),
            (BLOCKED, (count, maps_width), BF16),
            (BLOCKED, (count, maps_width), F32),
            (WHOLE, (NSTATE, channels), F32),
        ],
        steps=chunks,
    )
    state_in, _ = entering(local_end, own_decay, other_decay, before_weights, False)
    gate_pre = dot(normed[HALO:], gate_weight)
    full_cotangent = run(
        place_kernel, "place", count * width, [(WHOLE, cotangent_parts)],
        [(WHOLE, (count, width), BF16)],
    )[0]
    mixed_grad = dot_nt(full_cotangent, output_weight)
    mixer, stats, high, low = run(
        mixer_kernel, "mixer", count * channels * 1000,
        [
            (WHOLE, state_in), (BLOCKED, maps), (BLOCKED, weighted), (BLOCKED, conv),
            (BLOCKED, e_full), (WHOLE, factors), (WHOLE, skip_full), (BLOCKED, gate_pre),
            (BLOCKED, mixed_grad), (WHOLE, gated_gain[None]),
        ],
        [
            (BLOCKED, (count, channels), F32),
            (LANES, (8, count), F32),
            (LEADING, (chunks, NSTATE, channels), BF16),
            (LEADING, (chunks, NSTATE, channels), BF16),
        ],
        steps=chunks,
        scratch=[pltpu.VMEM((NSTATE, channels), F32)],
    )
    mixed, gate_grad, mixer_grad, gate_small, start_grad = run(
        functools.partial(gate_kernel, float(channels * head_size), chunks, head_size),
        "gate", count * channels * 600,
        [(LANES, part) for part in turn_all(stats, "head")]
        + [
            (BLOCKED, mixer), (BLOCKED, gate_pre), (BLOCKED, mixed_grad), (WHOLE, gated_gain[None]),
            (BLOCKED, conv), (BLOCKED, e_full), (WHOLE, factors), (BLOCKED, maps),
        ],
        [
            (BLOCKED, (count, channels), BF16),
            (BLOCKED, (count, channels), BF16),
            (BLOCKED, (count, channels), F32),
            (WHOLE, (8, channels), F32),
            (WHOLE, (NSTATE, channels), F32),
        ],
        steps=chunks,
        backward=True,
    )
    grad_after, pair = entering(start_grad, own_decay, other_decay, after_weights, True)

    out_parts = run(
        out_kernel, "out", 2 * count * channels * width,
        [(LOOSE, start_grad), (WHOLE, mixed), (WHOLE, output_weight)],
        [(WHOLE, (head_size, count, own_width), BF16)],
    )[0]
    step, out_rows = width // seq_size, channels // seq_size
    rows = step + out_rows * (width // channels)
    early_kept, early_given, early_gain = run(
        early_kernel, "early", 4 * count * channels * width,
        [
            (LOOSE, pair), core, (WHOLE, normed), (WHOLE, gate_grad), (WHOLE, mixed),
            (WHOLE, full_cotangent), (WHOLE, gate_weight),
        ],
        [(WHOLE, (chips, rows, channels), BF16)] * 2 + [(WHOLE, (1, width), F32)],
        scratch=[pltpu.VMEM((channels, width), F32)],
    )
    early_gate, early_out, early_mark = sum_pieces(
        chip, early_kept, early_given, step, False, "early"
    )
    branch = jnp.sum(deal(out_parts, "head").astype(F32), axis=0)
    block_out = (tokens.astype(F32) + branch).astype(BF16)

    value_grads, map_grads = run(
        functools.partial(back_kernel, chunks), "back", count * channels * 2000,
        [
            (LOOSE, early_given), (LOOSE, out_parts), (WHOLE, grad_after), (BLOCKED, mixer_grad), (BLOCKED, e_full),
            (BLOCKED, f_full), (WHOLE, factors), (BLOCKED, weighted), (LEADING, high),
            (LEADING, low), (BLOCKED, maps), (BLOCKED, value_slope), (BLOCKED, map_slope),
            (WHOLE, skip_full),
        ],
        [(BLOCKED, (count, channels), F32), (BLOCKED, (count, maps_width), F32)],
        steps=chunks,
        backward=True,
        scratch=[pltpu.VMEM((NSTATE, channels), F32)],
    )
    after = from_behind(jnp.concatenate([value_grads[:8], map_grads[:8]], axis=1), -1)
    value_raw_grad, state_raw_grad, value_small, state_small = run(
        functools.partial(conv_back_kernel, chunks), "conv_back", count * channels * 100,
        [
            (LOOSE, early_mark), (BLOCKED, value_grads), (BLOCKED, map_grads), (WHOLE, after),
            (WHOLE, value_raw), (WHOLE, state_raw), (WHOLE, value_kernel), (WHOLE, state_kernel),
        ],
        [
            (BLOCKED, (count, channels), BF16),
            (BLOCKED, (count, maps_width), BF16),
            (WHOLE, (8, channels), F32),
            (WHOLE, (8, maps_width), F32),
        ],
        steps=chunks,
        backward=True,
        scratch=[pltpu.VMEM((8, channels), F32), pltpu.VMEM((8, maps_width), F32)],
    )
    lanes = channels // 128
    state_rows = 2 * step // lanes
    late_rows = step + state_rows + HALO
    late_kept, late_given = run(
        late_kernel, "late", 3 * count * channels * width,
        [
            core, (WHOLE, normed), (WHOLE, value_raw_grad), (WHOLE, state_raw_grad),
            (WHOLE, value_small), (WHOLE, gate_small), (WHOLE, early_gain), (WHOLE, state_small),
            (WHOLE, value_weight), (WHOLE, state_weight), (WHOLE, gain_full),
        ],
        [(WHOLE, (chips, late_rows, channels), BF16)] * 2,
        scratch=[
            pltpu.VMEM((HALO, channels), F32),
            pltpu.VMEM((HALO, channels), F32),
            pltpu.VMEM((8, width), F32),
            pltpu.VMEM((width, channels + maps_width), F32),
        ],
    )
    normed_parts = run(
        normed_kernel, "normed", 4 * count * channels * width,
        [
            (LOOSE, late_given), (WHOLE, gate_grad), (WHOLE, value_raw_grad),
            (WHOLE, state_raw_grad), (WHOLE, gate_weight), (WHOLE, value_weight),
            (WHOLE, state_weight), (WHOLE, full), (WHOLE, gain_full),
        ],
        [(WHOLE, (head_size, count + HALO, own_width), BF16)],
    )[0]
    normed_parts = deal(normed_parts, "head")
    late_cut = step // 3 * 2 // 16 * 16
    late_first, late_rest, _ = sum_pieces(chip, late_kept, late_given, late_cut, True, "late")
    late_last, shared_piece = late_rest[: step - late_cut].astype(BF16), late_rest[step - late_cut :]
    summed = butterfly(shared_piece, "head")
    line = jnp.arange(late_rows - step)[:, None]
    own_line = (line >= state_rows) & (line < state_rows + 2)
    tail = summed[state_rows + 2 : state_rows + 3] + summed[state_rows + 3 : state_rows + 4]
    tail_high = tail.astype(BF16).astype(F32)
    summed = jnp.where(
        line == state_rows + 2, tail_high, jnp.where(line == state_rows + 3, tail - tail_high, summed)
    )
    shared_piece = jnp.where(own_line, shared_piece, summed).astype(BF16)

    def unpack(kernel, name, pieces, outs, flops, extra=(), scratch=()):
        groups = [collect(piece, order) for piece, order in pieces]
        bits = [[found[2] for found in group] for group in groups]
        arrays = [(WHOLE, value) for group in groups for found in group for value in found[:2]]
        return run(
            functools.partial(kernel, chips, bits, *extra), name, flops, [core, chip] + arrays, outs,
            steps=seq_size, scratch=scratch,
        )

    gate_weight_gradient, output_weight_gradient = unpack(
        early_out_kernel, "early_out", [(early_gate, (2, 1)), (early_out, (1, 2))],
        [(step, (width, channels), F32), (out_rows, (channels, width), F32)], 4 * channels * width,
    )
    value_weight_gradient = unpack(
        late_out_kernel, "late_out", [(late_first, (2, 1)), (late_last, (1, 2))],
        [(step, (width, channels), F32)], 2 * channels * width, extra=(late_cut,),
    )[0]
    (
        state_weight_gradient, value_kernel_gradient, value_bias_gradient, state_kernel_gradient,
        state_bias_gradient, skip_sums, gated_gain_gradient, gain_sums,
    ) = unpack(
        shared_out_kernel, "shared_out", [(shared_piece, (2, 1))],
        [
            (step, (width, maps_width), F32),
            (WHOLE, (KERNEL, channels), F32),
            (WHOLE, (1, channels), F32),
            (WHOLE, (KERNEL, maps_width), F32),
            (WHOLE, (1, maps_width), F32),
            (WHOLE, (1, channels), F32),
            (WHOLE, (1, channels), F32),
            (WHOLE, (1, width), F32),
        ],
        2 * maps_width * width,
        scratch=[pltpu.VMEM((HALO, channels), F32), pltpu.VMEM((HALO, channels), F32)],
    )
    value_bias_gradient, state_bias_gradient = value_bias_gradient[0], state_bias_gradient[0]
    gated_gain_gradient = gated_gain_gradient[0]
    skip_scale_gradient = jnp.sum(skip_sums.reshape(heads, HEAD_DIM), axis=1)
    norm_gain_gradient = lax.dynamic_slice_in_dim(
        gain_sums[0], lax.axis_index("head") * own_width, own_width, 0
    )

    tokens_gradient = run(
        functools.partial(last_kernel, float(width)), "last", count * own_width * 20,
        [
            (LOOSE, gate_weight_gradient), (WHOLE, normed_parts), (WHOLE, tokens), (WHOLE, scale_in),
            (WHOLE, norm_gain[None]), (WHOLE, cotangent),
        ],
        [(WHOLE, (count, own_width), BF16)],
    )[0]
    return (
        block_out[None],
        tokens_gradient[None],
        norm_gain_gradient,
        gate_weight_gradient,
        value_weight_gradient,
        state_weight_gradient,
        value_kernel_gradient,
        value_bias_gradient,
        state_kernel_gradient,
        state_bias_gradient,
        skip_scale_gradient,
        gated_gain_gradient,
        output_weight_gradient,
    )


def solution(mesh):
    seq_size, head_size = mesh.shape["seq"], mesh.shape["head"]
    mesh = Mesh(mesh.devices.reshape(seq_size // 2, 2, head_size), ("chip", "core", "head"))
    seq = ("chip", "core")
    in_specs = (
        P(None, seq, "head"),
        P(None, seq, "head"),
        P("head"),
        P(None, "head"),
        P(None, "head"),
        P(),
        P(None, "head"),
        P("head"),
        P(),
        P(),
        P("head"),
        P("head"),
        P("head", None),
        P(None, seq, "head"),
    )
    out_specs = (
        P(None, seq, "head"),
        P(None, seq, "head"),
        P("head"),
        P(None, "head"),
        P(None, "head"),
        P(),
        P(None, "head"),
        P("head"),
        P(),
        P(),
        P("head"),
        P("head"),
        P("head", None),
    )
    return jax.shard_map(
        per_device, mesh=mesh, in_specs=in_specs, out_specs=out_specs, check_vma=False
    )
```

```python
import functools

import jax
import jax.numpy as jnp
from jax import lax
from jax.experimental import pallas as pl
from jax.experimental.pallas import tpu as pltpu
from jax.sharding import Mesh
from jax.sharding import PartitionSpec as P

HEAD_DIM = 64
NSTATE = 128
KERNEL = 4
CHUNK = 128
BLOCK = 384
VMEM_LIMIT = 56 * 1024 * 1024
MARGIN = 32
HALO = 16


DECAY_STEP = 1.0 / 1048576.0
EPSILON = 1e-05
BF16 = jnp.bfloat16
F32 = jnp.float32


def tie_kernel(*refs):
    del refs


def tie(value, *others):
    return pl.pallas_call(
        tie_kernel,
        out_shape=jax.ShapeDtypeStruct(value.shape, value.dtype),
        in_specs=[pl.BlockSpec(memory_space=pl.ANY)] * (1 + len(others)),
        out_specs=pl.BlockSpec(memory_space=pl.ANY),
        input_output_aliases={0: 0},
        name="tie",
    )(value, *others)


def from_behind(value, by):
    axis = ("chip", "core")
    size = lax.axis_size("chip") * 2
    pairs = [(i, i + by) for i in range(size) if 0 <= i + by < size]
    return lax.ppermute(value, axis, pairs)


def beside(value):
    return lax.ppermute(value, "core", [(0, 1), (1, 0)])


def turn(value, axis, by):
    size = lax.axis_size(axis)
    return lax.ppermute(value, axis, [(i, (i + by) % size) for i in range(size)])


def turn_all(value, axis):
    return [value] + [turn(value, axis, by) for by in range(1, lax.axis_size(axis))]


def line_parts(value, axis, meanwhile):
    if lax.axis_size(axis) != 4:
        return turn_all(value, axis), value
    two = tie(turn(value, axis, 2), meanwhile)
    one = lax.ppermute(value, axis, [(0, 1), (1, 2), (2, 3)])
    three = lax.ppermute(value, axis, [(1, 0), (2, 1), (3, 2)])
    passed = lax.ppermute(two, axis, [(2, 3), (1, 0)])
    return [value, one, two, three], passed


def deal(parts, axis):
    return lax.all_to_all(parts, axis, 0, 0)


def cross(value, bits):
    return lax.ppermute(value, "chip", [(i, i ^ bits) for i in range(lax.axis_size("chip"))])


def cross_all(value):
    return [value] + [cross(value, bits) for bits in range(1, lax.axis_size("chip"))]


def butterfly(value, axis):
    bits = 1
    while bits < lax.axis_size(axis):
        size = lax.axis_size(axis)
        value = value + lax.ppermute(value, axis, [(i, i ^ bits) for i in range(size)])
        bits *= 2
    return value


def entering(total, weights, first_row, backward, meanwhile):
    core = lax.axis_index("core")
    receives = core == (0 if backward else 1)
    own_decay, other_decay = weights[16:17], weights[17:18]
    half = total.shape[0] // 2
    partner = tie(beside(total), meanwhile)
    part = lambda value: lax.dynamic_slice_in_dim(value, core * half, half, 0)
    pair = jnp.where(
        receives,
        own_decay * part(partner) + part(total),
        other_decay * part(total) + part(partner),
    )
    prefix, mark = jnp.zeros_like(pair), None
    for bits in range(1, lax.axis_size("chip")):
        arrived = cross(pair, bits)
        mark = arrived if mark is None else mark
        prefix = prefix + arrived * weights[first_row + bits : first_row + bits + 1]
    other = beside(prefix)
    whole = jnp.where(
        core == 0,
        jnp.concatenate([prefix, other], axis=0),
        jnp.concatenate([other, prefix], axis=0),
    )
    return jnp.where(receives, other_decay * whole + partner, whole), mark


def sum_pieces(chip, kept, given, cut, paired, name, square):
    chips, rows, channels = kept.shape
    arrived = beside(given)
    rest = rows - cut
    size = chips * rows * channels
    if chips != 4 or not square:
        halves = run(
            functools.partial(half_kernel, paired, chips), name + "_half", size,
            [chip, (WHOLE, kept), (WHOLE, arrived)],
            [(WHOLE, (rows, channels), F32)] + [(WHOLE, (rows, channels), BF16)] * (chips - 1),
        )
        parts = [halves[0]] + [cross(halves[bits], bits) for bits in range(1, chips)]
        first, last = run(
            functools.partial(piece_kernel, chips, paired, cut), name + "_piece", size,
            [(WHOLE, part) for part in parts],
            [(WHOLE, (cut, channels), BF16), (WHOLE, (rest, channels), F32 if paired else BF16)],
        )
        return first, last, halves[0], halves[0]
    first, first_give, last, last_give = run(
        functools.partial(square_half_kernel, paired), name + "_half", size,
        [chip, (WHOLE, kept), (WHOLE, arrived)],
        [
            (WHOLE, (2, cut, channels), F32), (WHOLE, (2, cut, channels), BF16),
            (WHOLE, (2, rest, channels), F32), (WHOLE, (2, rest, channels), BF16),
        ],
    )
    half_mark = first
    first, first_give, last, last_give = run(
        functools.partial(square_next_kernel, paired), name + "_next", size,
        [
            (WHOLE, first), (WHOLE, cross(first_give, 1)),
            (WHOLE, last), (WHOLE, cross(last_give, 2)),
        ],
        [
            (WHOLE, (cut, channels), F32), (WHOLE, (cut, channels), BF16),
            (WHOLE, (rest, channels), F32), (WHOLE, (rest, channels), BF16),
        ],
    )
    next_mark = first
    first, last = run(
        functools.partial(square_last_kernel, paired), name + "_piece", size,
        [
            (WHOLE, first), (WHOLE, cross(first_give, 2)),
            (WHOLE, last), (WHOLE, cross(last_give, 1)),
        ],
        [(WHOLE, (cut, channels), BF16), (WHOLE, (rest, channels), F32 if paired else BF16)],
    )
    return first, last, half_mark, next_mark


def collect(piece, order):
    chips = lax.axis_size("chip")
    if chips != 4 or order is None:
        found = [(value[None], (bits,)) for bits, value in enumerate(cross_all(piece))]
    else:
        near, far = order
        both = jnp.stack([piece, cross(piece, near)])
        found = [(both, (0, near)), (cross(both, far), (far, far ^ near))]
    return [(value, beside(value), bits) for value, bits in found]


def dot(left, right):
    return jnp.dot(left, right, preferred_element_type=F32)


def dot_nt(left, right):
    return lax.dot_general(left, right, (((1,), (1,)), ((), ())), preferred_element_type=F32)


def dot_tn(left, right):
    return lax.dot_general(left, right, (((0,), (0,)), ((), ())), preferred_element_type=F32)


def split(values):
    high = values.astype(BF16)
    return high, (values - high.astype(F32)).astype(BF16)


def lower_mask():
    row = lax.broadcasted_iota(jnp.int32, (CHUNK, CHUNK), 0)
    column = lax.broadcasted_iota(jnp.int32, (CHUNK, CHUNK), 1)
    return row >= column


def decay_kernel(codes_ref, weight_ref, e_ref, f_ref, k_ref, logs_ref):
    heads, channels = codes_ref.shape[1], e_ref.shape[1]
    row = lax.broadcasted_iota(jnp.int32, (heads, channels), 0)
    column = lax.broadcasted_iota(jnp.int32, (heads, channels), 1)
    first = row * HEAD_DIM
    spread = jnp.where((column >= first) & (column < first + HEAD_DIM), 1.0, 0.0).astype(BF16)

    def expand(values):
        high, low = split(values)
        return dot(high, spread) + dot(low, spread)

    lower = jnp.where(lower_mask(), 1.0, 0.0).astype(F32)
    count = codes_ref.shape[0] // CHUNK
    line = lax.broadcasted_iota(jnp.int32, (8, heads), 0)
    marks = jnp.zeros((8, heads), F32)
    total = jnp.zeros((1, heads), F32)
    for chunk in range(count):
        rows = pl.ds(chunk * CHUNK, CHUNK)
        logs = codes_ref[rows, :].astype(F32) * (-DECAY_STEP)
        cumulative = jnp.dot(
            lower, logs, precision=lax.Precision.HIGHEST, preferred_element_type=F32
        )
        last = cumulative[CHUNK - 1 :]
        middle = 0.5 * last
        e_ref[rows, :] = expand(jnp.exp(cumulative - middle))
        f_ref[rows, :] = expand(weight_ref[rows, :] * jnp.exp(middle - cumulative))
        marks = jnp.where(line == chunk, jnp.exp(middle), marks)
        total = total + last
    marks = jnp.where(line == 7, total, marks)
    high, low = split(marks)
    lowest = (marks - high.astype(F32) - low.astype(F32)).astype(BF16)
    factors = dot(high, spread) + dot(low, spread) + dot(lowest, spread)
    k_ref[...] = factors
    for place in range(logs_ref.shape[0]):
        logs_ref[place] = jnp.broadcast_to(factors[7:8], (8, channels))


def weights_kernel(core_ref, chip_ref, logs_ref, out_ref):
    chips = logs_ref.shape[0] // 2
    core, chip = core_ref[0], chip_ref[0]
    logs = [logs_ref[i, 0:1, :] for i in range(2 * chips)]
    pairs = [logs[2 * i] + logs[2 * i + 1] for i in range(chips)]
    zero = jnp.zeros_like(logs[0])
    out_ref[...] = jnp.zeros_like(out_ref)
    for bits in range(1, chips):
        source = lax.bitwise_xor(chip, bits)
        before, after = zero, zero
        for middle in range(chips):
            before = before + jnp.where((source < middle) & (middle < chip), pairs[middle], 0.0)
            after = after + jnp.where((source > middle) & (middle > chip), pairs[middle], 0.0)
        out_ref[bits : bits + 1, :] = jnp.where(source < chip, jnp.exp(before), 0.0)
        out_ref[8 + bits : 9 + bits, :] = jnp.where(source > chip, jnp.exp(after), 0.0)
    own, other = zero, zero
    for device in range(2 * chips):
        own = own + jnp.where(2 * chip + core == device, logs[device], 0.0)
        other = other + jnp.where(2 * chip + 1 - core == device, logs[device], 0.0)
    out_ref[16:17, :] = jnp.exp(own)
    out_ref[17:18, :] = jnp.exp(other)


def taps(window, kernel, bias, begin):
    summed = bias
    for offset in range(KERNEL):
        summed = summed + kernel[offset : offset + 1] * window[begin + offset : begin + offset + CHUNK]
    return summed


def silu_parts(values):
    sigmoid = jax.nn.sigmoid(values)
    return values * sigmoid, sigmoid * (1.0 + values * (1.0 - sigmoid))


def first_step(action):
    pl.when(pl.program_id(0) == 0)(action)


def clear(*refs):
    def action():
        for ref in refs:
            ref[...] = jnp.zeros_like(ref)

    first_step(action)


def place_parts(mine, parts, target, width, value):
    size = len(parts)
    if width % 128 == 0:
        for i in range(size):
            owner = lax.rem(mine + size - i, size)
            target[:, pl.ds(pl.multiple_of(owner * width, 128), width)] = value(i)
        return

    def write(me):
        for i in range(size):
            owner = (me + size - i) % size
            target[:, owner * width : (owner + 1) * width] = value(i)

    for me in range(size):
        pl.when(mine == me)(functools.partial(write, me))


def norm_kernel(size, head_ref, passed_ref, *refs):
    parts, gains = refs[:size], refs[size : 2 * size]
    passed_gain_ref, own_ref, normed_ref, scale_ref, copy_ref, gain_ref = refs[2 * size :]
    width = parts[0].shape[1]
    mine = head_ref[0]

    def pick(i, refs, passed):
        if size == 4 and i == 1:
            return jnp.where(mine == 0, passed[...], refs[i][...])
        if size == 4 and i == 3:
            return jnp.where(mine == 3, passed[...], refs[i][...])
        return refs[i][...]

    part = lambda i: pick(i, parts, passed_ref).astype(F32)
    gain = lambda i: pick(i, gains, passed_gain_ref)[0:1].astype(F32)
    squares = sum(jnp.sum(part(i) ** 2, axis=1, keepdims=True) for i in range(size))
    scale = lax.rsqrt(squares / (size * width) + EPSILON)
    scale_ref[...] = jnp.broadcast_to(scale, scale_ref.shape)
    place_parts(
        mine, parts, normed_ref, width,
        lambda i: (part(i) * scale_ref[:, 0:1] * gain(i)).astype(BF16),
    )
    place_parts(mine, parts, gain_ref, width, lambda i: jnp.broadcast_to(gain(i), (8, width)))
    for i in range(size):
        copy_ref[i] = own_ref[...]


def place_kernel(parts_ref, target):
    width = parts_ref.shape[2]
    for i in range(parts_ref.shape[0]):
        target[:, i * width : (i + 1) * width] = parts_ref[i]


def conv_kernel(
    value_ref, state_ref, value_kernel_ref, value_bias_ref, state_kernel_ref, state_bias_ref,
    f_ref, k_ref, conv_ref, weighted_ref, value_slope_ref, maps_ref, state_slope_ref, total_ref,
):
    chunk = pl.program_id(0)
    clear(total_ref)
    around = pl.ds(pl.multiple_of(chunk * CHUNK, CHUNK), CHUNK + HALO)
    pre = taps(
        state_ref[around, :].astype(F32), state_kernel_ref[...].astype(F32),
        state_bias_ref[...].astype(F32), HALO - KERNEL + 1,
    )
    conv, slope = silu_parts(pre)
    maps = conv.astype(BF16)
    maps_ref[...] = maps
    state_slope_ref[...] = slope
    pre = taps(
        value_ref[around, :].astype(F32), value_kernel_ref[...].astype(F32),
        value_bias_ref[...].astype(F32), HALO - KERNEL + 1,
    )
    conv, slope = silu_parts(pre)
    conv = conv.astype(BF16)
    conv_ref[...] = conv
    value_slope_ref[...] = slope
    weighted = (conv.astype(F32) * f_ref[...]).astype(BF16)
    weighted_ref[...] = weighted
    factor = k_ref[pl.ds(chunk, 1), :]
    total_ref[...] = factor * (factor * total_ref[...] + dot_tn(maps[:, :NSTATE], weighted))


def mixer_kernel(
    state_in_ref, maps_ref, weighted_ref, conv_ref, e_ref, k_ref, skip_ref, gate_ref, grad_ref, gain_ref,
    mixer_ref, stats_ref, high_ref, low_ref, state_ref,
):
    chunk = pl.program_id(0)

    def start():
        state_ref[...] = state_in_ref[...]

    first_step(start)
    lane = lax.broadcasted_iota(jnp.int32, (CHUNK, CHUNK), 1)
    factor = k_ref[pl.ds(chunk, 1), :]
    input_map, output_map = maps_ref[:, :NSTATE], maps_ref[:, NSTATE:]
    weighted = weighted_ref[...]
    scaled = factor * state_ref[...]
    high, low = split(scaled)
    high_ref[0], low_ref[0] = high, low
    scores = jnp.where(lower_mask(), dot_nt(output_map, input_map), 0.0).astype(BF16)
    mixed = dot(
        jnp.concatenate([scores, output_map], axis=1), jnp.concatenate([weighted, high], axis=0)
    )
    mixed = mixed + dot(output_map, low)
    mixer = e_ref[...] * mixed + skip_ref[...] * conv_ref[...].astype(F32)
    mixer_ref[...] = mixer
    gate = gate_ref[...]
    gated = mixer * (gate * jax.nn.sigmoid(gate))
    squares = jnp.sum(gated * gated, axis=1, keepdims=True)
    products = jnp.sum(gated * (grad_ref[...] * gain_ref[...].astype(F32)), axis=1, keepdims=True)
    sums = jnp.where(lane == 0, squares, jnp.where(lane == 1, products, 0.0))
    stats_ref[...] = sums.T[:8]
    state_ref[...] = factor * (scaled + dot_tn(input_map, weighted))


def column(row_block):
    rest = jnp.zeros((CHUNK - row_block.shape[0], CHUNK), F32)
    return jnp.concatenate([row_block, rest], axis=0).T


def row_of(sums):
    lane = lax.broadcasted_iota(jnp.int32, (CHUNK, CHUNK), 1)
    return jnp.where(lane == 0, sums, 0.0).T[:8]


def gate_kernel(
    inner, chunks, size, *refs
):
    stats_refs = refs[:size]
    (
        mixer_ref, gate_ref, grad_ref, gain_ref, conv_ref, e_ref, k_ref, maps_ref,
        mixed_ref, gate_grad_ref, mixer_grad_ref, small_ref, total_ref, cross_ref,
    ) = refs[size:]
    chunk = chunks - 1 - pl.program_id(0)
    clear(small_ref, total_ref)
    gain = gain_ref[...].astype(F32)
    stats = column(sum(ref[...] for ref in stats_refs))
    scale = lax.rsqrt(stats[:, 0:1] / inner + EPSILON)
    cross_term = stats[:, 1:2] * (scale * scale * scale) / inner
    gate = gate_ref[...]
    silu, slope = silu_parts(gate)
    mixer = mixer_ref[...]
    gated = mixer * silu
    normed = gated * scale
    mixed_ref[...] = (normed * gain).astype(BF16)
    grad = grad_ref[...]
    gated_grad = scale * (grad * gain) - gated * cross_term
    gate_grad = (gated_grad * mixer * slope).astype(BF16)
    gate_grad_ref[...] = gate_grad
    cross_ref[...] = row_of(jnp.sum(gate_grad.astype(F32) * gate, axis=1, keepdims=True))
    mixer_grad = gated_grad * silu
    mixer_grad_ref[...] = mixer_grad
    small_ref[0:1, :] += jnp.sum(grad * normed, axis=0, keepdims=True)
    small_ref[1:2, :] += jnp.sum(mixer_grad * conv_ref[...].astype(F32), axis=0, keepdims=True)
    high, low = split(e_ref[...] * mixer_grad)
    output_map = maps_ref[:, NSTATE:]
    factor = k_ref[pl.ds(chunk, 1), :]
    total_ref[...] = factor * (
        factor * total_ref[...] + (dot_tn(output_map, high) + dot_tn(output_map, low))
    )


def back_kernel(
    chunks, early_ref, out_ref, state_in_ref, mixer_grad_ref, e_ref, f_ref, k_ref, weighted_ref, high_ref, low_ref,
    maps_ref, value_slope_ref, state_slope_ref, skip_ref,
    value_ref, map_ref, state_ref,
):
    chunk = chunks - 1 - pl.program_id(0)

    def start():
        state_ref[...] = state_in_ref[...]

    first_step(start)
    lower = lower_mask()
    row = lax.broadcasted_iota(jnp.int32, (CHUNK, CHUNK), 0)
    upper = row <= lax.broadcasted_iota(jnp.int32, (CHUNK, CHUNK), 1)
    factor = k_ref[pl.ds(chunk, 1), :]
    input_map, output_map = maps_ref[:, :NSTATE], maps_ref[:, NSTATE:]
    weighted = weighted_ref[...]
    mixer_grad = mixer_grad_ref[...]
    high, low = split(e_ref[...] * mixer_grad)
    scaled = factor * state_ref[...]
    state_high, state_low = split(scaled)
    both = jnp.concatenate([weighted, high_ref[0]], axis=0)
    sums = dot_nt(high, both) + dot_nt(low, both)
    score_grad = jnp.where(lower, sums[:, :CHUNK], 0.0).astype(BF16)
    output_grad = sums[:, CHUNK:] + dot_nt(high, low_ref[0]) + dot(score_grad, input_map)
    sums = dot_nt(weighted, jnp.concatenate([state_high, state_low], axis=0))
    input_grad = sums[:, :NSTATE] + sums[:, NSTATE:] + dot_tn(score_grad, output_map)
    scores = jnp.where(upper, dot_nt(input_map, output_map), 0.0).astype(BF16)
    grads = dot(
        jnp.concatenate([scores, input_map], axis=1), jnp.concatenate([high, state_high], axis=0)
    )
    value_ref[...] = (f_ref[...] * grads + skip_ref[...] * mixer_grad) * value_slope_ref[...]
    slope = state_slope_ref[...]
    map_ref[:, :NSTATE] = input_grad * slope[:, :NSTATE]
    map_ref[:, NSTATE:] = output_grad * slope[:, NSTATE:]
    state_ref[...] = factor * (scaled + (dot_tn(output_map, high) + dot_tn(output_map, low)))


def conv_back_kernel(
    chunks, other_ref, value_ref, map_ref, after_ref, value_raw_ref, state_raw_ref, value_kernel_ref,
    state_kernel_ref, cross_in_ref,
    value_grad_ref, state_grad_ref, value_small_ref, state_small_ref, cross_ref, value_next_ref,
    state_next_ref,
):
    chunk = chunks - 1 - pl.program_id(0)
    channels = value_ref.shape[1]
    clear(value_small_ref, state_small_ref)

    def start():
        value_next_ref[...] = after_ref[:, :channels]
        state_next_ref[...] = after_ref[:, channels:]

    first_step(start)

    def back(slope_ref, next_ref, raw_ref, kernel_ref, grad_ref, small_ref):
        kernel = kernel_ref[...].astype(F32)
        slope = slope_ref[...]
        window = jnp.concatenate([slope, next_ref[...]], axis=0)
        around = pl.ds(pl.multiple_of(chunk * CHUNK, CHUNK), CHUNK + HALO)
        raw = raw_ref[around, :].astype(F32)
        grad = jnp.zeros_like(slope)
        for offset in range(KERNEL):
            back_by = KERNEL - 1 - offset
            grad = grad + kernel[offset : offset + 1] * window[back_by : back_by + CHUNK]
            begin = HALO - KERNEL + 1 + offset
            small_ref[offset : offset + 1, :] += jnp.sum(
                slope * raw[begin : begin + CHUNK], axis=0, keepdims=True
            )
        small_ref[KERNEL : KERNEL + 1, :] += jnp.sum(slope, axis=0, keepdims=True)
        grad = grad.astype(BF16)
        grad_ref[...] = grad
        next_ref[...] = slope[:8]
        return jnp.sum(grad.astype(F32) * raw[HALO:], axis=1, keepdims=True)

    crossed = back(map_ref, state_next_ref, state_raw_ref, state_kernel_ref, state_grad_ref, state_small_ref)
    crossed = crossed + back(
        value_ref, value_next_ref, value_raw_ref, value_kernel_ref, value_grad_ref, value_small_ref
    )
    cross_ref[...] = cross_in_ref[...] + row_of(crossed)


def out_kernel(pair_ref, mixed_ref, weight_ref, out_ref):
    width = out_ref.shape[2]
    for owner in range(out_ref.shape[0]):
        value = dot(mixed_ref[...], weight_ref[:, owner * width : (owner + 1) * width])
        out_ref[owner] = value.astype(BF16)


def normed_kernel(
    chunks, late_ref, gate_grad_ref, value_grad_ref, state_grad_ref, gate_weight_ref, value_weight_ref,
    state_weight_ref, cross_ref, out_ref
):
    value = (
        dot_nt(gate_grad_ref[...], gate_weight_ref[...])
        + dot_nt(value_grad_ref[...], value_weight_ref[...])
        + dot_nt(state_grad_ref[...], state_weight_ref[...])
    )
    count = value.shape[0]
    out_ref[0, :count, :] = value.astype(BF16)
    line = lax.broadcasted_iota(jnp.int32, (HALO, CHUNK), 0)
    packed = jnp.zeros((HALO, CHUNK), F32)
    for chunk in range(chunks):
        row = cross_ref[0:1, chunk * CHUNK : (chunk + 1) * CHUNK]
        high = row.astype(BF16).astype(F32)
        packed = jnp.where(line == chunk, high, packed)
        packed = jnp.where(line == chunks + chunk, row - high, packed)
    out_ref[0, count:, :] = jnp.zeros((HALO, value.shape[1]), BF16)
    out_ref[0, count:, :CHUNK] = packed.astype(BF16)


def last_kernel(full_width, loose_ref, parts_ref, tokens_ref, scale_ref, gain_ref, cotangent_ref, out_ref):
    count = tokens_ref.shape[0]
    chunks = count // CHUNK
    size = parts_ref.shape[0]
    crossed = sum(parts_ref[i, count:, :CHUNK].astype(F32) for i in range(size))
    crossed = crossed[:chunks] + crossed[chunks : 2 * chunks]
    for chunk in range(chunks):
        rows = slice(chunk * CHUNK, (chunk + 1) * CHUNK)
        normed_grad = sum(parts_ref[i, rows, :].astype(F32) for i in range(size))
        scale = scale_ref[HALO + chunk * CHUNK : HALO + (chunk + 1) * CHUNK, 0:1]
        total = column(jnp.broadcast_to(crossed[chunk : chunk + 1], (8, CHUNK)))[:, 0:1]
        out_ref[rows, :] = (
            scale * gain_ref[...].astype(F32) * normed_grad
            - tokens_ref[rows, :].astype(F32) * (scale * scale * total / full_width)
            + cotangent_ref[rows, :].astype(F32)
        ).astype(BF16)


def store_piece(core_ref, kept_ref, given_ref, place, begin, piece):
    chips = kept_ref.shape[0]
    core, chip = place // chips, lax.rem(place, chips)
    rows = slice(begin, begin + piece.shape[0])
    piece = piece.astype(BF16)

    @pl.when(core_ref[0] == core)
    def _():
        kept_ref[chip, rows, :] = piece

    @pl.when(core_ref[0] != core)
    def _():
        given_ref[chip, rows, :] = piece


def gain_row(weight, block):
    sums = jnp.sum(weight.astype(F32) * block, axis=1, keepdims=True)
    lane = lax.broadcasted_iota(jnp.int32, (CHUNK, CHUNK), 1)
    rows = [
        jnp.where(lane == 0, sums[i : i + CHUNK], 0.0).T[0:1] for i in range(0, BLOCK, CHUNK)
    ]
    return jnp.concatenate(rows, axis=1)


def early_kernel(
    loose_ref, core_ref, normed_ref, gate_ref, mixed_ref, grad_ref, weight_ref,
    kept_ref, given_ref, gain_ref, held_ref
):
    chips, rows, channels = kept_ref.shape
    at = pl.program_id(0)
    count, width = grad_ref.shape
    pieces = 2 * chips
    step = width // pieces
    out_rows = channels // pieces
    out_blocks = channels // BLOCK
    every = width // BLOCK // out_blocks

    @pl.when(lax.rem(at, every) == 0)
    def _():
        held_ref[...] = dot_tn(mixed_ref[...], grad_ref[...])

    block = dot_tn(normed_ref[HALO : HALO + count, :], gate_ref[...])
    gain_ref[...] = gain_row(weight_ref[...], block)
    for i in range(BLOCK // step):
        place = at * (BLOCK // step) + i
        begin = lax.rem(at, every) * (BLOCK // step * out_rows) + i * out_rows
        own = held_ref[pl.ds(pl.multiple_of(begin, 8), out_rows), :]
        parts = [block[i * step : (i + 1) * step]]
        parts += [own[:, j : j + channels] for j in range(0, width, channels)]
        store_piece(core_ref, kept_ref, given_ref, place, 0, jnp.concatenate(parts, axis=0))


def late_kernel(
    core_ref, normed_ref, value_ref, state_ref, value_small_ref, gate_small_ref, gain_ref,
    state_small_ref, value_weight_ref, state_weight_ref, gain_full_ref,
    kept_ref, given_ref, own_ref, shared_ref, gains_ref,
):
    chips, rows, channels = kept_ref.shape
    at = pl.program_id(0)
    count, maps_width = state_ref.shape
    width = gains_ref.shape[1]
    pieces = 2 * chips
    step = width // pieces
    lanes = channels // 128
    part = 2 * step // lanes
    columns = normed_ref[HALO : HALO + count, :]
    value = dot_tn(columns, value_ref[...])
    state = dot_tn(columns, state_ref[...])
    gain = (
        gain_ref[...] + gain_row(value_weight_ref[...], value) + gain_row(state_weight_ref[...], state)
    ) / gain_full_ref[0:1, :]
    gains_ref[0:1, pl.ds(pl.multiple_of(at * BLOCK, 128), BLOCK)] = gain
    for i in range(BLOCK // step):
        piece = slice(i * step, (i + 1) * step)
        stacked = jnp.concatenate([state[piece, :128], state[piece, 128:]], axis=0)
        stacked = jnp.concatenate(
            [stacked[j * part : (j + 1) * part] for j in range(lanes)], axis=1
        )
        store_piece(
            core_ref, kept_ref, given_ref, at * (BLOCK // step) + i, 0,
            jnp.concatenate([value[piece], stacked], axis=0),
        )

    @pl.when(at == width // BLOCK - 1)
    def _():
        own_ref[...] = jnp.zeros_like(own_ref)
        own_ref[: KERNEL + 1, :] = value_small_ref[: KERNEL + 1, :]
        own_ref[KERNEL + 1 : KERNEL + 3, :] = gate_small_ref[:2, :]
        shared_ref[...] = jnp.zeros_like(shared_ref)
        begin = width // channels
        for i in range(begin):
            shared_ref[i : i + 1, :] = gains_ref[0:1, i * channels : (i + 1) * channels]
        for i in range(0, (KERNEL + 1) * maps_width, 128):
            tap, column_from = divmod(i, maps_width)
            row, column_to = divmod(i, channels)
            shared_ref[begin + row : begin + row + 1, column_to : column_to + 128] = state_small_ref[
                tap : tap + 1, column_from : column_from + 128
            ]
        line = lax.broadcasted_iota(jnp.int32, (HALO, channels), 0)
        for place in range(pieces):
            own, shared = own_ref[place : place + 1, :], shared_ref[place : place + 1, :]
            own_high, shared_high = (v.astype(BF16).astype(F32) for v in (own, shared))
            small = jnp.zeros((HALO, channels), F32)
            for to, value in enumerate((own_high, own - own_high, shared_high, shared - shared_high)):
                small = jnp.where(line == to, value, small)
            store_piece(core_ref, kept_ref, given_ref, place, step + part, small)


def merge_pairs(block):
    tail = block[-HALO:]
    line = lax.broadcasted_iota(jnp.int32, tail.shape, 0)
    own, shared = tail[0:1] + tail[1:2], tail[2:3] + tail[3:4]
    own_high, shared_high = own.astype(BF16).astype(F32), shared.astype(BF16).astype(F32)
    new = jnp.zeros_like(tail)
    for at, value in enumerate((own_high, own - own_high, shared_high, shared - shared_high)):
        new = jnp.where(line == at, value, new)
    return jnp.concatenate([block[:-HALO], new], axis=0)


def half_kernel(paired, chips, chip_ref, kept_ref, arrived_ref, *outs):
    for bits in range(chips):
        place = lax.bitwise_xor(chip_ref[0], bits)
        value = kept_ref[place].astype(F32) + arrived_ref[place].astype(F32)
        if paired:
            value = merge_pairs(value)
        outs[bits][...] = value.astype(outs[bits].dtype)


def piece_kernel(parts, paired, cut, *refs):
    total = sum(ref[...].astype(F32) for ref in refs[:parts])
    first_ref, last_ref = refs[parts:]
    first_ref[...] = total[:cut].astype(BF16)
    last_ref[...] = (merge_pairs(total[cut:]) if paired else total[cut:]).astype(last_ref.dtype)


def square_half_kernel(
    paired, chip_ref, kept_ref, arrived_ref, first_ref, first_give_ref, last_ref, last_give_ref
):
    cut = first_ref.shape[1]
    for bits in range(4):
        place = lax.bitwise_xor(chip_ref[0], bits)
        value = kept_ref[place].astype(F32) + arrived_ref[place].astype(F32)
        first, last = value[:cut], value[cut:]
        if paired:
            last = merge_pairs(last)
        low, high = bits & 1, bits >> 1
        ref = first_give_ref if low else first_ref
        ref[high] = first.astype(ref.dtype)
        ref = last_give_ref if high else last_ref
        ref[low] = last.astype(ref.dtype)


def square_next_kernel(
    paired, first_ref, first_got_ref, last_ref, last_got_ref,
    first_out_ref, first_give_ref, last_out_ref, last_give_ref,
):
    merge = merge_pairs if paired else (lambda value: value)
    first_out_ref[...] = first_ref[0] + first_got_ref[0].astype(F32)
    first_give_ref[...] = (first_ref[1] + first_got_ref[1].astype(F32)).astype(BF16)
    last_out_ref[...] = merge(last_ref[0] + last_got_ref[0].astype(F32))
    last_give_ref[...] = merge(last_ref[1] + last_got_ref[1].astype(F32)).astype(BF16)


def square_last_kernel(
    paired, first_ref, first_got_ref, last_ref, last_got_ref, first_out_ref, last_out_ref
):
    merge = merge_pairs if paired else (lambda value: value)
    first_out_ref[...] = (first_ref[...] + first_got_ref[...].astype(F32)).astype(BF16)
    last_out_ref[...] = merge(last_ref[...] + last_got_ref[...].astype(F32)).astype(last_out_ref.dtype)


def spread_pieces(core_ref, chip_ref, chips, groups, refs, store):
    step = pl.program_id(0)
    core, chip = step // chips, lax.rem(step, chips)
    apart = lax.bitwise_xor(chip, chip_ref[0])
    refs = iter(refs)
    for part, bits_lists in enumerate(groups):
        for bits_list in bits_lists:
            own_ref, other_ref = next(refs), next(refs)
            for at, bits in enumerate(bits_list):

                @pl.when((apart == bits) & (core == core_ref[0]))
                def _(part=part, ref=own_ref, at=at):
                    store(part, ref[at].astype(F32))

                @pl.when((apart == bits) & (core != core_ref[0]))
                def _(part=part, ref=other_ref, at=at):
                    store(part, ref[at].astype(F32))


def early_out_kernel(chips, groups, core_ref, chip_ref, *refs):
    gate_ref, output_ref = refs[-2:]
    out_rows, width = output_ref.shape
    channels = gate_ref.shape[1]

    def store(part, value):
        if part == 0:
            gate_ref[...] = value
        else:
            output_ref[...] = jnp.concatenate(
                [value[i * out_rows : (i + 1) * out_rows] for i in range(width // channels)], axis=1
            )

    spread_pieces(core_ref, chip_ref, chips, groups, refs[:-2], store)


def late_out_kernel(chips, groups, core_ref, chip_ref, *refs):
    value_ref = refs[-1]

    def store(part, value):
        value_ref[...] = value

    spread_pieces(core_ref, chip_ref, chips, groups, refs[:-1], store)


def shared_out_kernel(chips, groups, core_ref, chip_ref, *refs):
    (
        state_ref, value_kernel_ref, value_bias_ref, state_kernel_ref, state_bias_ref, skip_ref,
        gated_ref, gain_ref, own_ref, shared_ref,
    ) = refs[-10:]
    step, maps_width = state_ref.shape
    channels = own_ref.shape[1]
    lanes = channels // 128
    rows = 2 * step // lanes
    at = pl.program_id(0)

    def store(part, piece):
        stacked = jnp.concatenate(
            [piece[:rows, i * 128 : (i + 1) * 128] for i in range(lanes)], axis=0
        )
        state_ref[...] = jnp.concatenate([stacked[:step], stacked[step:]], axis=1)
        own_ref[pl.ds(at, 1), :] = piece[rows : rows + 1] + piece[rows + 1 : rows + 2]
        shared_ref[pl.ds(at, 1), :] = piece[rows + 2 : rows + 3] + piece[rows + 3 : rows + 4]

    spread_pieces(core_ref, chip_ref, chips, groups, refs[:-10], store)

    @pl.when(at == 2 * chips - 1)
    def _():
        value_kernel_ref[...] = own_ref[:KERNEL, :]
        value_bias_ref[...] = own_ref[KERNEL : KERNEL + 1, :]
        gated_ref[...] = own_ref[KERNEL + 1 : KERNEL + 2, :]
        skip_ref[...] = own_ref[KERNEL + 2 : KERNEL + 3, :]
        gain_rows = gain_ref.shape[1] // channels
        for i in range(gain_rows):
            gain_ref[:, i * channels : (i + 1) * channels] = shared_ref[i : i + 1, :]
        for i in range(0, (KERNEL + 1) * maps_width, 128):
            tap, column_to = divmod(i, maps_width)
            row, column_from = divmod(i, channels)
            value = shared_ref[gain_rows + row : gain_rows + row + 1, column_from : column_from + 128]
            if tap < KERNEL:
                state_kernel_ref[tap : tap + 1, column_to : column_to + 128] = value
            else:
                state_bias_ref[:, column_to : column_to + 128] = value


SCALAR = "scalar"
WHOLE = "whole"
BLOCKED = "blocked"
LANES = "lanes"
LEADING = "leading"
LOOSE = "loose"


def run(kernel, name, flops, args, outs, steps=1, backward=False, scratch=()):
    at = (lambda i: steps - 1 - i) if backward else (lambda i: i)

    def spec(kind, shape):
        if isinstance(kind, int):
            return pl.BlockSpec((kind,) + shape[1:], lambda i: (at(i), 0))
        if kind == SCALAR:
            return pl.BlockSpec(memory_space=pltpu.SMEM)
        if kind == LOOSE:
            return pl.BlockSpec(memory_space=pl.ANY)
        if isinstance(kind, tuple):
            return pl.BlockSpec(*kind)
        if kind == BLOCKED:
            return pl.BlockSpec((CHUNK, shape[1]), lambda i: (at(i), 0))
        if kind == LANES:
            return pl.BlockSpec((shape[0], CHUNK), lambda i: (0, at(i)))
        if kind == LEADING:
            return pl.BlockSpec((1,) + shape[1:], lambda i: (at(i),) + (0,) * (len(shape) - 1))
        return pl.BlockSpec(shape, lambda i: (0,) * len(shape))

    moved = sum(a.size * a.dtype.itemsize for kind, a in args if kind != LOOSE)
    shapes = [jax.ShapeDtypeStruct(shape, dtype) for _, shape, dtype in outs]
    moved += sum(a.size * a.dtype.itemsize for a in shapes)
    return pl.pallas_call(
        kernel,
        out_shape=shapes,
        in_specs=[spec(kind, a.shape) for kind, a in args],
        out_specs=[spec(kind, shape) for kind, shape, _ in outs],
        scratch_shapes=list(scratch),
        compiler_params=pltpu.CompilerParams(vmem_limit_bytes=VMEM_LIMIT),
        cost_estimate=pl.CostEstimate(flops=flops, bytes_accessed=moved, transcendentals=0),
        name=name,
        grid=(steps,),
    )(*(a for _, a in args))


def per_device(
    tokens, decay_codes, norm_gain, gate_weight, value_weight, state_weight, value_kernel, value_bias,
    state_kernel, state_bias, skip_scale, gated_gain, output_weight, cotangent,
):
    tokens, decay_codes, cotangent = tokens[0], decay_codes[0], cotangent[0]
    count, own_width = tokens.shape
    heads = skip_scale.shape[0]
    channels = heads * HEAD_DIM
    head_size, chips = lax.axis_size("head"), lax.axis_size("chip")
    seq_size = 2 * chips
    width = own_width * head_size
    maps_width = 2 * NSTATE
    chunks = count // CHUNK
    core = (SCALAR, lax.axis_index("core").astype(jnp.int32)[None])
    chip = (SCALAR, lax.axis_index("chip").astype(jnp.int32)[None])
    head = (SCALAR, lax.axis_index("head").astype(jnp.int32)[None])

    rows = count + MARGIN
    packed = jnp.concatenate(
        [
            from_behind(tokens[-HALO:], 1),
            tokens,
            jnp.broadcast_to(norm_gain[None], (MARGIN - HALO, own_width)),
        ],
        axis=0,
    )
    logs = decay_codes.astype(F32) * (-DECAY_STEP)
    input_weight = jnp.sqrt(-jnp.expm1(2.0 * logs))
    e_full, f_full, factors, all_logs = run(
        decay_kernel, "decays", count * channels * 200,
        [(WHOLE, decay_codes), (WHOLE, input_weight)],
        [
            (WHOLE, (count, channels), F32),
            (WHOLE, (count, channels), F32),
            (WHOLE, (8, channels), F32),
            (WHOLE, (seq_size, 8, channels), F32),
        ],
    )
    all_logs = lax.all_to_all(all_logs, ("chip", "core"), 0, 0)
    weights = run(
        weights_kernel, "weights", channels * 1000, [core, chip, (WHOLE, all_logs)],
        [(WHOLE, (24, channels), F32)],
    )[0]
    parts, passed = line_parts(packed, "head", weights)
    skip_full = jnp.repeat(skip_scale, HEAD_DIM)[None]

    half = rows // 2
    gain_rows = ((MARGIN - HALO, own_width), lambda i: ((HALO + count) // (MARGIN - HALO), 0))
    normed, scale_in, cotangent_copy, gain_full = run(
        functools.partial(norm_kernel, head_size), "norm", count * width * 10,
        [head, (half, passed)] + [(half, part) for part in parts]
        + [(gain_rows, part) for part in parts]
        + [(gain_rows, passed), (count // 2, cotangent)],
        [
            (half, (rows, width), BF16),
            (half, (rows, 128), F32),
            (
                ((head_size, count // 2, own_width), lambda i: (0, i, 0)),
                (head_size, count, own_width), BF16,
            ),
            (WHOLE, (8, width), F32),
        ],
        steps=2,
    )
    cotangent_parts = deal(cotangent_copy, "head")
    value_raw = dot(normed, value_weight).astype(BF16)
    state_raw = dot(normed, state_weight).astype(BF16)
    conv, weighted, value_slope, maps, map_slope, local_end = run(
        conv_kernel, "conv", count * channels * 400,
        [
            (WHOLE, value_raw), (WHOLE, state_raw), (WHOLE, value_kernel), (WHOLE, value_bias[None]),
            (WHOLE, state_kernel), (WHOLE, state_bias[None]), (BLOCKED, f_full), (WHOLE, factors),
        ],
        [
            (BLOCKED, (count, channels), BF16),
            (BLOCKED, (count, channels), BF16),
            (BLOCKED, (count, channels), F32),
            (BLOCKED, (count, maps_width), BF16),
            (BLOCKED, (count, maps_width), F32),
            (WHOLE, (NSTATE, channels), F32),
        ],
        steps=chunks,
    )
    gate_pre = dot(normed, gate_weight)[HALO : HALO + count]
    state_in, _ = entering(local_end, weights, 0, False, gate_pre)
    full_cotangent = run(
        place_kernel, "place", count * width, [(WHOLE, cotangent_parts)],
        [(WHOLE, (count, width), BF16)],
    )[0]
    mixed_grad = dot_nt(full_cotangent, output_weight)
    mixer, stats, high, low = run(
        mixer_kernel, "mixer", count * channels * 1000,
        [
            (WHOLE, state_in), (BLOCKED, maps), (BLOCKED, weighted), (BLOCKED, conv),
            (BLOCKED, e_full), (WHOLE, factors), (WHOLE, skip_full), (BLOCKED, gate_pre),
            (BLOCKED, mixed_grad), (WHOLE, gated_gain[None]),
        ],
        [
            (BLOCKED, (count, channels), F32),
            (LANES, (8, count), F32),
            (LEADING, (chunks, NSTATE, channels), BF16),
            (LEADING, (chunks, NSTATE, channels), BF16),
        ],
        steps=chunks,
        scratch=[pltpu.VMEM((NSTATE, channels), F32)],
    )
    mixed, gate_grad, mixer_grad, gate_small, start_grad, gate_cross = run(
        functools.partial(gate_kernel, float(channels * head_size), chunks, head_size),
        "gate", count * channels * 600,
        [(LANES, part) for part in turn_all(stats, "head")]
        + [
            (BLOCKED, mixer), (BLOCKED, gate_pre), (BLOCKED, mixed_grad), (WHOLE, gated_gain[None]),
            (BLOCKED, conv), (BLOCKED, e_full), (WHOLE, factors), (BLOCKED, maps),
        ],
        [
            (BLOCKED, (count, channels), BF16),
            (BLOCKED, (count, channels), BF16),
            (BLOCKED, (count, channels), F32),
            (WHOLE, (8, channels), F32),
            (WHOLE, (NSTATE, channels), F32),
            (LANES, (8, count), F32),
        ],
        steps=chunks,
        backward=True,
    )
    out_parts = run(
        out_kernel, "out", 2 * count * channels * width,
        [(LOOSE, start_grad), (WHOLE, mixed), (WHOLE, output_weight)],
        [(WHOLE, (head_size, count, own_width), BF16)],
    )[0]
    grad_after, mark = entering(start_grad, weights, 8, True, out_parts)
    step, out_rows = width // seq_size, channels // seq_size
    early_rows = step + out_rows * (width // channels)
    features = width // BLOCK
    feature_block = ((rows, BLOCK), lambda i: (0, i))
    every = features // (channels // BLOCK)
    early_kept, early_given, early_gain = run(
        early_kernel, "early", 4 * count * channels * width,
        [
            (LOOSE, mark), core, (feature_block, normed), (WHOLE, gate_grad),
            (((count, BLOCK), lambda i: (0, i // every)), mixed), (WHOLE, full_cotangent),
            (BLOCK, gate_weight),
        ],
        [(WHOLE, (chips, early_rows, channels), BF16)] * 2
        + [(((1, BLOCK), lambda i: (0, i)), (1, width), F32)],
        steps=features,
        scratch=[pltpu.VMEM((BLOCK, width), F32)],
    )
    early_gate, early_out, half_mark, next_mark = sum_pieces(
        chip, early_kept, early_given, step, False, "early", True
    )
    branch = jnp.sum(deal(out_parts, "head").astype(F32), axis=0)
    block_out = (tokens.astype(F32) + branch).astype(BF16)

    value_grads, map_grads = run(
        functools.partial(back_kernel, chunks), "back", count * channels * 2000,
        [
            (LOOSE, half_mark), (LOOSE, out_parts), (WHOLE, grad_after), (BLOCKED, mixer_grad), (BLOCKED, e_full),
            (BLOCKED, f_full), (WHOLE, factors), (BLOCKED, weighted), (LEADING, high),
            (LEADING, low), (BLOCKED, maps), (BLOCKED, value_slope), (BLOCKED, map_slope),
            (WHOLE, skip_full),
        ],
        [(BLOCKED, (count, channels), F32), (BLOCKED, (count, maps_width), F32)],
        steps=chunks,
        backward=True,
        scratch=[pltpu.VMEM((NSTATE, channels), F32)],
    )
    after = from_behind(jnp.concatenate([value_grads[:8], map_grads[:8]], axis=1), -1)
    value_raw_grad, state_raw_grad, value_small, state_small, crossed = run(
        functools.partial(conv_back_kernel, chunks), "conv_back", count * channels * 100,
        [
            (LOOSE, next_mark), (BLOCKED, value_grads), (BLOCKED, map_grads), (WHOLE, after),
            (WHOLE, value_raw), (WHOLE, state_raw), (WHOLE, value_kernel), (WHOLE, state_kernel),
            (LANES, gate_cross),
        ],
        [
            (BLOCKED, (count, channels), BF16),
            (BLOCKED, (count, maps_width), BF16),
            (WHOLE, (8, channels), F32),
            (WHOLE, (8, maps_width), F32),
            (LANES, (8, count), F32),
        ],
        steps=chunks,
        backward=True,
        scratch=[pltpu.VMEM((8, channels), F32), pltpu.VMEM((8, maps_width), F32)],
    )
    lanes = channels // 128
    state_rows = 2 * step // lanes
    late_rows = step + state_rows + HALO
    late_kept, late_given = run(
        late_kernel, "late", 3 * count * channels * width,
        [
            core, (feature_block, normed), (WHOLE, value_raw_grad), (WHOLE, state_raw_grad),
            (WHOLE, value_small), (WHOLE, gate_small), (((1, BLOCK), lambda i: (0, i)), early_gain),
            (WHOLE, state_small), (BLOCK, value_weight), (BLOCK, state_weight),
            (((8, BLOCK), lambda i: (0, i)), gain_full),
        ],
        [(WHOLE, (chips, late_rows, channels), BF16)] * 2,
        steps=features,
        scratch=[
            pltpu.VMEM((HALO, channels), F32),
            pltpu.VMEM((HALO, channels), F32),
            pltpu.VMEM((8, width), F32),
        ],
    )
    normed_parts = run(
        functools.partial(normed_kernel, chunks), "normed", 4 * count * channels * width,
        [
            (LOOSE, late_given), (WHOLE, gate_grad), (WHOLE, value_raw_grad),
            (WHOLE, state_raw_grad), (own_width, gate_weight), (own_width, value_weight),
            (own_width, state_weight), (WHOLE, crossed),
        ],
        [(LEADING, (head_size, count + HALO, own_width), BF16)],
        steps=head_size,
    )[0]
    normed_parts = deal(normed_parts, "head")
    late_piece, shared_piece, _, _ = sum_pieces(
        chip, late_kept, late_given, step, True, "late", False
    )
    summed = butterfly(shared_piece, "head")
    line = jnp.arange(late_rows - step)[:, None]
    own_line = (line >= state_rows) & (line < state_rows + 2)
    tail = summed[state_rows + 2 : state_rows + 3] + summed[state_rows + 3 : state_rows + 4]
    tail_high = tail.astype(BF16).astype(F32)
    summed = jnp.where(
        line == state_rows + 2, tail_high, jnp.where(line == state_rows + 3, tail - tail_high, summed)
    )
    shared_piece = jnp.where(own_line, shared_piece, summed).astype(BF16)

    def unpack(kernel, name, pieces, outs, flops, extra=(), scratch=()):
        groups = [collect(piece, order) for piece, order in pieces]
        bits = [[found[2] for found in group] for group in groups]
        arrays = [(WHOLE, value) for group in groups for found in group for value in found[:2]]
        return run(
            functools.partial(kernel, chips, bits, *extra), name, flops, [core, chip] + arrays, outs,
            steps=seq_size, scratch=scratch,
        )

    gate_weight_gradient, output_weight_gradient = unpack(
        early_out_kernel, "early_out", [(early_gate, (2, 1)), (early_out, (1, 2))],
        [(step, (width, channels), F32), (out_rows, (channels, width), F32)], 4 * channels * width,
    )
    value_weight_gradient = unpack(
        late_out_kernel, "late_out", [(late_piece, None)],
        [(step, (width, channels), F32)], 2 * channels * width,
    )[0]
    (
        state_weight_gradient, value_kernel_gradient, value_bias_gradient, state_kernel_gradient,
        state_bias_gradient, skip_sums, gated_gain_gradient, gain_sums,
    ) = unpack(
        shared_out_kernel, "shared_out", [(shared_piece, (2, 1))],
        [
            (step, (width, maps_width), F32),
            (WHOLE, (KERNEL, channels), F32),
            (WHOLE, (1, channels), F32),
            (WHOLE, (KERNEL, maps_width), F32),
            (WHOLE, (1, maps_width), F32),
            (WHOLE, (1, channels), F32),
            (WHOLE, (1, channels), F32),
            (WHOLE, (1, width), F32),
        ],
        2 * maps_width * width,
        scratch=[pltpu.VMEM((HALO, channels), F32), pltpu.VMEM((HALO, channels), F32)],
    )
    value_bias_gradient, state_bias_gradient = value_bias_gradient[0], state_bias_gradient[0]
    gated_gain_gradient = gated_gain_gradient[0]
    skip_scale_gradient = jnp.sum(skip_sums.reshape(heads, HEAD_DIM), axis=1)
    norm_gain_gradient = lax.dynamic_slice_in_dim(
        gain_sums[0], lax.axis_index("head") * own_width, own_width, 0
    )

    tokens_gradient = run(
        functools.partial(last_kernel, float(width)), "last", count * own_width * 20,
        [
            (LOOSE, gate_weight_gradient), (WHOLE, normed_parts), (WHOLE, tokens), (WHOLE, scale_in),
            (WHOLE, norm_gain[None]), (WHOLE, cotangent),
        ],
        [(WHOLE, (count, own_width), BF16)],
    )[0]
    return (
        block_out[None],
        tokens_gradient[None],
        norm_gain_gradient,
        gate_weight_gradient,
        value_weight_gradient,
        state_weight_gradient,
        value_kernel_gradient,
        value_bias_gradient,
        state_kernel_gradient,
        state_bias_gradient,
        skip_scale_gradient,
        gated_gain_gradient,
        output_weight_gradient,
    )


def solution(mesh):
    seq_size, head_size = mesh.shape["seq"], mesh.shape["head"]
    mesh = Mesh(mesh.devices.reshape(seq_size // 2, 2, head_size), ("chip", "core", "head"))
    seq = ("chip", "core")
    in_specs = (
        P(None, seq, "head"),
        P(None, seq, "head"),
        P("head"),
        P(None, "head"),
        P(None, "head"),
        P(),
        P(None, "head"),
        P("head"),
        P(),
        P(),
        P("head"),
        P("head"),
        P("head", None),
        P(None, seq, "head"),
    )
    out_specs = (
        P(None, seq, "head"),
        P(None, seq, "head"),
        P("head"),
        P(None, "head"),
        P(None, "head"),
        P(),
        P(None, "head"),
        P("head"),
        P(),
        P(),
        P("head"),
        P("head"),
        P("head", None),
    )
    return jax.shard_map(
        per_device, mesh=mesh, in_specs=in_specs, out_specs=out_specs, check_vma=False
    )
```

```python
import functools

import jax
import jax.numpy as jnp
from jax import lax
from jax.experimental import pallas as pl
from jax.experimental.pallas import tpu as pltpu
from jax.sharding import Mesh
from jax.sharding import PartitionSpec as P

HEAD_DIM = 64
NSTATE = 128
KERNEL = 4
CHUNK = 128
BLOCK = 384
VMEM_LIMIT = 20 * 1024 * 1024
MARGIN = 32
HALO = 16


DECAY_STEP = 1.0 / 1048576.0
EPSILON = 1e-05
BF16 = jnp.bfloat16
F32 = jnp.float32


def tie_kernel(*refs):
    del refs


def tie(value, *others):
    return pl.pallas_call(
        tie_kernel,
        out_shape=jax.ShapeDtypeStruct(value.shape, value.dtype),
        in_specs=[pl.BlockSpec(memory_space=pl.ANY)] * (1 + len(others)),
        out_specs=pl.BlockSpec(memory_space=pl.ANY),
        input_output_aliases={0: 0},
        name="tie",
    )(value, *others)


def from_behind(value, by):
    axis = ("chip", "core")
    size = lax.axis_size("chip") * 2
    pairs = [(i, i + by) for i in range(size) if 0 <= i + by < size]
    return lax.ppermute(value, axis, pairs)


def beside(value):
    return lax.ppermute(value, "core", [(0, 1), (1, 0)])


def turn(value, axis, by):
    size = lax.axis_size(axis)
    return lax.ppermute(value, axis, [(i, (i + by) % size) for i in range(size)])


def turn_all(value, axis):
    return [value] + [turn(value, axis, by) for by in range(1, lax.axis_size(axis))]


def ring_parts(value, axis):
    parts = [value]
    for _ in range(1, lax.axis_size(axis)):
        parts.append(turn(parts[-1], axis, 1))
    return parts


def deal(parts, axis):
    return lax.all_to_all(parts, axis, 0, 0)


def cross(value, bits):
    return lax.ppermute(value, "chip", [(i, i ^ bits) for i in range(lax.axis_size("chip"))])


def cross_all(value):
    return [value] + [cross(value, bits) for bits in range(1, lax.axis_size("chip"))]


def heads_sum(piece):
    total, low = piece, piece.astype(BF16)
    bits, size = 1, lax.axis_size("head")
    while bits < size:
        arrived = lax.ppermute(low, "head", [(i, i ^ bits) for i in range(size)])
        total, low = run(
            heads_kernel, "heads", piece.size,
            [(WHOLE, piece), (WHOLE, total), (WHOLE, arrived)],
            [(WHOLE, piece.shape, F32), (WHOLE, piece.shape, BF16)],
        )
        bits *= 2
    return low


def entering(total, weights, first_row, backward, meanwhile):
    core = lax.axis_index("core")
    receives = core == (0 if backward else 1)
    own_decay, other_decay = weights[16:17], weights[17:18]
    half = total.shape[0] // 2
    partner = tie(beside(total), meanwhile)
    part = lambda value: lax.dynamic_slice_in_dim(value, core * half, half, 0)
    pair = jnp.where(
        receives,
        own_decay * part(partner) + part(total),
        other_decay * part(total) + part(partner),
    )
    prefix, mark = jnp.zeros_like(pair), None
    for bits in range(1, lax.axis_size("chip")):
        arrived = cross(pair, bits)
        mark = arrived if mark is None else mark
        prefix = prefix + arrived * weights[first_row + bits : first_row + bits + 1]
    other = beside(prefix)
    whole = jnp.where(
        core == 0,
        jnp.concatenate([prefix, other], axis=0),
        jnp.concatenate([other, prefix], axis=0),
    )
    return jnp.where(receives, other_decay * whole + partner, whole), mark


def sum_pieces(chip, kept, given, name, square, cut, paired, loose=()):
    chips, rows, channels = kept.shape
    arrived = beside(given)
    size = chips * rows * channels
    if paired:
        outs = [(WHOLE, (cut, channels), BF16), (WHOLE, (rows - cut, channels), F32)]
    else:
        outs = [(WHOLE, (rows, channels), BF16)]
    if chips != 4 or not square:
        halves = run(
            functools.partial(half_kernel, paired, chips), name + "_half", size,
            [chip, (WHOLE, kept), (WHOLE, arrived)],
            [(WHOLE, (rows, channels), F32)] + [(WHOLE, (rows, channels), BF16)] * (chips - 1),
        )
        parts = [halves[0]] + [cross(halves[bits], bits) for bits in range(1, chips)]
        found = run(
            functools.partial(piece_kernel, chips, paired, cut), name + "_piece", size,
            [(WHOLE, part) for part in parts] + [(LOOSE, mark) for mark in loose], outs,
        )
        return found, halves[0], halves[0]
    rest = rows - cut
    first, first_give, last, last_give = run(
        square_half_kernel, name + "_half", size,
        [chip, (WHOLE, kept), (WHOLE, arrived)],
        [
            (WHOLE, (2, cut, channels), F32), (WHOLE, (2, cut, channels), BF16),
            (WHOLE, (2, rest, channels), F32), (WHOLE, (2, rest, channels), BF16),
        ],
    )
    half_mark = first
    first, first_give, last, last_give = run(
        square_next_kernel, name + "_next", size,
        [
            (WHOLE, first), (WHOLE, cross(first_give, 1)),
            (WHOLE, last), (WHOLE, cross(last_give, 2)),
        ],
        [
            (WHOLE, (cut, channels), F32), (WHOLE, (cut, channels), BF16),
            (WHOLE, (rest, channels), F32), (WHOLE, (rest, channels), BF16),
        ],
    )
    next_mark = first
    found = run(
        square_last_kernel, name + "_piece", size,
        [
            (WHOLE, first), (WHOLE, cross(first_give, 2)),
            (WHOLE, last), (WHOLE, cross(last_give, 1)),
        ] + [(LOOSE, mark) for mark in loose],
        outs,
    )
    return found, half_mark, next_mark


def collect(piece, order):
    chips = lax.axis_size("chip")
    if chips != 4 or order is None:
        found = [(value[None], (bits,)) for bits, value in enumerate(cross_all(piece))]
    else:
        near, far = order
        both = jnp.stack([piece, cross(piece, near)])
        found = [(both, (0, near)), (cross(both, far), (far, far ^ near))]
    return [(value, beside(value), bits) for value, bits in found]


def dot(left, right):
    return jnp.dot(left, right, preferred_element_type=F32)


def dot_nt(left, right):
    return lax.dot_general(left, right, (((1,), (1,)), ((), ())), preferred_element_type=F32)


def dot_tn(left, right):
    return lax.dot_general(left, right, (((0,), (0,)), ((), ())), preferred_element_type=F32)


def split(values):
    high = values.astype(BF16)
    return high, (values - high.astype(F32)).astype(BF16)


def lower_mask():
    row = lax.broadcasted_iota(jnp.int32, (CHUNK, CHUNK), 0)
    column = lax.broadcasted_iota(jnp.int32, (CHUNK, CHUNK), 1)
    return row >= column


def spread_heads(heads, channels):
    row = lax.broadcasted_iota(jnp.int32, (heads, channels), 0) * HEAD_DIM
    place = lax.broadcasted_iota(jnp.int32, (heads, channels), 1)
    return jnp.where((place >= row) & (place < row + HEAD_DIM), 1.0, 0.0).astype(BF16)


def expand(values, channels):
    high, low = split(values)
    spread = spread_heads(values.shape[1], channels)
    return dot(high, spread) + dot(low, spread)


def decay_kernel(codes_ref, weight_ref, e_ref, f_ref, k_ref, logs_ref):
    heads, channels = codes_ref.shape[1], k_ref.shape[1]
    lower = jnp.where(lower_mask(), 1.0, 0.0).astype(F32)
    count = codes_ref.shape[0] // CHUNK
    line = lax.broadcasted_iota(jnp.int32, (8, heads), 0)
    marks = jnp.zeros((8, heads), F32)
    total = jnp.zeros((1, heads), F32)
    for chunk in range(count):
        rows = pl.ds(chunk * CHUNK, CHUNK)
        logs = codes_ref[rows, :].astype(F32) * (-DECAY_STEP)
        cumulative = jnp.dot(
            lower, logs, precision=lax.Precision.HIGHEST, preferred_element_type=F32
        )
        last = cumulative[CHUNK - 1 :]
        middle = 0.5 * last
        e_ref[rows, :] = jnp.exp(cumulative - middle)
        f_ref[rows, :] = weight_ref[rows, :] * jnp.exp(middle - cumulative)
        marks = jnp.where(line == chunk, jnp.exp(middle), marks)
        total = total + last
    marks = jnp.where(line == 7, total, marks)
    high, low = split(marks)
    lowest = (marks - high.astype(F32) - low.astype(F32)).astype(BF16)
    spread = spread_heads(heads, channels)
    factors = dot(high, spread) + dot(low, spread) + dot(lowest, spread)
    k_ref[...] = factors
    for place in range(logs_ref.shape[0]):
        logs_ref[place] = jnp.broadcast_to(factors[7:8], (8, channels))


def weights_kernel(core_ref, chip_ref, logs_ref, out_ref):
    chips = logs_ref.shape[0] // 2
    core, chip = core_ref[0], chip_ref[0]
    logs = [logs_ref[i, 0:1, :] for i in range(2 * chips)]
    pairs = [logs[2 * i] + logs[2 * i + 1] for i in range(chips)]
    zero = jnp.zeros_like(logs[0])
    out_ref[...] = jnp.zeros_like(out_ref)
    for bits in range(1, chips):
        source = lax.bitwise_xor(chip, bits)
        before, after = zero, zero
        for middle in range(chips):
            before = before + jnp.where((source < middle) & (middle < chip), pairs[middle], 0.0)
            after = after + jnp.where((source > middle) & (middle > chip), pairs[middle], 0.0)
        out_ref[bits : bits + 1, :] = jnp.where(source < chip, jnp.exp(before), 0.0)
        out_ref[8 + bits : 9 + bits, :] = jnp.where(source > chip, jnp.exp(after), 0.0)
    own, other = zero, zero
    for device in range(2 * chips):
        own = own + jnp.where(2 * chip + core == device, logs[device], 0.0)
        other = other + jnp.where(2 * chip + 1 - core == device, logs[device], 0.0)
    out_ref[16:17, :] = jnp.exp(own)
    out_ref[17:18, :] = jnp.exp(other)


def taps(window, kernel, bias, begin):
    summed = bias
    for offset in range(KERNEL):
        summed = summed + kernel[offset : offset + 1] * window[begin + offset : begin + offset + CHUNK]
    return summed


def silu_parts(values):
    sigmoid = jax.nn.sigmoid(values)
    return values * sigmoid, sigmoid * (1.0 + values * (1.0 - sigmoid))


def first_step(action):
    pl.when(pl.program_id(0) == 0)(action)


def clear(*refs):
    def action():
        for ref in refs:
            ref[...] = jnp.zeros_like(ref)

    first_step(action)


def place_parts(mine, parts, target, width, value):
    size = len(parts)
    if width % 128 == 0:
        for i in range(size):
            owner = lax.rem(mine + size - i, size)
            target[:, pl.ds(pl.multiple_of(owner * width, 128), width)] = value(i)
        return

    def write(me):
        for i in range(size):
            owner = (me + size - i) % size
            target[:, owner * width : (owner + 1) * width] = value(i)

    for me in range(size):
        pl.when(mine == me)(functools.partial(write, me))


def norm_kernel(size, head_ref, *refs):
    parts, gains = refs[:size], refs[size : 2 * size]
    own_ref, normed_ref, scale_ref, copy_ref, gain_ref = refs[2 * size :]
    width = parts[0].shape[1]
    mine = head_ref[0]
    part = lambda i: parts[i][...].astype(F32)
    gain = lambda i: gains[i][0:1].astype(F32)
    squares = sum(jnp.sum(part(i) ** 2, axis=1, keepdims=True) for i in range(size))
    scale = lax.rsqrt(squares / (size * width) + EPSILON)
    scale_ref[...] = jnp.broadcast_to(scale, scale_ref.shape)
    place_parts(
        mine, parts, normed_ref, width,
        lambda i: (part(i) * scale_ref[:, 0:1] * gain(i)).astype(BF16),
    )
    place_parts(mine, parts, gain_ref, width, lambda i: jnp.broadcast_to(gain(i), (8, width)))
    copy_ref[...] = own_ref[...]


def conv_kernel(
    value_ref, state_ref, value_kernel_ref, value_bias_ref, state_kernel_ref, state_bias_ref,
    f_ref, k_ref, conv_ref, weighted_ref, value_slope_ref, maps_ref, state_slope_ref, total_ref,
):
    chunk = pl.program_id(0)
    clear(total_ref)
    around = pl.ds(pl.multiple_of(chunk * CHUNK, CHUNK), CHUNK + HALO)
    pre = taps(
        state_ref[around, :].astype(F32), state_kernel_ref[...].astype(F32),
        state_bias_ref[...].astype(F32), HALO - KERNEL + 1,
    )
    conv, slope = silu_parts(pre)
    maps = conv.astype(BF16)
    maps_ref[...] = maps
    state_slope_ref[...] = slope
    pre = taps(
        value_ref[around, :].astype(F32), value_kernel_ref[...].astype(F32),
        value_bias_ref[...].astype(F32), HALO - KERNEL + 1,
    )
    conv, slope = silu_parts(pre)
    conv = conv.astype(BF16)
    conv_ref[...] = conv
    value_slope_ref[...] = slope
    weighted = (conv.astype(F32) * expand(f_ref[...], conv.shape[1])).astype(BF16)
    weighted_ref[...] = weighted
    factor = k_ref[pl.ds(chunk, 1), :]
    total_ref[...] = factor * (factor * total_ref[...] + dot_tn(maps[:, :NSTATE], weighted))


def mixer_kernel(
    state_in_ref, maps_ref, weighted_ref, conv_ref, e_ref, k_ref, skip_ref, gate_ref, grad_ref, gain_ref,
    mixer_ref, stats_ref, high_ref, low_ref, state_ref,
):
    chunk = pl.program_id(0)

    def start():
        state_ref[...] = state_in_ref[...]

    first_step(start)
    lane = lax.broadcasted_iota(jnp.int32, (CHUNK, CHUNK), 1)
    factor = k_ref[pl.ds(chunk, 1), :]
    input_map, output_map = maps_ref[:, :NSTATE], maps_ref[:, NSTATE:]
    weighted = weighted_ref[...]
    scaled = factor * state_ref[...]
    high, low = split(scaled)
    high_ref[0], low_ref[0] = high, low
    scores = jnp.where(lower_mask(), dot_nt(output_map, input_map), 0.0).astype(BF16)
    mixed = dot(
        jnp.concatenate([scores, output_map], axis=1), jnp.concatenate([weighted, high], axis=0)
    )
    mixed = mixed + dot(output_map, low)
    mixer = expand(e_ref[...], weighted.shape[1]) * mixed + skip_ref[...] * conv_ref[...].astype(F32)
    mixer_ref[...] = mixer
    gate = gate_ref[...]
    gated = mixer * (gate * jax.nn.sigmoid(gate))
    squares = jnp.sum(gated * gated, axis=1, keepdims=True)
    products = jnp.sum(gated * (grad_ref[...] * gain_ref[...].astype(F32)), axis=1, keepdims=True)
    sums = jnp.where(lane == 0, squares, jnp.where(lane == 1, products, 0.0))
    stats_ref[...] = sums.T[:8]
    state_ref[...] = factor * (scaled + dot_tn(input_map, weighted))


def column(row_block):
    rest = jnp.zeros((CHUNK - row_block.shape[0], CHUNK), F32)
    return jnp.concatenate([row_block, rest], axis=0).T


def row_of(sums):
    lane = lax.broadcasted_iota(jnp.int32, (CHUNK, CHUNK), 1)
    return jnp.where(lane == 0, sums, 0.0).T[:8]


def gate_kernel(
    inner, chunks, size, *refs
):
    stats_refs = refs[:size]
    (
        mixer_ref, gate_ref, grad_ref, gain_ref, conv_ref, e_ref, k_ref, maps_ref,
        mixed_ref, gate_grad_ref, mixer_grad_ref, small_ref, total_ref, cross_ref,
    ) = refs[size:]
    chunk = chunks - 1 - pl.program_id(0)
    clear(small_ref, total_ref)
    gain = gain_ref[...].astype(F32)
    stats = column(sum(ref[...] for ref in stats_refs))
    scale = lax.rsqrt(stats[:, 0:1] / inner + EPSILON)
    cross_term = stats[:, 1:2] * (scale * scale * scale) / inner
    gate = gate_ref[...]
    silu, slope = silu_parts(gate)
    mixer = mixer_ref[...]
    gated = mixer * silu
    normed = gated * scale
    mixed_ref[...] = (normed * gain).astype(BF16)
    grad = grad_ref[...]
    gated_grad = scale * (grad * gain) - gated * cross_term
    gate_grad = (gated_grad * mixer * slope).astype(BF16)
    gate_grad_ref[...] = gate_grad
    cross_ref[...] = row_of(jnp.sum(gate_grad.astype(F32) * gate, axis=1, keepdims=True))
    mixer_grad = gated_grad * silu
    mixer_grad_ref[...] = mixer_grad
    small_ref[0:1, :] += jnp.sum(grad * normed, axis=0, keepdims=True)
    small_ref[1:2, :] += jnp.sum(mixer_grad * conv_ref[...].astype(F32), axis=0, keepdims=True)
    high, low = split(expand(e_ref[...], grad.shape[1]) * mixer_grad)
    output_map = maps_ref[:, NSTATE:]
    factor = k_ref[pl.ds(chunk, 1), :]
    total_ref[...] = factor * (
        factor * total_ref[...] + (dot_tn(output_map, high) + dot_tn(output_map, low))
    )


def back_kernel(
    chunks, early_ref, state_in_ref, mixer_grad_ref, e_ref, f_ref, k_ref, weighted_ref, high_ref, low_ref,
    maps_ref, value_slope_ref, state_slope_ref, skip_ref,
    value_ref, map_ref, state_ref,
):
    chunk = chunks - 1 - pl.program_id(0)

    def start():
        state_ref[...] = state_in_ref[...]

    first_step(start)
    lower = lower_mask()
    row = lax.broadcasted_iota(jnp.int32, (CHUNK, CHUNK), 0)
    upper = row <= lax.broadcasted_iota(jnp.int32, (CHUNK, CHUNK), 1)
    factor = k_ref[pl.ds(chunk, 1), :]
    input_map, output_map = maps_ref[:, :NSTATE], maps_ref[:, NSTATE:]
    weighted = weighted_ref[...]
    mixer_grad = mixer_grad_ref[...]
    high, low = split(expand(e_ref[...], weighted.shape[1]) * mixer_grad)
    scaled = factor * state_ref[...]
    state_high, state_low = split(scaled)
    both = jnp.concatenate([weighted, high_ref[0]], axis=0)
    sums = dot_nt(high, both) + dot_nt(low, both)
    score_grad = jnp.where(lower, sums[:, :CHUNK], 0.0).astype(BF16)
    output_grad = sums[:, CHUNK:] + dot_nt(high, low_ref[0]) + dot(score_grad, input_map)
    sums = dot_nt(weighted, jnp.concatenate([state_high, state_low], axis=0))
    input_grad = sums[:, :NSTATE] + sums[:, NSTATE:] + dot_tn(score_grad, output_map)
    scores = jnp.where(upper, dot_nt(input_map, output_map), 0.0).astype(BF16)
    grads = dot(
        jnp.concatenate([scores, input_map], axis=1), jnp.concatenate([high, state_high], axis=0)
    )
    decayed = expand(f_ref[...], weighted.shape[1]) * grads
    value_ref[...] = (decayed + skip_ref[...] * mixer_grad) * value_slope_ref[...]
    slope = state_slope_ref[...]
    map_ref[:, :NSTATE] = input_grad * slope[:, :NSTATE]
    map_ref[:, NSTATE:] = output_grad * slope[:, NSTATE:]
    state_ref[...] = factor * (scaled + (dot_tn(output_map, high) + dot_tn(output_map, low)))


def conv_back_kernel(
    chunks, other_ref, value_ref, map_ref, after_ref, value_raw_ref, state_raw_ref, value_kernel_ref,
    state_kernel_ref, cross_in_ref,
    value_grad_ref, state_grad_ref, value_small_ref, state_small_ref, cross_ref, value_next_ref,
    state_next_ref,
):
    chunk = chunks - 1 - pl.program_id(0)
    channels = value_ref.shape[1]
    clear(value_small_ref, state_small_ref)

    def start():
        value_next_ref[...] = after_ref[:, :channels]
        state_next_ref[...] = after_ref[:, channels:]

    first_step(start)

    def back(slope_ref, next_ref, raw_ref, kernel_ref, grad_ref, small_ref):
        kernel = kernel_ref[...].astype(F32)
        slope = slope_ref[...]
        window = jnp.concatenate([slope, next_ref[...]], axis=0)
        around = pl.ds(pl.multiple_of(chunk * CHUNK, CHUNK), CHUNK + HALO)
        raw = raw_ref[around, :].astype(F32)
        grad = jnp.zeros_like(slope)
        for offset in range(KERNEL):
            back_by = KERNEL - 1 - offset
            grad = grad + kernel[offset : offset + 1] * window[back_by : back_by + CHUNK]
            begin = HALO - KERNEL + 1 + offset
            small_ref[offset : offset + 1, :] += jnp.sum(
                slope * raw[begin : begin + CHUNK], axis=0, keepdims=True
            )
        small_ref[KERNEL : KERNEL + 1, :] += jnp.sum(slope, axis=0, keepdims=True)
        grad = grad.astype(BF16)
        grad_ref[...] = grad
        next_ref[...] = slope[:8]
        return jnp.sum(grad.astype(F32) * raw[HALO:], axis=1, keepdims=True)

    crossed = back(map_ref, state_next_ref, state_raw_ref, state_kernel_ref, state_grad_ref, state_small_ref)
    crossed = crossed + back(
        value_ref, value_next_ref, value_raw_ref, value_kernel_ref, value_grad_ref, value_small_ref
    )
    cross_ref[...] = cross_in_ref[...] + row_of(crossed)


def normed_kernel(
    chunks, late_ref, gate_grad_ref, value_grad_ref, state_grad_ref, gate_weight_ref, value_weight_ref,
    state_weight_ref, cross_ref, out_ref
):
    value = (
        dot_nt(gate_grad_ref[...], gate_weight_ref[...])
        + dot_nt(value_grad_ref[...], value_weight_ref[...])
        + dot_nt(state_grad_ref[...], state_weight_ref[...])
    )
    count = value.shape[0]
    out_ref[0, :count, :] = value.astype(BF16)
    line = lax.broadcasted_iota(jnp.int32, (HALO, CHUNK), 0)
    packed = jnp.zeros((HALO, CHUNK), F32)
    for chunk in range(chunks):
        row = cross_ref[0:1, chunk * CHUNK : (chunk + 1) * CHUNK]
        high = row.astype(BF16).astype(F32)
        packed = jnp.where(line == chunk, high, packed)
        packed = jnp.where(line == chunks + chunk, row - high, packed)
    out_ref[0, count:, :] = jnp.zeros((HALO, value.shape[1]), BF16)
    out_ref[0, count:, :CHUNK] = packed.astype(BF16)


def last_kernel(full_width, parts_ref, tokens_ref, scale_ref, gain_ref, cotangent_ref, out_ref):
    count = tokens_ref.shape[0]
    chunks = count // CHUNK
    size = parts_ref.shape[0]
    crossed = sum(parts_ref[i, count:, :CHUNK].astype(F32) for i in range(size))
    crossed = crossed[:chunks] + crossed[chunks : 2 * chunks]
    for chunk in range(chunks):
        rows = slice(chunk * CHUNK, (chunk + 1) * CHUNK)
        normed_grad = sum(parts_ref[i, rows, :].astype(F32) for i in range(size))
        scale = scale_ref[HALO + chunk * CHUNK : HALO + (chunk + 1) * CHUNK, 0:1]
        total = column(jnp.broadcast_to(crossed[chunk : chunk + 1], (8, CHUNK)))[:, 0:1]
        out_ref[rows, :] = (
            scale * gain_ref[...].astype(F32) * normed_grad
            - tokens_ref[rows, :].astype(F32) * (scale * scale * total / full_width)
            + cotangent_ref[rows, :].astype(F32)
        ).astype(BF16)


def store_piece(core_ref, kept_ref, given_ref, place, begin, piece):
    chips = kept_ref.shape[0]
    core, chip = place // chips, lax.rem(place, chips)
    rows = slice(begin, begin + piece.shape[0])
    piece = piece.astype(BF16)

    @pl.when(core_ref[0] == core)
    def _():
        kept_ref[chip, rows, :] = piece

    @pl.when(core_ref[0] != core)
    def _():
        given_ref[chip, rows, :] = piece


def gain_row(weight, block):
    sums = jnp.sum(weight.astype(F32) * block, axis=1, keepdims=True)
    lane = lax.broadcasted_iota(jnp.int32, (CHUNK, CHUNK), 1)
    rows = [
        jnp.where(lane == 0, sums[i : i + CHUNK], 0.0).T[0:1] for i in range(0, BLOCK, CHUNK)
    ]
    return jnp.concatenate(rows, axis=1)


def early_kernel(
    loose_ref, core_ref, normed_ref, gate_ref, mixed_ref, grad_ref, weight_ref,
    kept_ref, given_ref, gain_ref, held_ref
):
    chips, rows, channels = kept_ref.shape
    at = pl.program_id(0)
    count, width = grad_ref.shape
    pieces = 2 * chips
    step = width // pieces
    out_rows = channels // pieces
    out_blocks = channels // BLOCK
    every = width // BLOCK // out_blocks

    @pl.when(lax.rem(at, every) == 0)
    def _():
        held_ref[...] = dot_tn(mixed_ref[...], grad_ref[...])

    block = dot_tn(normed_ref[HALO : HALO + count, :], gate_ref[...])
    gain_ref[...] = gain_row(weight_ref[...], block)
    for i in range(BLOCK // step):
        place = at * (BLOCK // step) + i
        begin = lax.rem(at, every) * (BLOCK // step * out_rows) + i * out_rows
        own = held_ref[pl.ds(pl.multiple_of(begin, 8), out_rows), :]
        parts = [block[i * step : (i + 1) * step]]
        parts += [own[:, j : j + channels] for j in range(0, width, channels)]
        store_piece(core_ref, kept_ref, given_ref, place, 0, jnp.concatenate(parts, axis=0))


def late_kernel(
    core_ref, normed_ref, value_ref, state_ref, value_small_ref, gate_small_ref, gain_ref,
    state_small_ref, value_weight_ref, state_weight_ref, gain_full_ref,
    kept_ref, given_ref, own_ref, shared_ref, gains_ref,
):
    chips, rows, channels = kept_ref.shape
    at = pl.program_id(0)
    count, maps_width = state_ref.shape
    width = gains_ref.shape[1]
    pieces = 2 * chips
    step = width // pieces
    lanes = channels // 128
    part = 2 * step // lanes
    columns = normed_ref[HALO : HALO + count, :]
    value = dot_tn(columns, value_ref[...])
    state = dot_tn(columns, state_ref[...])
    gain = (
        gain_ref[...] + gain_row(value_weight_ref[...], value) + gain_row(state_weight_ref[...], state)
    ) / gain_full_ref[0:1, :]
    gains_ref[0:1, pl.ds(pl.multiple_of(at * BLOCK, 128), BLOCK)] = gain
    for i in range(BLOCK // step):
        piece = slice(i * step, (i + 1) * step)
        stacked = jnp.concatenate([state[piece, :128], state[piece, 128:]], axis=0)
        stacked = jnp.concatenate(
            [stacked[j * part : (j + 1) * part] for j in range(lanes)], axis=1
        )
        store_piece(
            core_ref, kept_ref, given_ref, at * (BLOCK // step) + i, 0,
            jnp.concatenate([value[piece], stacked], axis=0),
        )

    @pl.when(at == width // BLOCK - 1)
    def _():
        own_ref[...] = jnp.zeros_like(own_ref)
        own_ref[: KERNEL + 1, :] = value_small_ref[: KERNEL + 1, :]
        own_ref[KERNEL + 1 : KERNEL + 3, :] = gate_small_ref[:2, :]
        shared_ref[...] = jnp.zeros_like(shared_ref)
        begin = width // channels
        for i in range(begin):
            shared_ref[i : i + 1, :] = gains_ref[0:1, i * channels : (i + 1) * channels]
        for i in range(0, (KERNEL + 1) * maps_width, 128):
            tap, column_from = divmod(i, maps_width)
            row, column_to = divmod(i, channels)
            shared_ref[begin + row : begin + row + 1, column_to : column_to + 128] = state_small_ref[
                tap : tap + 1, column_from : column_from + 128
            ]
        line = lax.broadcasted_iota(jnp.int32, (HALO, channels), 0)
        for place in range(pieces):
            own, shared = own_ref[place : place + 1, :], shared_ref[place : place + 1, :]
            own_high, shared_high = (v.astype(BF16).astype(F32) for v in (own, shared))
            small = jnp.zeros((HALO, channels), F32)
            for to, value in enumerate((own_high, own - own_high, shared_high, shared - shared_high)):
                small = jnp.where(line == to, value, small)
            store_piece(core_ref, kept_ref, given_ref, place, step + part, small)


def merge_pairs(block):
    tail = block[-HALO:]
    line = lax.broadcasted_iota(jnp.int32, tail.shape, 0)
    own, shared = tail[0:1] + tail[1:2], tail[2:3] + tail[3:4]
    own_high, shared_high = own.astype(BF16).astype(F32), shared.astype(BF16).astype(F32)
    new = jnp.zeros_like(tail)
    for at, value in enumerate((own_high, own - own_high, shared_high, shared - shared_high)):
        new = jnp.where(line == at, value, new)
    return jnp.concatenate([block[:-HALO], new], axis=0)


def heads_kernel(piece_ref, total_ref, arrived_ref, out_ref, low_ref):
    total = merge_pairs(total_ref[...] + arrived_ref[...].astype(F32))
    line = lax.broadcasted_iota(jnp.int32, total.shape, 0)
    first = total.shape[0] - HALO
    own = (line >= first) & (line < first + 2)
    out_ref[...] = total
    low_ref[...] = jnp.where(own, piece_ref[...], total).astype(BF16)


def half_kernel(paired, chips, chip_ref, kept_ref, arrived_ref, *outs):
    for bits in range(chips):
        place = lax.bitwise_xor(chip_ref[0], bits)
        value = kept_ref[place].astype(F32) + arrived_ref[place].astype(F32)
        if paired:
            value = merge_pairs(value)
        outs[bits][...] = value.astype(outs[bits].dtype)


def piece_kernel(parts, paired, cut, *refs):
    total = sum(ref[...].astype(F32) for ref in refs[:parts])
    if not paired:
        refs[-1][...] = total.astype(BF16)
        return
    first_ref, last_ref = refs[-2:]
    first_ref[...] = total[:cut].astype(BF16)
    last_ref[...] = merge_pairs(total[cut:])


def square_half_kernel(
    chip_ref, kept_ref, arrived_ref, first_ref, first_give_ref, last_ref, last_give_ref
):
    cut = first_ref.shape[1]
    for bits in range(4):
        place = lax.bitwise_xor(chip_ref[0], bits)
        value = kept_ref[place].astype(F32) + arrived_ref[place].astype(F32)
        low, high = bits & 1, bits >> 1
        ref = first_give_ref if low else first_ref
        ref[high] = value[:cut].astype(ref.dtype)
        ref = last_give_ref if high else last_ref
        ref[low] = value[cut:].astype(ref.dtype)


def square_next_kernel(
    first_ref, first_got_ref, last_ref, last_got_ref,
    first_out_ref, first_give_ref, last_out_ref, last_give_ref,
):
    first_out_ref[...] = first_ref[0] + first_got_ref[0].astype(F32)
    first_give_ref[...] = (first_ref[1] + first_got_ref[1].astype(F32)).astype(BF16)
    last_out_ref[...] = last_ref[0] + last_got_ref[0].astype(F32)
    last_give_ref[...] = (last_ref[1] + last_got_ref[1].astype(F32)).astype(BF16)


def square_last_kernel(first_ref, first_got_ref, last_ref, last_got_ref, *refs):
    out_ref = refs[-1]
    cut = first_ref.shape[0]
    out_ref[:cut, :] = (first_ref[...] + first_got_ref[...].astype(F32)).astype(BF16)
    out_ref[cut:, :] = (last_ref[...] + last_got_ref[...].astype(F32)).astype(BF16)


def spread_pieces(core_ref, chip_ref, chips, groups, refs, store):
    step = pl.program_id(0)
    core, chip = step // chips, lax.rem(step, chips)
    apart = lax.bitwise_xor(chip, chip_ref[0])
    refs = iter(refs)
    for part, bits_lists in enumerate(groups):
        for bits_list in bits_lists:
            own_ref, other_ref = next(refs), next(refs)
            for at, bits in enumerate(bits_list):

                @pl.when((apart == bits) & (core == core_ref[0]))
                def _(part=part, ref=own_ref, at=at):
                    store(part, ref[at].astype(F32))

                @pl.when((apart == bits) & (core != core_ref[0]))
                def _(part=part, ref=other_ref, at=at):
                    store(part, ref[at].astype(F32))


def early_out_kernel(piece_ref, gate_ref, output_ref):
    step, channels = gate_ref.shape
    out_rows, width = output_ref.shape
    piece = piece_ref[0].astype(F32)
    gate_ref[...] = piece[:step]
    output_ref[...] = jnp.concatenate(
        [piece[step + i * out_rows : step + (i + 1) * out_rows] for i in range(width // channels)],
        axis=1,
    )


def late_out_kernel(chips, groups, core_ref, chip_ref, *refs):
    value_ref = refs[-1]

    def store(part, value):
        value_ref[...] = value

    spread_pieces(core_ref, chip_ref, chips, groups, refs[:-1], store)


def shared_out_kernel(chips, groups, core_ref, chip_ref, *refs):
    (
        state_ref, value_kernel_ref, value_bias_ref, state_kernel_ref, state_bias_ref, skip_ref,
        gated_ref, gain_ref, own_ref, shared_ref,
    ) = refs[-10:]
    step, maps_width = state_ref.shape
    channels = own_ref.shape[1]
    lanes = channels // 128
    rows = 2 * step // lanes
    at = pl.program_id(0)

    def store(part, piece):
        stacked = jnp.concatenate(
            [piece[:rows, i * 128 : (i + 1) * 128] for i in range(lanes)], axis=0
        )
        state_ref[...] = jnp.concatenate([stacked[:step], stacked[step:]], axis=1)
        own_ref[pl.ds(at, 1), :] = piece[rows : rows + 1] + piece[rows + 1 : rows + 2]
        shared_ref[pl.ds(at, 1), :] = piece[rows + 2 : rows + 3] + piece[rows + 3 : rows + 4]

    spread_pieces(core_ref, chip_ref, chips, groups, refs[:-10], store)

    @pl.when(at == 2 * chips - 1)
    def _():
        value_kernel_ref[...] = own_ref[:KERNEL, :]
        value_bias_ref[...] = own_ref[KERNEL : KERNEL + 1, :]
        gated_ref[...] = own_ref[KERNEL + 1 : KERNEL + 2, :]
        skip_ref[...] = own_ref[KERNEL + 2 : KERNEL + 3, :]
        gain_rows = gain_ref.shape[1] // channels
        for i in range(gain_rows):
            gain_ref[:, i * channels : (i + 1) * channels] = shared_ref[i : i + 1, :]
        for i in range(0, (KERNEL + 1) * maps_width, 128):
            tap, column_to = divmod(i, maps_width)
            row, column_from = divmod(i, channels)
            value = shared_ref[gain_rows + row : gain_rows + row + 1, column_from : column_from + 128]
            if tap < KERNEL:
                state_kernel_ref[tap : tap + 1, column_to : column_to + 128] = value
            else:
                state_bias_ref[:, column_to : column_to + 128] = value


SCALAR = "scalar"
WHOLE = "whole"
BLOCKED = "blocked"
LANES = "lanes"
LEADING = "leading"
LOOSE = "loose"


def run(kernel, name, flops, args, outs, steps=None, backward=False, scratch=()):
    at = (lambda i: steps - 1 - i) if backward else (lambda i: i)

    def spec(kind, shape):
        if isinstance(kind, int):
            return pl.BlockSpec((kind,) + shape[1:], lambda i: (at(i), 0))
        if kind == SCALAR:
            return pl.BlockSpec(memory_space=pltpu.SMEM)
        if kind == LOOSE:
            return pl.BlockSpec(memory_space=pl.ANY)
        if isinstance(kind, tuple):
            return pl.BlockSpec(*kind)
        if steps is None:
            return pl.BlockSpec(memory_space=pltpu.VMEM)
        if kind == BLOCKED:
            return pl.BlockSpec((CHUNK, shape[1]), lambda i: (at(i), 0))
        if kind == LANES:
            return pl.BlockSpec((shape[0], CHUNK), lambda i: (0, at(i)))
        if kind == LEADING:
            return pl.BlockSpec((1,) + shape[1:], lambda i: (at(i),) + (0,) * (len(shape) - 1))
        return pl.BlockSpec(shape, lambda i: (0,) * len(shape))

    moved = sum(a.size * a.dtype.itemsize for kind, a in args if kind != LOOSE)
    shapes = [jax.ShapeDtypeStruct(shape, dtype) for _, shape, dtype in outs]
    moved += sum(a.size * a.dtype.itemsize for a in shapes)
    return pl.pallas_call(
        kernel,
        out_shape=shapes,
        in_specs=[spec(kind, a.shape) for kind, a in args],
        out_specs=[spec(kind, shape) for kind, shape, _ in outs],
        scratch_shapes=list(scratch),
        compiler_params=pltpu.CompilerParams(vmem_limit_bytes=VMEM_LIMIT),
        cost_estimate=pl.CostEstimate(flops=flops, bytes_accessed=moved, transcendentals=0),
        name=name,
        **({} if steps is None else {"grid": (steps,)}),
    )(*(a for _, a in args))


def per_device(
    tokens, decay_codes, norm_gain, gate_weight, value_weight, state_weight, value_kernel, value_bias,
    state_kernel, state_bias, skip_scale, gated_gain, output_weight, cotangent,
):
    tokens, decay_codes, cotangent = tokens[0], decay_codes[0], cotangent[0]
    count, own_width = tokens.shape
    heads = skip_scale.shape[0]
    channels = heads * HEAD_DIM
    head_size, chips = lax.axis_size("head"), lax.axis_size("chip")
    seq_size = 2 * chips
    width = own_width * head_size
    maps_width = 2 * NSTATE
    chunks = count // CHUNK
    core = (SCALAR, lax.axis_index("core").astype(jnp.int32)[None])
    chip = (SCALAR, lax.axis_index("chip").astype(jnp.int32)[None])
    head = (SCALAR, lax.axis_index("head").astype(jnp.int32)[None])

    rows = count + MARGIN
    packed = jnp.concatenate(
        [
            from_behind(tokens[-HALO:], 1),
            tokens,
            jnp.broadcast_to(norm_gain[None], (MARGIN - HALO, own_width)),
        ],
        axis=0,
    )
    logs = decay_codes.astype(F32) * (-DECAY_STEP)
    input_weight = jnp.sqrt(-jnp.expm1(2.0 * logs))
    e_full, f_full, factors, all_logs = run(
        decay_kernel, "decays", count * channels * 200,
        [(WHOLE, decay_codes), (WHOLE, input_weight)],
        [
            (WHOLE, (count, heads), F32),
            (WHOLE, (count, heads), F32),
            (WHOLE, (8, channels), F32),
            (WHOLE, (seq_size, 8, channels), F32),
        ],
    )
    all_logs = lax.all_to_all(all_logs, ("chip", "core"), 0, 0)
    weights = run(
        weights_kernel, "weights", channels * 1000, [core, chip, (WHOLE, all_logs)],
        [(WHOLE, (24, channels), F32)],
    )[0]
    parts = ring_parts(packed, "head")
    skip_full = jnp.repeat(skip_scale, HEAD_DIM)[None]

    half = rows // 2
    gain_rows = ((MARGIN - HALO, own_width), lambda i: ((HALO + count) // (MARGIN - HALO), 0))
    normed, scale_in, cotangent_copy, gain_full = run(
        functools.partial(norm_kernel, head_size), "norm", count * width * 10,
        [head] + [(half, part) for part in parts] + [(gain_rows, part) for part in parts]
        + [(count // 2, cotangent)],
        [
            (half, (rows, width), BF16),
            (half, (rows, 128), F32),
            (count // 2, (count, own_width), BF16),
            (WHOLE, (8, width), F32),
        ],
        steps=2,
    )
    full_cotangent = lax.all_gather(cotangent_copy, "head", axis=1, tiled=True)
    value_raw = dot(normed, value_weight).astype(BF16)
    state_raw = dot(normed, state_weight).astype(BF16)
    conv, weighted, value_slope, maps, map_slope, local_end = run(
        conv_kernel, "conv", count * channels * 400,
        [
            (WHOLE, value_raw), (WHOLE, state_raw), (WHOLE, value_kernel), (WHOLE, value_bias[None]),
            (WHOLE, state_kernel), (WHOLE, state_bias[None]), (BLOCKED, f_full), (WHOLE, factors),
        ],
        [
            (BLOCKED, (count, channels), BF16),
            (BLOCKED, (count, channels), BF16),
            (BLOCKED, (count, channels), F32),
            (BLOCKED, (count, maps_width), BF16),
            (BLOCKED, (count, maps_width), F32),
            (WHOLE, (NSTATE, channels), F32),
        ],
        steps=chunks,
    )
    gate_pre = dot(normed, gate_weight)[HALO : HALO + count]
    state_in, _ = entering(local_end, weights, 0, False, gate_pre)
    mixed_grad = dot_nt(full_cotangent, output_weight)
    mixer, stats, high, low = run(
        mixer_kernel, "mixer", count * channels * 1000,
        [
            (WHOLE, state_in), (BLOCKED, maps), (BLOCKED, weighted), (BLOCKED, conv),
            (BLOCKED, e_full), (WHOLE, factors), (WHOLE, skip_full), (BLOCKED, gate_pre),
            (BLOCKED, mixed_grad), (WHOLE, gated_gain[None]),
        ],
        [
            (BLOCKED, (count, channels), F32),
            (LANES, (8, count), F32),
            (LEADING, (chunks, NSTATE, channels), BF16),
            (LEADING, (chunks, NSTATE, channels), BF16),
        ],
        steps=chunks,
        scratch=[pltpu.VMEM((NSTATE, channels), F32)],
    )
    mixed, gate_grad, mixer_grad, gate_small, start_grad, gate_cross = run(
        functools.partial(gate_kernel, float(channels * head_size), chunks, head_size),
        "gate", count * channels * 600,
        [(LANES, part) for part in turn_all(stats, "head")]
        + [
            (BLOCKED, mixer), (BLOCKED, gate_pre), (BLOCKED, mixed_grad), (WHOLE, gated_gain[None]),
            (BLOCKED, conv), (BLOCKED, e_full), (WHOLE, factors), (BLOCKED, maps),
        ],
        [
            (BLOCKED, (count, channels), BF16),
            (BLOCKED, (count, channels), BF16),
            (BLOCKED, (count, channels), F32),
            (WHOLE, (8, channels), F32),
            (WHOLE, (NSTATE, channels), F32),
            (LANES, (8, count), F32),
        ],
        steps=chunks,
        backward=True,
    )
    partial_out = dot(mixed, output_weight).astype(BF16)
    grad_after, mark = entering(start_grad, weights, 8, True, partial_out)
    step, out_rows = width // seq_size, channels // seq_size
    early_rows = step + out_rows * (width // channels)
    features = width // BLOCK
    feature_block = ((rows, BLOCK), lambda i: (0, i))
    every = features // (channels // BLOCK)
    early_kept, early_given, early_gain = run(
        early_kernel, "early", 4 * count * channels * width,
        [
            (LOOSE, mark), core, (feature_block, normed), (WHOLE, gate_grad),
            (((count, BLOCK), lambda i: (0, i // every)), mixed), (WHOLE, full_cotangent),
            (BLOCK, gate_weight),
        ],
        [(WHOLE, (chips, early_rows, channels), BF16)] * 2
        + [(((1, BLOCK), lambda i: (0, i)), (1, width), F32)],
        steps=features,
        scratch=[pltpu.VMEM((BLOCK, width), F32)],
    )
    early_found, half_mark, next_mark = sum_pieces(
        chip, early_kept, early_given, "early", True, step, False
    )
    early = lax.all_gather(early_found[0], ("chip", "core"))
    branch = lax.psum_scatter(partial_out, "head", scatter_dimension=1, tiled=True).astype(F32)
    block_out = (tokens.astype(F32) + branch).astype(BF16)

    value_grads, map_grads = run(
        functools.partial(back_kernel, chunks), "back", count * channels * 2000,
        [
            (LOOSE, half_mark), (WHOLE, grad_after), (BLOCKED, mixer_grad), (BLOCKED, e_full),
            (BLOCKED, f_full), (WHOLE, factors), (BLOCKED, weighted), (LEADING, high),
            (LEADING, low), (BLOCKED, maps), (BLOCKED, value_slope), (BLOCKED, map_slope),
            (WHOLE, skip_full),
        ],
        [(BLOCKED, (count, channels), F32), (BLOCKED, (count, maps_width), F32)],
        steps=chunks,
        backward=True,
        scratch=[pltpu.VMEM((NSTATE, channels), F32)],
    )
    after = from_behind(jnp.concatenate([value_grads[:8], map_grads[:8]], axis=1), -1)
    value_raw_grad, state_raw_grad, value_small, state_small, crossed = run(
        functools.partial(conv_back_kernel, chunks), "conv_back", count * channels * 100,
        [
            (LOOSE, next_mark), (BLOCKED, value_grads), (BLOCKED, map_grads), (WHOLE, after),
            (WHOLE, value_raw), (WHOLE, state_raw), (WHOLE, value_kernel), (WHOLE, state_kernel),
            (LANES, gate_cross),
        ],
        [
            (BLOCKED, (count, channels), BF16),
            (BLOCKED, (count, maps_width), BF16),
            (WHOLE, (8, channels), F32),
            (WHOLE, (8, maps_width), F32),
            (LANES, (8, count), F32),
        ],
        steps=chunks,
        backward=True,
        scratch=[pltpu.VMEM((8, channels), F32), pltpu.VMEM((8, maps_width), F32)],
    )
    lanes = channels // 128
    state_rows = 2 * step // lanes
    late_rows = step + state_rows + HALO
    late_kept, late_given = run(
        late_kernel, "late", 3 * count * channels * width,
        [
            core, (feature_block, normed), (WHOLE, value_raw_grad), (WHOLE, state_raw_grad),
            (WHOLE, value_small), (WHOLE, gate_small), (((1, BLOCK), lambda i: (0, i)), early_gain),
            (WHOLE, state_small), (BLOCK, value_weight), (BLOCK, state_weight),
            (((8, BLOCK), lambda i: (0, i)), gain_full),
        ],
        [(WHOLE, (chips, late_rows, channels), BF16)] * 2,
        steps=features,
        scratch=[
            pltpu.VMEM((HALO, channels), F32),
            pltpu.VMEM((HALO, channels), F32),
            pltpu.VMEM((8, width), F32),
        ],
    )
    (late_piece, shared_piece), late_mark, _ = sum_pieces(
        chip, late_kept, late_given, "late", False, step, True
    )
    normed_parts = run(
        functools.partial(normed_kernel, chunks), "normed", 4 * count * channels * width,
        [
            (LOOSE, late_mark), (WHOLE, gate_grad), (WHOLE, value_raw_grad),
            (WHOLE, state_raw_grad), (own_width, gate_weight), (own_width, value_weight),
            (own_width, state_weight), (WHOLE, crossed),
        ],
        [(LEADING, (head_size, count + HALO, own_width), BF16)],
        steps=head_size,
    )[0]
    normed_parts = deal(normed_parts, "head")
    shared_piece = heads_sum(shared_piece)

    def unpack(kernel, name, pieces, outs, flops, extra=(), scratch=()):
        groups = [collect(piece, order) for piece, order in pieces]
        bits = [[found[2] for found in group] for group in groups]
        arrays = [(WHOLE, value) for group in groups for found in group for value in found[:2]]
        return run(
            functools.partial(kernel, chips, bits, *extra), name, flops, [core, chip] + arrays, outs,
            steps=seq_size, scratch=scratch,
        )

    gate_weight_gradient, output_weight_gradient = run(
        early_out_kernel, "early_out", 4 * channels * width,
        [
            (
                ((1, early_rows, channels), lambda i: (lax.rem(i, chips) * 2 + i // chips, 0, 0)),
                early,
            )
        ],
        [(step, (width, channels), F32), (out_rows, (channels, width), F32)],
        steps=seq_size,
    )
    value_weight_gradient = unpack(
        late_out_kernel, "late_out", [(late_piece, None)],
        [(step, (width, channels), F32)], 2 * channels * width,
    )[0]
    (
        state_weight_gradient, value_kernel_gradient, value_bias_gradient, state_kernel_gradient,
        state_bias_gradient, skip_sums, gated_gain_gradient, gain_sums,
    ) = unpack(
        shared_out_kernel, "shared_out", [(shared_piece, (2, 1))],
        [
            (step, (width, maps_width), F32),
            (WHOLE, (KERNEL, channels), F32),
            (WHOLE, (1, channels), F32),
            (WHOLE, (KERNEL, maps_width), F32),
            (WHOLE, (1, maps_width), F32),
            (WHOLE, (1, channels), F32),
            (WHOLE, (1, channels), F32),
            (WHOLE, (1, width), F32),
        ],
        2 * maps_width * width,
        scratch=[pltpu.VMEM((HALO, channels), F32), pltpu.VMEM((HALO, channels), F32)],
    )
    value_bias_gradient, state_bias_gradient = value_bias_gradient[0], state_bias_gradient[0]
    gated_gain_gradient = gated_gain_gradient[0]
    skip_scale_gradient = jnp.sum(skip_sums.reshape(heads, HEAD_DIM), axis=1)
    norm_gain_gradient = lax.dynamic_slice_in_dim(
        gain_sums[0], lax.axis_index("head") * own_width, own_width, 0
    )

    tokens_gradient = run(
        functools.partial(last_kernel, float(width)), "last", count * own_width * 20,
        [
            (WHOLE, normed_parts), (WHOLE, tokens), (WHOLE, scale_in),
            (WHOLE, norm_gain[None]), (WHOLE, cotangent),
        ],
        [(WHOLE, (count, own_width), BF16)],
    )[0]
    return (
        block_out[None],
        tokens_gradient[None],
        norm_gain_gradient,
        gate_weight_gradient,
        value_weight_gradient,
        state_weight_gradient,
        value_kernel_gradient,
        value_bias_gradient,
        state_kernel_gradient,
        state_bias_gradient,
        skip_scale_gradient,
        gated_gain_gradient,
        output_weight_gradient,
    )


def solution(mesh):
    seq_size, head_size = mesh.shape["seq"], mesh.shape["head"]
    mesh = Mesh(mesh.devices.reshape(seq_size // 2, 2, head_size), ("chip", "core", "head"))
    seq = ("chip", "core")
    in_specs = (
        P(None, seq, "head"),
        P(None, seq, "head"),
        P("head"),
        P(None, "head"),
        P(None, "head"),
        P(),
        P(None, "head"),
        P("head"),
        P(),
        P(),
        P("head"),
        P("head"),
        P("head", None),
        P(None, seq, "head"),
    )
    out_specs = (
        P(None, seq, "head"),
        P(None, seq, "head"),
        P("head"),
        P(None, "head"),
        P(None, "head"),
        P(),
        P(None, "head"),
        P("head"),
        P(),
        P(),
        P("head"),
        P("head"),
        P("head", None),
    )
    return jax.shard_map(
        per_device, mesh=mesh, in_specs=in_specs, out_specs=out_specs, check_vma=False
    )
```

```python
import functools

import jax
import jax.numpy as jnp
from jax import lax
from jax.experimental import pallas as pl
from jax.experimental.pallas import tpu as pltpu
from jax.sharding import Mesh
from jax.sharding import PartitionSpec as P

HEAD_DIM = 64
NSTATE = 128
KERNEL = 4
CHUNK = 128
BLOCK = 384
VMEM_LIMIT = 20 * 1024 * 1024
MARGIN = 32
HALO = 16


DECAY_STEP = 1.0 / 1048576.0
EPSILON = 1e-05
BF16 = jnp.bfloat16
F32 = jnp.float32


def tie_kernel(*refs):
    del refs


def tie(value, *others):
    return pl.pallas_call(
        tie_kernel,
        out_shape=jax.ShapeDtypeStruct(value.shape, value.dtype),
        in_specs=[pl.BlockSpec(memory_space=pl.ANY)] * (1 + len(others)),
        out_specs=pl.BlockSpec(memory_space=pl.ANY),
        input_output_aliases={0: 0},
        name="tie",
    )(value, *others)


def from_behind(value, by):
    axis = ("chip", "core")
    size = lax.axis_size("chip") * 2
    pairs = [(i, i + by) for i in range(size) if 0 <= i + by < size]
    return lax.ppermute(value, axis, pairs)


def beside(value):
    return lax.ppermute(value, "core", [(0, 1), (1, 0)])


def turn(value, axis, by):
    size = lax.axis_size(axis)
    return lax.ppermute(value, axis, [(i, (i + by) % size) for i in range(size)])


def turn_all(value, axis):
    return [value] + [turn(value, axis, by) for by in range(1, lax.axis_size(axis))]


def line_parts(value, axis):
    if lax.axis_size(axis) != 4:
        parts = turn_all(value, axis)
        return parts, value, parts[1]
    two = turn(value, axis, 2)
    one = lax.ppermute(value, axis, [(0, 1), (1, 2), (2, 3)])
    three = lax.ppermute(value, axis, [(1, 0), (2, 1), (3, 2)])
    passed = lax.ppermute(two, axis, [(2, 3), (1, 0)])
    return [value, one, two, three], passed, two


def deal(parts, axis):
    return lax.all_to_all(parts, axis, 0, 0)


def cross(value, bits):
    return lax.ppermute(value, "chip", [(i, i ^ bits) for i in range(lax.axis_size("chip"))])


def cross_all(value):
    return [value] + [cross(value, bits) for bits in range(1, lax.axis_size("chip"))]


def heads_sum(piece):
    total, low = piece, piece.astype(BF16)
    bits, size = 1, lax.axis_size("head")
    while bits < size:
        arrived = lax.ppermute(low, "head", [(i, i ^ bits) for i in range(size)])
        total, low = run(
            heads_kernel, "heads", piece.size,
            [(WHOLE, piece), (WHOLE, total), (WHOLE, arrived)],
            [(WHOLE, piece.shape, F32), (WHOLE, piece.shape, BF16)],
        )
        bits *= 2
    return low


def entering(total, weights, first_row, backward, meanwhile=None, later=None):
    core = lax.axis_index("core")
    receives = core == (0 if backward else 1)
    own_decay, other_decay = weights[16:17], weights[17:18]
    half = total.shape[0] // 2
    partner = beside(total)
    if meanwhile is not None:
        partner = tie(partner, meanwhile)
    part = lambda value: lax.dynamic_slice_in_dim(value, core * half, half, 0)
    pair = jnp.where(
        receives,
        own_decay * part(partner) + part(total),
        other_decay * part(total) + part(partner),
    )
    found = [cross(pair, bits) for bits in range(1, lax.axis_size("chip"))]
    if later is not None:
        found[-1] = tie(found[-1], later(pair))
    prefix = jnp.zeros_like(pair)
    for bits, value in enumerate(found, 1):
        prefix = prefix + value * weights[first_row + bits : first_row + bits + 1]
    other = beside(prefix)
    whole = jnp.where(
        core == 0,
        jnp.concatenate([prefix, other], axis=0),
        jnp.concatenate([other, prefix], axis=0),
    )
    return jnp.where(receives, other_decay * whole + partner, whole)


def sum_pieces(chip, kept, given, name, square, cut, paired, loose=()):
    chips, rows, channels = kept.shape
    arrived = beside(given)
    size = chips * rows * channels
    if paired:
        outs = [(WHOLE, (cut, channels), BF16), (WHOLE, (rows - cut, channels), F32)]
    else:
        outs = [(WHOLE, (rows, channels), BF16)]
    if chips != 4 or not square:
        halves = run(
            functools.partial(half_kernel, paired, chips), name + "_half", size,
            [chip, (WHOLE, kept), (WHOLE, arrived)],
            [(WHOLE, (rows, channels), F32)] + [(WHOLE, (rows, channels), BF16)] * (chips - 1),
        )
        parts = [halves[0]] + [cross(halves[bits], bits) for bits in range(1, chips)]
        found = run(
            functools.partial(piece_kernel, chips, paired, cut), name + "_piece", size,
            [(WHOLE, part) for part in parts] + [(LOOSE, mark) for mark in loose], outs,
        )
        return found, halves[0], halves[0]
    rest = rows - cut
    first, first_give, last, last_give = run(
        square_half_kernel, name + "_half", size,
        [chip, (WHOLE, kept), (WHOLE, arrived)],
        [
            (WHOLE, (2, cut, channels), F32), (WHOLE, (2, cut, channels), BF16),
            (WHOLE, (2, rest, channels), F32), (WHOLE, (2, rest, channels), BF16),
        ],
    )
    half_mark = first
    first, first_give, last, last_give = run(
        square_next_kernel, name + "_next", size,
        [
            (WHOLE, first), (WHOLE, cross(first_give, 1)),
            (WHOLE, last), (WHOLE, cross(last_give, 2)),
        ],
        [
            (WHOLE, (cut, channels), F32), (WHOLE, (cut, channels), BF16),
            (WHOLE, (rest, channels), F32), (WHOLE, (rest, channels), BF16),
        ],
    )
    next_mark = first
    found = run(
        square_last_kernel, name + "_piece", size,
        [
            (WHOLE, first), (WHOLE, cross(first_give, 2)),
            (WHOLE, last), (WHOLE, cross(last_give, 1)),
        ] + [(LOOSE, mark) for mark in loose],
        outs,
    )
    return found, half_mark, next_mark


def collect(piece, order):
    chips = lax.axis_size("chip")
    if chips != 4 or order is None:
        found = [(value[None], (bits,)) for bits, value in enumerate(cross_all(piece))]
    else:
        near, far = order
        both = jnp.stack([piece, cross(piece, near)])
        found = [(both, (0, near)), (cross(both, far), (far, far ^ near))]
    return [(value, beside(value), bits) for value, bits in found]


def dot(left, right):
    return jnp.dot(left, right, preferred_element_type=F32)


def dot_nt(left, right):
    return lax.dot_general(left, right, (((1,), (1,)), ((), ())), preferred_element_type=F32)


def dot_tn(left, right):
    return lax.dot_general(left, right, (((0,), (0,)), ((), ())), preferred_element_type=F32)


def split(values):
    high = values.astype(BF16)
    return high, (values - high.astype(F32)).astype(BF16)


def lower_mask():
    row = lax.broadcasted_iota(jnp.int32, (CHUNK, CHUNK), 0)
    column = lax.broadcasted_iota(jnp.int32, (CHUNK, CHUNK), 1)
    return row >= column


def spread_heads(heads, channels):
    row = lax.broadcasted_iota(jnp.int32, (heads, channels), 0) * HEAD_DIM
    place = lax.broadcasted_iota(jnp.int32, (heads, channels), 1)
    return jnp.where((place >= row) & (place < row + HEAD_DIM), 1.0, 0.0).astype(BF16)


def expand(values, channels):
    high, low = split(values)
    spread = spread_heads(values.shape[1], channels)
    return dot(high, spread) + dot(low, spread)


def decay_kernel(codes_ref, weight_ref, e_ref, f_ref, k_ref, logs_ref):
    heads, channels = codes_ref.shape[1], k_ref.shape[1]
    lower = jnp.where(lower_mask(), 1.0, 0.0).astype(F32)
    count = codes_ref.shape[0] // CHUNK
    line = lax.broadcasted_iota(jnp.int32, (8, heads), 0)
    marks = jnp.zeros((8, heads), F32)
    total = jnp.zeros((1, heads), F32)
    for chunk in range(count):
        rows = pl.ds(chunk * CHUNK, CHUNK)
        logs = codes_ref[rows, :].astype(F32) * (-DECAY_STEP)
        cumulative = jnp.dot(
            lower, logs, precision=lax.Precision.HIGHEST, preferred_element_type=F32
        )
        last = cumulative[CHUNK - 1 :]
        middle = 0.5 * last
        e_ref[rows, :] = jnp.exp(cumulative - middle)
        f_ref[rows, :] = weight_ref[rows, :] * jnp.exp(middle - cumulative)
        marks = jnp.where(line == chunk, jnp.exp(middle), marks)
        total = total + last
    marks = jnp.where(line == 7, total, marks)
    high, low = split(marks)
    lowest = (marks - high.astype(F32) - low.astype(F32)).astype(BF16)
    spread = spread_heads(heads, channels)
    factors = dot(high, spread) + dot(low, spread) + dot(lowest, spread)
    k_ref[...] = factors
    for place in range(logs_ref.shape[0]):
        logs_ref[place] = jnp.broadcast_to(factors[7:8], (8, channels))


def weights_kernel(core_ref, chip_ref, logs_ref, out_ref):
    chips = logs_ref.shape[0] // 2
    core, chip = core_ref[0], chip_ref[0]
    logs = [logs_ref[i, 0:1, :] for i in range(2 * chips)]
    pairs = [logs[2 * i] + logs[2 * i + 1] for i in range(chips)]
    zero = jnp.zeros_like(logs[0])
    out_ref[...] = jnp.zeros_like(out_ref)
    for bits in range(1, chips):
        source = lax.bitwise_xor(chip, bits)
        before, after = zero, zero
        for middle in range(chips):
            before = before + jnp.where((source < middle) & (middle < chip), pairs[middle], 0.0)
            after = after + jnp.where((source > middle) & (middle > chip), pairs[middle], 0.0)
        out_ref[bits : bits + 1, :] = jnp.where(source < chip, jnp.exp(before), 0.0)
        out_ref[8 + bits : 9 + bits, :] = jnp.where(source > chip, jnp.exp(after), 0.0)
    own, other = zero, zero
    for device in range(2 * chips):
        own = own + jnp.where(2 * chip + core == device, logs[device], 0.0)
        other = other + jnp.where(2 * chip + 1 - core == device, logs[device], 0.0)
    out_ref[16:17, :] = jnp.exp(own)
    out_ref[17:18, :] = jnp.exp(other)


def taps(window, kernel, bias, begin):
    summed = bias
    for offset in range(KERNEL):
        summed = summed + kernel[offset : offset + 1] * window[begin + offset : begin + offset + CHUNK]
    return summed


def silu_parts(values):
    sigmoid = jax.nn.sigmoid(values)
    return values * sigmoid, sigmoid * (1.0 + values * (1.0 - sigmoid))


def first_step(action):
    pl.when(pl.program_id(0) == 0)(action)


def clear(*refs):
    def action():
        for ref in refs:
            ref[...] = jnp.zeros_like(ref)

    first_step(action)


def place_parts(mine, parts, target, width, value):
    size = len(parts)
    if width % 128 == 0:
        for i in range(size):
            owner = lax.rem(mine + size - i, size)
            target[:, pl.ds(pl.multiple_of(owner * width, 128), width)] = value(i)
        return

    def write(me):
        for i in range(size):
            owner = (me + size - i) % size
            target[:, owner * width : (owner + 1) * width] = value(i)

    for me in range(size):
        pl.when(mine == me)(functools.partial(write, me))


def copies_kernel(loose_ref, own_ref, out_ref):
    for i in range(out_ref.shape[0]):
        out_ref[i] = own_ref[...]


def norm_kernel(size, loose_ref, head_ref, passed_ref, *refs):
    parts, gains = refs[:size], refs[size : 2 * size]
    passed_gain_ref, normed_ref, scale_ref, gain_ref = refs[2 * size :]
    width = parts[0].shape[1]
    mine = head_ref[0]

    def pick(i, refs, passed):
        if size == 4 and i == 1:
            return jnp.where(mine == 0, passed[...], refs[i][...])
        if size == 4 and i == 3:
            return jnp.where(mine == 3, passed[...], refs[i][...])
        return refs[i][...]

    part = lambda i: pick(i, parts, passed_ref).astype(F32)
    gain = lambda i: pick(i, gains, passed_gain_ref)[0:1].astype(F32)
    squares = sum(jnp.sum(part(i) ** 2, axis=1, keepdims=True) for i in range(size))
    scale = lax.rsqrt(squares / (size * width) + EPSILON)
    scale_ref[...] = jnp.broadcast_to(scale, scale_ref.shape)
    place_parts(
        mine, parts, normed_ref, width,
        lambda i: (part(i) * scale_ref[:, 0:1] * gain(i)).astype(BF16),
    )
    place_parts(mine, parts, gain_ref, width, lambda i: jnp.broadcast_to(gain(i), (8, width)))


def mixed_grad_kernel(parts_ref, weight_ref, out_ref, full_ref):
    size, _, width = parts_ref.shape
    for i in range(size):
        full_ref[:, i * width : (i + 1) * width] = parts_ref[i]
    out_ref[...] = dot_nt(full_ref[...], weight_ref[...])


def out_kernel(loose_ref, mixed_ref, weight_ref, out_ref):
    width = out_ref.shape[2]
    for owner in range(out_ref.shape[0]):
        value = dot(mixed_ref[...], weight_ref[:, owner * width : (owner + 1) * width])
        out_ref[owner] = value.astype(BF16)


def conv_kernel(
    value_ref, state_ref, value_kernel_ref, value_bias_ref, state_kernel_ref, state_bias_ref,
    f_ref, k_ref, conv_ref, weighted_ref, value_slope_ref, maps_ref, state_slope_ref, total_ref,
):
    chunk = pl.program_id(0)
    clear(total_ref)
    around = pl.ds(pl.multiple_of(chunk * CHUNK, CHUNK), CHUNK + HALO)
    pre = taps(
        state_ref[around, :].astype(F32), state_kernel_ref[...].astype(F32),
        state_bias_ref[...].astype(F32), HALO - KERNEL + 1,
    )
    conv, slope = silu_parts(pre)
    maps = conv.astype(BF16)
    maps_ref[...] = maps
    state_slope_ref[...] = slope
    pre = taps(
        value_ref[around, :].astype(F32), value_kernel_ref[...].astype(F32),
        value_bias_ref[...].astype(F32), HALO - KERNEL + 1,
    )
    conv, slope = silu_parts(pre)
    conv = conv.astype(BF16)
    conv_ref[...] = conv
    value_slope_ref[...] = slope
    weighted = (conv.astype(F32) * expand(f_ref[...], conv.shape[1])).astype(BF16)
    weighted_ref[...] = weighted
    factor = k_ref[pl.ds(chunk, 1), :]
    total_ref[...] = factor * (factor * total_ref[...] + dot_tn(maps[:, :NSTATE], weighted))


def mixer_kernel(
    state_in_ref, maps_ref, weighted_ref, conv_ref, e_ref, k_ref, skip_ref, gate_ref, grad_ref, gain_ref,
    mixer_ref, stats_ref, high_ref, low_ref, state_ref,
):
    chunk = pl.program_id(0)

    def start():
        state_ref[...] = state_in_ref[...]

    first_step(start)
    lane = lax.broadcasted_iota(jnp.int32, (CHUNK, CHUNK), 1)
    factor = k_ref[pl.ds(chunk, 1), :]
    input_map, output_map = maps_ref[:, :NSTATE], maps_ref[:, NSTATE:]
    weighted = weighted_ref[...]
    scaled = factor * state_ref[...]
    high, low = split(scaled)
    high_ref[0], low_ref[0] = high, low
    scores = jnp.where(lower_mask(), dot_nt(output_map, input_map), 0.0).astype(BF16)
    mixed = dot(
        jnp.concatenate([scores, output_map], axis=1), jnp.concatenate([weighted, high], axis=0)
    )
    mixed = mixed + dot(output_map, low)
    mixer = expand(e_ref[...], weighted.shape[1]) * mixed + skip_ref[...] * conv_ref[...].astype(F32)
    mixer_ref[...] = mixer
    gate = gate_ref[...]
    gated = mixer * (gate * jax.nn.sigmoid(gate))
    squares = jnp.sum(gated * gated, axis=1, keepdims=True)
    products = jnp.sum(gated * (grad_ref[...] * gain_ref[...].astype(F32)), axis=1, keepdims=True)
    sums = jnp.where(lane == 0, squares, jnp.where(lane == 1, products, 0.0))
    stats_ref[...] = sums.T[:8]
    state_ref[...] = factor * (scaled + dot_tn(input_map, weighted))


def column(row_block):
    rest = jnp.zeros((CHUNK - row_block.shape[0], CHUNK), F32)
    return jnp.concatenate([row_block, rest], axis=0).T


def row_of(sums):
    lane = lax.broadcasted_iota(jnp.int32, (CHUNK, CHUNK), 1)
    return jnp.where(lane == 0, sums, 0.0).T[:8]


def gate_kernel(
    inner, chunks, size, *refs
):
    stats_refs = refs[:size]
    (
        mixer_ref, gate_ref, grad_ref, gain_ref, conv_ref, e_ref, k_ref, maps_ref,
        mixed_ref, gate_grad_ref, mixer_grad_ref, small_ref, total_ref, cross_ref,
    ) = refs[size:]
    chunk = chunks - 1 - pl.program_id(0)
    clear(small_ref, total_ref)
    gain = gain_ref[...].astype(F32)
    stats = column(sum(ref[...] for ref in stats_refs))
    scale = lax.rsqrt(stats[:, 0:1] / inner + EPSILON)
    cross_term = stats[:, 1:2] * (scale * scale * scale) / inner
    gate = gate_ref[...]
    silu, slope = silu_parts(gate)
    mixer = mixer_ref[...]
    gated = mixer * silu
    normed = gated * scale
    mixed_ref[...] = (normed * gain).astype(BF16)
    grad = grad_ref[...]
    gated_grad = scale * (grad * gain) - gated * cross_term
    gate_grad = (gated_grad * mixer * slope).astype(BF16)
    gate_grad_ref[...] = gate_grad
    cross_ref[...] = row_of(jnp.sum(gate_grad.astype(F32) * gate, axis=1, keepdims=True))
    mixer_grad = gated_grad * silu
    mixer_grad_ref[...] = mixer_grad
    small_ref[0:1, :] += jnp.sum(grad * normed, axis=0, keepdims=True)
    small_ref[1:2, :] += jnp.sum(mixer_grad * conv_ref[...].astype(F32), axis=0, keepdims=True)
    high, low = split(expand(e_ref[...], grad.shape[1]) * mixer_grad)
    output_map = maps_ref[:, NSTATE:]
    factor = k_ref[pl.ds(chunk, 1), :]
    total_ref[...] = factor * (
        factor * total_ref[...] + (dot_tn(output_map, high) + dot_tn(output_map, low))
    )


def back_kernel(
    chunks, early_ref, state_in_ref, mixer_grad_ref, e_ref, f_ref, k_ref, weighted_ref, high_ref, low_ref,
    maps_ref, value_slope_ref, state_slope_ref, skip_ref,
    value_ref, map_ref, state_ref,
):
    chunk = chunks - 1 - pl.program_id(0)

    def start():
        state_ref[...] = state_in_ref[...]

    first_step(start)
    lower = lower_mask()
    row = lax.broadcasted_iota(jnp.int32, (CHUNK, CHUNK), 0)
    upper = row <= lax.broadcasted_iota(jnp.int32, (CHUNK, CHUNK), 1)
    factor = k_ref[pl.ds(chunk, 1), :]
    input_map, output_map = maps_ref[:, :NSTATE], maps_ref[:, NSTATE:]
    weighted = weighted_ref[...]
    mixer_grad = mixer_grad_ref[...]
    high, low = split(expand(e_ref[...], weighted.shape[1]) * mixer_grad)
    scaled = factor * state_ref[...]
    state_high, state_low = split(scaled)
    both = jnp.concatenate([weighted, high_ref[0]], axis=0)
    sums = dot_nt(high, both) + dot_nt(low, both)
    score_grad = jnp.where(lower, sums[:, :CHUNK], 0.0).astype(BF16)
    output_grad = sums[:, CHUNK:] + dot_nt(high, low_ref[0]) + dot(score_grad, input_map)
    sums = dot_nt(weighted, jnp.concatenate([state_high, state_low], axis=0))
    input_grad = sums[:, :NSTATE] + sums[:, NSTATE:] + dot_tn(score_grad, output_map)
    scores = jnp.where(upper, dot_nt(input_map, output_map), 0.0).astype(BF16)
    grads = dot(
        jnp.concatenate([scores, input_map], axis=1), jnp.concatenate([high, state_high], axis=0)
    )
    decayed = expand(f_ref[...], weighted.shape[1]) * grads
    value_ref[...] = (decayed + skip_ref[...] * mixer_grad) * value_slope_ref[...]
    slope = state_slope_ref[...]
    map_ref[:, :NSTATE] = input_grad * slope[:, :NSTATE]
    map_ref[:, NSTATE:] = output_grad * slope[:, NSTATE:]
    state_ref[...] = factor * (scaled + (dot_tn(output_map, high) + dot_tn(output_map, low)))


def conv_back_kernel(
    chunks, value_ref, map_ref, after_ref, value_raw_ref, state_raw_ref, value_kernel_ref,
    state_kernel_ref, cross_in_ref,
    value_grad_ref, state_grad_ref, value_small_ref, state_small_ref, cross_ref, value_next_ref,
    state_next_ref,
):
    chunk = chunks - 1 - pl.program_id(0)
    channels = value_ref.shape[1]
    clear(value_small_ref, state_small_ref)

    def start():
        value_next_ref[...] = after_ref[:, :channels]
        state_next_ref[...] = after_ref[:, channels:]

    first_step(start)

    def back(slope_ref, next_ref, raw_ref, kernel_ref, grad_ref, small_ref):
        kernel = kernel_ref[...].astype(F32)
        slope = slope_ref[...]
        window = jnp.concatenate([slope, next_ref[...]], axis=0)
        around = pl.ds(pl.multiple_of(chunk * CHUNK, CHUNK), CHUNK + HALO)
        raw = raw_ref[around, :].astype(F32)
        grad = jnp.zeros_like(slope)
        for offset in range(KERNEL):
            back_by = KERNEL - 1 - offset
            grad = grad + kernel[offset : offset + 1] * window[back_by : back_by + CHUNK]
            begin = HALO - KERNEL + 1 + offset
            small_ref[offset : offset + 1, :] += jnp.sum(
                slope * raw[begin : begin + CHUNK], axis=0, keepdims=True
            )
        small_ref[KERNEL : KERNEL + 1, :] += jnp.sum(slope, axis=0, keepdims=True)
        grad = grad.astype(BF16)
        grad_ref[...] = grad
        next_ref[...] = slope[:8]
        return jnp.sum(grad.astype(F32) * raw[HALO:], axis=1, keepdims=True)

    crossed = back(map_ref, state_next_ref, state_raw_ref, state_kernel_ref, state_grad_ref, state_small_ref)
    crossed = crossed + back(
        value_ref, value_next_ref, value_raw_ref, value_kernel_ref, value_grad_ref, value_small_ref
    )
    cross_ref[...] = cross_in_ref[...] + row_of(crossed)


def normed_kernel(
    chunks, late_ref, gate_grad_ref, value_grad_ref, state_grad_ref, gate_weight_ref, value_weight_ref,
    state_weight_ref, cross_ref, out_ref
):
    value = (
        dot_nt(gate_grad_ref[...], gate_weight_ref[...])
        + dot_nt(value_grad_ref[...], value_weight_ref[...])
        + dot_nt(state_grad_ref[...], state_weight_ref[...])
    )
    count = value.shape[0]
    out_ref[0, :count, :] = value.astype(BF16)
    line = lax.broadcasted_iota(jnp.int32, (HALO, CHUNK), 0)
    packed = jnp.zeros((HALO, CHUNK), F32)
    for chunk in range(chunks):
        row = cross_ref[0:1, chunk * CHUNK : (chunk + 1) * CHUNK]
        high = row.astype(BF16).astype(F32)
        packed = jnp.where(line == chunk, high, packed)
        packed = jnp.where(line == chunks + chunk, row - high, packed)
    out_ref[0, count:, :] = jnp.zeros((HALO, value.shape[1]), BF16)
    out_ref[0, count:, :CHUNK] = packed.astype(BF16)


def last_kernel(full_width, parts_ref, tokens_ref, scale_ref, gain_ref, cotangent_ref, out_ref):
    count = tokens_ref.shape[0]
    chunks = count // CHUNK
    size = parts_ref.shape[0]
    crossed = sum(parts_ref[i, count:, :CHUNK].astype(F32) for i in range(size))
    crossed = crossed[:chunks] + crossed[chunks : 2 * chunks]
    for chunk in range(chunks):
        rows = slice(chunk * CHUNK, (chunk + 1) * CHUNK)
        normed_grad = sum(parts_ref[i, rows, :].astype(F32) for i in range(size))
        scale = scale_ref[HALO + chunk * CHUNK : HALO + (chunk + 1) * CHUNK, 0:1]
        total = column(jnp.broadcast_to(crossed[chunk : chunk + 1], (8, CHUNK)))[:, 0:1]
        out_ref[rows, :] = (
            scale * gain_ref[...].astype(F32) * normed_grad
            - tokens_ref[rows, :].astype(F32) * (scale * scale * total / full_width)
            + cotangent_ref[rows, :].astype(F32)
        ).astype(BF16)


def store_piece(core_ref, kept_ref, given_ref, place, begin, piece):
    chips = kept_ref.shape[0]
    core, chip = place // chips, lax.rem(place, chips)
    rows = slice(begin, begin + piece.shape[0])
    piece = piece.astype(BF16)

    @pl.when(core_ref[0] == core)
    def _():
        kept_ref[chip, rows, :] = piece

    @pl.when(core_ref[0] != core)
    def _():
        given_ref[chip, rows, :] = piece


def gain_row(weight, block):
    sums = jnp.sum(weight.astype(F32) * block, axis=1, keepdims=True)
    lane = lax.broadcasted_iota(jnp.int32, (CHUNK, CHUNK), 1)
    rows = [
        jnp.where(lane == 0, sums[i : i + CHUNK], 0.0).T[0:1] for i in range(0, BLOCK, CHUNK)
    ]
    return jnp.concatenate(rows, axis=1)


def early_kernel(
    loose_ref, core_ref, normed_ref, gate_ref, mixed_ref, grad_ref, weight_ref,
    kept_ref, given_ref, gain_ref, held_ref
):
    chips, rows, channels = kept_ref.shape
    at = pl.program_id(0)
    count, width = grad_ref.shape
    pieces = 2 * chips
    step = width // pieces
    out_rows = channels // pieces
    out_blocks = channels // BLOCK
    every = width // BLOCK // out_blocks

    @pl.when(lax.rem(at, every) == 0)
    def _():
        held_ref[...] = dot_tn(mixed_ref[...], grad_ref[...])

    block = dot_tn(normed_ref[HALO : HALO + count, :], gate_ref[...])
    gain_ref[...] = gain_row(weight_ref[...], block)
    for i in range(BLOCK // step):
        place = at * (BLOCK // step) + i
        begin = lax.rem(at, every) * (BLOCK // step * out_rows) + i * out_rows
        own = held_ref[pl.ds(pl.multiple_of(begin, 8), out_rows), :]
        parts = [block[i * step : (i + 1) * step]]
        parts += [own[:, j : j + channels] for j in range(0, width, channels)]
        store_piece(core_ref, kept_ref, given_ref, place, 0, jnp.concatenate(parts, axis=0))


def late_kernel(
    early_ref, core_ref, normed_ref, value_ref, state_ref, value_small_ref, gate_small_ref, gain_ref,
    state_small_ref, value_weight_ref, state_weight_ref, gain_full_ref,
    kept_ref, given_ref, own_ref, shared_ref, gains_ref,
):
    chips, rows, channels = kept_ref.shape
    at = pl.program_id(0)
    count, maps_width = state_ref.shape
    width = gains_ref.shape[1]
    pieces = 2 * chips
    step = width // pieces
    lanes = channels // 128
    part = 2 * step // lanes
    columns = normed_ref[HALO : HALO + count, :]
    value = dot_tn(columns, value_ref[...])
    state = dot_tn(columns, state_ref[...])
    gain = (
        gain_ref[...] + gain_row(value_weight_ref[...], value) + gain_row(state_weight_ref[...], state)
    ) / gain_full_ref[0:1, :]
    gains_ref[0:1, pl.ds(pl.multiple_of(at * BLOCK, 128), BLOCK)] = gain
    for i in range(BLOCK // step):
        piece = slice(i * step, (i + 1) * step)
        stacked = jnp.concatenate([state[piece, :128], state[piece, 128:]], axis=0)
        stacked = jnp.concatenate(
            [stacked[j * part : (j + 1) * part] for j in range(lanes)], axis=1
        )
        store_piece(
            core_ref, kept_ref, given_ref, at * (BLOCK // step) + i, 0,
            jnp.concatenate([value[piece], stacked], axis=0),
        )

    @pl.when(at == width // BLOCK - 1)
    def _():
        own_ref[...] = jnp.zeros_like(own_ref)
        own_ref[: KERNEL + 1, :] = value_small_ref[: KERNEL + 1, :]
        own_ref[KERNEL + 1 : KERNEL + 3, :] = gate_small_ref[:2, :]
        shared_ref[...] = jnp.zeros_like(shared_ref)
        begin = width // channels
        for i in range(begin):
            shared_ref[i : i + 1, :] = gains_ref[0:1, i * channels : (i + 1) * channels]
        for i in range(0, (KERNEL + 1) * maps_width, 128):
            tap, column_from = divmod(i, maps_width)
            row, column_to = divmod(i, channels)
            shared_ref[begin + row : begin + row + 1, column_to : column_to + 128] = state_small_ref[
                tap : tap + 1, column_from : column_from + 128
            ]
        line = lax.broadcasted_iota(jnp.int32, (HALO, channels), 0)
        for place in range(pieces):
            own, shared = own_ref[place : place + 1, :], shared_ref[place : place + 1, :]
            own_high, shared_high = (v.astype(BF16).astype(F32) for v in (own, shared))
            small = jnp.zeros((HALO, channels), F32)
            for to, value in enumerate((own_high, own - own_high, shared_high, shared - shared_high)):
                small = jnp.where(line == to, value, small)
            store_piece(core_ref, kept_ref, given_ref, place, step + part, small)


def merge_pairs(block):
    tail = block[-HALO:]
    line = lax.broadcasted_iota(jnp.int32, tail.shape, 0)
    own, shared = tail[0:1] + tail[1:2], tail[2:3] + tail[3:4]
    own_high, shared_high = own.astype(BF16).astype(F32), shared.astype(BF16).astype(F32)
    new = jnp.zeros_like(tail)
    for at, value in enumerate((own_high, own - own_high, shared_high, shared - shared_high)):
        new = jnp.where(line == at, value, new)
    return jnp.concatenate([block[:-HALO], new], axis=0)


def heads_kernel(piece_ref, total_ref, arrived_ref, out_ref, low_ref):
    total = merge_pairs(total_ref[...] + arrived_ref[...].astype(F32))
    line = lax.broadcasted_iota(jnp.int32, total.shape, 0)
    first = total.shape[0] - HALO
    own = (line >= first) & (line < first + 2)
    out_ref[...] = total
    low_ref[...] = jnp.where(own, piece_ref[...], total).astype(BF16)


def half_kernel(paired, chips, chip_ref, kept_ref, arrived_ref, *outs):
    for bits in range(chips):
        place = lax.bitwise_xor(chip_ref[0], bits)
        value = kept_ref[place].astype(F32) + arrived_ref[place].astype(F32)
        if paired:
            value = merge_pairs(value)
        outs[bits][...] = value.astype(outs[bits].dtype)


def piece_kernel(parts, paired, cut, *refs):
    total = sum(ref[...].astype(F32) for ref in refs[:parts])
    if not paired:
        refs[-1][...] = total.astype(BF16)
        return
    first_ref, last_ref = refs[-2:]
    first_ref[...] = total[:cut].astype(BF16)
    last_ref[...] = merge_pairs(total[cut:])


def square_half_kernel(
    chip_ref, kept_ref, arrived_ref, first_ref, first_give_ref, last_ref, last_give_ref
):
    cut = first_ref.shape[1]
    for bits in range(4):
        place = lax.bitwise_xor(chip_ref[0], bits)
        value = kept_ref[place].astype(F32) + arrived_ref[place].astype(F32)
        low, high = bits & 1, bits >> 1
        ref = first_give_ref if low else first_ref
        ref[high] = value[:cut].astype(ref.dtype)
        ref = last_give_ref if high else last_ref
        ref[low] = value[cut:].astype(ref.dtype)


def square_next_kernel(
    first_ref, first_got_ref, last_ref, last_got_ref,
    first_out_ref, first_give_ref, last_out_ref, last_give_ref,
):
    first_out_ref[...] = first_ref[0] + first_got_ref[0].astype(F32)
    first_give_ref[...] = (first_ref[1] + first_got_ref[1].astype(F32)).astype(BF16)
    last_out_ref[...] = last_ref[0] + last_got_ref[0].astype(F32)
    last_give_ref[...] = (last_ref[1] + last_got_ref[1].astype(F32)).astype(BF16)


def square_last_kernel(first_ref, first_got_ref, last_ref, last_got_ref, *refs):
    out_ref = refs[-1]
    cut = first_ref.shape[0]
    out_ref[:cut, :] = (first_ref[...] + first_got_ref[...].astype(F32)).astype(BF16)
    out_ref[cut:, :] = (last_ref[...] + last_got_ref[...].astype(F32)).astype(BF16)


def spread_pieces(core_ref, chip_ref, chips, groups, refs, store):
    step = pl.program_id(0)
    core, chip = step // chips, lax.rem(step, chips)
    apart = lax.bitwise_xor(chip, chip_ref[0])
    refs = iter(refs)
    for part, bits_lists in enumerate(groups):
        for bits_list in bits_lists:
            own_ref, other_ref = next(refs), next(refs)
            for at, bits in enumerate(bits_list):

                @pl.when((apart == bits) & (core == core_ref[0]))
                def _(part=part, ref=own_ref, at=at):
                    store(part, ref[at].astype(F32))

                @pl.when((apart == bits) & (core != core_ref[0]))
                def _(part=part, ref=other_ref, at=at):
                    store(part, ref[at].astype(F32))


def early_out_kernel(chips, groups, core_ref, chip_ref, *refs):
    gate_ref, output_ref = refs[-2:]
    step, channels = gate_ref.shape
    out_rows, width = output_ref.shape

    def store(part, value):
        gate_ref[...] = value[:step]
        output_ref[...] = jnp.concatenate(
            [value[step + i * out_rows : step + (i + 1) * out_rows] for i in range(width // channels)],
            axis=1,
        )

    spread_pieces(core_ref, chip_ref, chips, groups, refs[:-2], store)


def late_out_kernel(chips, groups, core_ref, chip_ref, *refs):
    value_ref = refs[-1]

    def store(part, value):
        value_ref[...] = value

    spread_pieces(core_ref, chip_ref, chips, groups, refs[:-1], store)


def shared_out_kernel(chips, groups, core_ref, chip_ref, *refs):
    (
        state_ref, value_kernel_ref, value_bias_ref, state_kernel_ref, state_bias_ref, skip_ref,
        gated_ref, gain_ref, own_ref, shared_ref,
    ) = refs[-10:]
    step, maps_width = state_ref.shape
    channels = own_ref.shape[1]
    lanes = channels // 128
    rows = 2 * step // lanes
    at = pl.program_id(0)

    def store(part, piece):
        stacked = jnp.concatenate(
            [piece[:rows, i * 128 : (i + 1) * 128] for i in range(lanes)], axis=0
        )
        state_ref[...] = jnp.concatenate([stacked[:step], stacked[step:]], axis=1)
        own_ref[pl.ds(at, 1), :] = piece[rows : rows + 1] + piece[rows + 1 : rows + 2]
        shared_ref[pl.ds(at, 1), :] = piece[rows + 2 : rows + 3] + piece[rows + 3 : rows + 4]

    spread_pieces(core_ref, chip_ref, chips, groups, refs[:-10], store)

    @pl.when(at == 2 * chips - 1)
    def _():
        value_kernel_ref[...] = own_ref[:KERNEL, :]
        value_bias_ref[...] = own_ref[KERNEL : KERNEL + 1, :]
        gated_ref[...] = own_ref[KERNEL + 1 : KERNEL + 2, :]
        skip_ref[...] = own_ref[KERNEL + 2 : KERNEL + 3, :]
        gain_rows = gain_ref.shape[1] // channels
        for i in range(gain_rows):
            gain_ref[:, i * channels : (i + 1) * channels] = shared_ref[i : i + 1, :]
        for i in range(0, (KERNEL + 1) * maps_width, 128):
            tap, column_to = divmod(i, maps_width)
            row, column_from = divmod(i, channels)
            value = shared_ref[gain_rows + row : gain_rows + row + 1, column_from : column_from + 128]
            if tap < KERNEL:
                state_kernel_ref[tap : tap + 1, column_to : column_to + 128] = value
            else:
                state_bias_ref[:, column_to : column_to + 128] = value


SCALAR = "scalar"
WHOLE = "whole"
BLOCKED = "blocked"
LANES = "lanes"
LEADING = "leading"
LOOSE = "loose"


def run(kernel, name, flops, args, outs, steps=None, backward=False, scratch=()):
    at = (lambda i: steps - 1 - i) if backward else (lambda i: i)

    def spec(kind, shape):
        if isinstance(kind, int):
            return pl.BlockSpec((kind,) + shape[1:], lambda i: (at(i), 0))
        if kind == SCALAR:
            return pl.BlockSpec(memory_space=pltpu.SMEM)
        if kind == LOOSE:
            return pl.BlockSpec(memory_space=pl.ANY)
        if isinstance(kind, tuple):
            return pl.BlockSpec(*kind)
        if steps is None:
            return pl.BlockSpec(memory_space=pltpu.VMEM)
        if kind == BLOCKED:
            return pl.BlockSpec((CHUNK, shape[1]), lambda i: (at(i), 0))
        if kind == LANES:
            return pl.BlockSpec((shape[0], CHUNK), lambda i: (0, at(i)))
        if kind == LEADING:
            return pl.BlockSpec((1,) + shape[1:], lambda i: (at(i),) + (0,) * (len(shape) - 1))
        return pl.BlockSpec(shape, lambda i: (0,) * len(shape))

    moved = sum(a.size * a.dtype.itemsize for kind, a in args if kind != LOOSE)
    shapes = [jax.ShapeDtypeStruct(shape, dtype) for _, shape, dtype in outs]
    moved += sum(a.size * a.dtype.itemsize for a in shapes)
    return pl.pallas_call(
        kernel,
        out_shape=shapes,
        in_specs=[spec(kind, a.shape) for kind, a in args],
        out_specs=[spec(kind, shape) for kind, shape, _ in outs],
        scratch_shapes=list(scratch),
        compiler_params=pltpu.CompilerParams(vmem_limit_bytes=VMEM_LIMIT),
        cost_estimate=pl.CostEstimate(flops=flops, bytes_accessed=moved, transcendentals=0),
        name=name,
        **({} if steps is None else {"grid": (steps,)}),
    )(*(a for _, a in args))


def per_device(
    tokens, decay_codes, norm_gain, gate_weight, value_weight, state_weight, value_kernel, value_bias,
    state_kernel, state_bias, skip_scale, gated_gain, output_weight, cotangent,
):
    tokens, decay_codes, cotangent = tokens[0], decay_codes[0], cotangent[0]
    count, own_width = tokens.shape
    heads = skip_scale.shape[0]
    channels = heads * HEAD_DIM
    head_size, chips = lax.axis_size("head"), lax.axis_size("chip")
    seq_size = 2 * chips
    width = own_width * head_size
    maps_width = 2 * NSTATE
    chunks = count // CHUNK
    core = (SCALAR, lax.axis_index("core").astype(jnp.int32)[None])
    chip = (SCALAR, lax.axis_index("chip").astype(jnp.int32)[None])
    head = (SCALAR, lax.axis_index("head").astype(jnp.int32)[None])

    rows = count + MARGIN
    packed = jnp.concatenate(
        [
            from_behind(tokens[-HALO:], 1),
            tokens,
            jnp.broadcast_to(norm_gain[None], (MARGIN - HALO, own_width)),
        ],
        axis=0,
    )
    logs = decay_codes.astype(F32) * (-DECAY_STEP)
    input_weight = jnp.sqrt(-jnp.expm1(2.0 * logs))
    e_full, f_full, factors, all_logs = run(
        decay_kernel, "decays", count * channels * 200,
        [(WHOLE, decay_codes), (WHOLE, input_weight)],
        [
            (WHOLE, (count, heads), F32),
            (WHOLE, (count, heads), F32),
            (WHOLE, (8, channels), F32),
            (WHOLE, (seq_size, 8, channels), F32),
        ],
    )
    all_logs = lax.all_to_all(all_logs, ("chip", "core"), 0, 0)
    weights = run(
        weights_kernel, "weights", channels * 1000, [core, chip, (WHOLE, all_logs)],
        [(WHOLE, (24, channels), F32)],
    )[0]
    parts, passed, mark = line_parts(packed, "head")
    skip_full = jnp.repeat(skip_scale, HEAD_DIM)[None]

    half = rows // 2
    gain_rows = ((MARGIN - HALO, own_width), lambda i: ((HALO + count) // (MARGIN - HALO), 0))
    copies = run(
        copies_kernel, "copies", 1, [(LOOSE, mark), (WHOLE, cotangent)],
        [(WHOLE, (head_size, count, own_width), BF16)],
    )[0]
    cotangent_parts = deal(copies, "head")
    normed, scale_in, gain_full = run(
        functools.partial(norm_kernel, head_size), "norm", count * width * 10,
        [(LOOSE, copies), head, (half, passed)] + [(half, part) for part in parts]
        + [(gain_rows, part) for part in parts] + [(gain_rows, passed)],
        [(half, (rows, width), BF16), (half, (rows, 128), F32), (WHOLE, (8, width), F32)],
        steps=2,
    )
    value_raw = dot(normed, value_weight).astype(BF16)
    state_raw = dot(normed, state_weight).astype(BF16)
    conv, weighted, value_slope, maps, map_slope, local_end = run(
        conv_kernel, "conv", count * channels * 400,
        [
            (WHOLE, value_raw), (WHOLE, state_raw), (WHOLE, value_kernel), (WHOLE, value_bias[None]),
            (WHOLE, state_kernel), (WHOLE, state_bias[None]), (BLOCKED, f_full), (WHOLE, factors),
        ],
        [
            (BLOCKED, (count, channels), BF16),
            (BLOCKED, (count, channels), BF16),
            (BLOCKED, (count, channels), F32),
            (BLOCKED, (count, maps_width), BF16),
            (BLOCKED, (count, maps_width), F32),
            (WHOLE, (NSTATE, channels), F32),
        ],
        steps=chunks,
    )
    gate_pre = dot(normed, gate_weight)[HALO : HALO + count]
    state_in = entering(local_end, weights, 0, False, gate_pre)
    mixed_grad, full_cotangent = run(
        mixed_grad_kernel, "mixed_grad", 2 * count * width * channels,
        [(WHOLE, cotangent_parts), (WHOLE, output_weight)],
        [(WHOLE, (count, channels), F32), (WHOLE, (count, width), BF16)],
    )
    mixer, stats, high, low = run(
        mixer_kernel, "mixer", count * channels * 1000,
        [
            (WHOLE, state_in), (BLOCKED, maps), (BLOCKED, weighted), (BLOCKED, conv),
            (BLOCKED, e_full), (WHOLE, factors), (WHOLE, skip_full), (BLOCKED, gate_pre),
            (BLOCKED, mixed_grad), (WHOLE, gated_gain[None]),
        ],
        [
            (BLOCKED, (count, channels), F32),
            (LANES, (8, count), F32),
            (LEADING, (chunks, NSTATE, channels), BF16),
            (LEADING, (chunks, NSTATE, channels), BF16),
        ],
        steps=chunks,
        scratch=[pltpu.VMEM((NSTATE, channels), F32)],
    )
    mixed, gate_grad, mixer_grad, gate_small, start_grad, gate_cross = run(
        functools.partial(gate_kernel, float(channels * head_size), chunks, head_size),
        "gate", count * channels * 600,
        [(LANES, part) for part in turn_all(stats, "head")]
        + [
            (BLOCKED, mixer), (BLOCKED, gate_pre), (BLOCKED, mixed_grad), (WHOLE, gated_gain[None]),
            (BLOCKED, conv), (BLOCKED, e_full), (WHOLE, factors), (BLOCKED, maps),
        ],
        [
            (BLOCKED, (count, channels), BF16),
            (BLOCKED, (count, channels), BF16),
            (BLOCKED, (count, channels), F32),
            (WHOLE, (8, channels), F32),
            (WHOLE, (NSTATE, channels), F32),
            (LANES, (8, count), F32),
        ],
        steps=chunks,
        backward=True,
    )
    step, out_rows = width // seq_size, channels // seq_size
    early_rows = step + out_rows * (width // channels)
    features = width // BLOCK
    feature_block = ((rows, BLOCK), lambda i: (0, i))
    every = features // (channels // BLOCK)
    made = {}

    def out_and_early(pair):
        made["early"] = run(
            early_kernel, "early", 4 * count * channels * width,
            [
                (LOOSE, pair), core, (feature_block, normed), (WHOLE, gate_grad),
                (((count, BLOCK), lambda i: (0, i // every)), mixed), (WHOLE, full_cotangent),
                (BLOCK, gate_weight),
            ],
            [(WHOLE, (chips, early_rows, channels), BF16)] * 2
            + [(((1, BLOCK), lambda i: (0, i)), (1, width), F32)],
            steps=features,
            scratch=[pltpu.VMEM((BLOCK, width), F32)],
        )
        made["out"] = run(
            out_kernel, "out", 2 * count * channels * width,
            [(LOOSE, made["early"][0]), (WHOLE, mixed), (WHOLE, output_weight)],
            [(WHOLE, (head_size, count, own_width), BF16)],
        )[0]
        return made["out"]

    grad_after = entering(start_grad, weights, 8, True, later=out_and_early)
    early_kept, early_given, early_gain = made["early"]
    out_parts = made["out"]
    early_found, half_mark, next_mark = sum_pieces(
        chip, early_kept, early_given, "early", True, step, False
    )
    early_piece = early_found[0]
    branch = jnp.sum(deal(out_parts, "head").astype(F32), axis=0)
    block_out = (tokens.astype(F32) + branch).astype(BF16)

    value_grads, map_grads = run(
        functools.partial(back_kernel, chunks), "back", count * channels * 2000,
        [
            (LOOSE, half_mark), (WHOLE, grad_after), (BLOCKED, mixer_grad), (BLOCKED, e_full),
            (BLOCKED, f_full), (WHOLE, factors), (BLOCKED, weighted), (LEADING, high),
            (LEADING, low), (BLOCKED, maps), (BLOCKED, value_slope), (BLOCKED, map_slope),
            (WHOLE, skip_full),
        ],
        [(BLOCKED, (count, channels), F32), (BLOCKED, (count, maps_width), F32)],
        steps=chunks,
        backward=True,
        scratch=[pltpu.VMEM((NSTATE, channels), F32)],
    )
    after = from_behind(jnp.concatenate([value_grads[:8], map_grads[:8]], axis=1), -1)
    value_raw_grad, state_raw_grad, value_small, state_small, crossed = run(
        functools.partial(conv_back_kernel, chunks), "conv_back", count * channels * 100,
        [
            (BLOCKED, value_grads), (BLOCKED, map_grads), (WHOLE, after),
            (WHOLE, value_raw), (WHOLE, state_raw), (WHOLE, value_kernel), (WHOLE, state_kernel),
            (LANES, gate_cross),
        ],
        [
            (BLOCKED, (count, channels), BF16),
            (BLOCKED, (count, maps_width), BF16),
            (WHOLE, (8, channels), F32),
            (WHOLE, (8, maps_width), F32),
            (LANES, (8, count), F32),
        ],
        steps=chunks,
        backward=True,
        scratch=[pltpu.VMEM((8, channels), F32), pltpu.VMEM((8, maps_width), F32)],
    )
    lanes = channels // 128
    state_rows = 2 * step // lanes
    late_rows = step + state_rows + HALO
    late_kept, late_given = run(
        late_kernel, "late", 3 * count * channels * width,
        [
            (LOOSE, next_mark), core, (feature_block, normed), (WHOLE, value_raw_grad),
            (WHOLE, state_raw_grad),
            (WHOLE, value_small), (WHOLE, gate_small), (((1, BLOCK), lambda i: (0, i)), early_gain),
            (WHOLE, state_small), (BLOCK, value_weight), (BLOCK, state_weight),
            (((8, BLOCK), lambda i: (0, i)), gain_full),
        ],
        [(WHOLE, (chips, late_rows, channels), BF16)] * 2,
        steps=features,
        scratch=[
            pltpu.VMEM((HALO, channels), F32),
            pltpu.VMEM((HALO, channels), F32),
            pltpu.VMEM((8, width), F32),
        ],
    )
    normed_parts = run(
        functools.partial(normed_kernel, chunks), "normed", 4 * count * channels * width,
        [
            (LOOSE, late_given), (WHOLE, gate_grad), (WHOLE, value_raw_grad),
            (WHOLE, state_raw_grad), (own_width, gate_weight), (own_width, value_weight),
            (own_width, state_weight), (WHOLE, crossed),
        ],
        [(LEADING, (head_size, count + HALO, own_width), BF16)],
        steps=head_size,
    )[0]
    (late_piece, shared_piece), _, _ = sum_pieces(
        chip, late_kept, late_given, "late", False, step, True, loose=(normed_parts,)
    )
    normed_parts = deal(normed_parts, "head")
    shared_piece = heads_sum(shared_piece)

    def unpack(kernel, name, pieces, outs, flops, extra=(), scratch=()):
        groups = [collect(piece, order) for piece, order in pieces]
        bits = [[found[2] for found in group] for group in groups]
        arrays = [(WHOLE, value) for group in groups for found in group for value in found[:2]]
        return run(
            functools.partial(kernel, chips, bits, *extra), name, flops, [core, chip] + arrays, outs,
            steps=seq_size, scratch=scratch,
        )

    gate_weight_gradient, output_weight_gradient = unpack(
        early_out_kernel, "early_out", [(early_piece, (2, 1))],
        [(step, (width, channels), F32), (out_rows, (channels, width), F32)], 4 * channels * width,
    )
    value_weight_gradient = unpack(
        late_out_kernel, "late_out", [(late_piece, None)],
        [(step, (width, channels), F32)], 2 * channels * width,
    )[0]
    (
        state_weight_gradient, value_kernel_gradient, value_bias_gradient, state_kernel_gradient,
        state_bias_gradient, skip_sums, gated_gain_gradient, gain_sums,
    ) = unpack(
        shared_out_kernel, "shared_out", [(shared_piece, (2, 1))],
        [
            (step, (width, maps_width), F32),
            (WHOLE, (KERNEL, channels), F32),
            (WHOLE, (1, channels), F32),
            (WHOLE, (KERNEL, maps_width), F32),
            (WHOLE, (1, maps_width), F32),
            (WHOLE, (1, channels), F32),
            (WHOLE, (1, channels), F32),
            (WHOLE, (1, width), F32),
        ],
        2 * maps_width * width,
        scratch=[pltpu.VMEM((HALO, channels), F32), pltpu.VMEM((HALO, channels), F32)],
    )
    value_bias_gradient, state_bias_gradient = value_bias_gradient[0], state_bias_gradient[0]
    gated_gain_gradient = gated_gain_gradient[0]
    skip_scale_gradient = jnp.sum(skip_sums.reshape(heads, HEAD_DIM), axis=1)
    norm_gain_gradient = lax.dynamic_slice_in_dim(
        gain_sums[0], lax.axis_index("head") * own_width, own_width, 0
    )

    tokens_gradient = run(
        functools.partial(last_kernel, float(width)), "last", count * own_width * 20,
        [
            (WHOLE, normed_parts), (WHOLE, tokens), (WHOLE, scale_in),
            (WHOLE, norm_gain[None]), (WHOLE, cotangent),
        ],
        [(WHOLE, (count, own_width), BF16)],
    )[0]
    return (
        block_out[None],
        tokens_gradient[None],
        norm_gain_gradient,
        gate_weight_gradient,
        value_weight_gradient,
        state_weight_gradient,
        value_kernel_gradient,
        value_bias_gradient,
        state_kernel_gradient,
        state_bias_gradient,
        skip_scale_gradient,
        gated_gain_gradient,
        output_weight_gradient,
    )


def solution(mesh):
    seq_size, head_size = mesh.shape["seq"], mesh.shape["head"]
    mesh = Mesh(mesh.devices.reshape(seq_size // 2, 2, head_size), ("chip", "core", "head"))
    seq = ("chip", "core")
    in_specs = (
        P(None, seq, "head"),
        P(None, seq, "head"),
        P("head"),
        P(None, "head"),
        P(None, "head"),
        P(),
        P(None, "head"),
        P("head"),
        P(),
        P(),
        P("head"),
        P("head"),
        P("head", None),
        P(None, seq, "head"),
    )
    out_specs = (
        P(None, seq, "head"),
        P(None, seq, "head"),
        P("head"),
        P(None, "head"),
        P(None, "head"),
        P(),
        P(None, "head"),
        P("head"),
        P(),
        P(),
        P("head"),
        P("head"),
        P("head", None),
    )
    return jax.shard_map(
        per_device, mesh=mesh, in_specs=in_specs, out_specs=out_specs, check_vma=False
    )
```

```python
import functools

import jax
import jax.numpy as jnp
from jax import lax
from jax.experimental import pallas as pl
from jax.experimental.pallas import tpu as pltpu
from jax.sharding import Mesh
from jax.sharding import PartitionSpec as P

HEAD_DIM = 64
NSTATE = 128
KERNEL = 4
CHUNK = 128
BLOCK = 384
VMEM_LIMIT = 20 * 1024 * 1024
MARGIN = 32
HALO = 16


DECAY_STEP = 1.0 / 1048576.0
EPSILON = 1e-05
BF16 = jnp.bfloat16
F32 = jnp.float32


def tie_kernel(*refs):
    del refs


def tie(value, *others):
    return pl.pallas_call(
        tie_kernel,
        out_shape=jax.ShapeDtypeStruct(value.shape, value.dtype),
        in_specs=[pl.BlockSpec(memory_space=pl.ANY)] * (1 + len(others)),
        out_specs=pl.BlockSpec(memory_space=pl.ANY),
        input_output_aliases={0: 0},
        name="tie",
    )(value, *others)


def from_behind(value, by):
    axis = ("chip", "core")
    size = lax.axis_size("chip") * 2
    pairs = [(i, i + by) for i in range(size) if 0 <= i + by < size]
    return lax.ppermute(value, axis, pairs)


def beside(value):
    return lax.ppermute(value, "core", [(0, 1), (1, 0)])


def turn(value, axis, by):
    size = lax.axis_size(axis)
    return lax.ppermute(value, axis, [(i, (i + by) % size) for i in range(size)])


def turn_all(value, axis):
    return [value] + [turn(value, axis, by) for by in range(1, lax.axis_size(axis))]


def line_parts(value, axis):
    if lax.axis_size(axis) != 4:
        parts = turn_all(value, axis)
        return parts, value, parts[1]
    two = turn(value, axis, 2)
    one = lax.ppermute(value, axis, [(0, 1), (1, 2), (2, 3)])
    three = lax.ppermute(value, axis, [(1, 0), (2, 1), (3, 2)])
    passed = lax.ppermute(two, axis, [(2, 3), (1, 0)])
    return [value, one, two, three], passed, two


def deal(parts, axis):
    return lax.all_to_all(parts, axis, 0, 0)


def cross(value, bits):
    return lax.ppermute(value, "chip", [(i, i ^ bits) for i in range(lax.axis_size("chip"))])


def cross_all(value):
    return [value] + [cross(value, bits) for bits in range(1, lax.axis_size("chip"))]


def heads_sum(piece):
    total, low = piece, piece.astype(BF16)
    bits, size = 1, lax.axis_size("head")
    while bits < size:
        arrived = lax.ppermute(low, "head", [(i, i ^ bits) for i in range(size)])
        total, low = run(
            heads_kernel, "heads", piece.size,
            [(WHOLE, piece), (WHOLE, total), (WHOLE, arrived)],
            [(WHOLE, piece.shape, F32), (WHOLE, piece.shape, BF16)],
        )
        bits *= 2
    return low


def entering(core, chip, total, backward, meanwhile, later=lambda pair: ()):
    name = "after" if backward else "before"
    chips = lax.axis_size("chip")
    channels = total.shape[1]
    half = NSTATE // 2
    partner = beside(total)
    pair = run(
        functools.partial(pair_kernel, backward), name + "_pair", total.size,
        [core, (WHOLE, total), (WHOLE, partner)] + [(LOOSE, value) for value in meanwhile],
        [(WHOLE, (half + 8, channels), F32)],
    )[0]
    prefix = run(
        functools.partial(prefix_kernel, backward, chips), name + "_prefix", chips * pair.size,
        [chip] + [(WHOLE, value) for value in cross_all(pair)]
        + [(LOOSE, value) for value in later(pair)],
        [(WHOLE, (half, channels), F32)],
    )[0]
    return run(
        functools.partial(enter_kernel, backward), name + "_enter", total.size,
        [core, (WHOLE, partner), (WHOLE, prefix), (WHOLE, beside(prefix))],
        [(WHOLE, (NSTATE, channels), F32)],
    )[0]


def sum_pieces(chip, kept, given, name, square, cut, paired, meanwhile=lambda mark: ()):
    chips, rows, channels = kept.shape
    arrived = beside(given)
    size = chips * rows * channels
    if paired:
        outs = [(WHOLE, (cut, channels), BF16), (WHOLE, (rows - cut, channels), F32)]
    else:
        outs = [(WHOLE, (rows, channels), BF16)]
    if chips != 4 or not square:
        halves = run(
            functools.partial(half_kernel, paired, chips), name + "_half", size,
            [chip, (WHOLE, kept), (WHOLE, arrived)],
            [(WHOLE, (rows, channels), F32)] + [(WHOLE, (rows, channels), BF16)] * (chips - 1),
        )
        parts = [halves[0]] + [cross(halves[bits], bits) for bits in range(1, chips)]
        found = run(
            functools.partial(piece_kernel, chips, paired, cut), name + "_piece", size,
            [(WHOLE, part) for part in parts] + [(LOOSE, mark) for mark in meanwhile(halves[0])],
            outs,
        )
        return found, halves[0], halves[0]
    rest = rows - cut
    first, first_give, last, last_give = run(
        square_half_kernel, name + "_half", size,
        [chip, (WHOLE, kept), (WHOLE, arrived)],
        [
            (WHOLE, (2, cut, channels), F32), (WHOLE, (2, cut, channels), BF16),
            (WHOLE, (2, rest, channels), F32), (WHOLE, (2, rest, channels), BF16),
        ],
    )
    half_mark = first
    first, first_give, last, last_give = run(
        square_next_kernel, name + "_next", size,
        [
            (WHOLE, first), (WHOLE, cross(first_give, 1)),
            (WHOLE, last), (WHOLE, cross(last_give, 2)),
        ],
        [
            (WHOLE, (cut, channels), F32), (WHOLE, (cut, channels), BF16),
            (WHOLE, (rest, channels), F32), (WHOLE, (rest, channels), BF16),
        ],
    )
    next_mark = first
    found = run(
        square_last_kernel, name + "_piece", size,
        [
            (WHOLE, first), (WHOLE, cross(first_give, 2)),
            (WHOLE, last), (WHOLE, cross(last_give, 1)),
        ] + [(LOOSE, mark) for mark in meanwhile(half_mark)],
        outs,
    )
    return found, half_mark, next_mark


def collect(piece, order, mark=None):
    chips = lax.axis_size("chip")
    if chips != 4 or order is None:
        found = [(value[None], (bits,)) for bits, value in enumerate(cross_all(piece))]
    else:
        near, far = order
        both = jnp.stack([piece, cross(piece, near)])
        if mark is not None:
            both = tie(both, mark)
        found = [(both, (0, near)), (cross(both, far), (far, far ^ near))]
    return [(value, beside(value), bits) for value, bits in found]


def dot(left, right):
    return jnp.dot(left, right, preferred_element_type=F32)


def dot_nt(left, right):
    return lax.dot_general(left, right, (((1,), (1,)), ((), ())), preferred_element_type=F32)


def dot_tn(left, right):
    return lax.dot_general(left, right, (((0,), (0,)), ((), ())), preferred_element_type=F32)


def split(values):
    high = values.astype(BF16)
    return high, (values - high.astype(F32)).astype(BF16)


def lower_mask():
    row = lax.broadcasted_iota(jnp.int32, (CHUNK, CHUNK), 0)
    column = lax.broadcasted_iota(jnp.int32, (CHUNK, CHUNK), 1)
    return row >= column


def spread_heads(heads, channels):
    row = lax.broadcasted_iota(jnp.int32, (heads, channels), 0) * HEAD_DIM
    place = lax.broadcasted_iota(jnp.int32, (heads, channels), 1)
    return jnp.where((place >= row) & (place < row + HEAD_DIM), 1.0, 0.0).astype(BF16)


def expand(values, channels):
    high, low = split(values)
    spread = spread_heads(values.shape[1], channels)
    return dot(high, spread) + dot(low, spread)


def decay_kernel(codes_ref, weight_ref, e_ref, f_ref, k_ref):
    heads, channels = codes_ref.shape[1], k_ref.shape[1]
    lower = jnp.where(lower_mask(), 1.0, 0.0).astype(F32)
    count = codes_ref.shape[0] // CHUNK
    line = lax.broadcasted_iota(jnp.int32, (8, heads), 0)
    marks = jnp.zeros((8, heads), F32)
    total = jnp.zeros((1, heads), F32)
    for chunk in range(count):
        rows = pl.ds(chunk * CHUNK, CHUNK)
        logs = codes_ref[rows, :].astype(F32) * (-DECAY_STEP)
        cumulative = jnp.dot(
            lower, logs, precision=lax.Precision.HIGHEST, preferred_element_type=F32
        )
        last = cumulative[CHUNK - 1 :]
        middle = 0.5 * last
        e_ref[rows, :] = jnp.exp(cumulative - middle)
        f_ref[rows, :] = weight_ref[rows, :] * jnp.exp(middle - cumulative)
        marks = jnp.where(line == chunk, jnp.exp(middle), marks)
        total = total + last
    marks = jnp.where(line == 7, total, marks)
    high, low = split(marks)
    lowest = (marks - high.astype(F32) - low.astype(F32)).astype(BF16)
    spread = spread_heads(heads, channels)
    factors = dot(high, spread) + dot(low, spread) + dot(lowest, spread)
    k_ref[...] = factors


def pair_kernel(backward, core_ref, own_ref, other_ref, *refs):
    out_ref = refs[-1]
    half = NSTATE // 2
    logs, other_logs = own_ref[NSTATE:, :], other_ref[NSTATE:, :]
    for core in range(2):

        @pl.when(core_ref[0] == core)
        def _():
            rows = slice(core * half, (core + 1) * half)
            if core == (0 if backward else 1):
                out_ref[:half, :] = jnp.exp(logs[0:1]) * other_ref[rows, :] + own_ref[rows, :]
            else:
                out_ref[:half, :] = jnp.exp(other_logs[0:1]) * own_ref[rows, :] + other_ref[rows, :]

    out_ref[half:, :] = logs + other_logs


def prefix_kernel(backward, chips, chip_ref, *refs):
    parts, out_ref = refs[:chips], refs[-1]
    half = out_ref.shape[0]
    mine = chip_ref[0]
    total = jnp.zeros(out_ref.shape, F32)
    for bits in range(1, chips):
        source = lax.bitwise_xor(mine, bits)
        span = jnp.zeros((1, out_ref.shape[1]), F32)
        for other in range(1, chips):
            middle = lax.bitwise_xor(mine, other)
            if backward:
                between = (middle < source) & (middle > mine)
            else:
                between = (middle > source) & (middle < mine)
            span = span + jnp.where(between, parts[other][half : half + 1, :], 0.0)
        passes = source > mine if backward else source < mine
        total = total + jnp.where(passes, jnp.exp(span), 0.0) * parts[bits][:half, :]
    out_ref[...] = total


def enter_kernel(backward, core_ref, partner_ref, prefix_ref, other_ref, out_ref):
    half = prefix_ref.shape[0]
    decay = jnp.exp(partner_ref[NSTATE : NSTATE + 1, :])
    for core in range(2):

        @pl.when(core_ref[0] == core)
        def _():
            for place, ref in ((core, prefix_ref), (1 - core, other_ref)):
                rows = slice(place * half, (place + 1) * half)
                if core == (0 if backward else 1):
                    out_ref[rows, :] = decay * ref[...] + partner_ref[rows, :]
                else:
                    out_ref[rows, :] = ref[...]


def taps(window, kernel, bias, begin):
    summed = bias
    for offset in range(KERNEL):
        summed = summed + kernel[offset : offset + 1] * window[begin + offset : begin + offset + CHUNK]
    return summed


def silu_parts(values):
    sigmoid = jax.nn.sigmoid(values)
    return values * sigmoid, sigmoid * (1.0 + values * (1.0 - sigmoid))


def first_step(action):
    pl.when(pl.program_id(0) == 0)(action)


def clear(*refs):
    def action():
        for ref in refs:
            ref[...] = jnp.zeros_like(ref)

    first_step(action)


def place_parts(mine, parts, target, width, value):
    size = len(parts)
    if width % 128 == 0:
        for i in range(size):
            owner = lax.rem(mine + size - i, size)
            target[:, pl.ds(pl.multiple_of(owner * width, 128), width)] = value(i)
        return

    def write(me):
        for i in range(size):
            owner = (me + size - i) % size
            target[:, owner * width : (owner + 1) * width] = value(i)

    for me in range(size):
        pl.when(mine == me)(functools.partial(write, me))


def copies_kernel(loose_ref, own_ref, out_ref):
    for i in range(out_ref.shape[0]):
        out_ref[i] = own_ref[...]


def norm_kernel(size, loose_ref, head_ref, passed_ref, *refs):
    parts, gains = refs[:size], refs[size : 2 * size]
    passed_gain_ref, normed_ref, scale_ref, gain_ref = refs[2 * size :]
    width = parts[0].shape[1]
    mine = head_ref[0]

    def pick(i, refs, passed):
        if size == 4 and i == 1:
            return jnp.where(mine == 0, passed[...], refs[i][...])
        if size == 4 and i == 3:
            return jnp.where(mine == 3, passed[...], refs[i][...])
        return refs[i][...]

    part = lambda i: pick(i, parts, passed_ref).astype(F32)
    gain = lambda i: pick(i, gains, passed_gain_ref)[0:1].astype(F32)
    squares = sum(jnp.sum(part(i) ** 2, axis=1, keepdims=True) for i in range(size))
    scale = lax.rsqrt(squares / (size * width) + EPSILON)
    scale_ref[...] = jnp.broadcast_to(scale, scale_ref.shape)
    place_parts(
        mine, parts, normed_ref, width,
        lambda i: (part(i) * scale_ref[:, 0:1] * gain(i)).astype(BF16),
    )
    place_parts(mine, parts, gain_ref, width, lambda i: jnp.broadcast_to(gain(i), (8, width)))


def mixed_grad_kernel(parts_ref, weight_ref, out_ref, full_ref):
    size, _, width = parts_ref.shape
    for i in range(size):
        full_ref[:, i * width : (i + 1) * width] = parts_ref[i]
    out_ref[...] = dot_nt(full_ref[...], weight_ref[...])


def out_kernel(loose_ref, mixed_ref, weight_ref, out_ref):
    width = out_ref.shape[2]
    for owner in range(out_ref.shape[0]):
        value = dot(mixed_ref[...], weight_ref[:, owner * width : (owner + 1) * width])
        out_ref[owner] = value.astype(BF16)


def conv_kernel(
    value_ref, state_ref, value_kernel_ref, value_bias_ref, state_kernel_ref, state_bias_ref,
    f_ref, k_ref, conv_ref, weighted_ref, value_slope_ref, maps_ref, state_slope_ref, total_ref,
):
    chunk = pl.program_id(0)
    clear(total_ref)
    around = pl.ds(pl.multiple_of(chunk * CHUNK, CHUNK), CHUNK + HALO)
    pre = taps(
        state_ref[around, :].astype(F32), state_kernel_ref[...].astype(F32),
        state_bias_ref[...].astype(F32), HALO - KERNEL + 1,
    )
    conv, slope = silu_parts(pre)
    maps = conv.astype(BF16)
    maps_ref[...] = maps
    state_slope_ref[...] = slope
    pre = taps(
        value_ref[around, :].astype(F32), value_kernel_ref[...].astype(F32),
        value_bias_ref[...].astype(F32), HALO - KERNEL + 1,
    )
    conv, slope = silu_parts(pre)
    conv = conv.astype(BF16)
    conv_ref[...] = conv
    value_slope_ref[...] = slope
    weighted = (conv.astype(F32) * expand(f_ref[...], conv.shape[1])).astype(BF16)
    weighted_ref[...] = weighted
    factor = k_ref[pl.ds(chunk, 1), :]
    total_ref[:NSTATE, :] = factor * (
        factor * total_ref[:NSTATE, :] + dot_tn(maps[:, :NSTATE], weighted)
    )
    total_ref[NSTATE:, :] = jnp.broadcast_to(k_ref[7:8, :], (8, k_ref.shape[1]))


def mixer_kernel(
    state_in_ref, maps_ref, weighted_ref, conv_ref, e_ref, k_ref, skip_ref, gate_ref, grad_ref, gain_ref,
    mixer_ref, stats_ref, high_ref, low_ref, state_ref,
):
    chunk = pl.program_id(0)

    def start():
        state_ref[...] = state_in_ref[...]

    first_step(start)
    lane = lax.broadcasted_iota(jnp.int32, (CHUNK, CHUNK), 1)
    factor = k_ref[pl.ds(chunk, 1), :]
    input_map, output_map = maps_ref[:, :NSTATE], maps_ref[:, NSTATE:]
    weighted = weighted_ref[...]
    scaled = factor * state_ref[...]
    high, low = split(scaled)
    high_ref[0], low_ref[0] = high, low
    scores = jnp.where(lower_mask(), dot_nt(output_map, input_map), 0.0).astype(BF16)
    mixed = dot(
        jnp.concatenate([scores, output_map], axis=1), jnp.concatenate([weighted, high], axis=0)
    )
    mixed = mixed + dot(output_map, low)
    mixer = expand(e_ref[...], weighted.shape[1]) * mixed + skip_ref[...] * conv_ref[...].astype(F32)
    mixer_ref[...] = mixer
    gate = gate_ref[...]
    gated = mixer * (gate * jax.nn.sigmoid(gate))
    squares = jnp.sum(gated * gated, axis=1, keepdims=True)
    products = jnp.sum(gated * (grad_ref[...] * gain_ref[...].astype(F32)), axis=1, keepdims=True)
    sums = jnp.where(lane == 0, squares, jnp.where(lane == 1, products, 0.0))
    stats_ref[...] = sums.T[:8]
    state_ref[...] = factor * (scaled + dot_tn(input_map, weighted))


def column(row_block):
    rest = jnp.zeros((CHUNK - row_block.shape[0], CHUNK), F32)
    return jnp.concatenate([row_block, rest], axis=0).T


def row_of(sums):
    lane = lax.broadcasted_iota(jnp.int32, (CHUNK, CHUNK), 1)
    return jnp.where(lane == 0, sums, 0.0).T[:8]


def gate_kernel(
    inner, chunks, size, *refs
):
    stats_refs = refs[:size]
    (
        mixer_ref, gate_ref, grad_ref, gain_ref, conv_ref, e_ref, k_ref, maps_ref,
        mixed_ref, gate_grad_ref, mixer_grad_ref, small_ref, total_ref, cross_ref,
    ) = refs[size:]
    chunk = chunks - 1 - pl.program_id(0)
    clear(small_ref, total_ref)
    gain = gain_ref[...].astype(F32)
    stats = column(sum(ref[...] for ref in stats_refs))
    scale = lax.rsqrt(stats[:, 0:1] / inner + EPSILON)
    cross_term = stats[:, 1:2] * (scale * scale * scale) / inner
    gate = gate_ref[...]
    silu, slope = silu_parts(gate)
    mixer = mixer_ref[...]
    gated = mixer * silu
    normed = gated * scale
    mixed_ref[...] = (normed * gain).astype(BF16)
    grad = grad_ref[...]
    gated_grad = scale * (grad * gain) - gated * cross_term
    gate_grad = (gated_grad * mixer * slope).astype(BF16)
    gate_grad_ref[...] = gate_grad
    cross_ref[...] = row_of(jnp.sum(gate_grad.astype(F32) * gate, axis=1, keepdims=True))
    mixer_grad = gated_grad * silu
    mixer_grad_ref[...] = mixer_grad
    small_ref[0:1, :] += jnp.sum(grad * normed, axis=0, keepdims=True)
    small_ref[1:2, :] += jnp.sum(mixer_grad * conv_ref[...].astype(F32), axis=0, keepdims=True)
    high, low = split(expand(e_ref[...], grad.shape[1]) * mixer_grad)
    output_map = maps_ref[:, NSTATE:]
    factor = k_ref[pl.ds(chunk, 1), :]
    total_ref[:NSTATE, :] = factor * (
        factor * total_ref[:NSTATE, :] + (dot_tn(output_map, high) + dot_tn(output_map, low))
    )
    total_ref[NSTATE:, :] = jnp.broadcast_to(k_ref[7:8, :], (8, k_ref.shape[1]))


def back_kernel(
    chunks, early_ref, state_in_ref, mixer_grad_ref, e_ref, f_ref, k_ref, weighted_ref, high_ref, low_ref,
    maps_ref, value_slope_ref, state_slope_ref, skip_ref,
    value_ref, map_ref, state_ref,
):
    chunk = chunks - 1 - pl.program_id(0)

    def start():
        state_ref[...] = state_in_ref[...]

    first_step(start)
    lower = lower_mask()
    row = lax.broadcasted_iota(jnp.int32, (CHUNK, CHUNK), 0)
    upper = row <= lax.broadcasted_iota(jnp.int32, (CHUNK, CHUNK), 1)
    factor = k_ref[pl.ds(chunk, 1), :]
    input_map, output_map = maps_ref[:, :NSTATE], maps_ref[:, NSTATE:]
    weighted = weighted_ref[...]
    mixer_grad = mixer_grad_ref[...]
    high, low = split(expand(e_ref[...], weighted.shape[1]) * mixer_grad)
    scaled = factor * state_ref[...]
    state_high, state_low = split(scaled)
    both = jnp.concatenate([weighted, high_ref[0]], axis=0)
    sums = dot_nt(high, both) + dot_nt(low, both)
    score_grad = jnp.where(lower, sums[:, :CHUNK], 0.0).astype(BF16)
    output_grad = sums[:, CHUNK:] + dot_nt(high, low_ref[0]) + dot(score_grad, input_map)
    sums = dot_nt(weighted, jnp.concatenate([state_high, state_low], axis=0))
    input_grad = sums[:, :NSTATE] + sums[:, NSTATE:] + dot_tn(score_grad, output_map)
    scores = jnp.where(upper, dot_nt(input_map, output_map), 0.0).astype(BF16)
    grads = dot(
        jnp.concatenate([scores, input_map], axis=1), jnp.concatenate([high, state_high], axis=0)
    )
    decayed = expand(f_ref[...], weighted.shape[1]) * grads
    value_ref[...] = (decayed + skip_ref[...] * mixer_grad) * value_slope_ref[...]
    slope = state_slope_ref[...]
    map_ref[:, :NSTATE] = input_grad * slope[:, :NSTATE]
    map_ref[:, NSTATE:] = output_grad * slope[:, NSTATE:]
    state_ref[...] = factor * (scaled + (dot_tn(output_map, high) + dot_tn(output_map, low)))


def conv_back_kernel(
    chunks, value_ref, map_ref, after_ref, value_raw_ref, state_raw_ref, value_kernel_ref,
    state_kernel_ref, cross_in_ref,
    value_grad_ref, state_grad_ref, value_small_ref, state_small_ref, cross_ref, value_next_ref,
    state_next_ref,
):
    chunk = chunks - 1 - pl.program_id(0)
    channels = value_ref.shape[1]
    clear(value_small_ref, state_small_ref)

    def start():
        value_next_ref[...] = after_ref[:, :channels]
        state_next_ref[...] = after_ref[:, channels:]

    first_step(start)

    def back(slope_ref, next_ref, raw_ref, kernel_ref, grad_ref, small_ref):
        kernel = kernel_ref[...].astype(F32)
        slope = slope_ref[...]
        window = jnp.concatenate([slope, next_ref[...]], axis=0)
        around = pl.ds(pl.multiple_of(chunk * CHUNK, CHUNK), CHUNK + HALO)
        raw = raw_ref[around, :].astype(F32)
        grad = jnp.zeros_like(slope)
        for offset in range(KERNEL):
            back_by = KERNEL - 1 - offset
            grad = grad + kernel[offset : offset + 1] * window[back_by : back_by + CHUNK]
            begin = HALO - KERNEL + 1 + offset
            small_ref[offset : offset + 1, :] += jnp.sum(
                slope * raw[begin : begin + CHUNK], axis=0, keepdims=True
            )
        small_ref[KERNEL : KERNEL + 1, :] += jnp.sum(slope, axis=0, keepdims=True)
        grad = grad.astype(BF16)
        grad_ref[...] = grad
        next_ref[...] = slope[:8]
        return jnp.sum(grad.astype(F32) * raw[HALO:], axis=1, keepdims=True)

    crossed = back(map_ref, state_next_ref, state_raw_ref, state_kernel_ref, state_grad_ref, state_small_ref)
    crossed = crossed + back(
        value_ref, value_next_ref, value_raw_ref, value_kernel_ref, value_grad_ref, value_small_ref
    )
    cross_ref[...] = cross_in_ref[...] + row_of(crossed)


def normed_kernel(
    chunks, late_ref, gate_grad_ref, value_grad_ref, state_grad_ref, gate_weight_ref, value_weight_ref,
    state_weight_ref, cross_ref, out_ref
):
    value = (
        dot_nt(gate_grad_ref[...], gate_weight_ref[...])
        + dot_nt(value_grad_ref[...], value_weight_ref[...])
        + dot_nt(state_grad_ref[...], state_weight_ref[...])
    )
    count = value.shape[0]
    out_ref[0, :count, :] = value.astype(BF16)
    line = lax.broadcasted_iota(jnp.int32, (HALO, CHUNK), 0)
    packed = jnp.zeros((HALO, CHUNK), F32)
    for chunk in range(chunks):
        row = cross_ref[0:1, chunk * CHUNK : (chunk + 1) * CHUNK]
        high = row.astype(BF16).astype(F32)
        packed = jnp.where(line == chunk, high, packed)
        packed = jnp.where(line == chunks + chunk, row - high, packed)
    out_ref[0, count:, :] = jnp.zeros((HALO, value.shape[1]), BF16)
    out_ref[0, count:, :CHUNK] = packed.astype(BF16)


def last_kernel(full_width, parts_ref, tokens_ref, scale_ref, gain_ref, cotangent_ref, out_ref):
    count = tokens_ref.shape[0]
    chunks = count // CHUNK
    size = parts_ref.shape[0]
    crossed = sum(parts_ref[i, count:, :CHUNK].astype(F32) for i in range(size))
    crossed = crossed[:chunks] + crossed[chunks : 2 * chunks]
    for chunk in range(chunks):
        rows = slice(chunk * CHUNK, (chunk + 1) * CHUNK)
        normed_grad = sum(parts_ref[i, rows, :].astype(F32) for i in range(size))
        scale = scale_ref[HALO + chunk * CHUNK : HALO + (chunk + 1) * CHUNK, 0:1]
        total = column(jnp.broadcast_to(crossed[chunk : chunk + 1], (8, CHUNK)))[:, 0:1]
        out_ref[rows, :] = (
            scale * gain_ref[...].astype(F32) * normed_grad
            - tokens_ref[rows, :].astype(F32) * (scale * scale * total / full_width)
            + cotangent_ref[rows, :].astype(F32)
        ).astype(BF16)


def store_piece(core_ref, kept_ref, given_ref, place, begin, piece):
    chips = kept_ref.shape[0]
    core, chip = place // chips, lax.rem(place, chips)
    rows = slice(begin, begin + piece.shape[0])
    piece = piece.astype(BF16)

    @pl.when(core_ref[0] == core)
    def _():
        kept_ref[chip, rows, :] = piece

    @pl.when(core_ref[0] != core)
    def _():
        given_ref[chip, rows, :] = piece


def gain_row(weight, block):
    sums = jnp.sum(weight.astype(F32) * block, axis=1, keepdims=True)
    lane = lax.broadcasted_iota(jnp.int32, (CHUNK, CHUNK), 1)
    rows = [
        jnp.where(lane == 0, sums[i : i + CHUNK], 0.0).T[0:1] for i in range(0, BLOCK, CHUNK)
    ]
    return jnp.concatenate(rows, axis=1)


def early_kernel(
    loose_ref, core_ref, normed_ref, gate_ref, mixed_ref, grad_ref, weight_ref,
    kept_ref, given_ref, gain_ref, held_ref
):
    chips, rows, channels = kept_ref.shape
    at = pl.program_id(0)
    count, width = grad_ref.shape
    pieces = 2 * chips
    step = width // pieces
    out_rows = channels // pieces
    out_blocks = channels // BLOCK
    every = width // BLOCK // out_blocks

    @pl.when(lax.rem(at, every) == 0)
    def _():
        held_ref[...] = dot_tn(mixed_ref[...], grad_ref[...])

    block = dot_tn(normed_ref[HALO : HALO + count, :], gate_ref[...])
    gain_ref[...] = gain_row(weight_ref[...], block)
    for i in range(BLOCK // step):
        place = at * (BLOCK // step) + i
        begin = lax.rem(at, every) * (BLOCK // step * out_rows) + i * out_rows
        own = held_ref[pl.ds(pl.multiple_of(begin, 8), out_rows), :]
        parts = [block[i * step : (i + 1) * step]]
        parts += [own[:, j : j + channels] for j in range(0, width, channels)]
        store_piece(core_ref, kept_ref, given_ref, place, 0, jnp.concatenate(parts, axis=0))


def late_kernel(
    early_ref, core_ref, normed_ref, value_ref, state_ref, value_small_ref, gate_small_ref, gain_ref,
    state_small_ref, value_weight_ref, state_weight_ref, gain_full_ref,
    kept_ref, given_ref, own_ref, shared_ref, gains_ref,
):
    chips, rows, channels = kept_ref.shape
    at = pl.program_id(0)
    count, maps_width = state_ref.shape
    width = gains_ref.shape[1]
    pieces = 2 * chips
    step = width // pieces
    lanes = channels // 128
    part = 2 * step // lanes
    columns = normed_ref[HALO : HALO + count, :]
    value = dot_tn(columns, value_ref[...])
    state = dot_tn(columns, state_ref[...])
    gain = (
        gain_ref[...] + gain_row(value_weight_ref[...], value) + gain_row(state_weight_ref[...], state)
    ) / gain_full_ref[0:1, :]
    gains_ref[0:1, pl.ds(pl.multiple_of(at * BLOCK, 128), BLOCK)] = gain
    for i in range(BLOCK // step):
        piece = slice(i * step, (i + 1) * step)
        stacked = jnp.concatenate([state[piece, :128], state[piece, 128:]], axis=0)
        stacked = jnp.concatenate(
            [stacked[j * part : (j + 1) * part] for j in range(lanes)], axis=1
        )
        store_piece(
            core_ref, kept_ref, given_ref, at * (BLOCK // step) + i, 0,
            jnp.concatenate([value[piece], stacked], axis=0),
        )

    @pl.when(at == width // BLOCK - 1)
    def _():
        own_ref[...] = jnp.zeros_like(own_ref)
        own_ref[: KERNEL + 1, :] = value_small_ref[: KERNEL + 1, :]
        own_ref[KERNEL + 1 : KERNEL + 3, :] = gate_small_ref[:2, :]
        shared_ref[...] = jnp.zeros_like(shared_ref)
        begin = width // channels
        for i in range(begin):
            shared_ref[i : i + 1, :] = gains_ref[0:1, i * channels : (i + 1) * channels]
        for i in range(0, (KERNEL + 1) * maps_width, 128):
            tap, column_from = divmod(i, maps_width)
            row, column_to = divmod(i, channels)
            shared_ref[begin + row : begin + row + 1, column_to : column_to + 128] = state_small_ref[
                tap : tap + 1, column_from : column_from + 128
            ]
        line = lax.broadcasted_iota(jnp.int32, (HALO, channels), 0)
        for place in range(pieces):
            own, shared = own_ref[place : place + 1, :], shared_ref[place : place + 1, :]
            own_high, shared_high = (v.astype(BF16).astype(F32) for v in (own, shared))
            small = jnp.zeros((HALO, channels), F32)
            for to, value in enumerate((own_high, own - own_high, shared_high, shared - shared_high)):
                small = jnp.where(line == to, value, small)
            store_piece(core_ref, kept_ref, given_ref, place, step + part, small)


def merge_pairs(block):
    tail = block[-HALO:]
    line = lax.broadcasted_iota(jnp.int32, tail.shape, 0)
    own, shared = tail[0:1] + tail[1:2], tail[2:3] + tail[3:4]
    own_high, shared_high = own.astype(BF16).astype(F32), shared.astype(BF16).astype(F32)
    new = jnp.zeros_like(tail)
    for at, value in enumerate((own_high, own - own_high, shared_high, shared - shared_high)):
        new = jnp.where(line == at, value, new)
    return jnp.concatenate([block[:-HALO], new], axis=0)


def heads_kernel(piece_ref, total_ref, arrived_ref, out_ref, low_ref):
    total = merge_pairs(total_ref[...] + arrived_ref[...].astype(F32))
    line = lax.broadcasted_iota(jnp.int32, total.shape, 0)
    first = total.shape[0] - HALO
    own = (line >= first) & (line < first + 2)
    out_ref[...] = total
    low_ref[...] = jnp.where(own, piece_ref[...], total).astype(BF16)


def half_kernel(paired, chips, chip_ref, kept_ref, arrived_ref, *outs):
    for bits in range(chips):
        place = lax.bitwise_xor(chip_ref[0], bits)
        value = kept_ref[place].astype(F32) + arrived_ref[place].astype(F32)
        if paired:
            value = merge_pairs(value)
        outs[bits][...] = value.astype(outs[bits].dtype)


def piece_kernel(parts, paired, cut, *refs):
    total = sum(ref[...].astype(F32) for ref in refs[:parts])
    if not paired:
        refs[-1][...] = total.astype(BF16)
        return
    first_ref, last_ref = refs[-2:]
    first_ref[...] = total[:cut].astype(BF16)
    last_ref[...] = merge_pairs(total[cut:])


def square_half_kernel(
    chip_ref, kept_ref, arrived_ref, first_ref, first_give_ref, last_ref, last_give_ref
):
    cut = first_ref.shape[1]
    for bits in range(4):
        place = lax.bitwise_xor(chip_ref[0], bits)
        value = kept_ref[place].astype(F32) + arrived_ref[place].astype(F32)
        low, high = bits & 1, bits >> 1
        ref = first_give_ref if low else first_ref
        ref[high] = value[:cut].astype(ref.dtype)
        ref = last_give_ref if high else last_ref
        ref[low] = value[cut:].astype(ref.dtype)


def square_next_kernel(
    first_ref, first_got_ref, last_ref, last_got_ref,
    first_out_ref, first_give_ref, last_out_ref, last_give_ref,
):
    first_out_ref[...] = first_ref[0] + first_got_ref[0].astype(F32)
    first_give_ref[...] = (first_ref[1] + first_got_ref[1].astype(F32)).astype(BF16)
    last_out_ref[...] = last_ref[0] + last_got_ref[0].astype(F32)
    last_give_ref[...] = (last_ref[1] + last_got_ref[1].astype(F32)).astype(BF16)


def square_last_kernel(first_ref, first_got_ref, last_ref, last_got_ref, *refs):
    out_ref = refs[-1]
    cut = first_ref.shape[0]
    out_ref[:cut, :] = (first_ref[...] + first_got_ref[...].astype(F32)).astype(BF16)
    out_ref[cut:, :] = (last_ref[...] + last_got_ref[...].astype(F32)).astype(BF16)


def spread_pieces(core_ref, chip_ref, chips, groups, refs, store):
    step = pl.program_id(0)
    core, chip = step // chips, lax.rem(step, chips)
    apart = lax.bitwise_xor(chip, chip_ref[0])
    refs = iter(refs)
    for part, bits_lists in enumerate(groups):
        for bits_list in bits_lists:
            own_ref, other_ref = next(refs), next(refs)
            for at, bits in enumerate(bits_list):

                @pl.when((apart == bits) & (core == core_ref[0]))
                def _(part=part, ref=own_ref, at=at):
                    store(part, ref[at].astype(F32))

                @pl.when((apart == bits) & (core != core_ref[0]))
                def _(part=part, ref=other_ref, at=at):
                    store(part, ref[at].astype(F32))


def early_out_kernel(chips, groups, core_ref, chip_ref, *refs):
    gate_ref, output_ref = refs[-2:]
    step, channels = gate_ref.shape
    out_rows, width = output_ref.shape

    def store(part, value):
        gate_ref[...] = value[:step]
        output_ref[...] = jnp.concatenate(
            [value[step + i * out_rows : step + (i + 1) * out_rows] for i in range(width // channels)],
            axis=1,
        )

    spread_pieces(core_ref, chip_ref, chips, groups, refs[:-2], store)


def late_out_kernel(chips, groups, core_ref, chip_ref, *refs):
    value_ref = refs[-1]

    def store(part, value):
        value_ref[...] = value

    spread_pieces(core_ref, chip_ref, chips, groups, refs[:-1], store)


def shared_out_kernel(chips, groups, size, core_ref, chip_ref, head_ref, *refs):
    (
        state_ref, value_kernel_ref, value_bias_ref, state_kernel_ref, state_bias_ref, skip_ref,
        gated_ref, gain_ref, own_ref, shared_ref,
    ) = refs[-10:]
    step, maps_width = state_ref.shape
    channels = own_ref.shape[1]
    lanes = channels // 128
    rows = 2 * step // lanes
    at = pl.program_id(0)

    def store(part, piece):
        stacked = jnp.concatenate(
            [piece[:rows, i * 128 : (i + 1) * 128] for i in range(lanes)], axis=0
        )
        state_ref[...] = jnp.concatenate([stacked[:step], stacked[step:]], axis=1)
        own_ref[pl.ds(at, 1), :] = piece[rows : rows + 1] + piece[rows + 1 : rows + 2]
        shared_ref[pl.ds(at, 1), :] = piece[rows + 2 : rows + 3] + piece[rows + 3 : rows + 4]

    spread_pieces(core_ref, chip_ref, chips, groups, refs[:-10], store)

    @pl.when(at == 2 * chips - 1)
    def _():
        value_kernel_ref[...] = own_ref[:KERNEL, :]
        value_bias_ref[...] = own_ref[KERNEL, :]
        gated_ref[...] = own_ref[KERNEL + 1, :]
        heads = skip_ref.shape[0]
        place = lax.broadcasted_iota(jnp.int32, (heads, channels), 1)
        row = lax.broadcasted_iota(jnp.int32, (heads, channels), 0) * HEAD_DIM
        inside = (place >= row) & (place < row + HEAD_DIM)
        skip_ref[...] = jnp.sum(jnp.where(inside, own_ref[KERNEL + 2 : KERNEL + 3, :], 0.0), axis=1)
        own_width = gain_ref.shape[0]
        gain_rows = -(-own_width * size // channels)
        for head in range(size):
            row, begin = divmod(head * own_width, channels)

            @pl.when(head_ref[0] == head)
            def _():
                gain_ref[...] = shared_ref[row, begin : begin + own_width]
        for i in range(0, (KERNEL + 1) * maps_width, 128):
            tap, column_to = divmod(i, maps_width)
            row, column_from = divmod(i, channels)
            value = shared_ref[gain_rows + row : gain_rows + row + 1, column_from : column_from + 128]
            if tap < KERNEL:
                state_kernel_ref[tap : tap + 1, column_to : column_to + 128] = value
            else:
                state_bias_ref[column_to : column_to + 128] = value[0]


SCALAR = "scalar"
WHOLE = "whole"
BLOCKED = "blocked"
LANES = "lanes"
LEADING = "leading"
LOOSE = "loose"


def run(kernel, name, flops, args, outs, steps=None, backward=False, scratch=()):
    at = (lambda i: steps - 1 - i) if backward else (lambda i: i)

    def spec(kind, shape):
        if isinstance(kind, int):
            return pl.BlockSpec((kind,) + shape[1:], lambda i: (at(i), 0))
        if kind == SCALAR:
            return pl.BlockSpec(memory_space=pltpu.SMEM)
        if kind == LOOSE:
            return pl.BlockSpec(memory_space=pl.ANY)
        if isinstance(kind, tuple):
            return pl.BlockSpec(*kind)
        if steps is None:
            return pl.BlockSpec(memory_space=pltpu.VMEM)
        if kind == BLOCKED:
            return pl.BlockSpec((CHUNK, shape[1]), lambda i: (at(i), 0))
        if kind == LANES:
            return pl.BlockSpec((shape[0], CHUNK), lambda i: (0, at(i)))
        if kind == LEADING:
            return pl.BlockSpec((1,) + shape[1:], lambda i: (at(i),) + (0,) * (len(shape) - 1))
        return pl.BlockSpec(shape, lambda i: (0,) * len(shape))

    moved = sum(a.size * a.dtype.itemsize for kind, a in args if kind != LOOSE)
    shapes = [jax.ShapeDtypeStruct(shape, dtype) for _, shape, dtype in outs]
    moved += sum(a.size * a.dtype.itemsize for a in shapes)
    return pl.pallas_call(
        kernel,
        out_shape=shapes,
        in_specs=[spec(kind, a.shape) for kind, a in args],
        out_specs=[spec(kind, shape) for kind, shape, _ in outs],
        scratch_shapes=list(scratch),
        compiler_params=pltpu.CompilerParams(vmem_limit_bytes=VMEM_LIMIT),
        cost_estimate=pl.CostEstimate(flops=flops, bytes_accessed=moved, transcendentals=0),
        name=name,
        **({} if steps is None else {"grid": (steps,)}),
    )(*(a for _, a in args))


def per_device(
    tokens, decay_codes, norm_gain, gate_weight, value_weight, state_weight, value_kernel, value_bias,
    state_kernel, state_bias, skip_scale, gated_gain, output_weight, cotangent,
):
    tokens, decay_codes, cotangent = tokens[0], decay_codes[0], cotangent[0]
    count, own_width = tokens.shape
    heads = skip_scale.shape[0]
    channels = heads * HEAD_DIM
    head_size, chips = lax.axis_size("head"), lax.axis_size("chip")
    seq_size = 2 * chips
    width = own_width * head_size
    maps_width = 2 * NSTATE
    chunks = count // CHUNK
    core = (SCALAR, lax.axis_index("core").astype(jnp.int32)[None])
    chip = (SCALAR, lax.axis_index("chip").astype(jnp.int32)[None])
    head = (SCALAR, lax.axis_index("head").astype(jnp.int32)[None])

    rows = count + MARGIN
    packed = jnp.concatenate(
        [
            from_behind(tokens[-HALO:], 1),
            tokens,
            jnp.broadcast_to(norm_gain[None], (MARGIN - HALO, own_width)),
        ],
        axis=0,
    )
    logs = decay_codes.astype(F32) * (-DECAY_STEP)
    input_weight = jnp.sqrt(-jnp.expm1(2.0 * logs))
    e_full, f_full, factors = run(
        decay_kernel, "decays", count * channels * 200,
        [(WHOLE, decay_codes), (WHOLE, input_weight)],
        [
            (WHOLE, (count, heads), F32),
            (WHOLE, (count, heads), F32),
            (WHOLE, (8, channels), F32),
        ],
    )
    parts, passed, mark = line_parts(packed, "head")
    skip_full = jnp.repeat(skip_scale, HEAD_DIM)[None]

    half = rows // 2
    gain_rows = ((MARGIN - HALO, own_width), lambda i: ((HALO + count) // (MARGIN - HALO), 0))
    copies = run(
        copies_kernel, "copies", 1, [(LOOSE, mark), (WHOLE, cotangent)],
        [(WHOLE, (head_size, count, own_width), BF16)],
    )[0]
    cotangent_parts = deal(copies, "head")
    normed, scale_in, gain_full = run(
        functools.partial(norm_kernel, head_size), "norm", count * width * 10,
        [(LOOSE, copies), head, (half, passed)] + [(half, part) for part in parts]
        + [(gain_rows, part) for part in parts] + [(gain_rows, passed)],
        [(half, (rows, width), BF16), (half, (rows, 128), F32), (WHOLE, (8, width), F32)],
        steps=2,
    )
    value_raw = dot(normed, value_weight).astype(BF16)
    state_raw = dot(normed, state_weight).astype(BF16)
    conv, weighted, value_slope, maps, map_slope, local_end = run(
        conv_kernel, "conv", count * channels * 400,
        [
            (WHOLE, value_raw), (WHOLE, state_raw), (WHOLE, value_kernel), (WHOLE, value_bias[None]),
            (WHOLE, state_kernel), (WHOLE, state_bias[None]), (BLOCKED, f_full), (WHOLE, factors),
        ],
        [
            (BLOCKED, (count, channels), BF16),
            (BLOCKED, (count, channels), BF16),
            (BLOCKED, (count, channels), F32),
            (BLOCKED, (count, maps_width), BF16),
            (BLOCKED, (count, maps_width), F32),
            (WHOLE, (NSTATE + 8, channels), F32),
        ],
        steps=chunks,
    )
    gate_pre = dot(normed, gate_weight)[HALO : HALO + count]
    state_in = entering(core, chip, local_end, False, (gate_pre,))
    mixed_grad, full_cotangent = run(
        mixed_grad_kernel, "mixed_grad", 2 * count * width * channels,
        [(WHOLE, cotangent_parts), (WHOLE, output_weight)],
        [(WHOLE, (count, channels), F32), (WHOLE, (count, width), BF16)],
    )
    mixer, stats, high, low = run(
        mixer_kernel, "mixer", count * channels * 1000,
        [
            (WHOLE, state_in), (BLOCKED, maps), (BLOCKED, weighted), (BLOCKED, conv),
            (BLOCKED, e_full), (WHOLE, factors), (WHOLE, skip_full), (BLOCKED, gate_pre),
            (BLOCKED, mixed_grad), (WHOLE, gated_gain[None]),
        ],
        [
            (BLOCKED, (count, channels), F32),
            (LANES, (8, count), F32),
            (LEADING, (chunks, NSTATE, channels), BF16),
            (LEADING, (chunks, NSTATE, channels), BF16),
        ],
        steps=chunks,
        scratch=[pltpu.VMEM((NSTATE, channels), F32)],
    )
    mixed, gate_grad, mixer_grad, gate_small, start_grad, gate_cross = run(
        functools.partial(gate_kernel, float(channels * head_size), chunks, head_size),
        "gate", count * channels * 600,
        [(LANES, part) for part in turn_all(stats, "head")]
        + [
            (BLOCKED, mixer), (BLOCKED, gate_pre), (BLOCKED, mixed_grad), (WHOLE, gated_gain[None]),
            (BLOCKED, conv), (BLOCKED, e_full), (WHOLE, factors), (BLOCKED, maps),
        ],
        [
            (BLOCKED, (count, channels), BF16),
            (BLOCKED, (count, channels), BF16),
            (BLOCKED, (count, channels), F32),
            (WHOLE, (8, channels), F32),
            (WHOLE, (NSTATE + 8, channels), F32),
            (LANES, (8, count), F32),
        ],
        steps=chunks,
        backward=True,
    )
    step, out_rows = width // seq_size, channels // seq_size
    early_rows = step + out_rows * (width // channels)
    features = width // BLOCK
    feature_block = ((rows, BLOCK), lambda i: (0, i))
    every = features // (channels // BLOCK)
    out_parts = run(
        out_kernel, "out", 2 * count * channels * width,
        [(LOOSE, start_grad), (WHOLE, mixed), (WHOLE, output_weight)],
        [(WHOLE, (head_size, count, own_width), BF16)],
    )[0]
    early_made = []

    def make_early(pair):
        early_made.extend(
            run(
                early_kernel, "early", 4 * count * channels * width,
                [
                    (LOOSE, pair), core, (feature_block, normed), (WHOLE, gate_grad),
                    (((count, BLOCK), lambda i: (0, i // every)), mixed), (WHOLE, full_cotangent),
                    (BLOCK, gate_weight),
                ],
                [(WHOLE, (chips, early_rows, channels), BF16)] * 2
                + [(((1, BLOCK), lambda i: (0, i)), (1, width), F32)],
                steps=features,
                scratch=[pltpu.VMEM((BLOCK, width), F32)],
            )
        )
        return early_made[1:2]

    grad_after = entering(core, chip, start_grad, True, (out_parts,), make_early)
    early_kept, early_given, early_gain = early_made
    early_found, half_mark, next_mark = sum_pieces(
        chip, early_kept, early_given, "early", True, step, False
    )
    early_piece = early_found[0]
    branch = jnp.sum(deal(out_parts, "head").astype(F32), axis=0)
    block_out = (tokens.astype(F32) + branch).astype(BF16)

    value_grads, map_grads = run(
        functools.partial(back_kernel, chunks), "back", count * channels * 2000,
        [
            (LOOSE, half_mark), (WHOLE, grad_after), (BLOCKED, mixer_grad), (BLOCKED, e_full),
            (BLOCKED, f_full), (WHOLE, factors), (BLOCKED, weighted), (LEADING, high),
            (LEADING, low), (BLOCKED, maps), (BLOCKED, value_slope), (BLOCKED, map_slope),
            (WHOLE, skip_full),
        ],
        [(BLOCKED, (count, channels), F32), (BLOCKED, (count, maps_width), F32)],
        steps=chunks,
        backward=True,
        scratch=[pltpu.VMEM((NSTATE, channels), F32)],
    )
    after = from_behind(jnp.concatenate([value_grads[:8], map_grads[:8]], axis=1), -1)
    value_raw_grad, state_raw_grad, value_small, state_small, crossed = run(
        functools.partial(conv_back_kernel, chunks), "conv_back", count * channels * 100,
        [
            (BLOCKED, value_grads), (BLOCKED, map_grads), (WHOLE, after),
            (WHOLE, value_raw), (WHOLE, state_raw), (WHOLE, value_kernel), (WHOLE, state_kernel),
            (LANES, gate_cross),
        ],
        [
            (BLOCKED, (count, channels), BF16),
            (BLOCKED, (count, maps_width), BF16),
            (WHOLE, (8, channels), F32),
            (WHOLE, (8, maps_width), F32),
            (LANES, (8, count), F32),
        ],
        steps=chunks,
        backward=True,
        scratch=[pltpu.VMEM((8, channels), F32), pltpu.VMEM((8, maps_width), F32)],
    )
    lanes = channels // 128
    state_rows = 2 * step // lanes
    late_rows = step + state_rows + HALO
    late_kept, late_given = run(
        late_kernel, "late", 3 * count * channels * width,
        [
            (LOOSE, next_mark), core, (feature_block, normed), (WHOLE, value_raw_grad),
            (WHOLE, state_raw_grad),
            (WHOLE, value_small), (WHOLE, gate_small), (((1, BLOCK), lambda i: (0, i)), early_gain),
            (WHOLE, state_small), (BLOCK, value_weight), (BLOCK, state_weight),
            (((8, BLOCK), lambda i: (0, i)), gain_full),
        ],
        [(WHOLE, (chips, late_rows, channels), BF16)] * 2,
        steps=features,
        scratch=[
            pltpu.VMEM((HALO, channels), F32),
            pltpu.VMEM((HALO, channels), F32),
            pltpu.VMEM((8, width), F32),
        ],
    )
    made = []

    def make_normed(mark):
        made.extend(
            run(
                functools.partial(normed_kernel, chunks), "normed", 4 * count * channels * width,
                [
                    (LOOSE, mark), (WHOLE, gate_grad), (WHOLE, value_raw_grad),
                    (WHOLE, state_raw_grad), (own_width, gate_weight), (own_width, value_weight),
                    (own_width, state_weight), (WHOLE, crossed),
                ],
                [(LEADING, (head_size, count + HALO, own_width), BF16)],
                steps=head_size,
            )
        )
        return made

    (late_piece, shared_piece), late_mark, _ = sum_pieces(
        chip, late_kept, late_given, "late", False, step, True, make_normed
    )
    normed_parts = made[0]
    normed_parts = deal(normed_parts, "head")
    shared_piece = heads_sum(shared_piece)

    def unpack(kernel, name, pieces, outs, flops, extra=(), scratch=()):
        groups = [collect(*piece) for piece in pieces]
        bits = [[found[2] for found in group] for group in groups]
        arrays = [(WHOLE, value) for group in groups for found in group for value in found[:2]]
        scalars = [core, chip] + ([head] if extra else [])
        return run(
            functools.partial(kernel, chips, bits, *extra), name, flops, scalars + arrays, outs,
            steps=seq_size, scratch=scratch,
        )

    gate_weight_gradient, output_weight_gradient = unpack(
        early_out_kernel, "early_out", [(early_piece, (2, 1), late_mark)],
        [(step, (width, channels), F32), (out_rows, (channels, width), F32)], 4 * channels * width,
    )
    value_weight_gradient = unpack(
        late_out_kernel, "late_out", [(late_piece, None)],
        [(step, (width, channels), F32)], 2 * channels * width,
    )[0]
    (
        state_weight_gradient, value_kernel_gradient, value_bias_gradient, state_kernel_gradient,
        state_bias_gradient, skip_scale_gradient, gated_gain_gradient, norm_gain_gradient,
    ) = unpack(
        shared_out_kernel, "shared_out", [(shared_piece, (2, 1))],
        [
            (step, (width, maps_width), F32),
            (WHOLE, (KERNEL, channels), F32),
            (WHOLE, (channels,), F32),
            (WHOLE, (KERNEL, maps_width), F32),
            (WHOLE, (maps_width,), F32),
            (WHOLE, (heads,), F32),
            (WHOLE, (channels,), F32),
            (WHOLE, (own_width,), F32),
        ],
        2 * maps_width * width,
        extra=(head_size,),
        scratch=[pltpu.VMEM((HALO, channels), F32), pltpu.VMEM((HALO, channels), F32)],
    )
    tokens_gradient = run(
        functools.partial(last_kernel, float(width)), "last", count * own_width * 20,
        [
            (WHOLE, normed_parts), (WHOLE, tokens), (WHOLE, scale_in),
            (WHOLE, norm_gain[None]), (WHOLE, cotangent),
        ],
        [(WHOLE, (count, own_width), BF16)],
    )[0]
    return (
        block_out[None],
        tokens_gradient[None],
        norm_gain_gradient,
        gate_weight_gradient,
        value_weight_gradient,
        state_weight_gradient,
        value_kernel_gradient,
        value_bias_gradient,
        state_kernel_gradient,
        state_bias_gradient,
        skip_scale_gradient,
        gated_gain_gradient,
        output_weight_gradient,
    )


def solution(mesh):
    seq_size, head_size = mesh.shape["seq"], mesh.shape["head"]
    mesh = Mesh(mesh.devices.reshape(seq_size // 2, 2, head_size), ("chip", "core", "head"))
    seq = ("chip", "core")
    in_specs = (
        P(None, seq, "head"),
        P(None, seq, "head"),
        P("head"),
        P(None, "head"),
        P(None, "head"),
        P(),
        P(None, "head"),
        P("head"),
        P(),
        P(),
        P("head"),
        P("head"),
        P("head", None),
        P(None, seq, "head"),
    )
    out_specs = (
        P(None, seq, "head"),
        P(None, seq, "head"),
        P("head"),
        P(None, "head"),
        P(None, "head"),
        P(),
        P(None, "head"),
        P("head"),
        P(),
        P(),
        P("head"),
        P("head"),
        P("head", None),
    )
    return jax.shard_map(
        per_device, mesh=mesh, in_specs=in_specs, out_specs=out_specs, check_vma=False
    )
```

```python
import functools

import jax
import jax.numpy as jnp
from jax import lax
from jax.experimental import pallas as pl
from jax.experimental.pallas import tpu as pltpu
from jax.sharding import Mesh
from jax.sharding import PartitionSpec as P

HEAD_DIM = 64
NSTATE = 128
KERNEL = 4
CHUNK = 128
BLOCK = 384
VMEM_LIMIT = 20 * 1024 * 1024
MARGIN = 32
HALO = 16


DECAY_STEP = 1.0 / 1048576.0
EPSILON = 1e-05
BF16 = jnp.bfloat16
F32 = jnp.float32


def tie_kernel(*refs):
    del refs


def tie(value, *others):
    return pl.pallas_call(
        tie_kernel,
        out_shape=jax.ShapeDtypeStruct(value.shape, value.dtype),
        in_specs=[pl.BlockSpec(memory_space=pl.ANY)] * (1 + len(others)),
        out_specs=pl.BlockSpec(memory_space=pl.ANY),
        input_output_aliases={0: 0},
        name="tie",
    )(value, *others)


def from_behind(value, by):
    axis = ("chip", "core")
    size = lax.axis_size("chip") * 2
    pairs = [(i, i + by) for i in range(size) if 0 <= i + by < size]
    return lax.ppermute(value, axis, pairs)


def beside(value):
    return lax.ppermute(value, "core", [(0, 1), (1, 0)])


def turn(value, axis, by):
    size = lax.axis_size(axis)
    return lax.ppermute(value, axis, [(i, (i + by) % size) for i in range(size)])


def turn_all(value, axis):
    return [value] + [turn(value, axis, by) for by in range(1, lax.axis_size(axis))]


def line_parts(value, axis):
    if lax.axis_size(axis) != 4:
        parts = turn_all(value, axis)
        return parts, value
    two = turn(value, axis, 2)
    one = lax.ppermute(value, axis, [(0, 1), (1, 2), (2, 3)])
    three = lax.ppermute(value, axis, [(1, 0), (2, 1), (3, 2)])
    passed = lax.ppermute(two, axis, [(2, 3), (1, 0)])
    return [value, one, two, three], passed


def deal(parts, axis):
    return lax.all_to_all(parts, axis, 0, 0)


def cross(value, bits):
    return lax.ppermute(value, "chip", [(i, i ^ bits) for i in range(lax.axis_size("chip"))])


def cross_all(value):
    return [value] + [cross(value, bits) for bits in range(1, lax.axis_size("chip"))]


def heads_sum(piece):
    total, low = piece, piece.astype(BF16)
    bits, size = 1, lax.axis_size("head")
    while bits < size:
        arrived = lax.ppermute(low, "head", [(i, i ^ bits) for i in range(size)])
        total, low = run(
            heads_kernel, "heads", piece.size,
            [(WHOLE, piece), (WHOLE, total), (WHOLE, arrived)],
            [(WHOLE, piece.shape, F32), (WHOLE, piece.shape, BF16)],
        )
        bits *= 2
    return low


def entering(core, chip, total, backward, meanwhile, later=lambda pair: ()):
    name = "after" if backward else "before"
    chips = lax.axis_size("chip")
    channels = total.shape[1]
    half = NSTATE // 2
    partner = beside(total)
    pair = run(
        functools.partial(pair_kernel, backward), name + "_pair", total.size,
        [core, (WHOLE, total), (WHOLE, partner)] + [(LOOSE, value) for value in meanwhile],
        [(WHOLE, (half + 8, channels), F32)],
    )[0]
    prefix = run(
        functools.partial(prefix_kernel, backward, chips), name + "_prefix", chips * pair.size,
        [chip] + [(WHOLE, value) for value in cross_all(pair)]
        + [(LOOSE, value) for value in later(pair)],
        [(WHOLE, (half, channels), F32)],
    )[0]
    return run(
        functools.partial(enter_kernel, backward), name + "_enter", total.size,
        [core, (WHOLE, partner), (WHOLE, prefix), (WHOLE, beside(prefix))],
        [(WHOLE, (NSTATE, channels), F32)],
    )[0]


def sum_pieces(chip, kept, given, name, square, cut, paired, before_half=()):
    chips, rows, channels = kept.shape
    arrived = beside(given)
    size = chips * rows * channels
    if paired:
        outs = [(WHOLE, (cut, channels), BF16), (WHOLE, (rows - cut, channels), F32)]
    else:
        outs = [(WHOLE, (rows, channels), BF16)]
    if chips != 4 or not square:
        halves = run(
            functools.partial(half_kernel, paired, chips), name + "_half", size,
            [chip, (WHOLE, kept), (WHOLE, arrived)] + [(LOOSE, mark) for mark in before_half],
            [(WHOLE, (rows, channels), F32)] + [(WHOLE, (rows, channels), BF16)] * (chips - 1),
        )
        parts = [halves[0]] + [cross(halves[bits], bits) for bits in range(1, chips)]
        found = run(
            functools.partial(piece_kernel, chips, paired, cut), name + "_piece", size,
            [(WHOLE, part) for part in parts], outs,
        )
        return found, halves[0]
    rest = rows - cut
    first, first_give, last, last_give = run(
        square_half_kernel, name + "_half", size,
        [chip, (WHOLE, kept), (WHOLE, arrived)],
        [
            (WHOLE, (2, cut, channels), F32), (WHOLE, (2, cut, channels), BF16),
            (WHOLE, (2, rest, channels), F32), (WHOLE, (2, rest, channels), BF16),
        ],
    )
    half_mark = first
    first, first_give, last, last_give = run(
        square_next_kernel, name + "_next", size,
        [
            (WHOLE, first), (WHOLE, cross(first_give, 1)),
            (WHOLE, last), (WHOLE, cross(last_give, 2)),
        ],
        [
            (WHOLE, (cut, channels), F32), (WHOLE, (cut, channels), BF16),
            (WHOLE, (rest, channels), F32), (WHOLE, (rest, channels), BF16),
        ],
    )
    return (first, first_give, last, last_give), half_mark


def square_end(name, state, outs, size, mark):
    first, first_give, last, last_give = state
    return run(
        square_last_kernel, name + "_piece", size,
        [
            (WHOLE, first), (WHOLE, cross(first_give, 2)),
            (WHOLE, last), (WHOLE, cross(last_give, 1)), (LOOSE, mark),
        ],
        outs,
    )


def collect(piece, order, mark=None):
    chips = lax.axis_size("chip")
    if chips != 4 or order is None:
        found = [(value[None], (bits,)) for bits, value in enumerate(cross_all(piece))]
    else:
        near, far = order
        both = jnp.stack([piece, cross(piece, near)])
        if mark is not None:
            both = tie(both, mark)
        found = [(both, (0, near)), (cross(both, far), (far, far ^ near))]
    return [(value, beside(value), bits) for value, bits in found]


def dot(left, right):
    return jnp.dot(left, right, preferred_element_type=F32)


def dot_nt(left, right):
    return lax.dot_general(left, right, (((1,), (1,)), ((), ())), preferred_element_type=F32)


def dot_tn(left, right):
    return lax.dot_general(left, right, (((0,), (0,)), ((), ())), preferred_element_type=F32)


def split(values):
    high = values.astype(BF16)
    return high, (values - high.astype(F32)).astype(BF16)


def lower_mask():
    row = lax.broadcasted_iota(jnp.int32, (CHUNK, CHUNK), 0)
    column = lax.broadcasted_iota(jnp.int32, (CHUNK, CHUNK), 1)
    return row >= column


def spread_heads(heads, channels):
    row = lax.broadcasted_iota(jnp.int32, (heads, channels), 0) * HEAD_DIM
    place = lax.broadcasted_iota(jnp.int32, (heads, channels), 1)
    return jnp.where((place >= row) & (place < row + HEAD_DIM), 1.0, 0.0).astype(BF16)


def expand(values, channels):
    high, low = split(values)
    spread = spread_heads(values.shape[1], channels)
    return dot(high, spread) + dot(low, spread)


def decay_kernel(codes_ref, weight_ref, e_ref, f_ref, k_ref):
    heads, channels = codes_ref.shape[1], k_ref.shape[1]
    lower = jnp.where(lower_mask(), 1.0, 0.0).astype(F32)
    count = codes_ref.shape[0] // CHUNK
    line = lax.broadcasted_iota(jnp.int32, (8, heads), 0)
    marks = jnp.zeros((8, heads), F32)
    total = jnp.zeros((1, heads), F32)
    for chunk in range(count):
        rows = pl.ds(chunk * CHUNK, CHUNK)
        logs = codes_ref[rows, :].astype(F32) * (-DECAY_STEP)
        cumulative = jnp.dot(
            lower, logs, precision=lax.Precision.HIGHEST, preferred_element_type=F32
        )
        last = cumulative[CHUNK - 1 :]
        middle = 0.5 * last
        e_ref[rows, :] = jnp.exp(cumulative - middle)
        f_ref[rows, :] = weight_ref[rows, :] * jnp.exp(middle - cumulative)
        marks = jnp.where(line == chunk, jnp.exp(middle), marks)
        total = total + last
    marks = jnp.where(line == 7, total, marks)
    high, low = split(marks)
    lowest = (marks - high.astype(F32) - low.astype(F32)).astype(BF16)
    spread = spread_heads(heads, channels)
    factors = dot(high, spread) + dot(low, spread) + dot(lowest, spread)
    k_ref[...] = factors


def pair_kernel(backward, core_ref, own_ref, other_ref, *refs):
    out_ref = refs[-1]
    half = NSTATE // 2
    logs, other_logs = own_ref[NSTATE:, :], other_ref[NSTATE:, :]
    for core in range(2):

        @pl.when(core_ref[0] == core)
        def _():
            rows = slice(core * half, (core + 1) * half)
            if core == (0 if backward else 1):
                out_ref[:half, :] = jnp.exp(logs[0:1]) * other_ref[rows, :] + own_ref[rows, :]
            else:
                out_ref[:half, :] = jnp.exp(other_logs[0:1]) * own_ref[rows, :] + other_ref[rows, :]

    out_ref[half:, :] = logs + other_logs


def prefix_kernel(backward, chips, chip_ref, *refs):
    parts, out_ref = refs[:chips], refs[-1]
    half = out_ref.shape[0]
    mine = chip_ref[0]
    total = jnp.zeros(out_ref.shape, F32)
    for bits in range(1, chips):
        source = lax.bitwise_xor(mine, bits)
        span = jnp.zeros((1, out_ref.shape[1]), F32)
        for other in range(1, chips):
            middle = lax.bitwise_xor(mine, other)
            if backward:
                between = (middle < source) & (middle > mine)
            else:
                between = (middle > source) & (middle < mine)
            span = span + jnp.where(between, parts[other][half : half + 1, :], 0.0)
        passes = source > mine if backward else source < mine
        total = total + jnp.where(passes, jnp.exp(span), 0.0) * parts[bits][:half, :]
    out_ref[...] = total


def enter_kernel(backward, core_ref, partner_ref, prefix_ref, other_ref, out_ref):
    half = prefix_ref.shape[0]
    decay = jnp.exp(partner_ref[NSTATE : NSTATE + 1, :])
    for core in range(2):

        @pl.when(core_ref[0] == core)
        def _():
            for place, ref in ((core, prefix_ref), (1 - core, other_ref)):
                rows = slice(place * half, (place + 1) * half)
                if core == (0 if backward else 1):
                    out_ref[rows, :] = decay * ref[...] + partner_ref[rows, :]
                else:
                    out_ref[rows, :] = ref[...]


def taps(window, kernel, bias, begin):
    summed = bias
    for offset in range(KERNEL):
        summed = summed + kernel[offset : offset + 1] * window[begin + offset : begin + offset + CHUNK]
    return summed


def silu_parts(values):
    sigmoid = jax.nn.sigmoid(values)
    return values * sigmoid, sigmoid * (1.0 + values * (1.0 - sigmoid))


def first_step(action):
    pl.when(pl.program_id(0) == 0)(action)


def clear(*refs):
    def action():
        for ref in refs:
            ref[...] = jnp.zeros_like(ref)

    first_step(action)


def place_parts(mine, parts, target, width, value):
    size = len(parts)
    if width % 128 == 0:
        for i in range(size):
            owner = lax.rem(mine + size - i, size)
            target[:, pl.ds(pl.multiple_of(owner * width, 128), width)] = value(i)
        return

    def write(me):
        for i in range(size):
            owner = (me + size - i) % size
            target[:, owner * width : (owner + 1) * width] = value(i)

    for me in range(size):
        pl.when(mine == me)(functools.partial(write, me))


def copies_kernel(loose_ref, own_ref, out_ref):
    for i in range(out_ref.shape[0]):
        out_ref[i] = own_ref[...]


def norm_kernel(size, head_ref, passed_ref, *refs):
    parts, gains = refs[:size], refs[size : 2 * size]
    passed_gain_ref, normed_ref, scale_ref, gain_ref = refs[2 * size :]
    width = parts[0].shape[1]
    mine = head_ref[0]

    def pick(i, refs, passed):
        if size == 4 and i == 1:
            return jnp.where(mine == 0, passed[...], refs[i][...])
        if size == 4 and i == 3:
            return jnp.where(mine == 3, passed[...], refs[i][...])
        return refs[i][...]

    part = lambda i: pick(i, parts, passed_ref).astype(F32)
    gain = lambda i: pick(i, gains, passed_gain_ref)[0:1].astype(F32)
    squares = sum(jnp.sum(part(i) ** 2, axis=1, keepdims=True) for i in range(size))
    scale = lax.rsqrt(squares / (size * width) + EPSILON)
    scale_ref[...] = jnp.broadcast_to(scale, scale_ref.shape)
    place_parts(
        mine, parts, normed_ref, width,
        lambda i: (part(i) * scale_ref[:, 0:1] * gain(i)).astype(BF16),
    )
    place_parts(mine, parts, gain_ref, width, lambda i: jnp.broadcast_to(gain(i), (8, width)))


def mixed_grad_kernel(parts_ref, weight_ref, out_ref, full_ref):
    size, _, width = parts_ref.shape
    for i in range(size):
        full_ref[:, i * width : (i + 1) * width] = parts_ref[i]
    out_ref[...] = dot_nt(full_ref[...], weight_ref[...])


def out_kernel(loose_ref, mixed_ref, weight_ref, out_ref):
    width = out_ref.shape[2]
    for owner in range(out_ref.shape[0]):
        value = dot(mixed_ref[...], weight_ref[:, owner * width : (owner + 1) * width])
        out_ref[owner] = value.astype(BF16)


def conv_kernel(
    value_ref, state_ref, value_kernel_ref, value_bias_ref, state_kernel_ref, state_bias_ref,
    f_ref, k_ref, conv_ref, weighted_ref, value_slope_ref, maps_ref, state_slope_ref, total_ref,
):
    chunk = pl.program_id(0)
    clear(total_ref)
    around = pl.ds(pl.multiple_of(chunk * CHUNK, CHUNK), CHUNK + HALO)
    pre = taps(
        state_ref[around, :].astype(F32), state_kernel_ref[...].astype(F32),
        state_bias_ref[...].astype(F32), HALO - KERNEL + 1,
    )
    conv, slope = silu_parts(pre)
    maps = conv.astype(BF16)
    maps_ref[...] = maps
    state_slope_ref[...] = slope
    pre = taps(
        value_ref[around, :].astype(F32), value_kernel_ref[...].astype(F32),
        value_bias_ref[...].astype(F32), HALO - KERNEL + 1,
    )
    conv, slope = silu_parts(pre)
    conv = conv.astype(BF16)
    conv_ref[...] = conv
    value_slope_ref[...] = slope
    weighted = (conv.astype(F32) * expand(f_ref[...], conv.shape[1])).astype(BF16)
    weighted_ref[...] = weighted
    factor = k_ref[pl.ds(chunk, 1), :]
    total_ref[:NSTATE, :] = factor * (
        factor * total_ref[:NSTATE, :] + dot_tn(maps[:, :NSTATE], weighted)
    )
    total_ref[NSTATE:, :] = jnp.broadcast_to(k_ref[7:8, :], (8, k_ref.shape[1]))


def mixer_kernel(
    state_in_ref, maps_ref, weighted_ref, conv_ref, e_ref, k_ref, skip_ref, gate_ref, grad_ref, gain_ref,
    mixer_ref, stats_ref, high_ref, low_ref, state_ref,
):
    chunk = pl.program_id(0)

    def start():
        state_ref[...] = state_in_ref[...]

    first_step(start)
    lane = lax.broadcasted_iota(jnp.int32, (CHUNK, CHUNK), 1)
    factor = k_ref[pl.ds(chunk, 1), :]
    input_map, output_map = maps_ref[:, :NSTATE], maps_ref[:, NSTATE:]
    weighted = weighted_ref[...]
    scaled = factor * state_ref[...]
    high, low = split(scaled)
    high_ref[0], low_ref[0] = high, low
    scores = jnp.where(lower_mask(), dot_nt(output_map, input_map), 0.0).astype(BF16)
    mixed = dot(
        jnp.concatenate([scores, output_map], axis=1), jnp.concatenate([weighted, high], axis=0)
    )
    mixed = mixed + dot(output_map, low)
    mixer = expand(e_ref[...], weighted.shape[1]) * mixed + skip_ref[...] * conv_ref[...].astype(F32)
    mixer_ref[...] = mixer
    gate = gate_ref[...]
    gated = mixer * (gate * jax.nn.sigmoid(gate))
    squares = jnp.sum(gated * gated, axis=1, keepdims=True)
    products = jnp.sum(gated * (grad_ref[...] * gain_ref[...].astype(F32)), axis=1, keepdims=True)
    sums = jnp.where(lane == 0, squares, jnp.where(lane == 1, products, 0.0))
    stats_ref[...] = sums.T[:8]
    state_ref[...] = factor * (scaled + dot_tn(input_map, weighted))


def column(row_block):
    rest = jnp.zeros((CHUNK - row_block.shape[0], CHUNK), F32)
    return jnp.concatenate([row_block, rest], axis=0).T


def row_of(sums):
    lane = lax.broadcasted_iota(jnp.int32, (CHUNK, CHUNK), 1)
    return jnp.where(lane == 0, sums, 0.0).T[:8]


def gate_kernel(
    inner, chunks, size, *refs
):
    stats_refs = refs[:size]
    (
        mixer_ref, gate_ref, grad_ref, gain_ref, conv_ref, e_ref, k_ref, maps_ref,
        mixed_ref, gate_grad_ref, mixer_grad_ref, small_ref, total_ref, cross_ref,
    ) = refs[size:]
    chunk = chunks - 1 - pl.program_id(0)
    clear(small_ref, total_ref)
    gain = gain_ref[...].astype(F32)
    stats = column(sum(ref[...] for ref in stats_refs))
    scale = lax.rsqrt(stats[:, 0:1] / inner + EPSILON)
    cross_term = stats[:, 1:2] * (scale * scale * scale) / inner
    gate = gate_ref[...]
    silu, slope = silu_parts(gate)
    mixer = mixer_ref[...]
    gated = mixer * silu
    normed = gated * scale
    mixed_ref[...] = (normed * gain).astype(BF16)
    grad = grad_ref[...]
    gated_grad = scale * (grad * gain) - gated * cross_term
    gate_grad = (gated_grad * mixer * slope).astype(BF16)
    gate_grad_ref[...] = gate_grad
    cross_ref[...] = row_of(jnp.sum(gate_grad.astype(F32) * gate, axis=1, keepdims=True))
    mixer_grad = gated_grad * silu
    mixer_grad_ref[...] = mixer_grad
    small_ref[0:1, :] += jnp.sum(grad * normed, axis=0, keepdims=True)
    small_ref[1:2, :] += jnp.sum(mixer_grad * conv_ref[...].astype(F32), axis=0, keepdims=True)
    high, low = split(expand(e_ref[...], grad.shape[1]) * mixer_grad)
    output_map = maps_ref[:, NSTATE:]
    factor = k_ref[pl.ds(chunk, 1), :]
    total_ref[:NSTATE, :] = factor * (
        factor * total_ref[:NSTATE, :] + (dot_tn(output_map, high) + dot_tn(output_map, low))
    )
    total_ref[NSTATE:, :] = jnp.broadcast_to(k_ref[7:8, :], (8, k_ref.shape[1]))


def back_kernel(
    chunks, early_ref, state_in_ref, mixer_grad_ref, e_ref, f_ref, k_ref, weighted_ref, high_ref, low_ref,
    maps_ref, value_slope_ref, state_slope_ref, skip_ref,
    value_ref, map_ref, state_ref,
):
    chunk = chunks - 1 - pl.program_id(0)

    def start():
        state_ref[...] = state_in_ref[...]

    first_step(start)
    lower = lower_mask()
    row = lax.broadcasted_iota(jnp.int32, (CHUNK, CHUNK), 0)
    upper = row <= lax.broadcasted_iota(jnp.int32, (CHUNK, CHUNK), 1)
    factor = k_ref[pl.ds(chunk, 1), :]
    input_map, output_map = maps_ref[:, :NSTATE], maps_ref[:, NSTATE:]
    weighted = weighted_ref[...]
    mixer_grad = mixer_grad_ref[...]
    high, low = split(expand(e_ref[...], weighted.shape[1]) * mixer_grad)
    scaled = factor * state_ref[...]
    state_high, state_low = split(scaled)
    both = jnp.concatenate([weighted, high_ref[0]], axis=0)
    sums = dot_nt(high, both) + dot_nt(low, both)
    score_grad = jnp.where(lower, sums[:, :CHUNK], 0.0).astype(BF16)
    output_grad = sums[:, CHUNK:] + dot_nt(high, low_ref[0]) + dot(score_grad, input_map)
    sums = dot_nt(weighted, jnp.concatenate([state_high, state_low], axis=0))
    input_grad = sums[:, :NSTATE] + sums[:, NSTATE:] + dot_tn(score_grad, output_map)
    scores = jnp.where(upper, dot_nt(input_map, output_map), 0.0).astype(BF16)
    grads = dot(
        jnp.concatenate([scores, input_map], axis=1), jnp.concatenate([high, state_high], axis=0)
    )
    decayed = expand(f_ref[...], weighted.shape[1]) * grads
    value_ref[...] = (decayed + skip_ref[...] * mixer_grad) * value_slope_ref[...]
    slope = state_slope_ref[...]
    map_ref[:, :NSTATE] = input_grad * slope[:, :NSTATE]
    map_ref[:, NSTATE:] = output_grad * slope[:, NSTATE:]
    state_ref[...] = factor * (scaled + (dot_tn(output_map, high) + dot_tn(output_map, low)))


def conv_back_kernel(
    chunks, value_ref, map_ref, after_ref, value_raw_ref, state_raw_ref, value_kernel_ref,
    state_kernel_ref, cross_in_ref,
    value_grad_ref, state_grad_ref, value_small_ref, state_small_ref, cross_ref, value_next_ref,
    state_next_ref,
):
    chunk = chunks - 1 - pl.program_id(0)
    channels = value_ref.shape[1]
    clear(value_small_ref, state_small_ref)

    def start():
        value_next_ref[...] = after_ref[:, :channels]
        state_next_ref[...] = after_ref[:, channels:]

    first_step(start)

    def back(slope_ref, next_ref, raw_ref, kernel_ref, grad_ref, small_ref):
        kernel = kernel_ref[...].astype(F32)
        slope = slope_ref[...]
        window = jnp.concatenate([slope, next_ref[...]], axis=0)
        around = pl.ds(pl.multiple_of(chunk * CHUNK, CHUNK), CHUNK + HALO)
        raw = raw_ref[around, :].astype(F32)
        grad = jnp.zeros_like(slope)
        for offset in range(KERNEL):
            back_by = KERNEL - 1 - offset
            grad = grad + kernel[offset : offset + 1] * window[back_by : back_by + CHUNK]
            begin = HALO - KERNEL + 1 + offset
            small_ref[offset : offset + 1, :] += jnp.sum(
                slope * raw[begin : begin + CHUNK], axis=0, keepdims=True
            )
        small_ref[KERNEL : KERNEL + 1, :] += jnp.sum(slope, axis=0, keepdims=True)
        grad = grad.astype(BF16)
        grad_ref[...] = grad
        next_ref[...] = slope[:8]
        return jnp.sum(grad.astype(F32) * raw[HALO:], axis=1, keepdims=True)

    crossed = back(map_ref, state_next_ref, state_raw_ref, state_kernel_ref, state_grad_ref, state_small_ref)
    crossed = crossed + back(
        value_ref, value_next_ref, value_raw_ref, value_kernel_ref, value_grad_ref, value_small_ref
    )
    cross_ref[...] = cross_in_ref[...] + row_of(crossed)


def normed_kernel(
    chunks, late_ref, gate_grad_ref, value_grad_ref, state_grad_ref, gate_weight_ref, value_weight_ref,
    state_weight_ref, cross_ref, out_ref
):
    value = (
        dot_nt(gate_grad_ref[...], gate_weight_ref[...])
        + dot_nt(value_grad_ref[...], value_weight_ref[...])
        + dot_nt(state_grad_ref[...], state_weight_ref[...])
    )
    count = value.shape[0]
    out_ref[0, :count, :] = value.astype(BF16)
    line = lax.broadcasted_iota(jnp.int32, (HALO, CHUNK), 0)
    packed = jnp.zeros((HALO, CHUNK), F32)
    for chunk in range(chunks):
        row = cross_ref[0:1, chunk * CHUNK : (chunk + 1) * CHUNK]
        high = row.astype(BF16).astype(F32)
        packed = jnp.where(line == chunk, high, packed)
        packed = jnp.where(line == chunks + chunk, row - high, packed)
    out_ref[0, count:, :] = jnp.zeros((HALO, value.shape[1]), BF16)
    out_ref[0, count:, :CHUNK] = packed.astype(BF16)


def last_kernel(full_width, parts_ref, tokens_ref, scale_ref, gain_ref, cotangent_ref, out_ref):
    count = tokens_ref.shape[0]
    chunks = count // CHUNK
    size = parts_ref.shape[0]
    crossed = sum(parts_ref[i, count:, :CHUNK].astype(F32) for i in range(size))
    crossed = crossed[:chunks] + crossed[chunks : 2 * chunks]
    for chunk in range(chunks):
        rows = slice(chunk * CHUNK, (chunk + 1) * CHUNK)
        normed_grad = sum(parts_ref[i, rows, :].astype(F32) for i in range(size))
        scale = scale_ref[HALO + chunk * CHUNK : HALO + (chunk + 1) * CHUNK, 0:1]
        total = column(jnp.broadcast_to(crossed[chunk : chunk + 1], (8, CHUNK)))[:, 0:1]
        out_ref[rows, :] = (
            scale * gain_ref[...].astype(F32) * normed_grad
            - tokens_ref[rows, :].astype(F32) * (scale * scale * total / full_width)
            + cotangent_ref[rows, :].astype(F32)
        ).astype(BF16)


def store_piece(core_ref, kept_ref, given_ref, place, begin, piece):
    chips = kept_ref.shape[0]
    core, chip = place // chips, lax.rem(place, chips)
    rows = slice(begin, begin + piece.shape[0])
    piece = piece.astype(BF16)

    @pl.when(core_ref[0] == core)
    def _():
        kept_ref[chip, rows, :] = piece

    @pl.when(core_ref[0] != core)
    def _():
        given_ref[chip, rows, :] = piece


def gain_row(weight, block):
    sums = jnp.sum(weight.astype(F32) * block, axis=1, keepdims=True)
    lane = lax.broadcasted_iota(jnp.int32, (CHUNK, CHUNK), 1)
    rows = [
        jnp.where(lane == 0, sums[i : i + CHUNK], 0.0).T[0:1] for i in range(0, BLOCK, CHUNK)
    ]
    return jnp.concatenate(rows, axis=1)


def early_kernel(
    loose_ref, core_ref, normed_ref, gate_ref, mixed_ref, grad_ref, weight_ref,
    kept_ref, given_ref, gain_ref, held_ref
):
    chips, rows, channels = kept_ref.shape
    at = pl.program_id(0)
    count, width = grad_ref.shape
    pieces = 2 * chips
    step = width // pieces
    out_rows = channels // pieces
    out_blocks = channels // BLOCK
    every = width // BLOCK // out_blocks

    @pl.when(lax.rem(at, every) == 0)
    def _():
        held_ref[...] = dot_tn(mixed_ref[...], grad_ref[...])

    block = dot_tn(normed_ref[HALO : HALO + count, :], gate_ref[...])
    gain_ref[...] = gain_row(weight_ref[...], block)
    for i in range(BLOCK // step):
        place = at * (BLOCK // step) + i
        begin = lax.rem(at, every) * (BLOCK // step * out_rows) + i * out_rows
        own = held_ref[pl.ds(pl.multiple_of(begin, 8), out_rows), :]
        parts = [block[i * step : (i + 1) * step]]
        parts += [own[:, j : j + channels] for j in range(0, width, channels)]
        store_piece(core_ref, kept_ref, given_ref, place, 0, jnp.concatenate(parts, axis=0))


def late_kernel(
    early_ref, core_ref, normed_ref, value_ref, state_ref, value_small_ref, gate_small_ref, gain_ref,
    state_small_ref, value_weight_ref, state_weight_ref, gain_full_ref,
    kept_ref, given_ref, own_ref, shared_ref, gains_ref,
):
    chips, rows, channels = kept_ref.shape
    at = pl.program_id(0)
    count, maps_width = state_ref.shape
    width = gains_ref.shape[1]
    pieces = 2 * chips
    step = width // pieces
    lanes = channels // 128
    part = 2 * step // lanes
    columns = normed_ref[HALO : HALO + count, :]
    value = dot_tn(columns, value_ref[...])
    state = dot_tn(columns, state_ref[...])
    gain = (
        gain_ref[...] + gain_row(value_weight_ref[...], value) + gain_row(state_weight_ref[...], state)
    ) / gain_full_ref[0:1, :]
    gains_ref[0:1, pl.ds(pl.multiple_of(at * BLOCK, 128), BLOCK)] = gain
    for i in range(BLOCK // step):
        piece = slice(i * step, (i + 1) * step)
        stacked = jnp.concatenate([state[piece, :128], state[piece, 128:]], axis=0)
        stacked = jnp.concatenate(
            [stacked[j * part : (j + 1) * part] for j in range(lanes)], axis=1
        )
        store_piece(
            core_ref, kept_ref, given_ref, at * (BLOCK // step) + i, 0,
            jnp.concatenate([value[piece], stacked], axis=0),
        )

    @pl.when(at == width // BLOCK - 1)
    def _():
        own_ref[...] = jnp.zeros_like(own_ref)
        own_ref[: KERNEL + 1, :] = value_small_ref[: KERNEL + 1, :]
        own_ref[KERNEL + 1 : KERNEL + 3, :] = gate_small_ref[:2, :]
        shared_ref[...] = jnp.zeros_like(shared_ref)
        begin = width // channels
        for i in range(begin):
            shared_ref[i : i + 1, :] = gains_ref[0:1, i * channels : (i + 1) * channels]
        for i in range(0, (KERNEL + 1) * maps_width, 128):
            tap, column_from = divmod(i, maps_width)
            row, column_to = divmod(i, channels)
            shared_ref[begin + row : begin + row + 1, column_to : column_to + 128] = state_small_ref[
                tap : tap + 1, column_from : column_from + 128
            ]
        line = lax.broadcasted_iota(jnp.int32, (HALO, channels), 0)
        for place in range(pieces):
            own, shared = own_ref[place : place + 1, :], shared_ref[place : place + 1, :]
            own_high, shared_high = (v.astype(BF16).astype(F32) for v in (own, shared))
            small = jnp.zeros((HALO, channels), F32)
            for to, value in enumerate((own_high, own - own_high, shared_high, shared - shared_high)):
                small = jnp.where(line == to, value, small)
            store_piece(core_ref, kept_ref, given_ref, place, step + part, small)


def merge_pairs(block):
    tail = block[-HALO:]
    line = lax.broadcasted_iota(jnp.int32, tail.shape, 0)
    own, shared = tail[0:1] + tail[1:2], tail[2:3] + tail[3:4]
    own_high, shared_high = own.astype(BF16).astype(F32), shared.astype(BF16).astype(F32)
    new = jnp.zeros_like(tail)
    for at, value in enumerate((own_high, own - own_high, shared_high, shared - shared_high)):
        new = jnp.where(line == at, value, new)
    return jnp.concatenate([block[:-HALO], new], axis=0)


def heads_kernel(piece_ref, total_ref, arrived_ref, out_ref, low_ref):
    total = merge_pairs(total_ref[...] + arrived_ref[...].astype(F32))
    line = lax.broadcasted_iota(jnp.int32, total.shape, 0)
    first = total.shape[0] - HALO
    own = (line >= first) & (line < first + 2)
    out_ref[...] = total
    low_ref[...] = jnp.where(own, piece_ref[...], total).astype(BF16)


def half_kernel(paired, chips, chip_ref, kept_ref, arrived_ref, *refs):
    outs = refs[-chips:]
    for bits in range(chips):
        place = lax.bitwise_xor(chip_ref[0], bits)
        value = kept_ref[place].astype(F32) + arrived_ref[place].astype(F32)
        if paired:
            value = merge_pairs(value)
        outs[bits][...] = value.astype(outs[bits].dtype)


def piece_kernel(parts, paired, cut, *refs):
    total = sum(ref[...].astype(F32) for ref in refs[:parts])
    if not paired:
        refs[-1][...] = total.astype(BF16)
        return
    first_ref, last_ref = refs[-2:]
    first_ref[...] = total[:cut].astype(BF16)
    last_ref[...] = merge_pairs(total[cut:])


def square_half_kernel(
    chip_ref, kept_ref, arrived_ref, first_ref, first_give_ref, last_ref, last_give_ref
):
    cut = first_ref.shape[1]
    for bits in range(4):
        place = lax.bitwise_xor(chip_ref[0], bits)
        value = kept_ref[place].astype(F32) + arrived_ref[place].astype(F32)
        low, high = bits & 1, bits >> 1
        ref = first_give_ref if low else first_ref
        ref[high] = value[:cut].astype(ref.dtype)
        ref = last_give_ref if high else last_ref
        ref[low] = value[cut:].astype(ref.dtype)


def square_next_kernel(
    first_ref, first_got_ref, last_ref, last_got_ref,
    first_out_ref, first_give_ref, last_out_ref, last_give_ref,
):
    first_out_ref[...] = first_ref[0] + first_got_ref[0].astype(F32)
    first_give_ref[...] = (first_ref[1] + first_got_ref[1].astype(F32)).astype(BF16)
    last_out_ref[...] = last_ref[0] + last_got_ref[0].astype(F32)
    last_give_ref[...] = (last_ref[1] + last_got_ref[1].astype(F32)).astype(BF16)


def square_last_kernel(first_ref, first_got_ref, last_ref, last_got_ref, loose_ref, *outs):
    outs[0][...] = (first_ref[...] + first_got_ref[...].astype(F32)).astype(BF16)
    outs[1][...] = (last_ref[...] + last_got_ref[...].astype(F32)).astype(BF16)


def spread_pieces(core_ref, chip_ref, chips, groups, refs, store):
    step = pl.program_id(0)
    core, chip = step // chips, lax.rem(step, chips)
    apart = lax.bitwise_xor(chip, chip_ref[0])
    refs = iter(refs)
    for part, bits_lists in enumerate(groups):
        for bits_list in bits_lists:
            own_ref, other_ref = next(refs), next(refs)
            for at, bits in enumerate(bits_list):

                @pl.when((apart == bits) & (core == core_ref[0]))
                def _(part=part, ref=own_ref, at=at):
                    store(part, ref[at].astype(F32))

                @pl.when((apart == bits) & (core != core_ref[0]))
                def _(part=part, ref=other_ref, at=at):
                    store(part, ref[at].astype(F32))


def early_out_kernel(chips, groups, core_ref, chip_ref, *refs):
    gate_ref, output_ref = refs[-2:]
    step, channels = gate_ref.shape
    out_rows, width = output_ref.shape

    def store(part, value):
        if part == 0:
            gate_ref[...] = value
        else:
            output_ref[...] = jnp.concatenate(
                [value[i * out_rows : (i + 1) * out_rows] for i in range(width // channels)], axis=1
            )

    spread_pieces(core_ref, chip_ref, chips, groups, refs[:-2], store)


def late_out_kernel(chips, groups, core_ref, chip_ref, *refs):
    value_ref = refs[-1]

    def store(part, value):
        value_ref[...] = value

    spread_pieces(core_ref, chip_ref, chips, groups, refs[:-1], store)


def shared_out_kernel(chips, groups, size, core_ref, chip_ref, head_ref, *refs):
    (
        state_ref, value_kernel_ref, value_bias_ref, state_kernel_ref, state_bias_ref, skip_ref,
        gated_ref, gain_ref, own_ref, shared_ref,
    ) = refs[-10:]
    step, maps_width = state_ref.shape
    channels = own_ref.shape[1]
    lanes = channels // 128
    rows = 2 * step // lanes
    at = pl.program_id(0)

    def store(part, piece):
        stacked = jnp.concatenate(
            [piece[:rows, i * 128 : (i + 1) * 128] for i in range(lanes)], axis=0
        )
        state_ref[...] = jnp.concatenate([stacked[:step], stacked[step:]], axis=1)
        own_ref[pl.ds(at, 1), :] = piece[rows : rows + 1] + piece[rows + 1 : rows + 2]
        shared_ref[pl.ds(at, 1), :] = piece[rows + 2 : rows + 3] + piece[rows + 3 : rows + 4]

    spread_pieces(core_ref, chip_ref, chips, groups, refs[:-10], store)

    @pl.when(at == 2 * chips - 1)
    def _():
        value_kernel_ref[...] = own_ref[:KERNEL, :]
        value_bias_ref[...] = own_ref[KERNEL, :]
        gated_ref[...] = own_ref[KERNEL + 1, :]
        heads = skip_ref.shape[0]
        place = lax.broadcasted_iota(jnp.int32, (heads, channels), 1)
        row = lax.broadcasted_iota(jnp.int32, (heads, channels), 0) * HEAD_DIM
        inside = (place >= row) & (place < row + HEAD_DIM)
        skip_ref[...] = jnp.sum(jnp.where(inside, own_ref[KERNEL + 2 : KERNEL + 3, :], 0.0), axis=1)
        own_width = gain_ref.shape[0]
        gain_rows = -(-own_width * size // channels)
        for head in range(size):
            row, begin = divmod(head * own_width, channels)

            @pl.when(head_ref[0] == head)
            def _():
                gain_ref[...] = shared_ref[row, begin : begin + own_width]
        for i in range(0, (KERNEL + 1) * maps_width, 128):
            tap, column_to = divmod(i, maps_width)
            row, column_from = divmod(i, channels)
            value = shared_ref[gain_rows + row : gain_rows + row + 1, column_from : column_from + 128]
            if tap < KERNEL:
                state_kernel_ref[tap : tap + 1, column_to : column_to + 128] = value
            else:
                state_bias_ref[column_to : column_to + 128] = value[0]


SCALAR = "scalar"
WHOLE = "whole"
BLOCKED = "blocked"
LANES = "lanes"
LEADING = "leading"
LOOSE = "loose"


def run(kernel, name, flops, args, outs, steps=None, backward=False, scratch=()):
    at = (lambda i: steps - 1 - i) if backward else (lambda i: i)

    def spec(kind, shape):
        if isinstance(kind, int):
            return pl.BlockSpec((kind,) + shape[1:], lambda i: (at(i), 0))
        if kind == SCALAR:
            return pl.BlockSpec(memory_space=pltpu.SMEM)
        if kind == LOOSE:
            return pl.BlockSpec(memory_space=pl.ANY)
        if isinstance(kind, tuple):
            return pl.BlockSpec(*kind)
        if steps is None:
            return pl.BlockSpec(memory_space=pltpu.VMEM)
        if kind == BLOCKED:
            return pl.BlockSpec((CHUNK, shape[1]), lambda i: (at(i), 0))
        if kind == LANES:
            return pl.BlockSpec((shape[0], CHUNK), lambda i: (0, at(i)))
        if kind == LEADING:
            return pl.BlockSpec((1,) + shape[1:], lambda i: (at(i),) + (0,) * (len(shape) - 1))
        return pl.BlockSpec(shape, lambda i: (0,) * len(shape))

    moved = sum(a.size * a.dtype.itemsize for kind, a in args if kind != LOOSE)
    shapes = [jax.ShapeDtypeStruct(shape, dtype) for _, shape, dtype in outs]
    moved += sum(a.size * a.dtype.itemsize for a in shapes)
    return pl.pallas_call(
        kernel,
        out_shape=shapes,
        in_specs=[spec(kind, a.shape) for kind, a in args],
        out_specs=[spec(kind, shape) for kind, shape, _ in outs],
        scratch_shapes=list(scratch),
        compiler_params=pltpu.CompilerParams(vmem_limit_bytes=VMEM_LIMIT),
        cost_estimate=pl.CostEstimate(flops=flops, bytes_accessed=moved, transcendentals=0),
        name=name,
        **({} if steps is None else {"grid": (steps,)}),
    )(*(a for _, a in args))


def per_device(
    tokens, decay_codes, norm_gain, gate_weight, value_weight, state_weight, value_kernel, value_bias,
    state_kernel, state_bias, skip_scale, gated_gain, output_weight, cotangent,
):
    tokens, decay_codes, cotangent = tokens[0], decay_codes[0], cotangent[0]
    count, own_width = tokens.shape
    heads = skip_scale.shape[0]
    channels = heads * HEAD_DIM
    head_size, chips = lax.axis_size("head"), lax.axis_size("chip")
    seq_size = 2 * chips
    width = own_width * head_size
    maps_width = 2 * NSTATE
    chunks = count // CHUNK
    core = (SCALAR, lax.axis_index("core").astype(jnp.int32)[None])
    chip = (SCALAR, lax.axis_index("chip").astype(jnp.int32)[None])
    head = (SCALAR, lax.axis_index("head").astype(jnp.int32)[None])

    rows = count + MARGIN
    packed = jnp.concatenate(
        [
            from_behind(tokens[-HALO:], 1),
            tokens,
            jnp.broadcast_to(norm_gain[None], (MARGIN - HALO, own_width)),
        ],
        axis=0,
    )
    logs = decay_codes.astype(F32) * (-DECAY_STEP)
    input_weight = jnp.sqrt(-jnp.expm1(2.0 * logs))
    e_full, f_full, factors = run(
        decay_kernel, "decays", count * channels * 200,
        [(WHOLE, decay_codes), (WHOLE, input_weight)],
        [
            (WHOLE, (count, heads), F32),
            (WHOLE, (count, heads), F32),
            (WHOLE, (8, channels), F32),
        ],
    )
    parts, passed = line_parts(packed, "head")
    skip_full = jnp.repeat(skip_scale, HEAD_DIM)[None]

    half = rows // 2
    gain_rows = ((MARGIN - HALO, own_width), lambda i: ((HALO + count) // (MARGIN - HALO), 0))
    normed, scale_in, gain_full = run(
        functools.partial(norm_kernel, head_size), "norm", count * width * 10,
        [head, (half, passed)] + [(half, part) for part in parts]
        + [(gain_rows, part) for part in parts] + [(gain_rows, passed)],
        [(half, (rows, width), BF16), (half, (rows, 128), F32), (WHOLE, (8, width), F32)],
        steps=2,
    )
    cotangent_parts = deal(
        run(
            copies_kernel, "copies", 1, [(LOOSE, normed), (WHOLE, cotangent)],
            [(WHOLE, (head_size, count, own_width), BF16)],
        )[0],
        "head",
    )
    value_raw = dot(normed, value_weight).astype(BF16)
    state_raw = dot(normed, state_weight).astype(BF16)
    conv, weighted, value_slope, maps, map_slope, local_end = run(
        conv_kernel, "conv", count * channels * 400,
        [
            (WHOLE, value_raw), (WHOLE, state_raw), (WHOLE, value_kernel), (WHOLE, value_bias[None]),
            (WHOLE, state_kernel), (WHOLE, state_bias[None]), (BLOCKED, f_full), (WHOLE, factors),
        ],
        [
            (BLOCKED, (count, channels), BF16),
            (BLOCKED, (count, channels), BF16),
            (BLOCKED, (count, channels), F32),
            (BLOCKED, (count, maps_width), BF16),
            (BLOCKED, (count, maps_width), F32),
            (WHOLE, (NSTATE + 8, channels), F32),
        ],
        steps=chunks,
    )
    gate_pre = dot(normed, gate_weight)[HALO : HALO + count]
    state_in = entering(core, chip, local_end, False, (gate_pre,))
    mixed_grad, full_cotangent = run(
        mixed_grad_kernel, "mixed_grad", 2 * count * width * channels,
        [(WHOLE, cotangent_parts), (WHOLE, output_weight)],
        [(WHOLE, (count, channels), F32), (WHOLE, (count, width), BF16)],
    )
    mixer, stats, high, low = run(
        mixer_kernel, "mixer", count * channels * 1000,
        [
            (WHOLE, state_in), (BLOCKED, maps), (BLOCKED, weighted), (BLOCKED, conv),
            (BLOCKED, e_full), (WHOLE, factors), (WHOLE, skip_full), (BLOCKED, gate_pre),
            (BLOCKED, mixed_grad), (WHOLE, gated_gain[None]),
        ],
        [
            (BLOCKED, (count, channels), F32),
            (LANES, (8, count), F32),
            (LEADING, (chunks, NSTATE, channels), BF16),
            (LEADING, (chunks, NSTATE, channels), BF16),
        ],
        steps=chunks,
        scratch=[pltpu.VMEM((NSTATE, channels), F32)],
    )
    mixed, gate_grad, mixer_grad, gate_small, start_grad, gate_cross = run(
        functools.partial(gate_kernel, float(channels * head_size), chunks, head_size),
        "gate", count * channels * 600,
        [(LANES, part) for part in turn_all(stats, "head")]
        + [
            (BLOCKED, mixer), (BLOCKED, gate_pre), (BLOCKED, mixed_grad), (WHOLE, gated_gain[None]),
            (BLOCKED, conv), (BLOCKED, e_full), (WHOLE, factors), (BLOCKED, maps),
        ],
        [
            (BLOCKED, (count, channels), BF16),
            (BLOCKED, (count, channels), BF16),
            (BLOCKED, (count, channels), F32),
            (WHOLE, (8, channels), F32),
            (WHOLE, (NSTATE + 8, channels), F32),
            (LANES, (8, count), F32),
        ],
        steps=chunks,
        backward=True,
    )
    step, out_rows = width // seq_size, channels // seq_size
    early_rows = step + out_rows * (width // channels)
    features = width // BLOCK
    feature_block = ((rows, BLOCK), lambda i: (0, i))
    every = features // (channels // BLOCK)
    out_parts = run(
        out_kernel, "out", 2 * count * channels * width,
        [(LOOSE, start_grad), (WHOLE, mixed), (WHOLE, output_weight)],
        [(WHOLE, (head_size, count, own_width), BF16)],
    )[0]
    early_made = []

    def make_early(pair):
        early_made.extend(
            run(
                early_kernel, "early", 4 * count * channels * width,
                [
                    (LOOSE, pair), core, (feature_block, normed), (WHOLE, gate_grad),
                    (((count, BLOCK), lambda i: (0, i // every)), mixed), (WHOLE, full_cotangent),
                    (BLOCK, gate_weight),
                ],
                [(WHOLE, (chips, early_rows, channels), BF16)] * 2
                + [(((1, BLOCK), lambda i: (0, i)), (1, width), F32)],
                steps=features,
                scratch=[pltpu.VMEM((BLOCK, width), F32)],
            )
        )
        return early_made[1:2]

    grad_after = entering(core, chip, start_grad, True, (out_parts,), make_early)
    early_kept, early_given, early_gain = early_made
    early_state, half_mark = sum_pieces(chip, early_kept, early_given, "early", True, step, False)
    next_mark = early_state[0]
    branch = jnp.sum(deal(out_parts, "head").astype(F32), axis=0)
    block_out = (tokens.astype(F32) + branch).astype(BF16)

    value_grads, map_grads = run(
        functools.partial(back_kernel, chunks), "back", count * channels * 2000,
        [
            (LOOSE, half_mark), (WHOLE, grad_after), (BLOCKED, mixer_grad), (BLOCKED, e_full),
            (BLOCKED, f_full), (WHOLE, factors), (BLOCKED, weighted), (LEADING, high),
            (LEADING, low), (BLOCKED, maps), (BLOCKED, value_slope), (BLOCKED, map_slope),
            (WHOLE, skip_full),
        ],
        [(BLOCKED, (count, channels), F32), (BLOCKED, (count, maps_width), F32)],
        steps=chunks,
        backward=True,
        scratch=[pltpu.VMEM((NSTATE, channels), F32)],
    )
    after = from_behind(jnp.concatenate([value_grads[:8], map_grads[:8]], axis=1), -1)
    value_raw_grad, state_raw_grad, value_small, state_small, crossed = run(
        functools.partial(conv_back_kernel, chunks), "conv_back", count * channels * 100,
        [
            (BLOCKED, value_grads), (BLOCKED, map_grads), (WHOLE, after),
            (WHOLE, value_raw), (WHOLE, state_raw), (WHOLE, value_kernel), (WHOLE, state_kernel),
            (LANES, gate_cross),
        ],
        [
            (BLOCKED, (count, channels), BF16),
            (BLOCKED, (count, maps_width), BF16),
            (WHOLE, (8, channels), F32),
            (WHOLE, (8, maps_width), F32),
            (LANES, (8, count), F32),
        ],
        steps=chunks,
        backward=True,
        scratch=[pltpu.VMEM((8, channels), F32), pltpu.VMEM((8, maps_width), F32)],
    )
    lanes = channels // 128
    state_rows = 2 * step // lanes
    late_rows = step + state_rows + HALO
    late_kept, late_given = run(
        late_kernel, "late", 3 * count * channels * width,
        [
            (LOOSE, next_mark), core, (feature_block, normed), (WHOLE, value_raw_grad),
            (WHOLE, state_raw_grad),
            (WHOLE, value_small), (WHOLE, gate_small), (((1, BLOCK), lambda i: (0, i)), early_gain),
            (WHOLE, state_small), (BLOCK, value_weight), (BLOCK, state_weight),
            (((8, BLOCK), lambda i: (0, i)), gain_full),
        ],
        [(WHOLE, (chips, late_rows, channels), BF16)] * 2,
        steps=features,
        scratch=[
            pltpu.VMEM((HALO, channels), F32),
            pltpu.VMEM((HALO, channels), F32),
            pltpu.VMEM((8, width), F32),
        ],
    )
    normed_parts = run(
        functools.partial(normed_kernel, chunks), "normed", 4 * count * channels * width,
        [
            (LOOSE, late_given), (WHOLE, gate_grad), (WHOLE, value_raw_grad),
            (WHOLE, state_raw_grad), (own_width, gate_weight), (own_width, value_weight),
            (own_width, state_weight), (WHOLE, crossed),
        ],
        [(LEADING, (head_size, count + HALO, own_width), BF16)],
        steps=head_size,
    )[0]
    (late_piece, shared_piece), late_mark = sum_pieces(
        chip, late_kept, late_given, "late", False, step, True, (normed_parts,)
    )
    if chips == 4:
        early_gate, early_out = square_end(
            "early", early_state,
            [(WHOLE, (step, channels), BF16), (WHOLE, (early_rows - step, channels), BF16)],
            early_rows * channels, late_mark,
        )
    else:
        early_gate, early_out = early_state[0][:step], early_state[0][step:]
    normed_parts = deal(normed_parts, "head")
    shared_piece = heads_sum(shared_piece)

    def unpack(kernel, name, pieces, outs, flops, extra=(), scratch=()):
        groups = [collect(*piece) for piece in pieces]
        bits = [[found[2] for found in group] for group in groups]
        arrays = [(WHOLE, value) for group in groups for found in group for value in found[:2]]
        scalars = [core, chip] + ([head] if extra else [])
        return run(
            functools.partial(kernel, chips, bits, *extra), name, flops, scalars + arrays, outs,
            steps=seq_size, scratch=scratch,
        )

    gate_weight_gradient, output_weight_gradient = unpack(
        early_out_kernel, "early_out", [(early_gate, (2, 1), late_piece), (early_out, (1, 2), late_piece)],
        [(step, (width, channels), F32), (out_rows, (channels, width), F32)], 4 * channels * width,
    )
    value_weight_gradient = unpack(
        late_out_kernel, "late_out", [(late_piece, None)],
        [(step, (width, channels), F32)], 2 * channels * width,
    )[0]
    (
        state_weight_gradient, value_kernel_gradient, value_bias_gradient, state_kernel_gradient,
        state_bias_gradient, skip_scale_gradient, gated_gain_gradient, norm_gain_gradient,
    ) = unpack(
        shared_out_kernel, "shared_out", [(shared_piece, (2, 1))],
        [
            (step, (width, maps_width), F32),
            (WHOLE, (KERNEL, channels), F32),
            (WHOLE, (channels,), F32),
            (WHOLE, (KERNEL, maps_width), F32),
            (WHOLE, (maps_width,), F32),
            (WHOLE, (heads,), F32),
            (WHOLE, (channels,), F32),
            (WHOLE, (own_width,), F32),
        ],
        2 * maps_width * width,
        extra=(head_size,),
        scratch=[pltpu.VMEM((HALO, channels), F32), pltpu.VMEM((HALO, channels), F32)],
    )
    tokens_gradient = run(
        functools.partial(last_kernel, float(width)), "last", count * own_width * 20,
        [
            (WHOLE, normed_parts), (WHOLE, tokens), (WHOLE, scale_in),
            (WHOLE, norm_gain[None]), (WHOLE, cotangent),
        ],
        [(WHOLE, (count, own_width), BF16)],
    )[0]
    return (
        block_out[None],
        tokens_gradient[None],
        norm_gain_gradient,
        gate_weight_gradient,
        value_weight_gradient,
        state_weight_gradient,
        value_kernel_gradient,
        value_bias_gradient,
        state_kernel_gradient,
        state_bias_gradient,
        skip_scale_gradient,
        gated_gain_gradient,
        output_weight_gradient,
    )


def solution(mesh):
    seq_size, head_size = mesh.shape["seq"], mesh.shape["head"]
    mesh = Mesh(mesh.devices.reshape(seq_size // 2, 2, head_size), ("chip", "core", "head"))
    seq = ("chip", "core")
    in_specs = (
        P(None, seq, "head"),
        P(None, seq, "head"),
        P("head"),
        P(None, "head"),
        P(None, "head"),
        P(),
        P(None, "head"),
        P("head"),
        P(),
        P(),
        P("head"),
        P("head"),
        P("head", None),
        P(None, seq, "head"),
    )
    out_specs = (
        P(None, seq, "head"),
        P(None, seq, "head"),
        P("head"),
        P(None, "head"),
        P(None, "head"),
        P(),
        P(None, "head"),
        P("head"),
        P(),
        P(),
        P("head"),
        P("head"),
        P("head", None),
    )
    return jax.shard_map(
        per_device, mesh=mesh, in_specs=in_specs, out_specs=out_specs, check_vma=False
    )
```

```python
import functools

import jax
import jax.numpy as jnp
from jax import lax
from jax.experimental import pallas as pl
from jax.experimental.pallas import tpu as pltpu
from jax.sharding import Mesh
from jax.sharding import PartitionSpec as P

HEAD_DIM = 64
NSTATE = 128
KERNEL = 4
CHUNK = 128
BLOCK = 384
VMEM_LIMIT = 20 * 1024 * 1024
MARGIN = 32
HALO = 16


DECAY_STEP = 1.0 / 1048576.0
EPSILON = 1e-05
BF16 = jnp.bfloat16
F32 = jnp.float32


def tie_kernel(*refs):
    del refs


def tie(value, *others):
    return pl.pallas_call(
        tie_kernel,
        out_shape=jax.ShapeDtypeStruct(value.shape, value.dtype),
        in_specs=[pl.BlockSpec(memory_space=pl.ANY)] * (1 + len(others)),
        out_specs=pl.BlockSpec(memory_space=pl.ANY),
        input_output_aliases={0: 0},
        name="tie",
    )(value, *others)


def from_behind(value, by):
    axis = ("chip", "core")
    size = lax.axis_size("chip") * 2
    pairs = [(i, i + by) for i in range(size) if 0 <= i + by < size]
    return lax.ppermute(value, axis, pairs)


def beside(value):
    return lax.ppermute(value, "core", [(0, 1), (1, 0)])


def turn(value, axis, by):
    size = lax.axis_size(axis)
    return lax.ppermute(value, axis, [(i, (i + by) % size) for i in range(size)])


def turn_all(value, axis):
    return [value] + [turn(value, axis, by) for by in range(1, lax.axis_size(axis))]


def line_parts(value, axis):
    if lax.axis_size(axis) != 4:
        parts = turn_all(value, axis)
        return parts, value
    two = turn(value, axis, 2)
    one = lax.ppermute(value, axis, [(0, 1), (1, 2), (2, 3)])
    three = lax.ppermute(value, axis, [(1, 0), (2, 1), (3, 2)])
    passed = lax.ppermute(two, axis, [(2, 3), (1, 0)])
    return [value, one, two, three], passed


def deal(parts, axis):
    return lax.all_to_all(parts, axis, 0, 0)


def cross(value, bits):
    return lax.ppermute(value, "chip", [(i, i ^ bits) for i in range(lax.axis_size("chip"))])


def cross_all(value):
    return [value] + [cross(value, bits) for bits in range(1, lax.axis_size("chip"))]


def heads_sum(piece):
    total, low = piece, piece.astype(BF16)
    bits, size = 1, lax.axis_size("head")
    while bits < size:
        arrived = lax.ppermute(low, "head", [(i, i ^ bits) for i in range(size)])
        total, low = run(
            heads_kernel, "heads", piece.size,
            [(WHOLE, piece), (WHOLE, total), (WHOLE, arrived)],
            [(WHOLE, piece.shape, F32), (WHOLE, piece.shape, BF16)],
        )
        bits *= 2
    return low


def entering(core, chip, total, backward, meanwhile, later=lambda pair: ()):
    name = "after" if backward else "before"
    chips = lax.axis_size("chip")
    channels = total.shape[1]
    half = NSTATE // 2
    partner = beside(total)
    pair = run(
        functools.partial(pair_kernel, backward), name + "_pair", total.size,
        [core, (WHOLE, total), (WHOLE, partner)] + [(LOOSE, value) for value in meanwhile],
        [(WHOLE, (half + 8, channels), F32)],
    )[0]
    prefix = run(
        functools.partial(prefix_kernel, backward, chips), name + "_prefix", chips * pair.size,
        [chip] + [(WHOLE, value) for value in cross_all(pair)]
        + [(LOOSE, value) for value in later(pair)],
        [(WHOLE, (half, channels), F32)],
    )[0]
    return run(
        functools.partial(enter_kernel, backward), name + "_enter", total.size,
        [core, (WHOLE, partner), (WHOLE, prefix), (WHOLE, beside(prefix))],
        [(WHOLE, (NSTATE, channels), F32)],
    )[0]


def sum_pieces(chip, kept, given, name, cut, paired, before_half=()):
    chips, rows, channels = kept.shape
    arrived = beside(given)
    size = chips * rows * channels
    halves = run(
        functools.partial(half_kernel, paired, chips), name + "_half", size,
        [chip, (WHOLE, kept), (WHOLE, arrived)] + [(LOOSE, mark) for mark in before_half],
        [(WHOLE, (rows, channels), F32)] + [(WHOLE, (rows, channels), BF16)] * (chips - 1),
    )
    parts = [halves[0]] + [cross(halves[bits], bits) for bits in range(1, chips)]
    return run(
        functools.partial(piece_kernel, chips, paired, cut), name + "_piece", size,
        [(WHOLE, part) for part in parts],
        [(WHOLE, (cut, channels), BF16), (WHOLE, (rows - cut, channels), F32 if paired else BF16)],
    ), halves[0]


def collect(piece, order, mark=None):
    chips = lax.axis_size("chip")
    if chips != 4 or order is None:
        found = [(value[None], (bits,)) for bits, value in enumerate(cross_all(piece))]
    else:
        near, far = order
        both = jnp.stack([piece, cross(piece, near)])
        if mark is not None:
            both = tie(both, mark)
        found = [(both, (0, near)), (cross(both, far), (far, far ^ near))]
    return [(value, beside(value), bits) for value, bits in found]


def dot(left, right):
    return jnp.dot(left, right, preferred_element_type=F32)


def dot_nt(left, right):
    return lax.dot_general(left, right, (((1,), (1,)), ((), ())), preferred_element_type=F32)


def dot_tn(left, right):
    return lax.dot_general(left, right, (((0,), (0,)), ((), ())), preferred_element_type=F32)


def split(values):
    high = values.astype(BF16)
    return high, (values - high.astype(F32)).astype(BF16)


def lower_mask():
    row = lax.broadcasted_iota(jnp.int32, (CHUNK, CHUNK), 0)
    column = lax.broadcasted_iota(jnp.int32, (CHUNK, CHUNK), 1)
    return row >= column


def spread_heads(heads, channels):
    row = lax.broadcasted_iota(jnp.int32, (heads, channels), 0) * HEAD_DIM
    place = lax.broadcasted_iota(jnp.int32, (heads, channels), 1)
    return jnp.where((place >= row) & (place < row + HEAD_DIM), 1.0, 0.0).astype(BF16)


def expand(values, channels):
    high, low = split(values)
    spread = spread_heads(values.shape[1], channels)
    return dot(high, spread) + dot(low, spread)


def decay_kernel(codes_ref, weight_ref, e_ref, f_ref, k_ref):
    heads, channels = codes_ref.shape[1], k_ref.shape[1]
    lower = jnp.where(lower_mask(), 1.0, 0.0).astype(F32)
    count = codes_ref.shape[0] // CHUNK
    line = lax.broadcasted_iota(jnp.int32, (8, heads), 0)
    marks = jnp.zeros((8, heads), F32)
    total = jnp.zeros((1, heads), F32)
    for chunk in range(count):
        rows = pl.ds(chunk * CHUNK, CHUNK)
        logs = codes_ref[rows, :].astype(F32) * (-DECAY_STEP)
        cumulative = jnp.dot(
            lower, logs, precision=lax.Precision.HIGHEST, preferred_element_type=F32
        )
        last = cumulative[CHUNK - 1 :]
        middle = 0.5 * last
        e_ref[rows, :] = jnp.exp(cumulative - middle)
        f_ref[rows, :] = weight_ref[rows, :] * jnp.exp(middle - cumulative)
        marks = jnp.where(line == chunk, jnp.exp(middle), marks)
        total = total + last
    marks = jnp.where(line == 7, total, marks)
    high, low = split(marks)
    lowest = (marks - high.astype(F32) - low.astype(F32)).astype(BF16)
    spread = spread_heads(heads, channels)
    factors = dot(high, spread) + dot(low, spread) + dot(lowest, spread)
    k_ref[...] = factors


def pair_kernel(backward, core_ref, own_ref, other_ref, *refs):
    out_ref = refs[-1]
    half = NSTATE // 2
    logs, other_logs = own_ref[NSTATE:, :], other_ref[NSTATE:, :]
    for core in range(2):

        @pl.when(core_ref[0] == core)
        def _():
            rows = slice(core * half, (core + 1) * half)
            if core == (0 if backward else 1):
                out_ref[:half, :] = jnp.exp(logs[0:1]) * other_ref[rows, :] + own_ref[rows, :]
            else:
                out_ref[:half, :] = jnp.exp(other_logs[0:1]) * own_ref[rows, :] + other_ref[rows, :]

    out_ref[half:, :] = logs + other_logs


def prefix_kernel(backward, chips, chip_ref, *refs):
    parts, out_ref = refs[:chips], refs[-1]
    half = out_ref.shape[0]
    mine = chip_ref[0]
    total = jnp.zeros(out_ref.shape, F32)
    for bits in range(1, chips):
        source = lax.bitwise_xor(mine, bits)
        span = jnp.zeros((1, out_ref.shape[1]), F32)
        for other in range(1, chips):
            middle = lax.bitwise_xor(mine, other)
            if backward:
                between = (middle < source) & (middle > mine)
            else:
                between = (middle > source) & (middle < mine)
            span = span + jnp.where(between, parts[other][half : half + 1, :], 0.0)
        passes = source > mine if backward else source < mine
        total = total + jnp.where(passes, jnp.exp(span), 0.0) * parts[bits][:half, :]
    out_ref[...] = total


def enter_kernel(backward, core_ref, partner_ref, prefix_ref, other_ref, out_ref):
    half = prefix_ref.shape[0]
    decay = jnp.exp(partner_ref[NSTATE : NSTATE + 1, :])
    for core in range(2):

        @pl.when(core_ref[0] == core)
        def _():
            for place, ref in ((core, prefix_ref), (1 - core, other_ref)):
                rows = slice(place * half, (place + 1) * half)
                if core == (0 if backward else 1):
                    out_ref[rows, :] = decay * ref[...] + partner_ref[rows, :]
                else:
                    out_ref[rows, :] = ref[...]


def taps(window, kernel, bias, begin):
    summed = bias
    for offset in range(KERNEL):
        summed = summed + kernel[offset : offset + 1] * window[begin + offset : begin + offset + CHUNK]
    return summed


def silu_parts(values):
    sigmoid = jax.nn.sigmoid(values)
    return values * sigmoid, sigmoid * (1.0 + values * (1.0 - sigmoid))


def first_step(action):
    pl.when(pl.program_id(0) == 0)(action)


def clear(*refs):
    def action():
        for ref in refs:
            ref[...] = jnp.zeros_like(ref)

    first_step(action)


def place_parts(mine, parts, target, width, value):
    size = len(parts)
    if width % 128 == 0:
        for i in range(size):
            owner = lax.rem(mine + size - i, size)
            target[:, pl.ds(pl.multiple_of(owner * width, 128), width)] = value(i)
        return

    def write(me):
        for i in range(size):
            owner = (me + size - i) % size
            target[:, owner * width : (owner + 1) * width] = value(i)

    for me in range(size):
        pl.when(mine == me)(functools.partial(write, me))


def copies_kernel(one_ref, three_ref, own_ref, out_ref):
    for i in range(out_ref.shape[0]):
        out_ref[i] = own_ref[...]


def norm_kernel(size, head_ref, passed_ref, *refs):
    parts, gains = refs[:size], refs[size : 2 * size]
    passed_gain_ref, normed_ref, scale_ref, gain_ref = refs[2 * size :]
    width = parts[0].shape[1]
    mine = head_ref[0]

    def pick(i, refs, passed):
        if size == 4 and i == 1:
            return jnp.where(mine == 0, passed[...], refs[i][...])
        if size == 4 and i == 3:
            return jnp.where(mine == 3, passed[...], refs[i][...])
        return refs[i][...]

    part = lambda i: pick(i, parts, passed_ref).astype(F32)
    gain = lambda i: pick(i, gains, passed_gain_ref)[0:1].astype(F32)
    squares = sum(jnp.sum(part(i) ** 2, axis=1, keepdims=True) for i in range(size))
    scale = lax.rsqrt(squares / (size * width) + EPSILON)
    scale_ref[...] = jnp.broadcast_to(scale, scale_ref.shape)
    place_parts(
        mine, parts, normed_ref, width,
        lambda i: (part(i) * scale_ref[:, 0:1] * gain(i)).astype(BF16),
    )
    place_parts(mine, parts, gain_ref, width, lambda i: jnp.broadcast_to(gain(i), (8, width)))


def mixed_grad_kernel(parts_ref, weight_ref, out_ref, full_ref):
    size, _, width = parts_ref.shape
    for i in range(size):
        full_ref[:, i * width : (i + 1) * width] = parts_ref[i]
    out_ref[...] = dot_nt(full_ref[...], weight_ref[...])


def out_kernel(loose_ref, mixed_ref, weight_ref, out_ref):
    width = out_ref.shape[2]
    for owner in range(out_ref.shape[0]):
        value = dot(mixed_ref[...], weight_ref[:, owner * width : (owner + 1) * width])
        out_ref[owner] = value.astype(BF16)


def conv_kernel(
    value_ref, state_ref, value_kernel_ref, value_bias_ref, state_kernel_ref, state_bias_ref,
    f_ref, k_ref, conv_ref, weighted_ref, value_slope_ref, maps_ref, state_slope_ref, total_ref,
):
    chunk = pl.program_id(0)
    clear(total_ref)
    around = pl.ds(pl.multiple_of(chunk * CHUNK, CHUNK), CHUNK + HALO)
    pre = taps(
        state_ref[around, :].astype(F32), state_kernel_ref[...].astype(F32),
        state_bias_ref[...].astype(F32), HALO - KERNEL + 1,
    )
    conv, slope = silu_parts(pre)
    maps = conv.astype(BF16)
    maps_ref[...] = maps
    state_slope_ref[...] = slope
    pre = taps(
        value_ref[around, :].astype(F32), value_kernel_ref[...].astype(F32),
        value_bias_ref[...].astype(F32), HALO - KERNEL + 1,
    )
    conv, slope = silu_parts(pre)
    conv = conv.astype(BF16)
    conv_ref[...] = conv
    value_slope_ref[...] = slope
    weighted = (conv.astype(F32) * expand(f_ref[...], conv.shape[1])).astype(BF16)
    weighted_ref[...] = weighted
    factor = k_ref[pl.ds(chunk, 1), :]
    total_ref[:NSTATE, :] = factor * (
        factor * total_ref[:NSTATE, :] + dot_tn(maps[:, :NSTATE], weighted)
    )
    total_ref[NSTATE:, :] = jnp.broadcast_to(k_ref[7:8, :], (8, k_ref.shape[1]))


def mixer_kernel(
    state_in_ref, maps_ref, weighted_ref, conv_ref, e_ref, k_ref, skip_ref, gate_ref, grad_ref, gain_ref,
    mixer_ref, stats_ref, high_ref, low_ref, state_ref,
):
    chunk = pl.program_id(0)

    def start():
        state_ref[...] = state_in_ref[...]

    first_step(start)
    lane = lax.broadcasted_iota(jnp.int32, (CHUNK, CHUNK), 1)
    factor = k_ref[pl.ds(chunk, 1), :]
    input_map, output_map = maps_ref[:, :NSTATE], maps_ref[:, NSTATE:]
    weighted = weighted_ref[...]
    scaled = factor * state_ref[...]
    high, low = split(scaled)
    high_ref[0], low_ref[0] = high, low
    scores = jnp.where(lower_mask(), dot_nt(output_map, input_map), 0.0).astype(BF16)
    mixed = dot(
        jnp.concatenate([scores, output_map], axis=1), jnp.concatenate([weighted, high], axis=0)
    )
    mixed = mixed + dot(output_map, low)
    mixer = expand(e_ref[...], weighted.shape[1]) * mixed + skip_ref[...] * conv_ref[...].astype(F32)
    mixer_ref[...] = mixer
    gate = gate_ref[...]
    gated = mixer * (gate * jax.nn.sigmoid(gate))
    squares = jnp.sum(gated * gated, axis=1, keepdims=True)
    products = jnp.sum(gated * (grad_ref[...] * gain_ref[...].astype(F32)), axis=1, keepdims=True)
    sums = jnp.where(lane == 0, squares, jnp.where(lane == 1, products, 0.0))
    stats_ref[...] = sums.T[:8]
    state_ref[...] = factor * (scaled + dot_tn(input_map, weighted))


def column(row_block):
    rest = jnp.zeros((CHUNK - row_block.shape[0], CHUNK), F32)
    return jnp.concatenate([row_block, rest], axis=0).T


def row_of(sums):
    lane = lax.broadcasted_iota(jnp.int32, (CHUNK, CHUNK), 1)
    return jnp.where(lane == 0, sums, 0.0).T[:8]


def gate_kernel(
    inner, chunks, size, *refs
):
    stats_refs = refs[:size]
    (
        mixer_ref, gate_ref, grad_ref, gain_ref, conv_ref, e_ref, k_ref, maps_ref,
        mixed_ref, gate_grad_ref, mixer_grad_ref, small_ref, total_ref, cross_ref,
    ) = refs[size:]
    chunk = chunks - 1 - pl.program_id(0)
    clear(small_ref, total_ref)
    gain = gain_ref[...].astype(F32)
    stats = column(sum(ref[...] for ref in stats_refs))
    scale = lax.rsqrt(stats[:, 0:1] / inner + EPSILON)
    cross_term = stats[:, 1:2] * (scale * scale * scale) / inner
    gate = gate_ref[...]
    silu, slope = silu_parts(gate)
    mixer = mixer_ref[...]
    gated = mixer * silu
    normed = gated * scale
    mixed_ref[...] = (normed * gain).astype(BF16)
    grad = grad_ref[...]
    gated_grad = scale * (grad * gain) - gated * cross_term
    gate_grad = (gated_grad * mixer * slope).astype(BF16)
    gate_grad_ref[...] = gate_grad
    cross_ref[...] = row_of(jnp.sum(gate_grad.astype(F32) * gate, axis=1, keepdims=True))
    mixer_grad = gated_grad * silu
    mixer_grad_ref[...] = mixer_grad
    small_ref[0:1, :] += jnp.sum(grad * normed, axis=0, keepdims=True)
    small_ref[1:2, :] += jnp.sum(mixer_grad * conv_ref[...].astype(F32), axis=0, keepdims=True)
    high, low = split(expand(e_ref[...], grad.shape[1]) * mixer_grad)
    output_map = maps_ref[:, NSTATE:]
    factor = k_ref[pl.ds(chunk, 1), :]
    total_ref[:NSTATE, :] = factor * (
        factor * total_ref[:NSTATE, :] + (dot_tn(output_map, high) + dot_tn(output_map, low))
    )
    total_ref[NSTATE:, :] = jnp.broadcast_to(k_ref[7:8, :], (8, k_ref.shape[1]))


def back_kernel(
    chunks, early_ref, state_in_ref, mixer_grad_ref, e_ref, f_ref, k_ref, weighted_ref, high_ref, low_ref,
    maps_ref, value_slope_ref, state_slope_ref, skip_ref,
    value_ref, map_ref, state_ref,
):
    chunk = chunks - 1 - pl.program_id(0)

    def start():
        state_ref[...] = state_in_ref[...]

    first_step(start)
    lower = lower_mask()
    row = lax.broadcasted_iota(jnp.int32, (CHUNK, CHUNK), 0)
    upper = row <= lax.broadcasted_iota(jnp.int32, (CHUNK, CHUNK), 1)
    factor = k_ref[pl.ds(chunk, 1), :]
    input_map, output_map = maps_ref[:, :NSTATE], maps_ref[:, NSTATE:]
    weighted = weighted_ref[...]
    mixer_grad = mixer_grad_ref[...]
    high, low = split(expand(e_ref[...], weighted.shape[1]) * mixer_grad)
    scaled = factor * state_ref[...]
    state_high, state_low = split(scaled)
    both = jnp.concatenate([weighted, high_ref[0]], axis=0)
    sums = dot_nt(high, both) + dot_nt(low, both)
    score_grad = jnp.where(lower, sums[:, :CHUNK], 0.0).astype(BF16)
    output_grad = sums[:, CHUNK:] + dot_nt(high, low_ref[0]) + dot(score_grad, input_map)
    sums = dot_nt(weighted, jnp.concatenate([state_high, state_low], axis=0))
    input_grad = sums[:, :NSTATE] + sums[:, NSTATE:] + dot_tn(score_grad, output_map)
    scores = jnp.where(upper, dot_nt(input_map, output_map), 0.0).astype(BF16)
    grads = dot(
        jnp.concatenate([scores, input_map], axis=1), jnp.concatenate([high, state_high], axis=0)
    )
    decayed = expand(f_ref[...], weighted.shape[1]) * grads
    value_ref[...] = (decayed + skip_ref[...] * mixer_grad) * value_slope_ref[...]
    slope = state_slope_ref[...]
    map_ref[:, :NSTATE] = input_grad * slope[:, :NSTATE]
    map_ref[:, NSTATE:] = output_grad * slope[:, NSTATE:]
    state_ref[...] = factor * (scaled + (dot_tn(output_map, high) + dot_tn(output_map, low)))


def conv_back_kernel(
    chunks, value_ref, map_ref, after_ref, value_raw_ref, state_raw_ref, value_kernel_ref,
    state_kernel_ref, cross_in_ref,
    value_grad_ref, state_grad_ref, value_small_ref, state_small_ref, cross_ref, value_next_ref,
    state_next_ref,
):
    chunk = chunks - 1 - pl.program_id(0)
    channels = value_ref.shape[1]
    clear(value_small_ref, state_small_ref)

    def start():
        value_next_ref[...] = after_ref[:, :channels]
        state_next_ref[...] = after_ref[:, channels:]

    first_step(start)

    def back(slope_ref, next_ref, raw_ref, kernel_ref, grad_ref, small_ref):
        kernel = kernel_ref[...].astype(F32)
        slope = slope_ref[...]
        window = jnp.concatenate([slope, next_ref[...]], axis=0)
        around = pl.ds(pl.multiple_of(chunk * CHUNK, CHUNK), CHUNK + HALO)
        raw = raw_ref[around, :].astype(F32)
        grad = jnp.zeros_like(slope)
        for offset in range(KERNEL):
            back_by = KERNEL - 1 - offset
            grad = grad + kernel[offset : offset + 1] * window[back_by : back_by + CHUNK]
            begin = HALO - KERNEL + 1 + offset
            small_ref[offset : offset + 1, :] += jnp.sum(
                slope * raw[begin : begin + CHUNK], axis=0, keepdims=True
            )
        small_ref[KERNEL : KERNEL + 1, :] += jnp.sum(slope, axis=0, keepdims=True)
        grad = grad.astype(BF16)
        grad_ref[...] = grad
        next_ref[...] = slope[:8]
        return jnp.sum(grad.astype(F32) * raw[HALO:], axis=1, keepdims=True)

    crossed = back(map_ref, state_next_ref, state_raw_ref, state_kernel_ref, state_grad_ref, state_small_ref)
    crossed = crossed + back(
        value_ref, value_next_ref, value_raw_ref, value_kernel_ref, value_grad_ref, value_small_ref
    )
    cross_ref[...] = cross_in_ref[...] + row_of(crossed)


def normed_kernel(
    chunks, late_ref, gate_grad_ref, value_grad_ref, state_grad_ref, gate_weight_ref, value_weight_ref,
    state_weight_ref, cross_ref, out_ref
):
    value = (
        dot_nt(gate_grad_ref[...], gate_weight_ref[...])
        + dot_nt(value_grad_ref[...], value_weight_ref[...])
        + dot_nt(state_grad_ref[...], state_weight_ref[...])
    )
    count = value.shape[0]
    out_ref[0, :count, :] = value.astype(BF16)
    line = lax.broadcasted_iota(jnp.int32, (HALO, CHUNK), 0)
    packed = jnp.zeros((HALO, CHUNK), F32)
    for chunk in range(chunks):
        row = cross_ref[0:1, chunk * CHUNK : (chunk + 1) * CHUNK]
        high = row.astype(BF16).astype(F32)
        packed = jnp.where(line == chunk, high, packed)
        packed = jnp.where(line == chunks + chunk, row - high, packed)
    out_ref[0, count:, :] = jnp.zeros((HALO, value.shape[1]), BF16)
    out_ref[0, count:, :CHUNK] = packed.astype(BF16)


def last_kernel(full_width, parts_ref, tokens_ref, scale_ref, gain_ref, cotangent_ref, out_ref):
    count = tokens_ref.shape[0]
    chunks = count // CHUNK
    size = parts_ref.shape[0]
    crossed = sum(parts_ref[i, count:, :CHUNK].astype(F32) for i in range(size))
    crossed = crossed[:chunks] + crossed[chunks : 2 * chunks]
    for chunk in range(chunks):
        rows = slice(chunk * CHUNK, (chunk + 1) * CHUNK)
        normed_grad = sum(parts_ref[i, rows, :].astype(F32) for i in range(size))
        scale = scale_ref[HALO + chunk * CHUNK : HALO + (chunk + 1) * CHUNK, 0:1]
        total = column(jnp.broadcast_to(crossed[chunk : chunk + 1], (8, CHUNK)))[:, 0:1]
        out_ref[rows, :] = (
            scale * gain_ref[...].astype(F32) * normed_grad
            - tokens_ref[rows, :].astype(F32) * (scale * scale * total / full_width)
            + cotangent_ref[rows, :].astype(F32)
        ).astype(BF16)


def store_piece(core_ref, kept_ref, given_ref, place, begin, piece):
    chips = kept_ref.shape[0]
    core, chip = place // chips, lax.rem(place, chips)
    rows = slice(begin, begin + piece.shape[0])
    piece = piece.astype(BF16)

    @pl.when(core_ref[0] == core)
    def _():
        kept_ref[chip, rows, :] = piece

    @pl.when(core_ref[0] != core)
    def _():
        given_ref[chip, rows, :] = piece


def gain_row(weight, block):
    sums = jnp.sum(weight.astype(F32) * block, axis=1, keepdims=True)
    lane = lax.broadcasted_iota(jnp.int32, (CHUNK, CHUNK), 1)
    rows = [
        jnp.where(lane == 0, sums[i : i + CHUNK], 0.0).T[0:1] for i in range(0, BLOCK, CHUNK)
    ]
    return jnp.concatenate(rows, axis=1)


def early_kernel(
    loose_ref, core_ref, normed_ref, gate_ref, mixed_ref, grad_ref, weight_ref,
    kept_ref, given_ref, gain_ref, held_ref
):
    chips, rows, channels = kept_ref.shape
    at = pl.program_id(0)
    count, width = grad_ref.shape
    pieces = 2 * chips
    step = width // pieces
    out_rows = channels // pieces
    out_blocks = channels // BLOCK
    every = width // BLOCK // out_blocks

    @pl.when(lax.rem(at, every) == 0)
    def _():
        held_ref[...] = dot_tn(mixed_ref[...], grad_ref[...])

    block = dot_tn(normed_ref[HALO : HALO + count, :], gate_ref[...])
    gain_ref[...] = gain_row(weight_ref[...], block)
    for i in range(BLOCK // step):
        place = at * (BLOCK // step) + i
        begin = lax.rem(at, every) * (BLOCK // step * out_rows) + i * out_rows
        own = held_ref[pl.ds(pl.multiple_of(begin, 8), out_rows), :]
        parts = [block[i * step : (i + 1) * step]]
        parts += [own[:, j : j + channels] for j in range(0, width, channels)]
        store_piece(core_ref, kept_ref, given_ref, place, 0, jnp.concatenate(parts, axis=0))


def late_kernel(
    early_ref, core_ref, normed_ref, value_ref, state_ref, value_small_ref, gate_small_ref, gain_ref,
    state_small_ref, value_weight_ref, state_weight_ref, gain_full_ref,
    kept_ref, given_ref, own_ref, shared_ref, gains_ref,
):
    chips, rows, channels = kept_ref.shape
    at = pl.program_id(0)
    count, maps_width = state_ref.shape
    width = gains_ref.shape[1]
    pieces = 2 * chips
    step = width // pieces
    lanes = channels // 128
    part = 2 * step // lanes
    columns = normed_ref[HALO : HALO + count, :]
    value = dot_tn(columns, value_ref[...])
    state = dot_tn(columns, state_ref[...])
    gain = (
        gain_ref[...] + gain_row(value_weight_ref[...], value) + gain_row(state_weight_ref[...], state)
    ) / gain_full_ref[0:1, :]
    gains_ref[0:1, pl.ds(pl.multiple_of(at * BLOCK, 128), BLOCK)] = gain
    for i in range(BLOCK // step):
        piece = slice(i * step, (i + 1) * step)
        stacked = jnp.concatenate([state[piece, :128], state[piece, 128:]], axis=0)
        stacked = jnp.concatenate(
            [stacked[j * part : (j + 1) * part] for j in range(lanes)], axis=1
        )
        store_piece(
            core_ref, kept_ref, given_ref, at * (BLOCK // step) + i, 0,
            jnp.concatenate([value[piece], stacked], axis=0),
        )

    @pl.when(at == width // BLOCK - 1)
    def _():
        own_ref[...] = jnp.zeros_like(own_ref)
        own_ref[: KERNEL + 1, :] = value_small_ref[: KERNEL + 1, :]
        own_ref[KERNEL + 1 : KERNEL + 3, :] = gate_small_ref[:2, :]
        shared_ref[...] = jnp.zeros_like(shared_ref)
        begin = width // channels
        for i in range(begin):
            shared_ref[i : i + 1, :] = gains_ref[0:1, i * channels : (i + 1) * channels]
        for i in range(0, (KERNEL + 1) * maps_width, 128):
            tap, column_from = divmod(i, maps_width)
            row, column_to = divmod(i, channels)
            shared_ref[begin + row : begin + row + 1, column_to : column_to + 128] = state_small_ref[
                tap : tap + 1, column_from : column_from + 128
            ]
        line = lax.broadcasted_iota(jnp.int32, (HALO, channels), 0)
        for place in range(pieces):
            own, shared = own_ref[place : place + 1, :], shared_ref[place : place + 1, :]
            own_high, shared_high = (v.astype(BF16).astype(F32) for v in (own, shared))
            small = jnp.zeros((HALO, channels), F32)
            for to, value in enumerate((own_high, own - own_high, shared_high, shared - shared_high)):
                small = jnp.where(line == to, value, small)
            store_piece(core_ref, kept_ref, given_ref, place, step + part, small)


def merge_pairs(block):
    tail = block[-HALO:]
    line = lax.broadcasted_iota(jnp.int32, tail.shape, 0)
    own, shared = tail[0:1] + tail[1:2], tail[2:3] + tail[3:4]
    own_high, shared_high = own.astype(BF16).astype(F32), shared.astype(BF16).astype(F32)
    new = jnp.zeros_like(tail)
    for at, value in enumerate((own_high, own - own_high, shared_high, shared - shared_high)):
        new = jnp.where(line == at, value, new)
    return jnp.concatenate([block[:-HALO], new], axis=0)


def heads_kernel(piece_ref, total_ref, arrived_ref, out_ref, low_ref):
    total = merge_pairs(total_ref[...] + arrived_ref[...].astype(F32))
    line = lax.broadcasted_iota(jnp.int32, total.shape, 0)
    first = total.shape[0] - HALO
    own = (line >= first) & (line < first + 2)
    out_ref[...] = total
    low_ref[...] = jnp.where(own, piece_ref[...], total).astype(BF16)


def half_kernel(paired, chips, chip_ref, kept_ref, arrived_ref, *refs):
    outs = refs[-chips:]
    for bits in range(chips):
        place = lax.bitwise_xor(chip_ref[0], bits)
        value = kept_ref[place].astype(F32) + arrived_ref[place].astype(F32)
        if paired:
            value = merge_pairs(value)
        outs[bits][...] = value.astype(outs[bits].dtype)


def piece_kernel(parts, paired, cut, *refs):
    total = sum(ref[...].astype(F32) for ref in refs[:parts])
    first_ref, last_ref = refs[parts:]
    first_ref[...] = total[:cut].astype(BF16)
    last_ref[...] = merge_pairs(total[cut:]) if paired else total[cut:].astype(BF16)


def each_piece(core_ref, chip_ref, chips, groups, refs):
    refs = iter(refs)
    for part, bits_lists in enumerate(groups):
        number = 0
        for bits_list in bits_lists:
            for core, ref in ((core_ref[0], next(refs)), (1 - core_ref[0], next(refs))):
                for at, bits in enumerate(bits_list):
                    place = core * chips + lax.bitwise_xor(chip_ref[0], bits)
                    yield part, number, place, ref[at].astype(F32)
                    number += 1


def send_rows(buffer_ref, number, target_ref, place, sem_ref):
    rows = buffer_ref.shape[1]
    copy = pltpu.make_async_copy(
        buffer_ref.at[number],
        target_ref.at[pl.ds(pl.multiple_of(place * rows, 8), rows), :],
        sem_ref.at[number],
    )
    copy.start()
    return copy


def early_out_kernel(chips, groups, core_ref, chip_ref, *refs):
    gate_ref, output_ref, gate_buffer, output_buffer, gate_sems, output_sems = refs[-6:]
    out_rows, width = output_buffer.shape[1:]
    channels = gate_buffer.shape[2]
    copies = []
    for part, number, place, value in each_piece(core_ref, chip_ref, chips, groups, refs[:-6]):
        if part == 0:
            gate_buffer[number] = value
            copies.append(send_rows(gate_buffer, number, gate_ref, place, gate_sems))
        else:
            output_buffer[number] = jnp.concatenate(
                [value[i * out_rows : (i + 1) * out_rows] for i in range(width // channels)], axis=1
            )
            copies.append(send_rows(output_buffer, number, output_ref, place, output_sems))
    for copy in copies:
        copy.wait()


def late_out_kernel(chips, groups, core_ref, chip_ref, *refs):
    value_ref, buffer, sems = refs[-3:]
    copies = []
    for _, number, place, value in each_piece(core_ref, chip_ref, chips, groups, refs[:-3]):
        buffer[number] = value
        copies.append(send_rows(buffer, number, value_ref, place, sems))
    for copy in copies:
        copy.wait()


def shared_out_kernel(chips, groups, size, core_ref, chip_ref, head_ref, loose_ref, *refs):
    (
        state_ref, value_kernel_ref, value_bias_ref, state_kernel_ref, state_bias_ref, skip_ref,
        gated_ref, gain_ref, buffer, sems, own_ref, shared_ref,
    ) = refs[-12:]
    step, maps_width = buffer.shape[1:]
    channels = own_ref.shape[1]
    lanes = channels // 128
    rows = 2 * step // lanes
    copies = []
    for _, number, place, piece in each_piece(core_ref, chip_ref, chips, groups, refs[:-12]):
        stacked = jnp.concatenate(
            [piece[:rows, i * 128 : (i + 1) * 128] for i in range(lanes)], axis=0
        )
        buffer[number] = jnp.concatenate([stacked[:step], stacked[step:]], axis=1)
        copies.append(send_rows(buffer, number, state_ref, place, sems))
        own_ref[pl.ds(place, 1), :] = piece[rows : rows + 1] + piece[rows + 1 : rows + 2]
        shared_ref[pl.ds(place, 1), :] = piece[rows + 2 : rows + 3] + piece[rows + 3 : rows + 4]
    value_kernel_ref[...] = own_ref[:KERNEL, :]
    value_bias_ref[...] = own_ref[KERNEL, :]
    gated_ref[...] = own_ref[KERNEL + 1, :]
    heads = skip_ref.shape[0]
    at = lax.broadcasted_iota(jnp.int32, (heads, channels), 1)
    row = lax.broadcasted_iota(jnp.int32, (heads, channels), 0) * HEAD_DIM
    inside = (at >= row) & (at < row + HEAD_DIM)
    skip_ref[...] = jnp.sum(jnp.where(inside, own_ref[KERNEL + 2 : KERNEL + 3, :], 0.0), axis=1)
    own_width = gain_ref.shape[0]
    gain_rows = -(-own_width * size // channels)
    for head in range(size):
        row, begin = divmod(head * own_width, channels)

        @pl.when(head_ref[0] == head)
        def _(row=row, begin=begin):
            gain_ref[...] = shared_ref[row, begin : begin + own_width]

    for i in range(0, (KERNEL + 1) * maps_width, 128):
        tap, column_to = divmod(i, maps_width)
        row, column_from = divmod(i, channels)
        value = shared_ref[gain_rows + row : gain_rows + row + 1, column_from : column_from + 128]
        if tap < KERNEL:
            state_kernel_ref[tap : tap + 1, column_to : column_to + 128] = value
        else:
            state_bias_ref[column_to : column_to + 128] = value[0]
    for copy in copies:
        copy.wait()


SCALAR = "scalar"
WHOLE = "whole"
BLOCKED = "blocked"
LANES = "lanes"
LEADING = "leading"
LOOSE = "loose"


def run(kernel, name, flops, args, outs, steps=None, backward=False, scratch=()):
    at = (lambda i: steps - 1 - i) if backward else (lambda i: i)

    def spec(kind, shape):
        if isinstance(kind, int):
            return pl.BlockSpec((kind,) + shape[1:], lambda i: (at(i), 0))
        if kind == SCALAR:
            return pl.BlockSpec(memory_space=pltpu.SMEM)
        if kind == LOOSE:
            return pl.BlockSpec(memory_space=pl.ANY)
        if isinstance(kind, tuple):
            return pl.BlockSpec(*kind)
        if steps is None:
            return pl.BlockSpec(memory_space=pltpu.VMEM)
        if kind == BLOCKED:
            return pl.BlockSpec((CHUNK, shape[1]), lambda i: (at(i), 0))
        if kind == LANES:
            return pl.BlockSpec((shape[0], CHUNK), lambda i: (0, at(i)))
        if kind == LEADING:
            return pl.BlockSpec((1,) + shape[1:], lambda i: (at(i),) + (0,) * (len(shape) - 1))
        return pl.BlockSpec(shape, lambda i: (0,) * len(shape))

    moved = sum(a.size * a.dtype.itemsize for kind, a in args if kind != LOOSE)
    shapes = [jax.ShapeDtypeStruct(shape, dtype) for _, shape, dtype in outs]
    moved += sum(a.size * a.dtype.itemsize for a in shapes)
    return pl.pallas_call(
        kernel,
        out_shape=shapes,
        in_specs=[spec(kind, a.shape) for kind, a in args],
        out_specs=[spec(kind, shape) for kind, shape, _ in outs],
        scratch_shapes=list(scratch),
        compiler_params=pltpu.CompilerParams(vmem_limit_bytes=VMEM_LIMIT),
        cost_estimate=pl.CostEstimate(flops=flops, bytes_accessed=moved, transcendentals=0),
        name=name,
        **({} if steps is None else {"grid": (steps,)}),
    )(*(a for _, a in args))


def per_device(
    tokens, decay_codes, norm_gain, gate_weight, value_weight, state_weight, value_kernel, value_bias,
    state_kernel, state_bias, skip_scale, gated_gain, output_weight, cotangent,
):
    tokens, decay_codes, cotangent = tokens[0], decay_codes[0], cotangent[0]
    count, own_width = tokens.shape
    heads = skip_scale.shape[0]
    channels = heads * HEAD_DIM
    head_size, chips = lax.axis_size("head"), lax.axis_size("chip")
    seq_size = 2 * chips
    width = own_width * head_size
    maps_width = 2 * NSTATE
    chunks = count // CHUNK
    core = (SCALAR, lax.axis_index("core").astype(jnp.int32)[None])
    chip = (SCALAR, lax.axis_index("chip").astype(jnp.int32)[None])
    head = (SCALAR, lax.axis_index("head").astype(jnp.int32)[None])

    rows = count + MARGIN
    packed = jnp.concatenate(
        [
            from_behind(tokens[-HALO:], 1),
            tokens,
            jnp.broadcast_to(norm_gain[None], (MARGIN - HALO, own_width)),
        ],
        axis=0,
    )
    logs = decay_codes.astype(F32) * (-DECAY_STEP)
    input_weight = jnp.sqrt(-jnp.expm1(2.0 * logs))
    e_full, f_full, factors = run(
        decay_kernel, "decays", count * channels * 200,
        [(WHOLE, decay_codes), (WHOLE, input_weight)],
        [
            (WHOLE, (count, heads), F32),
            (WHOLE, (count, heads), F32),
            (WHOLE, (8, channels), F32),
        ],
    )
    parts, passed = line_parts(packed, "head")
    cotangent_parts = deal(
        run(
            copies_kernel, "copies", 1,
            [(LOOSE, parts[1]), (LOOSE, parts[-1]), (WHOLE, cotangent)],
            [(WHOLE, (head_size, count, own_width), BF16)],
        )[0],
        "head",
    )
    skip_full = jnp.repeat(skip_scale, HEAD_DIM)[None]

    half = rows // 2
    gain_rows = ((MARGIN - HALO, own_width), lambda i: ((HALO + count) // (MARGIN - HALO), 0))
    normed, scale_in, gain_full = run(
        functools.partial(norm_kernel, head_size), "norm", count * width * 10,
        [head, (half, passed)] + [(half, part) for part in parts]
        + [(gain_rows, part) for part in parts] + [(gain_rows, passed)],
        [(half, (rows, width), BF16), (half, (rows, 128), F32), (WHOLE, (8, width), F32)],
        steps=2,
    )
    value_raw = dot(normed, value_weight).astype(BF16)
    state_raw = dot(normed, state_weight).astype(BF16)
    conv, weighted, value_slope, maps, map_slope, local_end = run(
        conv_kernel, "conv", count * channels * 400,
        [
            (WHOLE, value_raw), (WHOLE, state_raw), (WHOLE, value_kernel), (WHOLE, value_bias[None]),
            (WHOLE, state_kernel), (WHOLE, state_bias[None]), (BLOCKED, f_full), (WHOLE, factors),
        ],
        [
            (BLOCKED, (count, channels), BF16),
            (BLOCKED, (count, channels), BF16),
            (BLOCKED, (count, channels), F32),
            (BLOCKED, (count, maps_width), BF16),
            (BLOCKED, (count, maps_width), F32),
            (WHOLE, (NSTATE + 8, channels), F32),
        ],
        steps=chunks,
    )
    gate_pre = dot(normed, gate_weight)[HALO : HALO + count]
    state_in = entering(core, chip, local_end, False, (gate_pre,))
    mixed_grad, full_cotangent = run(
        mixed_grad_kernel, "mixed_grad", 2 * count * width * channels,
        [(WHOLE, cotangent_parts), (WHOLE, output_weight)],
        [(WHOLE, (count, channels), F32), (WHOLE, (count, width), BF16)],
    )
    mixer, stats, high, low = run(
        mixer_kernel, "mixer", count * channels * 1000,
        [
            (WHOLE, state_in), (BLOCKED, maps), (BLOCKED, weighted), (BLOCKED, conv),
            (BLOCKED, e_full), (WHOLE, factors), (WHOLE, skip_full), (BLOCKED, gate_pre),
            (BLOCKED, mixed_grad), (WHOLE, gated_gain[None]),
        ],
        [
            (BLOCKED, (count, channels), F32),
            (LANES, (8, count), F32),
            (LEADING, (chunks, NSTATE, channels), BF16),
            (LEADING, (chunks, NSTATE, channels), BF16),
        ],
        steps=chunks,
        scratch=[pltpu.VMEM((NSTATE, channels), F32)],
    )
    mixed, gate_grad, mixer_grad, gate_small, start_grad, gate_cross = run(
        functools.partial(gate_kernel, float(channels * head_size), chunks, head_size),
        "gate", count * channels * 600,
        [(LANES, part) for part in turn_all(stats, "head")]
        + [
            (BLOCKED, mixer), (BLOCKED, gate_pre), (BLOCKED, mixed_grad), (WHOLE, gated_gain[None]),
            (BLOCKED, conv), (BLOCKED, e_full), (WHOLE, factors), (BLOCKED, maps),
        ],
        [
            (BLOCKED, (count, channels), BF16),
            (BLOCKED, (count, channels), BF16),
            (BLOCKED, (count, channels), F32),
            (WHOLE, (8, channels), F32),
            (WHOLE, (NSTATE + 8, channels), F32),
            (LANES, (8, count), F32),
        ],
        steps=chunks,
        backward=True,
    )
    step, out_rows = width // seq_size, channels // seq_size
    early_rows = step + out_rows * (width // channels)
    features = width // BLOCK
    feature_block = ((rows, BLOCK), lambda i: (0, i))
    every = features // (channels // BLOCK)
    out_parts = run(
        out_kernel, "out", 2 * count * channels * width,
        [(LOOSE, start_grad), (WHOLE, mixed), (WHOLE, output_weight)],
        [(WHOLE, (head_size, count, own_width), BF16)],
    )[0]
    early_made = []

    def make_early(pair):
        early_made.extend(
            run(
                early_kernel, "early", 4 * count * channels * width,
                [
                    (LOOSE, pair), core, (feature_block, normed), (WHOLE, gate_grad),
                    (((count, BLOCK), lambda i: (0, i // every)), mixed), (WHOLE, full_cotangent),
                    (BLOCK, gate_weight),
                ],
                [(WHOLE, (chips, early_rows, channels), BF16)] * 2
                + [(((1, BLOCK), lambda i: (0, i)), (1, width), F32)],
                steps=features,
                scratch=[pltpu.VMEM((BLOCK, width), F32)],
            )
        )
        return early_made[1:2]

    grad_after = entering(core, chip, start_grad, True, (out_parts,), make_early)
    early_kept, early_given, early_gain = early_made
    (early_gate, early_out), half_mark = sum_pieces(
        chip, early_kept, early_given, "early", step, False
    )
    branch = jnp.sum(deal(out_parts, "head").astype(F32), axis=0)
    block_out = (tokens.astype(F32) + branch).astype(BF16)

    value_grads, map_grads = run(
        functools.partial(back_kernel, chunks), "back", count * channels * 2000,
        [
            (LOOSE, half_mark), (WHOLE, grad_after), (BLOCKED, mixer_grad), (BLOCKED, e_full),
            (BLOCKED, f_full), (WHOLE, factors), (BLOCKED, weighted), (LEADING, high),
            (LEADING, low), (BLOCKED, maps), (BLOCKED, value_slope), (BLOCKED, map_slope),
            (WHOLE, skip_full),
        ],
        [(BLOCKED, (count, channels), F32), (BLOCKED, (count, maps_width), F32)],
        steps=chunks,
        backward=True,
        scratch=[pltpu.VMEM((NSTATE, channels), F32)],
    )
    after = from_behind(jnp.concatenate([value_grads[:8], map_grads[:8]], axis=1), -1)
    value_raw_grad, state_raw_grad, value_small, state_small, crossed = run(
        functools.partial(conv_back_kernel, chunks), "conv_back", count * channels * 100,
        [
            (BLOCKED, value_grads), (BLOCKED, map_grads), (WHOLE, after),
            (WHOLE, value_raw), (WHOLE, state_raw), (WHOLE, value_kernel), (WHOLE, state_kernel),
            (LANES, gate_cross),
        ],
        [
            (BLOCKED, (count, channels), BF16),
            (BLOCKED, (count, maps_width), BF16),
            (WHOLE, (8, channels), F32),
            (WHOLE, (8, maps_width), F32),
            (LANES, (8, count), F32),
        ],
        steps=chunks,
        backward=True,
        scratch=[pltpu.VMEM((8, channels), F32), pltpu.VMEM((8, maps_width), F32)],
    )
    lanes = channels // 128
    state_rows = 2 * step // lanes
    late_rows = step + state_rows + HALO
    late_kept, late_given = run(
        late_kernel, "late", 3 * count * channels * width,
        [
            (LOOSE, early_gate), core, (feature_block, normed), (WHOLE, value_raw_grad),
            (WHOLE, state_raw_grad),
            (WHOLE, value_small), (WHOLE, gate_small), (((1, BLOCK), lambda i: (0, i)), early_gain),
            (WHOLE, state_small), (BLOCK, value_weight), (BLOCK, state_weight),
            (((8, BLOCK), lambda i: (0, i)), gain_full),
        ],
        [(WHOLE, (chips, late_rows, channels), BF16)] * 2,
        steps=features,
        scratch=[
            pltpu.VMEM((HALO, channels), F32),
            pltpu.VMEM((HALO, channels), F32),
            pltpu.VMEM((8, width), F32),
        ],
    )
    normed_parts = run(
        functools.partial(normed_kernel, chunks), "normed", 4 * count * channels * width,
        [
            (LOOSE, late_given), (WHOLE, gate_grad), (WHOLE, value_raw_grad),
            (WHOLE, state_raw_grad), (own_width, gate_weight), (own_width, value_weight),
            (own_width, state_weight), (WHOLE, crossed),
        ],
        [(LEADING, (head_size, count + HALO, own_width), BF16)],
        steps=head_size,
    )[0]
    (late_piece, shared_piece), late_mark = sum_pieces(
        chip, late_kept, late_given, "late", step, True, (normed_parts,)
    )
    normed_parts = deal(normed_parts, "head")
    shared_piece = heads_sum(shared_piece)

    def unpack(kernel, name, pieces, outs, flops, scratch, extra=(), args=()):
        groups = [collect(*piece) for piece in pieces]
        bits = [[found[2] for found in group] for group in groups]
        arrays = [(WHOLE, value) for group in groups for found in group for value in found[:2]]
        return run(
            functools.partial(kernel, chips, bits, *extra), name, flops,
            [core, chip, *args] + arrays, outs, scratch=scratch,
        )

    sems = pltpu.SemaphoreType.DMA((seq_size,))
    gate_weight_gradient, output_weight_gradient = unpack(
        early_out_kernel, "early_out",
        [(early_gate, (2, 1), late_mark), (early_out, (1, 2), late_mark)],
        [(LOOSE, (width, channels), F32), (LOOSE, (channels, width), F32)], 4 * channels * width,
        [
            pltpu.VMEM((seq_size, step, channels), F32),
            pltpu.VMEM((seq_size, out_rows, width), F32),
            sems,
            sems,
        ],
    )
    value_weight_gradient = unpack(
        late_out_kernel, "late_out", [(late_piece, None)],
        [(LOOSE, (width, channels), F32)], 2 * channels * width,
        [pltpu.VMEM((seq_size, step, channels), F32), sems],
    )[0]
    (
        state_weight_gradient, value_kernel_gradient, value_bias_gradient, state_kernel_gradient,
        state_bias_gradient, skip_scale_gradient, gated_gain_gradient, norm_gain_gradient,
    ) = unpack(
        shared_out_kernel, "shared_out", [(shared_piece, (2, 1))],
        [
            (LOOSE, (width, maps_width), F32),
            (WHOLE, (KERNEL, channels), F32),
            (WHOLE, (channels,), F32),
            (WHOLE, (KERNEL, maps_width), F32),
            (WHOLE, (maps_width,), F32),
            (WHOLE, (heads,), F32),
            (WHOLE, (channels,), F32),
            (WHOLE, (own_width,), F32),
        ],
        2 * maps_width * width,
        [
            pltpu.VMEM((seq_size, step, maps_width), F32),
            sems,
            pltpu.VMEM((HALO, channels), F32),
            pltpu.VMEM((HALO, channels), F32),
        ],
        extra=(head_size,),
        args=[head, (LOOSE, gate_weight_gradient)],
    )
    tokens_gradient = run(
        functools.partial(last_kernel, float(width)), "last", count * own_width * 20,
        [
            (WHOLE, normed_parts), (WHOLE, tokens), (WHOLE, scale_in),
            (WHOLE, norm_gain[None]), (WHOLE, cotangent),
        ],
        [(WHOLE, (count, own_width), BF16)],
    )[0]
    return (
        block_out[None],
        tokens_gradient[None],
        norm_gain_gradient,
        gate_weight_gradient,
        value_weight_gradient,
        state_weight_gradient,
        value_kernel_gradient,
        value_bias_gradient,
        state_kernel_gradient,
        state_bias_gradient,
        skip_scale_gradient,
        gated_gain_gradient,
        output_weight_gradient,
    )


def solution(mesh):
    seq_size, head_size = mesh.shape["seq"], mesh.shape["head"]
    mesh = Mesh(mesh.devices.reshape(seq_size // 2, 2, head_size), ("chip", "core", "head"))
    seq = ("chip", "core")
    in_specs = (
        P(None, seq, "head"),
        P(None, seq, "head"),
        P("head"),
        P(None, "head"),
        P(None, "head"),
        P(),
        P(None, "head"),
        P("head"),
        P(),
        P(),
        P("head"),
        P("head"),
        P("head", None),
        P(None, seq, "head"),
    )
    out_specs = (
        P(None, seq, "head"),
        P(None, seq, "head"),
        P("head"),
        P(None, "head"),
        P(None, "head"),
        P(),
        P(None, "head"),
        P("head"),
        P(),
        P(),
        P("head"),
        P("head"),
        P("head", None),
    )
    return jax.shard_map(
        per_device, mesh=mesh, in_specs=in_specs, out_specs=out_specs, check_vma=False
    )
```

```python
import functools

import jax
import jax.numpy as jnp
from jax import lax
from jax.experimental import pallas as pl
from jax.experimental.pallas import tpu as pltpu
from jax.sharding import Mesh
from jax.sharding import PartitionSpec as P

HEAD_DIM = 64
NSTATE = 128
KERNEL = 4
CHUNK = 128
BLOCK = 384
VMEM_LIMIT = 20 * 1024 * 1024
MARGIN = 32
HALO = 16


DECAY_STEP = 1.0 / 1048576.0
EPSILON = 1e-05
BF16 = jnp.bfloat16
F32 = jnp.float32


def tie_kernel(*refs):
    del refs


def tie(value, *others):
    return pl.pallas_call(
        tie_kernel,
        out_shape=jax.ShapeDtypeStruct(value.shape, value.dtype),
        in_specs=[pl.BlockSpec(memory_space=pl.ANY)] * (1 + len(others)),
        out_specs=pl.BlockSpec(memory_space=pl.ANY),
        input_output_aliases={0: 0},
        name="tie",
    )(value, *others)


def from_behind(value, by):
    axis = ("chip", "core")
    size = lax.axis_size("chip") * 2
    pairs = [(i, i + by) for i in range(size) if 0 <= i + by < size]
    return lax.ppermute(value, axis, pairs)


def beside(value):
    return lax.ppermute(value, "core", [(0, 1), (1, 0)])


def turn(value, axis, by):
    size = lax.axis_size(axis)
    return lax.ppermute(value, axis, [(i, (i + by) % size) for i in range(size)])


def turn_all(value, axis):
    return [value] + [turn(value, axis, by) for by in range(1, lax.axis_size(axis))]


def line_parts(value, axis):
    if lax.axis_size(axis) != 4:
        parts = turn_all(value, axis)
        return parts, value
    two = turn(value, axis, 2)
    one = lax.ppermute(value, axis, [(0, 1), (1, 2), (2, 3)])
    three = lax.ppermute(value, axis, [(1, 0), (2, 1), (3, 2)])
    passed = lax.ppermute(two, axis, [(2, 3), (1, 0)])
    return [value, one, two, three], passed


def deal(parts, axis):
    return lax.all_to_all(parts, axis, 0, 0)


def cross(value, bits):
    return lax.ppermute(value, "chip", [(i, i ^ bits) for i in range(lax.axis_size("chip"))])


def cross_all(value):
    return [value] + [cross(value, bits) for bits in range(1, lax.axis_size("chip"))]


def heads_sum(piece):
    total, low = piece, piece.astype(BF16)
    bits, size = 1, lax.axis_size("head")
    while bits < size:
        arrived = lax.ppermute(low, "head", [(i, i ^ bits) for i in range(size)])
        total, low = run(
            heads_kernel, "heads", piece.size,
            [(WHOLE, piece), (WHOLE, total), (WHOLE, arrived)],
            [(WHOLE, piece.shape, F32), (WHOLE, piece.shape, BF16)],
        )
        bits *= 2
    return low


def entering(core, chip, total, backward, meanwhile, later=lambda pair: ()):
    name = "after" if backward else "before"
    chips = lax.axis_size("chip")
    channels = total.shape[1]
    half = NSTATE // 2
    partner = beside(total)
    pair = run(
        functools.partial(pair_kernel, backward), name + "_pair", total.size,
        [core, (WHOLE, total), (WHOLE, partner)] + [(LOOSE, value) for value in meanwhile],
        [(WHOLE, (half + 8, channels), F32)],
    )[0]
    prefix = run(
        functools.partial(prefix_kernel, backward, chips), name + "_prefix", chips * pair.size,
        [chip] + [(WHOLE, value) for value in cross_all(pair)]
        + [(LOOSE, value) for value in later(pair)],
        [(WHOLE, (half, channels), F32)],
    )[0]
    return run(
        functools.partial(enter_kernel, backward), name + "_enter", total.size,
        [core, (WHOLE, partner), (WHOLE, prefix), (WHOLE, beside(prefix))],
        [(WHOLE, (NSTATE, channels), F32)],
    )[0], prefix


def sum_pieces(chip, kept, given, name, square, cut, paired, before_half=()):
    chips, rows, channels = kept.shape
    arrived = beside(given)
    size = chips * rows * channels
    if paired:
        outs = [(WHOLE, (cut, channels), BF16), (WHOLE, (rows - cut, channels), F32)]
    else:
        outs = [(WHOLE, (rows, channels), BF16)]
    if chips != 4 or not square:
        halves = run(
            functools.partial(half_kernel, paired, chips), name + "_half", size,
            [chip, (WHOLE, kept), (WHOLE, arrived)] + [(LOOSE, mark) for mark in before_half],
            [(WHOLE, (rows, channels), F32)] + [(WHOLE, (rows, channels), BF16)] * (chips - 1),
        )
        parts = [halves[0]] + [cross(halves[bits], bits) for bits in range(1, chips)]
        found = run(
            functools.partial(piece_kernel, chips, paired, cut), name + "_piece", size,
            [(WHOLE, part) for part in parts], outs,
        )
        return found, halves[0]
    rest = rows - cut
    state = run(
        square_half_kernel, name + "_half", size,
        [chip, (WHOLE, kept), (WHOLE, arrived)] + [(LOOSE, mark) for mark in before_half],
        [
            (WHOLE, (2, cut, channels), F32), (WHOLE, (2, cut, channels), BF16),
            (WHOLE, (2, rest, channels), F32), (WHOLE, (2, rest, channels), BF16),
        ],
    )
    return state, state[0]


def square_next(name, state, size, mark):
    first, first_give, last, last_give = state
    _, cut, channels = first.shape
    rest = last.shape[1]
    return run(
        square_next_kernel, name + "_next", size,
        [
            (WHOLE, first), (WHOLE, cross(first_give, 1)),
            (WHOLE, last), (WHOLE, cross(last_give, 2)), (LOOSE, mark),
        ],
        [
            (WHOLE, (cut, channels), F32), (WHOLE, (cut, channels), BF16),
            (WHOLE, (rest, channels), F32), (WHOLE, (rest, channels), BF16),
        ],
    )


def square_end(name, state, outs, size, mark):
    first, first_give, last, last_give = state
    return run(
        square_last_kernel, name + "_piece", size,
        [
            (WHOLE, first), (WHOLE, cross(first_give, 2)),
            (WHOLE, last), (WHOLE, cross(last_give, 1)), (LOOSE, mark),
        ],
        outs,
    )


def collect(piece, order, mark=None):
    chips = lax.axis_size("chip")
    if chips != 4 or order is None:
        found = [(value[None], (bits,)) for bits, value in enumerate(cross_all(piece))]
    else:
        near, far = order
        both = jnp.stack([piece, cross(piece, near)])
        if mark is not None:
            both = tie(both, mark)
        found = [(both, (0, near)), (cross(both, far), (far, far ^ near))]
    return [(value, beside(value), bits) for value, bits in found]


def dot(left, right):
    return jnp.dot(left, right, preferred_element_type=F32)


def dot_nt(left, right):
    return lax.dot_general(left, right, (((1,), (1,)), ((), ())), preferred_element_type=F32)


def dot_tn(left, right):
    return lax.dot_general(left, right, (((0,), (0,)), ((), ())), preferred_element_type=F32)


def split(values):
    high = values.astype(BF16)
    return high, (values - high.astype(F32)).astype(BF16)


def lower_mask():
    row = lax.broadcasted_iota(jnp.int32, (CHUNK, CHUNK), 0)
    column = lax.broadcasted_iota(jnp.int32, (CHUNK, CHUNK), 1)
    return row >= column


def spread_heads(heads, channels):
    row = lax.broadcasted_iota(jnp.int32, (heads, channels), 0) * HEAD_DIM
    place = lax.broadcasted_iota(jnp.int32, (heads, channels), 1)
    return jnp.where((place >= row) & (place < row + HEAD_DIM), 1.0, 0.0).astype(BF16)


def expand(values, channels):
    high, low = split(values)
    spread = spread_heads(values.shape[1], channels)
    return dot(high, spread) + dot(low, spread)


def decay_kernel(codes_ref, weight_ref, e_ref, f_ref, k_ref):
    heads, channels = codes_ref.shape[1], k_ref.shape[1]
    lower = jnp.where(lower_mask(), 1.0, 0.0).astype(F32)
    count = codes_ref.shape[0] // CHUNK
    line = lax.broadcasted_iota(jnp.int32, (8, heads), 0)
    marks = jnp.zeros((8, heads), F32)
    total = jnp.zeros((1, heads), F32)
    for chunk in range(count):
        rows = pl.ds(chunk * CHUNK, CHUNK)
        logs = codes_ref[rows, :].astype(F32) * (-DECAY_STEP)
        cumulative = jnp.dot(
            lower, logs, precision=lax.Precision.HIGHEST, preferred_element_type=F32
        )
        last = cumulative[CHUNK - 1 :]
        middle = 0.5 * last
        e_ref[rows, :] = jnp.exp(cumulative - middle)
        f_ref[rows, :] = weight_ref[rows, :] * jnp.exp(middle - cumulative)
        marks = jnp.where(line == chunk, jnp.exp(middle), marks)
        total = total + last
    marks = jnp.where(line == 7, total, marks)
    high, low = split(marks)
    lowest = (marks - high.astype(F32) - low.astype(F32)).astype(BF16)
    spread = spread_heads(heads, channels)
    factors = dot(high, spread) + dot(low, spread) + dot(lowest, spread)
    k_ref[...] = factors


def pair_kernel(backward, core_ref, own_ref, other_ref, *refs):
    out_ref = refs[-1]
    half = NSTATE // 2
    logs, other_logs = own_ref[NSTATE:, :], other_ref[NSTATE:, :]
    for core in range(2):

        @pl.when(core_ref[0] == core)
        def _():
            rows = slice(core * half, (core + 1) * half)
            if core == (0 if backward else 1):
                out_ref[:half, :] = jnp.exp(logs[0:1]) * other_ref[rows, :] + own_ref[rows, :]
            else:
                out_ref[:half, :] = jnp.exp(other_logs[0:1]) * own_ref[rows, :] + other_ref[rows, :]

    out_ref[half:, :] = logs + other_logs


def prefix_kernel(backward, chips, chip_ref, *refs):
    parts, out_ref = refs[:chips], refs[-1]
    half = out_ref.shape[0]
    mine = chip_ref[0]
    total = jnp.zeros(out_ref.shape, F32)
    for bits in range(1, chips):
        source = lax.bitwise_xor(mine, bits)
        span = jnp.zeros((1, out_ref.shape[1]), F32)
        for other in range(1, chips):
            middle = lax.bitwise_xor(mine, other)
            if backward:
                between = (middle < source) & (middle > mine)
            else:
                between = (middle > source) & (middle < mine)
            span = span + jnp.where(between, parts[other][half : half + 1, :], 0.0)
        passes = source > mine if backward else source < mine
        total = total + jnp.where(passes, jnp.exp(span), 0.0) * parts[bits][:half, :]
    out_ref[...] = total


def enter_kernel(backward, core_ref, partner_ref, prefix_ref, other_ref, out_ref):
    half = prefix_ref.shape[0]
    decay = jnp.exp(partner_ref[NSTATE : NSTATE + 1, :])
    for core in range(2):

        @pl.when(core_ref[0] == core)
        def _():
            for place, ref in ((core, prefix_ref), (1 - core, other_ref)):
                rows = slice(place * half, (place + 1) * half)
                if core == (0 if backward else 1):
                    out_ref[rows, :] = decay * ref[...] + partner_ref[rows, :]
                else:
                    out_ref[rows, :] = ref[...]


def taps(window, kernel, bias, begin):
    summed = bias
    for offset in range(KERNEL):
        summed = summed + kernel[offset : offset + 1] * window[begin + offset : begin + offset + CHUNK]
    return summed


def silu_parts(values):
    sigmoid = jax.nn.sigmoid(values)
    return values * sigmoid, sigmoid * (1.0 + values * (1.0 - sigmoid))


def first_step(action):
    pl.when(pl.program_id(0) == 0)(action)


def clear(*refs):
    def action():
        for ref in refs:
            ref[...] = jnp.zeros_like(ref)

    first_step(action)


def place_parts(mine, parts, target, width, value):
    size = len(parts)
    if width % 128 == 0:
        for i in range(size):
            owner = lax.rem(mine + size - i, size)
            target[:, pl.ds(pl.multiple_of(owner * width, 128), width)] = value(i)
        return

    def write(me):
        for i in range(size):
            owner = (me + size - i) % size
            target[:, owner * width : (owner + 1) * width] = value(i)

    for me in range(size):
        pl.when(mine == me)(functools.partial(write, me))


def copies_kernel(loose_ref, own_ref, out_ref):
    for i in range(out_ref.shape[0]):
        out_ref[i] = own_ref[...]


def norm_kernel(size, head_ref, passed_ref, *refs):
    parts, gains = refs[:size], refs[size : 2 * size]
    passed_gain_ref, normed_ref, scale_ref, gain_ref = refs[2 * size :]
    width = parts[0].shape[1]
    mine = head_ref[0]

    def pick(i, refs, passed):
        if size == 4 and i == 1:
            return jnp.where(mine == 0, passed[...], refs[i][...])
        if size == 4 and i == 3:
            return jnp.where(mine == 3, passed[...], refs[i][...])
        return refs[i][...]

    part = lambda i: pick(i, parts, passed_ref).astype(F32)
    gain = lambda i: pick(i, gains, passed_gain_ref)[0:1].astype(F32)
    squares = sum(jnp.sum(part(i) ** 2, axis=1, keepdims=True) for i in range(size))
    scale = lax.rsqrt(squares / (size * width) + EPSILON)
    scale_ref[...] = jnp.broadcast_to(scale, scale_ref.shape)
    place_parts(
        mine, parts, normed_ref, width,
        lambda i: (part(i) * scale_ref[:, 0:1] * gain(i)).astype(BF16),
    )
    place_parts(mine, parts, gain_ref, width, lambda i: jnp.broadcast_to(gain(i), (8, width)))


def mixed_grad_kernel(parts_ref, weight_ref, out_ref, full_ref):
    size, _, width = parts_ref.shape
    for i in range(size):
        full_ref[:, i * width : (i + 1) * width] = parts_ref[i]
    out_ref[...] = dot_nt(full_ref[...], weight_ref[...])


def out_kernel(loose_ref, mixed_ref, weight_ref, out_ref):
    width = out_ref.shape[2]
    for owner in range(out_ref.shape[0]):
        value = dot(mixed_ref[...], weight_ref[:, owner * width : (owner + 1) * width])
        out_ref[owner] = value.astype(BF16)


def conv_kernel(
    value_ref, state_ref, value_kernel_ref, value_bias_ref, state_kernel_ref, state_bias_ref,
    f_ref, k_ref, conv_ref, weighted_ref, value_slope_ref, maps_ref, state_slope_ref, total_ref,
):
    chunk = pl.program_id(0)
    clear(total_ref)
    around = pl.ds(pl.multiple_of(chunk * CHUNK, CHUNK), CHUNK + HALO)
    pre = taps(
        state_ref[around, :].astype(F32), state_kernel_ref[...].astype(F32),
        state_bias_ref[...].astype(F32), HALO - KERNEL + 1,
    )
    conv, slope = silu_parts(pre)
    maps = conv.astype(BF16)
    maps_ref[...] = maps
    state_slope_ref[...] = slope
    pre = taps(
        value_ref[around, :].astype(F32), value_kernel_ref[...].astype(F32),
        value_bias_ref[...].astype(F32), HALO - KERNEL + 1,
    )
    conv, slope = silu_parts(pre)
    conv = conv.astype(BF16)
    conv_ref[...] = conv
    value_slope_ref[...] = slope
    weighted = (conv.astype(F32) * expand(f_ref[...], conv.shape[1])).astype(BF16)
    weighted_ref[...] = weighted
    factor = k_ref[pl.ds(chunk, 1), :]
    total_ref[:NSTATE, :] = factor * (
        factor * total_ref[:NSTATE, :] + dot_tn(maps[:, :NSTATE], weighted)
    )
    total_ref[NSTATE:, :] = jnp.broadcast_to(k_ref[7:8, :], (8, k_ref.shape[1]))


def mixer_kernel(
    state_in_ref, maps_ref, weighted_ref, conv_ref, e_ref, k_ref, skip_ref, gate_ref, grad_ref, gain_ref,
    mixer_ref, stats_ref, high_ref, low_ref, state_ref,
):
    chunk = pl.program_id(0)

    def start():
        state_ref[...] = state_in_ref[...]

    first_step(start)
    lane = lax.broadcasted_iota(jnp.int32, (CHUNK, CHUNK), 1)
    factor = k_ref[pl.ds(chunk, 1), :]
    input_map, output_map = maps_ref[:, :NSTATE], maps_ref[:, NSTATE:]
    weighted = weighted_ref[...]
    scaled = factor * state_ref[...]
    high, low = split(scaled)
    high_ref[0], low_ref[0] = high, low
    scores = jnp.where(lower_mask(), dot_nt(output_map, input_map), 0.0).astype(BF16)
    mixed = dot(
        jnp.concatenate([scores, output_map], axis=1), jnp.concatenate([weighted, high], axis=0)
    )
    mixed = mixed + dot(output_map, low)
    mixer = expand(e_ref[...], weighted.shape[1]) * mixed + skip_ref[...] * conv_ref[...].astype(F32)
    mixer_ref[...] = mixer
    gate = gate_ref[...]
    gated = mixer * (gate * jax.nn.sigmoid(gate))
    squares = jnp.sum(gated * gated, axis=1, keepdims=True)
    products = jnp.sum(gated * (grad_ref[...] * gain_ref[...].astype(F32)), axis=1, keepdims=True)
    sums = jnp.where(lane == 0, squares, jnp.where(lane == 1, products, 0.0))
    stats_ref[...] = sums.T[:8]
    state_ref[...] = factor * (scaled + dot_tn(input_map, weighted))


def column(row_block):
    rest = jnp.zeros((CHUNK - row_block.shape[0], CHUNK), F32)
    return jnp.concatenate([row_block, rest], axis=0).T


def row_of(sums):
    lane = lax.broadcasted_iota(jnp.int32, (CHUNK, CHUNK), 1)
    return jnp.where(lane == 0, sums, 0.0).T[:8]


def gate_kernel(
    inner, chunks, size, *refs
):
    stats_refs = refs[:size]
    (
        mixer_ref, gate_ref, grad_ref, gain_ref, conv_ref, e_ref, k_ref, maps_ref,
        mixed_ref, gate_grad_ref, mixer_grad_ref, small_ref, total_ref, cross_ref,
    ) = refs[size:]
    chunk = chunks - 1 - pl.program_id(0)
    clear(small_ref, total_ref)
    gain = gain_ref[...].astype(F32)
    stats = column(sum(ref[...] for ref in stats_refs))
    scale = lax.rsqrt(stats[:, 0:1] / inner + EPSILON)
    cross_term = stats[:, 1:2] * (scale * scale * scale) / inner
    gate = gate_ref[...]
    silu, slope = silu_parts(gate)
    mixer = mixer_ref[...]
    gated = mixer * silu
    normed = gated * scale
    mixed_ref[...] = (normed * gain).astype(BF16)
    grad = grad_ref[...]
    gated_grad = scale * (grad * gain) - gated * cross_term
    gate_grad = (gated_grad * mixer * slope).astype(BF16)
    gate_grad_ref[...] = gate_grad
    cross_ref[...] = row_of(jnp.sum(gate_grad.astype(F32) * gate, axis=1, keepdims=True))
    mixer_grad = gated_grad * silu
    mixer_grad_ref[...] = mixer_grad
    small_ref[0:1, :] += jnp.sum(grad * normed, axis=0, keepdims=True)
    small_ref[1:2, :] += jnp.sum(mixer_grad * conv_ref[...].astype(F32), axis=0, keepdims=True)
    high, low = split(expand(e_ref[...], grad.shape[1]) * mixer_grad)
    output_map = maps_ref[:, NSTATE:]
    factor = k_ref[pl.ds(chunk, 1), :]
    total_ref[:NSTATE, :] = factor * (
        factor * total_ref[:NSTATE, :] + (dot_tn(output_map, high) + dot_tn(output_map, low))
    )
    total_ref[NSTATE:, :] = jnp.broadcast_to(k_ref[7:8, :], (8, k_ref.shape[1]))


def back_kernel(
    chunks, early_ref, state_in_ref, mixer_grad_ref, e_ref, f_ref, k_ref, weighted_ref, high_ref, low_ref,
    maps_ref, value_slope_ref, state_slope_ref, skip_ref,
    value_ref, map_ref, state_ref,
):
    chunk = chunks - 1 - pl.program_id(0)

    def start():
        state_ref[...] = state_in_ref[...]

    first_step(start)
    lower = lower_mask()
    row = lax.broadcasted_iota(jnp.int32, (CHUNK, CHUNK), 0)
    upper = row <= lax.broadcasted_iota(jnp.int32, (CHUNK, CHUNK), 1)
    factor = k_ref[pl.ds(chunk, 1), :]
    input_map, output_map = maps_ref[:, :NSTATE], maps_ref[:, NSTATE:]
    weighted = weighted_ref[...]
    mixer_grad = mixer_grad_ref[...]
    high, low = split(expand(e_ref[...], weighted.shape[1]) * mixer_grad)
    scaled = factor * state_ref[...]
    state_high, state_low = split(scaled)
    both = jnp.concatenate([weighted, high_ref[0]], axis=0)
    sums = dot_nt(high, both) + dot_nt(low, both)
    score_grad = jnp.where(lower, sums[:, :CHUNK], 0.0).astype(BF16)
    output_grad = sums[:, CHUNK:] + dot_nt(high, low_ref[0]) + dot(score_grad, input_map)
    sums = dot_nt(weighted, jnp.concatenate([state_high, state_low], axis=0))
    input_grad = sums[:, :NSTATE] + sums[:, NSTATE:] + dot_tn(score_grad, output_map)
    scores = jnp.where(upper, dot_nt(input_map, output_map), 0.0).astype(BF16)
    grads = dot(
        jnp.concatenate([scores, input_map], axis=1), jnp.concatenate([high, state_high], axis=0)
    )
    decayed = expand(f_ref[...], weighted.shape[1]) * grads
    value_ref[...] = (decayed + skip_ref[...] * mixer_grad) * value_slope_ref[...]
    slope = state_slope_ref[...]
    map_ref[:, :NSTATE] = input_grad * slope[:, :NSTATE]
    map_ref[:, NSTATE:] = output_grad * slope[:, NSTATE:]
    state_ref[...] = factor * (scaled + (dot_tn(output_map, high) + dot_tn(output_map, low)))


def conv_back_kernel(
    chunks, value_ref, map_ref, after_ref, value_raw_ref, state_raw_ref, value_kernel_ref,
    state_kernel_ref, cross_in_ref,
    value_grad_ref, state_grad_ref, value_small_ref, state_small_ref, cross_ref, value_next_ref,
    state_next_ref,
):
    chunk = chunks - 1 - pl.program_id(0)
    channels = value_ref.shape[1]
    clear(value_small_ref, state_small_ref)

    def start():
        value_next_ref[...] = after_ref[:, :channels]
        state_next_ref[...] = after_ref[:, channels:]

    first_step(start)

    def back(slope_ref, next_ref, raw_ref, kernel_ref, grad_ref, small_ref):
        kernel = kernel_ref[...].astype(F32)
        slope = slope_ref[...]
        window = jnp.concatenate([slope, next_ref[...]], axis=0)
        around = pl.ds(pl.multiple_of(chunk * CHUNK, CHUNK), CHUNK + HALO)
        raw = raw_ref[around, :].astype(F32)
        grad = jnp.zeros_like(slope)
        for offset in range(KERNEL):
            back_by = KERNEL - 1 - offset
            grad = grad + kernel[offset : offset + 1] * window[back_by : back_by + CHUNK]
            begin = HALO - KERNEL + 1 + offset
            small_ref[offset : offset + 1, :] += jnp.sum(
                slope * raw[begin : begin + CHUNK], axis=0, keepdims=True
            )
        small_ref[KERNEL : KERNEL + 1, :] += jnp.sum(slope, axis=0, keepdims=True)
        grad = grad.astype(BF16)
        grad_ref[...] = grad
        next_ref[...] = slope[:8]
        return jnp.sum(grad.astype(F32) * raw[HALO:], axis=1, keepdims=True)

    crossed = back(map_ref, state_next_ref, state_raw_ref, state_kernel_ref, state_grad_ref, state_small_ref)
    crossed = crossed + back(
        value_ref, value_next_ref, value_raw_ref, value_kernel_ref, value_grad_ref, value_small_ref
    )
    cross_ref[...] = cross_in_ref[...] + row_of(crossed)


def normed_kernel(
    chunks, late_ref, gate_grad_ref, value_grad_ref, state_grad_ref, gate_weight_ref, value_weight_ref,
    state_weight_ref, cross_ref, out_ref
):
    value = (
        dot_nt(gate_grad_ref[...], gate_weight_ref[...])
        + dot_nt(value_grad_ref[...], value_weight_ref[...])
        + dot_nt(state_grad_ref[...], state_weight_ref[...])
    )
    count = value.shape[0]
    out_ref[0, :count, :] = value.astype(BF16)
    line = lax.broadcasted_iota(jnp.int32, (HALO, CHUNK), 0)
    packed = jnp.zeros((HALO, CHUNK), F32)
    for chunk in range(chunks):
        row = cross_ref[0:1, chunk * CHUNK : (chunk + 1) * CHUNK]
        high = row.astype(BF16).astype(F32)
        packed = jnp.where(line == chunk, high, packed)
        packed = jnp.where(line == chunks + chunk, row - high, packed)
    out_ref[0, count:, :] = jnp.zeros((HALO, value.shape[1]), BF16)
    out_ref[0, count:, :CHUNK] = packed.astype(BF16)


def last_kernel(full_width, parts_ref, tokens_ref, scale_ref, gain_ref, cotangent_ref, out_ref):
    count = tokens_ref.shape[0]
    chunks = count // CHUNK
    size = parts_ref.shape[0]
    crossed = sum(parts_ref[i, count:, :CHUNK].astype(F32) for i in range(size))
    crossed = crossed[:chunks] + crossed[chunks : 2 * chunks]
    for chunk in range(chunks):
        rows = slice(chunk * CHUNK, (chunk + 1) * CHUNK)
        normed_grad = sum(parts_ref[i, rows, :].astype(F32) for i in range(size))
        scale = scale_ref[HALO + chunk * CHUNK : HALO + (chunk + 1) * CHUNK, 0:1]
        total = column(jnp.broadcast_to(crossed[chunk : chunk + 1], (8, CHUNK)))[:, 0:1]
        out_ref[rows, :] = (
            scale * gain_ref[...].astype(F32) * normed_grad
            - tokens_ref[rows, :].astype(F32) * (scale * scale * total / full_width)
            + cotangent_ref[rows, :].astype(F32)
        ).astype(BF16)


def store_piece(core_ref, kept_ref, given_ref, place, begin, piece):
    chips = kept_ref.shape[0]
    core, chip = place // chips, lax.rem(place, chips)
    rows = slice(begin, begin + piece.shape[0])
    piece = piece.astype(BF16)

    @pl.when(core_ref[0] == core)
    def _():
        kept_ref[chip, rows, :] = piece

    @pl.when(core_ref[0] != core)
    def _():
        given_ref[chip, rows, :] = piece


def gain_row(weight, block):
    sums = jnp.sum(weight.astype(F32) * block, axis=1, keepdims=True)
    lane = lax.broadcasted_iota(jnp.int32, (CHUNK, CHUNK), 1)
    rows = [
        jnp.where(lane == 0, sums[i : i + CHUNK], 0.0).T[0:1] for i in range(0, BLOCK, CHUNK)
    ]
    return jnp.concatenate(rows, axis=1)


def early_kernel(
    loose_ref, core_ref, normed_ref, gate_ref, mixed_ref, grad_ref, weight_ref,
    kept_ref, given_ref, gain_ref, held_ref
):
    chips, rows, channels = kept_ref.shape
    at = pl.program_id(0)
    count, width = grad_ref.shape
    pieces = 2 * chips
    step = width // pieces
    out_rows = channels // pieces
    out_blocks = channels // BLOCK
    every = width // BLOCK // out_blocks

    @pl.when(lax.rem(at, every) == 0)
    def _():
        held_ref[...] = dot_tn(mixed_ref[...], grad_ref[...])

    block = dot_tn(normed_ref[HALO : HALO + count, :], gate_ref[...])
    gain_ref[...] = gain_row(weight_ref[...], block)
    for i in range(BLOCK // step):
        place = at * (BLOCK // step) + i
        begin = lax.rem(at, every) * (BLOCK // step * out_rows) + i * out_rows
        own = held_ref[pl.ds(pl.multiple_of(begin, 8), out_rows), :]
        parts = [block[i * step : (i + 1) * step]]
        parts += [own[:, j : j + channels] for j in range(0, width, channels)]
        store_piece(core_ref, kept_ref, given_ref, place, 0, jnp.concatenate(parts, axis=0))


def late_kernel(
    early_ref, core_ref, normed_ref, value_ref, state_ref, value_small_ref, gate_small_ref, gain_ref,
    state_small_ref, value_weight_ref, state_weight_ref, gain_full_ref,
    kept_ref, given_ref, own_ref, shared_ref, gains_ref,
):
    chips, rows, channels = kept_ref.shape
    at = pl.program_id(0)
    count, maps_width = state_ref.shape
    width = gains_ref.shape[1]
    pieces = 2 * chips
    step = width // pieces
    lanes = channels // 128
    part = 2 * step // lanes
    columns = normed_ref[HALO : HALO + count, :]
    value = dot_tn(columns, value_ref[...])
    state = dot_tn(columns, state_ref[...])
    gain = (
        gain_ref[...] + gain_row(value_weight_ref[...], value) + gain_row(state_weight_ref[...], state)
    ) / gain_full_ref[0:1, :]
    gains_ref[0:1, pl.ds(pl.multiple_of(at * BLOCK, 128), BLOCK)] = gain
    for i in range(BLOCK // step):
        piece = slice(i * step, (i + 1) * step)
        stacked = jnp.concatenate([state[piece, :128], state[piece, 128:]], axis=0)
        stacked = jnp.concatenate(
            [stacked[j * part : (j + 1) * part] for j in range(lanes)], axis=1
        )
        store_piece(
            core_ref, kept_ref, given_ref, at * (BLOCK // step) + i, 0,
            jnp.concatenate([value[piece], stacked], axis=0),
        )

    @pl.when(at == width // BLOCK - 1)
    def _():
        own_ref[...] = jnp.zeros_like(own_ref)
        own_ref[: KERNEL + 1, :] = value_small_ref[: KERNEL + 1, :]
        own_ref[KERNEL + 1 : KERNEL + 3, :] = gate_small_ref[:2, :]
        shared_ref[...] = jnp.zeros_like(shared_ref)
        begin = width // channels
        for i in range(begin):
            shared_ref[i : i + 1, :] = gains_ref[0:1, i * channels : (i + 1) * channels]
        for i in range(0, (KERNEL + 1) * maps_width, 128):
            tap, column_from = divmod(i, maps_width)
            row, column_to = divmod(i, channels)
            shared_ref[begin + row : begin + row + 1, column_to : column_to + 128] = state_small_ref[
                tap : tap + 1, column_from : column_from + 128
            ]
        line = lax.broadcasted_iota(jnp.int32, (HALO, channels), 0)
        for place in range(pieces):
            own, shared = own_ref[place : place + 1, :], shared_ref[place : place + 1, :]
            own_high, shared_high = (v.astype(BF16).astype(F32) for v in (own, shared))
            small = jnp.zeros((HALO, channels), F32)
            for to, value in enumerate((own_high, own - own_high, shared_high, shared - shared_high)):
                small = jnp.where(line == to, value, small)
            store_piece(core_ref, kept_ref, given_ref, place, step + part, small)


def merge_pairs(block):
    tail = block[-HALO:]
    line = lax.broadcasted_iota(jnp.int32, tail.shape, 0)
    own, shared = tail[0:1] + tail[1:2], tail[2:3] + tail[3:4]
    own_high, shared_high = own.astype(BF16).astype(F32), shared.astype(BF16).astype(F32)
    new = jnp.zeros_like(tail)
    for at, value in enumerate((own_high, own - own_high, shared_high, shared - shared_high)):
        new = jnp.where(line == at, value, new)
    return jnp.concatenate([block[:-HALO], new], axis=0)


def heads_kernel(piece_ref, total_ref, arrived_ref, out_ref, low_ref):
    total = merge_pairs(total_ref[...] + arrived_ref[...].astype(F32))
    line = lax.broadcasted_iota(jnp.int32, total.shape, 0)
    first = total.shape[0] - HALO
    own = (line >= first) & (line < first + 2)
    out_ref[...] = total
    low_ref[...] = jnp.where(own, piece_ref[...], total).astype(BF16)


def half_kernel(paired, chips, chip_ref, kept_ref, arrived_ref, *refs):
    outs = refs[-chips:]
    for bits in range(chips):
        place = lax.bitwise_xor(chip_ref[0], bits)
        value = kept_ref[place].astype(F32) + arrived_ref[place].astype(F32)
        if paired:
            value = merge_pairs(value)
        outs[bits][...] = value.astype(outs[bits].dtype)


def piece_kernel(parts, paired, cut, *refs):
    total = sum(ref[...].astype(F32) for ref in refs[:parts])
    if not paired:
        refs[-1][...] = total.astype(BF16)
        return
    first_ref, last_ref = refs[-2:]
    first_ref[...] = total[:cut].astype(BF16)
    last_ref[...] = merge_pairs(total[cut:])


def square_half_kernel(
    chip_ref, kept_ref, arrived_ref, loose_ref, first_ref, first_give_ref, last_ref, last_give_ref
):
    cut = first_ref.shape[1]
    for bits in range(4):
        place = lax.bitwise_xor(chip_ref[0], bits)
        value = kept_ref[place].astype(F32) + arrived_ref[place].astype(F32)
        low, high = bits & 1, bits >> 1
        ref = first_give_ref if low else first_ref
        ref[high] = value[:cut].astype(ref.dtype)
        ref = last_give_ref if high else last_ref
        ref[low] = value[cut:].astype(ref.dtype)


def square_next_kernel(
    first_ref, first_got_ref, last_ref, last_got_ref, loose_ref,
    first_out_ref, first_give_ref, last_out_ref, last_give_ref,
):
    first_out_ref[...] = first_ref[0] + first_got_ref[0].astype(F32)
    first_give_ref[...] = (first_ref[1] + first_got_ref[1].astype(F32)).astype(BF16)
    last_out_ref[...] = last_ref[0] + last_got_ref[0].astype(F32)
    last_give_ref[...] = (last_ref[1] + last_got_ref[1].astype(F32)).astype(BF16)


def square_last_kernel(first_ref, first_got_ref, last_ref, last_got_ref, loose_ref, *outs):
    outs[0][...] = (first_ref[...] + first_got_ref[...].astype(F32)).astype(BF16)
    outs[1][...] = (last_ref[...] + last_got_ref[...].astype(F32)).astype(BF16)


def each_piece(core_ref, chip_ref, chips, groups, refs):
    refs = iter(refs)
    for part, bits_lists in enumerate(groups):
        number = 0
        for bits_list in bits_lists:
            for core, ref in ((core_ref[0], next(refs)), (1 - core_ref[0], next(refs))):
                for at, bits in enumerate(bits_list):
                    place = core * chips + lax.bitwise_xor(chip_ref[0], bits)
                    yield part, number, place, ref[at].astype(F32)
                    number += 1


def send_rows(buffer_ref, number, target_ref, place, sem_ref):
    rows = buffer_ref.shape[1]
    copy = pltpu.make_async_copy(
        buffer_ref.at[number],
        target_ref.at[pl.ds(pl.multiple_of(place * rows, 8), rows), :],
        sem_ref.at[number],
    )
    copy.start()
    return copy


def early_out_kernel(chips, groups, core_ref, chip_ref, *refs):
    gate_ref, output_ref, gate_buffer, output_buffer, gate_sems, output_sems = refs[-6:]
    out_rows, width = output_buffer.shape[1:]
    channels = gate_buffer.shape[2]
    copies = []
    for part, number, place, value in each_piece(core_ref, chip_ref, chips, groups, refs[:-6]):
        if part == 0:
            gate_buffer[number] = value
            copies.append(send_rows(gate_buffer, number, gate_ref, place, gate_sems))
        else:
            output_buffer[number] = jnp.concatenate(
                [value[i * out_rows : (i + 1) * out_rows] for i in range(width // channels)], axis=1
            )
            copies.append(send_rows(output_buffer, number, output_ref, place, output_sems))
    for copy in copies:
        copy.wait()


def late_out_kernel(chips, groups, core_ref, chip_ref, *refs):
    value_ref, buffer, sems = refs[-3:]
    copies = []
    for _, number, place, value in each_piece(core_ref, chip_ref, chips, groups, refs[:-3]):
        buffer[number] = value
        copies.append(send_rows(buffer, number, value_ref, place, sems))
    for copy in copies:
        copy.wait()


def shared_out_kernel(chips, groups, size, core_ref, chip_ref, head_ref, loose_ref, *refs):
    (
        state_ref, value_kernel_ref, value_bias_ref, state_kernel_ref, state_bias_ref, skip_ref,
        gated_ref, gain_ref, buffer, sems, own_ref, shared_ref,
    ) = refs[-12:]
    step, maps_width = buffer.shape[1:]
    channels = own_ref.shape[1]
    lanes = channels // 128
    rows = 2 * step // lanes
    copies = []
    for _, number, place, piece in each_piece(core_ref, chip_ref, chips, groups, refs[:-12]):
        stacked = jnp.concatenate(
            [piece[:rows, i * 128 : (i + 1) * 128] for i in range(lanes)], axis=0
        )
        buffer[number] = jnp.concatenate([stacked[:step], stacked[step:]], axis=1)
        copies.append(send_rows(buffer, number, state_ref, place, sems))
        own_ref[pl.ds(place, 1), :] = piece[rows : rows + 1] + piece[rows + 1 : rows + 2]
        shared_ref[pl.ds(place, 1), :] = piece[rows + 2 : rows + 3] + piece[rows + 3 : rows + 4]
    value_kernel_ref[...] = own_ref[:KERNEL, :]
    value_bias_ref[...] = own_ref[KERNEL, :]
    gated_ref[...] = own_ref[KERNEL + 1, :]
    heads = skip_ref.shape[0]
    at = lax.broadcasted_iota(jnp.int32, (heads, channels), 1)
    row = lax.broadcasted_iota(jnp.int32, (heads, channels), 0) * HEAD_DIM
    inside = (at >= row) & (at < row + HEAD_DIM)
    skip_ref[...] = jnp.sum(jnp.where(inside, own_ref[KERNEL + 2 : KERNEL + 3, :], 0.0), axis=1)
    own_width = gain_ref.shape[0]
    gain_rows = -(-own_width * size // channels)
    for head in range(size):
        row, begin = divmod(head * own_width, channels)

        @pl.when(head_ref[0] == head)
        def _(row=row, begin=begin):
            gain_ref[...] = shared_ref[row, begin : begin + own_width]

    for i in range(0, (KERNEL + 1) * maps_width, 128):
        tap, column_to = divmod(i, maps_width)
        row, column_from = divmod(i, channels)
        value = shared_ref[gain_rows + row : gain_rows + row + 1, column_from : column_from + 128]
        if tap < KERNEL:
            state_kernel_ref[tap : tap + 1, column_to : column_to + 128] = value
        else:
            state_bias_ref[column_to : column_to + 128] = value[0]
    for copy in copies:
        copy.wait()


SCALAR = "scalar"
WHOLE = "whole"
BLOCKED = "blocked"
LANES = "lanes"
LEADING = "leading"
LOOSE = "loose"


def run(kernel, name, flops, args, outs, steps=None, backward=False, scratch=()):
    at = (lambda i: steps - 1 - i) if backward else (lambda i: i)

    def spec(kind, shape):
        if isinstance(kind, int):
            return pl.BlockSpec((kind,) + shape[1:], lambda i: (at(i), 0))
        if kind == SCALAR:
            return pl.BlockSpec(memory_space=pltpu.SMEM)
        if kind == LOOSE:
            return pl.BlockSpec(memory_space=pl.ANY)
        if isinstance(kind, tuple):
            return pl.BlockSpec(*kind)
        if steps is None:
            return pl.BlockSpec(memory_space=pltpu.VMEM)
        if kind == BLOCKED:
            return pl.BlockSpec((CHUNK, shape[1]), lambda i: (at(i), 0))
        if kind == LANES:
            return pl.BlockSpec((shape[0], CHUNK), lambda i: (0, at(i)))
        if kind == LEADING:
            return pl.BlockSpec((1,) + shape[1:], lambda i: (at(i),) + (0,) * (len(shape) - 1))
        return pl.BlockSpec(shape, lambda i: (0,) * len(shape))

    moved = sum(a.size * a.dtype.itemsize for kind, a in args if kind != LOOSE)
    shapes = [jax.ShapeDtypeStruct(shape, dtype) for _, shape, dtype in outs]
    moved += sum(a.size * a.dtype.itemsize for a in shapes)
    return pl.pallas_call(
        kernel,
        out_shape=shapes,
        in_specs=[spec(kind, a.shape) for kind, a in args],
        out_specs=[spec(kind, shape) for kind, shape, _ in outs],
        scratch_shapes=list(scratch),
        compiler_params=pltpu.CompilerParams(vmem_limit_bytes=VMEM_LIMIT),
        cost_estimate=pl.CostEstimate(flops=flops, bytes_accessed=moved, transcendentals=0),
        name=name,
        **({} if steps is None else {"grid": (steps,)}),
    )(*(a for _, a in args))


def per_device(
    tokens, decay_codes, norm_gain, gate_weight, value_weight, state_weight, value_kernel, value_bias,
    state_kernel, state_bias, skip_scale, gated_gain, output_weight, cotangent,
):
    tokens, decay_codes, cotangent = tokens[0], decay_codes[0], cotangent[0]
    count, own_width = tokens.shape
    heads = skip_scale.shape[0]
    channels = heads * HEAD_DIM
    head_size, chips = lax.axis_size("head"), lax.axis_size("chip")
    seq_size = 2 * chips
    width = own_width * head_size
    maps_width = 2 * NSTATE
    chunks = count // CHUNK
    core = (SCALAR, lax.axis_index("core").astype(jnp.int32)[None])
    chip = (SCALAR, lax.axis_index("chip").astype(jnp.int32)[None])
    head = (SCALAR, lax.axis_index("head").astype(jnp.int32)[None])

    rows = count + MARGIN
    packed = jnp.concatenate(
        [
            from_behind(tokens[-HALO:], 1),
            tokens,
            jnp.broadcast_to(norm_gain[None], (MARGIN - HALO, own_width)),
        ],
        axis=0,
    )
    logs = decay_codes.astype(F32) * (-DECAY_STEP)
    input_weight = jnp.sqrt(-jnp.expm1(2.0 * logs))
    e_full, f_full, factors = run(
        decay_kernel, "decays", count * channels * 200,
        [(WHOLE, decay_codes), (WHOLE, input_weight)],
        [
            (WHOLE, (count, heads), F32),
            (WHOLE, (count, heads), F32),
            (WHOLE, (8, channels), F32),
        ],
    )
    parts, passed = line_parts(packed, "head")
    skip_full = jnp.repeat(skip_scale, HEAD_DIM)[None]

    half = rows // 2
    gain_rows = ((MARGIN - HALO, own_width), lambda i: ((HALO + count) // (MARGIN - HALO), 0))
    normed, scale_in, gain_full = run(
        functools.partial(norm_kernel, head_size), "norm", count * width * 10,
        [head, (half, passed)] + [(half, part) for part in parts]
        + [(gain_rows, part) for part in parts] + [(gain_rows, passed)],
        [(half, (rows, width), BF16), (half, (rows, 128), F32), (WHOLE, (8, width), F32)],
        steps=2,
    )
    cotangent_parts = deal(
        run(
            copies_kernel, "copies", 1, [(LOOSE, normed), (WHOLE, cotangent)],
            [(WHOLE, (head_size, count, own_width), BF16)],
        )[0],
        "head",
    )
    value_raw = dot(normed, value_weight).astype(BF16)
    state_raw = dot(normed, state_weight).astype(BF16)
    conv, weighted, value_slope, maps, map_slope, local_end = run(
        conv_kernel, "conv", count * channels * 400,
        [
            (WHOLE, value_raw), (WHOLE, state_raw), (WHOLE, value_kernel), (WHOLE, value_bias[None]),
            (WHOLE, state_kernel), (WHOLE, state_bias[None]), (BLOCKED, f_full), (WHOLE, factors),
        ],
        [
            (BLOCKED, (count, channels), BF16),
            (BLOCKED, (count, channels), BF16),
            (BLOCKED, (count, channels), F32),
            (BLOCKED, (count, maps_width), BF16),
            (BLOCKED, (count, maps_width), F32),
            (WHOLE, (NSTATE + 8, channels), F32),
        ],
        steps=chunks,
    )
    gate_pre = dot(normed, gate_weight)[HALO : HALO + count]
    state_in, _ = entering(core, chip, local_end, False, (gate_pre,))
    mixed_grad, full_cotangent = run(
        mixed_grad_kernel, "mixed_grad", 2 * count * width * channels,
        [(WHOLE, cotangent_parts), (WHOLE, output_weight)],
        [(WHOLE, (count, channels), F32), (WHOLE, (count, width), BF16)],
    )
    mixer, stats, high, low = run(
        mixer_kernel, "mixer", count * channels * 1000,
        [
            (WHOLE, state_in), (BLOCKED, maps), (BLOCKED, weighted), (BLOCKED, conv),
            (BLOCKED, e_full), (WHOLE, factors), (WHOLE, skip_full), (BLOCKED, gate_pre),
            (BLOCKED, mixed_grad), (WHOLE, gated_gain[None]),
        ],
        [
            (BLOCKED, (count, channels), F32),
            (LANES, (8, count), F32),
            (LEADING, (chunks, NSTATE, channels), BF16),
            (LEADING, (chunks, NSTATE, channels), BF16),
        ],
        steps=chunks,
        scratch=[pltpu.VMEM((NSTATE, channels), F32)],
    )
    mixed, gate_grad, mixer_grad, gate_small, start_grad, gate_cross = run(
        functools.partial(gate_kernel, float(channels * head_size), chunks, head_size),
        "gate", count * channels * 600,
        [(LANES, part) for part in turn_all(stats, "head")]
        + [
            (BLOCKED, mixer), (BLOCKED, gate_pre), (BLOCKED, mixed_grad), (WHOLE, gated_gain[None]),
            (BLOCKED, conv), (BLOCKED, e_full), (WHOLE, factors), (BLOCKED, maps),
        ],
        [
            (BLOCKED, (count, channels), BF16),
            (BLOCKED, (count, channels), BF16),
            (BLOCKED, (count, channels), F32),
            (WHOLE, (8, channels), F32),
            (WHOLE, (NSTATE + 8, channels), F32),
            (LANES, (8, count), F32),
        ],
        steps=chunks,
        backward=True,
    )
    step, out_rows = width // seq_size, channels // seq_size
    early_rows = step + out_rows * (width // channels)
    features = width // BLOCK
    feature_block = ((rows, BLOCK), lambda i: (0, i))
    every = features // (channels // BLOCK)
    out_parts = run(
        out_kernel, "out", 2 * count * channels * width,
        [(LOOSE, start_grad), (WHOLE, mixed), (WHOLE, output_weight)],
        [(WHOLE, (head_size, count, own_width), BF16)],
    )[0]
    early_made = []

    def make_early(pair):
        early_made.extend(
            run(
                early_kernel, "early", 4 * count * channels * width,
                [
                    (LOOSE, pair), core, (feature_block, normed), (WHOLE, gate_grad),
                    (((count, BLOCK), lambda i: (0, i // every)), mixed), (WHOLE, full_cotangent),
                    (BLOCK, gate_weight),
                ],
                [(WHOLE, (chips, early_rows, channels), BF16)] * 2
                + [(((1, BLOCK), lambda i: (0, i)), (1, width), F32)],
                steps=features,
                scratch=[pltpu.VMEM((BLOCK, width), F32)],
            )
        )
        return early_made[1:2]

    grad_after, after_prefix = entering(core, chip, start_grad, True, (out_parts,), make_early)
    early_kept, early_given, early_gain = early_made
    early_state, half_mark = sum_pieces(
        chip, early_kept, early_given, "early", True, step, False, (after_prefix,)
    )
    branch = jnp.sum(deal(out_parts, "head").astype(F32), axis=0)
    block_out = (tokens.astype(F32) + branch).astype(BF16)

    value_grads, map_grads = run(
        functools.partial(back_kernel, chunks), "back", count * channels * 2000,
        [
            (LOOSE, half_mark), (WHOLE, grad_after), (BLOCKED, mixer_grad), (BLOCKED, e_full),
            (BLOCKED, f_full), (WHOLE, factors), (BLOCKED, weighted), (LEADING, high),
            (LEADING, low), (BLOCKED, maps), (BLOCKED, value_slope), (BLOCKED, map_slope),
            (WHOLE, skip_full),
        ],
        [(BLOCKED, (count, channels), F32), (BLOCKED, (count, maps_width), F32)],
        steps=chunks,
        backward=True,
        scratch=[pltpu.VMEM((NSTATE, channels), F32)],
    )
    after = from_behind(jnp.concatenate([value_grads[:8], map_grads[:8]], axis=1), -1)
    value_raw_grad, state_raw_grad, value_small, state_small, crossed = run(
        functools.partial(conv_back_kernel, chunks), "conv_back", count * channels * 100,
        [
            (BLOCKED, value_grads), (BLOCKED, map_grads), (WHOLE, after),
            (WHOLE, value_raw), (WHOLE, state_raw), (WHOLE, value_kernel), (WHOLE, state_kernel),
            (LANES, gate_cross),
        ],
        [
            (BLOCKED, (count, channels), BF16),
            (BLOCKED, (count, maps_width), BF16),
            (WHOLE, (8, channels), F32),
            (WHOLE, (8, maps_width), F32),
            (LANES, (8, count), F32),
        ],
        steps=chunks,
        backward=True,
        scratch=[pltpu.VMEM((8, channels), F32), pltpu.VMEM((8, maps_width), F32)],
    )
    next_mark = early_state[0]
    if chips == 4:
        early_state = square_next("early", early_state, early_rows * channels, crossed)
        next_mark = early_state[0]
    normed_parts = run(
        functools.partial(normed_kernel, chunks), "normed", 4 * count * channels * width,
        [
            (LOOSE, next_mark), (WHOLE, gate_grad), (WHOLE, value_raw_grad),
            (WHOLE, state_raw_grad), (own_width, gate_weight), (own_width, value_weight),
            (own_width, state_weight), (WHOLE, crossed),
        ],
        [(LEADING, (head_size, count + HALO, own_width), BF16)],
        steps=head_size,
    )[0]
    if chips == 4:
        early_gate, early_out = square_end(
            "early", early_state,
            [(WHOLE, (step, channels), BF16), (WHOLE, (early_rows - step, channels), BF16)],
            early_rows * channels, normed_parts,
        )
    else:
        early_gate, early_out = early_state[0][:step], early_state[0][step:]
    lanes = channels // 128
    state_rows = 2 * step // lanes
    late_rows = step + state_rows + HALO
    late_kept, late_given = run(
        late_kernel, "late", 3 * count * channels * width,
        [
            (LOOSE, early_gate), core, (feature_block, normed), (WHOLE, value_raw_grad),
            (WHOLE, state_raw_grad),
            (WHOLE, value_small), (WHOLE, gate_small), (((1, BLOCK), lambda i: (0, i)), early_gain),
            (WHOLE, state_small), (BLOCK, value_weight), (BLOCK, state_weight),
            (((8, BLOCK), lambda i: (0, i)), gain_full),
        ],
        [(WHOLE, (chips, late_rows, channels), BF16)] * 2,
        steps=features,
        scratch=[
            pltpu.VMEM((HALO, channels), F32),
            pltpu.VMEM((HALO, channels), F32),
            pltpu.VMEM((8, width), F32),
        ],
    )
    (late_piece, shared_piece), late_mark = sum_pieces(
        chip, late_kept, late_given, "late", False, step, True
    )
    normed_parts = deal(normed_parts, "head")
    shared_piece = heads_sum(shared_piece)

    def unpack(kernel, name, pieces, outs, flops, scratch, extra=(), args=()):
        groups = [collect(*piece) for piece in pieces]
        bits = [[found[2] for found in group] for group in groups]
        arrays = [(WHOLE, value) for group in groups for found in group for value in found[:2]]
        return run(
            functools.partial(kernel, chips, bits, *extra), name, flops,
            [core, chip, *args] + arrays, outs, scratch=scratch,
        )

    sems = pltpu.SemaphoreType.DMA((seq_size,))
    gate_weight_gradient, output_weight_gradient = unpack(
        early_out_kernel, "early_out",
        [(early_gate, (2, 1), late_mark), (early_out, (1, 2), late_mark)],
        [(LOOSE, (width, channels), F32), (LOOSE, (channels, width), F32)], 4 * channels * width,
        [
            pltpu.VMEM((seq_size, step, channels), F32),
            pltpu.VMEM((seq_size, out_rows, width), F32),
            sems,
            sems,
        ],
    )
    value_weight_gradient = unpack(
        late_out_kernel, "late_out", [(late_piece, None)],
        [(LOOSE, (width, channels), F32)], 2 * channels * width,
        [pltpu.VMEM((seq_size, step, channels), F32), sems],
    )[0]
    (
        state_weight_gradient, value_kernel_gradient, value_bias_gradient, state_kernel_gradient,
        state_bias_gradient, skip_scale_gradient, gated_gain_gradient, norm_gain_gradient,
    ) = unpack(
        shared_out_kernel, "shared_out", [(shared_piece, (2, 1))],
        [
            (LOOSE, (width, maps_width), F32),
            (WHOLE, (KERNEL, channels), F32),
            (WHOLE, (channels,), F32),
            (WHOLE, (KERNEL, maps_width), F32),
            (WHOLE, (maps_width,), F32),
            (WHOLE, (heads,), F32),
            (WHOLE, (channels,), F32),
            (WHOLE, (own_width,), F32),
        ],
        2 * maps_width * width,
        [
            pltpu.VMEM((seq_size, step, maps_width), F32),
            sems,
            pltpu.VMEM((HALO, channels), F32),
            pltpu.VMEM((HALO, channels), F32),
        ],
        extra=(head_size,),
        args=[head, (LOOSE, gate_weight_gradient)],
    )
    tokens_gradient = run(
        functools.partial(last_kernel, float(width)), "last", count * own_width * 20,
        [
            (WHOLE, normed_parts), (WHOLE, tokens), (WHOLE, scale_in),
            (WHOLE, norm_gain[None]), (WHOLE, cotangent),
        ],
        [(WHOLE, (count, own_width), BF16)],
    )[0]
    return (
        block_out[None],
        tokens_gradient[None],
        norm_gain_gradient,
        gate_weight_gradient,
        value_weight_gradient,
        state_weight_gradient,
        value_kernel_gradient,
        value_bias_gradient,
        state_kernel_gradient,
        state_bias_gradient,
        skip_scale_gradient,
        gated_gain_gradient,
        output_weight_gradient,
    )


def solution(mesh):
    seq_size, head_size = mesh.shape["seq"], mesh.shape["head"]
    mesh = Mesh(mesh.devices.reshape(seq_size // 2, 2, head_size), ("chip", "core", "head"))
    seq = ("chip", "core")
    in_specs = (
        P(None, seq, "head"),
        P(None, seq, "head"),
        P("head"),
        P(None, "head"),
        P(None, "head"),
        P(),
        P(None, "head"),
        P("head"),
        P(),
        P(),
        P("head"),
        P("head"),
        P("head", None),
        P(None, seq, "head"),
    )
    out_specs = (
        P(None, seq, "head"),
        P(None, seq, "head"),
        P("head"),
        P(None, "head"),
        P(None, "head"),
        P(),
        P(None, "head"),
        P("head"),
        P(),
        P(),
        P("head"),
        P("head"),
        P("head", None),
    )
    return jax.shard_map(
        per_device, mesh=mesh, in_specs=in_specs, out_specs=out_specs, check_vma=False
    )
```

```python
import functools

import jax
import jax.numpy as jnp
from jax import lax
from jax.experimental import pallas as pl
from jax.experimental.pallas import tpu as pltpu
from jax.sharding import Mesh
from jax.sharding import PartitionSpec as P

HEAD_DIM = 64
NSTATE = 128
KERNEL = 4
CHUNK = 128
BLOCK = 384
VMEM_LIMIT = 20 * 1024 * 1024
MARGIN = 32
HALO = 16


DECAY_STEP = 1.0 / 1048576.0
EPSILON = 1e-05
BF16 = jnp.bfloat16
F32 = jnp.float32


def tie_kernel(*refs):
    del refs


def tie(value, *others):
    return pl.pallas_call(
        tie_kernel,
        out_shape=jax.ShapeDtypeStruct(value.shape, value.dtype),
        in_specs=[pl.BlockSpec(memory_space=pl.ANY)] * (1 + len(others)),
        out_specs=pl.BlockSpec(memory_space=pl.ANY),
        input_output_aliases={0: 0},
        name="tie",
    )(value, *others)


def from_behind(value, by):
    axis = ("chip", "core")
    size = lax.axis_size("chip") * 2
    pairs = [(i, i + by) for i in range(size) if 0 <= i + by < size]
    return lax.ppermute(value, axis, pairs)


def beside(value):
    return lax.ppermute(value, "core", [(0, 1), (1, 0)])


def turn(value, axis, by):
    size = lax.axis_size(axis)
    return lax.ppermute(value, axis, [(i, (i + by) % size) for i in range(size)])


def turn_all(value, axis):
    return [value] + [turn(value, axis, by) for by in range(1, lax.axis_size(axis))]


def line_parts(value, axis):
    if lax.axis_size(axis) != 4:
        parts = turn_all(value, axis)
        return parts, value
    two = turn(value, axis, 2)
    one = lax.ppermute(value, axis, [(0, 1), (1, 2), (2, 3)])
    three = lax.ppermute(value, axis, [(1, 0), (2, 1), (3, 2)])
    passed = lax.ppermute(two, axis, [(2, 3), (1, 0)])
    return [value, one, two, three], passed


def deal(parts, axis):
    return lax.all_to_all(parts, axis, 0, 0)


def cross(value, bits):
    return lax.ppermute(value, "chip", [(i, i ^ bits) for i in range(lax.axis_size("chip"))])


def cross_all(value):
    return [value] + [cross(value, bits) for bits in range(1, lax.axis_size("chip"))]


def heads_sum(piece):
    total, low = piece, piece.astype(BF16)
    bits, size = 1, lax.axis_size("head")
    while bits < size:
        arrived = lax.ppermute(low, "head", [(i, i ^ bits) for i in range(size)])
        total, low = run(
            heads_kernel, "heads", piece.size,
            [(WHOLE, piece), (WHOLE, total), (WHOLE, arrived)],
            [(WHOLE, piece.shape, F32), (WHOLE, piece.shape, BF16)],
        )
        bits *= 2
    return low


def entering(core, chip, total, backward, meanwhile, later=lambda pair: ()):
    name = "after" if backward else "before"
    chips = lax.axis_size("chip")
    channels = total.shape[1]
    half = NSTATE // 2
    partner = beside(total)
    pair = run(
        functools.partial(pair_kernel, backward), name + "_pair", total.size,
        [core, (WHOLE, total), (WHOLE, partner)] + [(LOOSE, value) for value in meanwhile],
        [(WHOLE, (half + 8, channels), F32)],
    )[0]
    found = cross_all(pair)
    prefix = run(
        functools.partial(prefix_kernel, backward, chips), name + "_prefix", chips * pair.size,
        [chip] + [(WHOLE, value) for value in found]
        + [(LOOSE, value) for value in later(pair)],
        [(WHOLE, (half, channels), F32)],
    )[0]
    return run(
        functools.partial(enter_kernel, backward), name + "_enter", total.size,
        [core, (WHOLE, partner), (WHOLE, prefix), (WHOLE, beside(prefix))],
        [(WHOLE, (NSTATE, channels), F32)],
    )[0], prefix, found[1]


def sum_pieces(chip, kept, given, name, square, cut, paired, before_half=()):
    chips, rows, channels = kept.shape
    arrived = beside(given)
    size = chips * rows * channels
    if paired:
        outs = [(WHOLE, (cut, channels), BF16), (WHOLE, (rows - cut, channels), F32)]
    else:
        outs = [(WHOLE, (rows, channels), BF16)]
    if chips != 4 or not square:
        halves = run(
            functools.partial(half_kernel, paired, chips), name + "_half", size,
            [chip, (WHOLE, kept), (WHOLE, arrived)] + [(LOOSE, mark) for mark in before_half],
            [(WHOLE, (rows, channels), F32)] + [(WHOLE, (rows, channels), BF16)] * (chips - 1),
        )
        parts = [halves[0]] + [cross(halves[bits], bits) for bits in range(1, chips)]
        found = run(
            functools.partial(piece_kernel, chips, paired, cut), name + "_piece", size,
            [(WHOLE, part) for part in parts], outs,
        )
        return found, halves[0]
    rest = rows - cut
    state = run(
        square_half_kernel, name + "_half", size,
        [chip, (WHOLE, kept), (WHOLE, arrived)] + [(LOOSE, mark) for mark in before_half],
        [
            (WHOLE, (2, cut, channels), F32), (WHOLE, (2, cut, channels), BF16),
            (WHOLE, (2, rest, channels), F32), (WHOLE, (2, rest, channels), BF16),
        ],
    )
    return state, state[0]


def square_next(name, state, size, mark):
    first, first_give, last, last_give = state
    _, cut, channels = first.shape
    rest = last.shape[1]
    return run(
        square_next_kernel, name + "_next", size,
        [
            (WHOLE, first), (WHOLE, cross(first_give, 1)),
            (WHOLE, last), (WHOLE, cross(last_give, 2)), (LOOSE, mark),
        ],
        [
            (WHOLE, (cut, channels), F32), (WHOLE, (cut, channels), BF16),
            (WHOLE, (rest, channels), F32), (WHOLE, (rest, channels), BF16),
        ],
    )


def square_end(name, state, outs, size, mark):
    first, first_give, last, last_give = state
    return run(
        square_last_kernel, name + "_piece", size,
        [
            (WHOLE, first), (WHOLE, cross(first_give, 2)),
            (WHOLE, last), (WHOLE, cross(last_give, 1)), (LOOSE, mark),
        ],
        outs,
    )


def collect(piece, order, mark=None):
    chips = lax.axis_size("chip")
    if chips != 4 or order is None:
        found = [(value[None], (bits,)) for bits, value in enumerate(cross_all(piece))]
    else:
        near, far = order
        both = jnp.stack([piece, cross(piece, near)])
        if mark is not None:
            both = tie(both, mark)
        found = [(both, (0, near)), (cross(both, far), (far, far ^ near))]
    return [(value, beside(value), bits) for value, bits in found]


def dot(left, right):
    return jnp.dot(left, right, preferred_element_type=F32)


def dot_nt(left, right):
    return lax.dot_general(left, right, (((1,), (1,)), ((), ())), preferred_element_type=F32)


def dot_tn(left, right):
    return lax.dot_general(left, right, (((0,), (0,)), ((), ())), preferred_element_type=F32)


def split(values):
    high = values.astype(BF16)
    return high, (values - high.astype(F32)).astype(BF16)


def lower_mask():
    row = lax.broadcasted_iota(jnp.int32, (CHUNK, CHUNK), 0)
    column = lax.broadcasted_iota(jnp.int32, (CHUNK, CHUNK), 1)
    return row >= column


def spread_heads(heads, channels):
    row = lax.broadcasted_iota(jnp.int32, (heads, channels), 0) * HEAD_DIM
    place = lax.broadcasted_iota(jnp.int32, (heads, channels), 1)
    return jnp.where((place >= row) & (place < row + HEAD_DIM), 1.0, 0.0).astype(BF16)


def expand(values, channels):
    high, low = split(values)
    spread = spread_heads(values.shape[1], channels)
    return dot(high, spread) + dot(low, spread)


def decay_kernel(codes_ref, weight_ref, e_ref, f_ref, k_ref):
    heads, channels = codes_ref.shape[1], k_ref.shape[1]
    lower = jnp.where(lower_mask(), 1.0, 0.0).astype(F32)
    count = codes_ref.shape[0] // CHUNK
    line = lax.broadcasted_iota(jnp.int32, (8, heads), 0)
    marks = jnp.zeros((8, heads), F32)
    total = jnp.zeros((1, heads), F32)
    for chunk in range(count):
        rows = pl.ds(chunk * CHUNK, CHUNK)
        logs = codes_ref[rows, :].astype(F32) * (-DECAY_STEP)
        cumulative = jnp.dot(
            lower, logs, precision=lax.Precision.HIGHEST, preferred_element_type=F32
        )
        last = cumulative[CHUNK - 1 :]
        middle = 0.5 * last
        e_ref[rows, :] = jnp.exp(cumulative - middle)
        f_ref[rows, :] = weight_ref[rows, :] * jnp.exp(middle - cumulative)
        marks = jnp.where(line == chunk, jnp.exp(middle), marks)
        total = total + last
    marks = jnp.where(line == 7, total, marks)
    high, low = split(marks)
    lowest = (marks - high.astype(F32) - low.astype(F32)).astype(BF16)
    spread = spread_heads(heads, channels)
    factors = dot(high, spread) + dot(low, spread) + dot(lowest, spread)
    k_ref[...] = factors


def pair_kernel(backward, core_ref, own_ref, other_ref, *refs):
    out_ref = refs[-1]
    half = NSTATE // 2
    logs, other_logs = own_ref[NSTATE:, :], other_ref[NSTATE:, :]
    for core in range(2):

        @pl.when(core_ref[0] == core)
        def _():
            rows = slice(core * half, (core + 1) * half)
            if core == (0 if backward else 1):
                out_ref[:half, :] = jnp.exp(logs[0:1]) * other_ref[rows, :] + own_ref[rows, :]
            else:
                out_ref[:half, :] = jnp.exp(other_logs[0:1]) * own_ref[rows, :] + other_ref[rows, :]

    out_ref[half:, :] = logs + other_logs


def prefix_kernel(backward, chips, chip_ref, *refs):
    parts, out_ref = refs[:chips], refs[-1]
    half = out_ref.shape[0]
    mine = chip_ref[0]
    total = jnp.zeros(out_ref.shape, F32)
    for bits in range(1, chips):
        source = lax.bitwise_xor(mine, bits)
        span = jnp.zeros((1, out_ref.shape[1]), F32)
        for other in range(1, chips):
            middle = lax.bitwise_xor(mine, other)
            if backward:
                between = (middle < source) & (middle > mine)
            else:
                between = (middle > source) & (middle < mine)
            span = span + jnp.where(between, parts[other][half : half + 1, :], 0.0)
        passes = source > mine if backward else source < mine
        total = total + jnp.where(passes, jnp.exp(span), 0.0) * parts[bits][:half, :]
    out_ref[...] = total


def enter_kernel(backward, core_ref, partner_ref, prefix_ref, other_ref, out_ref):
    half = prefix_ref.shape[0]
    decay = jnp.exp(partner_ref[NSTATE : NSTATE + 1, :])
    for core in range(2):

        @pl.when(core_ref[0] == core)
        def _():
            for place, ref in ((core, prefix_ref), (1 - core, other_ref)):
                rows = slice(place * half, (place + 1) * half)
                if core == (0 if backward else 1):
                    out_ref[rows, :] = decay * ref[...] + partner_ref[rows, :]
                else:
                    out_ref[rows, :] = ref[...]


def taps(window, kernel, bias, begin):
    summed = bias
    for offset in range(KERNEL):
        summed = summed + kernel[offset : offset + 1] * window[begin + offset : begin + offset + CHUNK]
    return summed


def silu_parts(values):
    sigmoid = jax.nn.sigmoid(values)
    return values * sigmoid, sigmoid * (1.0 + values * (1.0 - sigmoid))


def first_step(action):
    pl.when(pl.program_id(0) == 0)(action)


def clear(*refs):
    def action():
        for ref in refs:
            ref[...] = jnp.zeros_like(ref)

    first_step(action)


def place_parts(mine, parts, target, width, value):
    size = len(parts)
    if width % 128 == 0:
        for i in range(size):
            owner = lax.rem(mine + size - i, size)
            target[:, pl.ds(pl.multiple_of(owner * width, 128), width)] = value(i)
        return

    def write(me):
        for i in range(size):
            owner = (me + size - i) % size
            target[:, owner * width : (owner + 1) * width] = value(i)

    for me in range(size):
        pl.when(mine == me)(functools.partial(write, me))


def norm_kernel(size, head_ref, passed_ref, *refs):
    parts, gains = refs[:size], refs[size : 2 * size]
    passed_gain_ref, own_ref, normed_ref, scale_ref, gain_ref, copy_ref = refs[2 * size :]
    for i in range(size):
        copy_ref[i] = own_ref[...]
    width = parts[0].shape[1]
    mine = head_ref[0]

    def pick(i, refs, passed):
        if size == 4 and i == 1:
            return jnp.where(mine == 0, passed[...], refs[i][...])
        if size == 4 and i == 3:
            return jnp.where(mine == 3, passed[...], refs[i][...])
        return refs[i][...]

    part = lambda i: pick(i, parts, passed_ref).astype(F32)
    gain = lambda i: pick(i, gains, passed_gain_ref)[0:1].astype(F32)
    squares = sum(jnp.sum(part(i) ** 2, axis=1, keepdims=True) for i in range(size))
    scale = lax.rsqrt(squares / (size * width) + EPSILON)
    scale_ref[...] = jnp.broadcast_to(scale, scale_ref.shape)
    place_parts(
        mine, parts, normed_ref, width,
        lambda i: (part(i) * scale_ref[:, 0:1] * gain(i)).astype(BF16),
    )
    place_parts(mine, parts, gain_ref, width, lambda i: jnp.broadcast_to(gain(i), (8, width)))


def mixed_grad_kernel(parts_ref, weight_ref, out_ref, full_ref):
    size, _, width = parts_ref.shape
    for i in range(size):
        full_ref[:, i * width : (i + 1) * width] = parts_ref[i]
    out_ref[...] = dot_nt(full_ref[...], weight_ref[...])


def out_kernel(loose_ref, mixed_ref, weight_ref, out_ref):
    width = out_ref.shape[2]
    for owner in range(out_ref.shape[0]):
        value = dot(mixed_ref[...], weight_ref[:, owner * width : (owner + 1) * width])
        out_ref[owner] = value.astype(BF16)


def conv_kernel(
    value_ref, state_ref, value_kernel_ref, value_bias_ref, state_kernel_ref, state_bias_ref,
    f_ref, k_ref, conv_ref, weighted_ref, value_slope_ref, maps_ref, state_slope_ref, total_ref,
):
    chunk = pl.program_id(0)
    clear(total_ref)
    around = pl.ds(pl.multiple_of(chunk * CHUNK, CHUNK), CHUNK + HALO)
    pre = taps(
        state_ref[around, :].astype(F32), state_kernel_ref[...].astype(F32),
        state_bias_ref[...].astype(F32), HALO - KERNEL + 1,
    )
    conv, slope = silu_parts(pre)
    maps = conv.astype(BF16)
    maps_ref[...] = maps
    state_slope_ref[...] = slope
    pre = taps(
        value_ref[around, :].astype(F32), value_kernel_ref[...].astype(F32),
        value_bias_ref[...].astype(F32), HALO - KERNEL + 1,
    )
    conv, slope = silu_parts(pre)
    conv = conv.astype(BF16)
    conv_ref[...] = conv
    value_slope_ref[...] = slope
    weighted = (conv.astype(F32) * expand(f_ref[...], conv.shape[1])).astype(BF16)
    weighted_ref[...] = weighted
    factor = k_ref[pl.ds(chunk, 1), :]
    total_ref[:NSTATE, :] = factor * (
        factor * total_ref[:NSTATE, :] + dot_tn(maps[:, :NSTATE], weighted)
    )
    total_ref[NSTATE:, :] = jnp.broadcast_to(k_ref[7:8, :], (8, k_ref.shape[1]))


def mixer_kernel(
    state_in_ref, maps_ref, weighted_ref, conv_ref, e_ref, k_ref, skip_ref, gate_ref, grad_ref, gain_ref,
    mixer_ref, stats_ref, high_ref, low_ref, state_ref,
):
    chunk = pl.program_id(0)

    def start():
        state_ref[...] = state_in_ref[...]

    first_step(start)
    lane = lax.broadcasted_iota(jnp.int32, (CHUNK, CHUNK), 1)
    factor = k_ref[pl.ds(chunk, 1), :]
    input_map, output_map = maps_ref[:, :NSTATE], maps_ref[:, NSTATE:]
    weighted = weighted_ref[...]
    scaled = factor * state_ref[...]
    high, low = split(scaled)
    high_ref[0], low_ref[0] = high, low
    scores = jnp.where(lower_mask(), dot_nt(output_map, input_map), 0.0).astype(BF16)
    mixed = dot(
        jnp.concatenate([scores, output_map], axis=1), jnp.concatenate([weighted, high], axis=0)
    )
    mixed = mixed + dot(output_map, low)
    mixer = expand(e_ref[...], weighted.shape[1]) * mixed + skip_ref[...] * conv_ref[...].astype(F32)
    mixer_ref[...] = mixer
    gate = gate_ref[...]
    gated = mixer * (gate * jax.nn.sigmoid(gate))
    squares = jnp.sum(gated * gated, axis=1, keepdims=True)
    products = jnp.sum(gated * (grad_ref[...] * gain_ref[...].astype(F32)), axis=1, keepdims=True)
    sums = jnp.where(lane == 0, squares, jnp.where(lane == 1, products, 0.0))
    stats_ref[...] = sums.T[:8]
    state_ref[...] = factor * (scaled + dot_tn(input_map, weighted))


def column(row_block):
    rest = jnp.zeros((CHUNK - row_block.shape[0], CHUNK), F32)
    return jnp.concatenate([row_block, rest], axis=0).T


def row_of(sums):
    lane = lax.broadcasted_iota(jnp.int32, (CHUNK, CHUNK), 1)
    return jnp.where(lane == 0, sums, 0.0).T[:8]


def gate_kernel(
    inner, chunks, size, *refs
):
    stats_refs = refs[:size]
    (
        mixer_ref, gate_ref, grad_ref, gain_ref, conv_ref, e_ref, k_ref, maps_ref,
        mixed_ref, gate_grad_ref, mixer_grad_ref, small_ref, total_ref, cross_ref,
    ) = refs[size:]
    chunk = chunks - 1 - pl.program_id(0)
    clear(small_ref, total_ref)
    gain = gain_ref[...].astype(F32)
    stats = column(sum(ref[...] for ref in stats_refs))
    scale = lax.rsqrt(stats[:, 0:1] / inner + EPSILON)
    cross_term = stats[:, 1:2] * (scale * scale * scale) / inner
    gate = gate_ref[...]
    silu, slope = silu_parts(gate)
    mixer = mixer_ref[...]
    gated = mixer * silu
    normed = gated * scale
    mixed_ref[...] = (normed * gain).astype(BF16)
    grad = grad_ref[...]
    gated_grad = scale * (grad * gain) - gated * cross_term
    gate_grad = (gated_grad * mixer * slope).astype(BF16)
    gate_grad_ref[...] = gate_grad
    cross_ref[...] = row_of(jnp.sum(gate_grad.astype(F32) * gate, axis=1, keepdims=True))
    mixer_grad = gated_grad * silu
    mixer_grad_ref[...] = mixer_grad
    small_ref[0:1, :] += jnp.sum(grad * normed, axis=0, keepdims=True)
    small_ref[1:2, :] += jnp.sum(mixer_grad * conv_ref[...].astype(F32), axis=0, keepdims=True)
    high, low = split(expand(e_ref[...], grad.shape[1]) * mixer_grad)
    output_map = maps_ref[:, NSTATE:]
    factor = k_ref[pl.ds(chunk, 1), :]
    total_ref[:NSTATE, :] = factor * (
        factor * total_ref[:NSTATE, :] + (dot_tn(output_map, high) + dot_tn(output_map, low))
    )
    total_ref[NSTATE:, :] = jnp.broadcast_to(k_ref[7:8, :], (8, k_ref.shape[1]))


def back_kernel(
    chunks, early_ref, state_in_ref, mixer_grad_ref, e_ref, f_ref, k_ref, weighted_ref, high_ref, low_ref,
    maps_ref, value_slope_ref, state_slope_ref, skip_ref,
    value_ref, map_ref, state_ref,
):
    chunk = chunks - 1 - pl.program_id(0)

    def start():
        state_ref[...] = state_in_ref[...]

    first_step(start)
    lower = lower_mask()
    row = lax.broadcasted_iota(jnp.int32, (CHUNK, CHUNK), 0)
    upper = row <= lax.broadcasted_iota(jnp.int32, (CHUNK, CHUNK), 1)
    factor = k_ref[pl.ds(chunk, 1), :]
    input_map, output_map = maps_ref[:, :NSTATE], maps_ref[:, NSTATE:]
    weighted = weighted_ref[...]
    mixer_grad = mixer_grad_ref[...]
    high, low = split(expand(e_ref[...], weighted.shape[1]) * mixer_grad)
    scaled = factor * state_ref[...]
    state_high, state_low = split(scaled)
    both = jnp.concatenate([weighted, high_ref[0]], axis=0)
    sums = dot_nt(high, both) + dot_nt(low, both)
    score_grad = jnp.where(lower, sums[:, :CHUNK], 0.0).astype(BF16)
    output_grad = sums[:, CHUNK:] + dot_nt(high, low_ref[0]) + dot(score_grad, input_map)
    sums = dot_nt(weighted, jnp.concatenate([state_high, state_low], axis=0))
    input_grad = sums[:, :NSTATE] + sums[:, NSTATE:] + dot_tn(score_grad, output_map)
    scores = jnp.where(upper, dot_nt(input_map, output_map), 0.0).astype(BF16)
    grads = dot(
        jnp.concatenate([scores, input_map], axis=1), jnp.concatenate([high, state_high], axis=0)
    )
    decayed = expand(f_ref[...], weighted.shape[1]) * grads
    value_ref[...] = (decayed + skip_ref[...] * mixer_grad) * value_slope_ref[...]
    slope = state_slope_ref[...]
    map_ref[:, :NSTATE] = input_grad * slope[:, :NSTATE]
    map_ref[:, NSTATE:] = output_grad * slope[:, NSTATE:]
    state_ref[...] = factor * (scaled + (dot_tn(output_map, high) + dot_tn(output_map, low)))


def conv_back_kernel(
    chunks, value_ref, map_ref, after_ref, value_raw_ref, state_raw_ref, value_kernel_ref,
    state_kernel_ref, cross_in_ref,
    value_grad_ref, state_grad_ref, value_small_ref, state_small_ref, cross_ref, value_next_ref,
    state_next_ref,
):
    chunk = chunks - 1 - pl.program_id(0)
    channels = value_ref.shape[1]
    clear(value_small_ref, state_small_ref)

    def start():
        value_next_ref[...] = after_ref[:, :channels]
        state_next_ref[...] = after_ref[:, channels:]

    first_step(start)

    def back(slope_ref, next_ref, raw_ref, kernel_ref, grad_ref, small_ref):
        kernel = kernel_ref[...].astype(F32)
        slope = slope_ref[...]
        window = jnp.concatenate([slope, next_ref[...]], axis=0)
        around = pl.ds(pl.multiple_of(chunk * CHUNK, CHUNK), CHUNK + HALO)
        raw = raw_ref[around, :].astype(F32)
        grad = jnp.zeros_like(slope)
        for offset in range(KERNEL):
            back_by = KERNEL - 1 - offset
            grad = grad + kernel[offset : offset + 1] * window[back_by : back_by + CHUNK]
            begin = HALO - KERNEL + 1 + offset
            small_ref[offset : offset + 1, :] += jnp.sum(
                slope * raw[begin : begin + CHUNK], axis=0, keepdims=True
            )
        small_ref[KERNEL : KERNEL + 1, :] += jnp.sum(slope, axis=0, keepdims=True)
        grad = grad.astype(BF16)
        grad_ref[...] = grad
        next_ref[...] = slope[:8]
        return jnp.sum(grad.astype(F32) * raw[HALO:], axis=1, keepdims=True)

    crossed = back(map_ref, state_next_ref, state_raw_ref, state_kernel_ref, state_grad_ref, state_small_ref)
    crossed = crossed + back(
        value_ref, value_next_ref, value_raw_ref, value_kernel_ref, value_grad_ref, value_small_ref
    )
    cross_ref[...] = cross_in_ref[...] + row_of(crossed)


def normed_kernel(
    chunks, early_ref, out_ref_in, gate_grad_ref, value_grad_ref, state_grad_ref, gate_weight_ref, value_weight_ref,
    state_weight_ref, cross_ref, out_ref
):
    value = (
        dot_nt(gate_grad_ref[...], gate_weight_ref[...])
        + dot_nt(value_grad_ref[...], value_weight_ref[...])
        + dot_nt(state_grad_ref[...], state_weight_ref[...])
    )
    count = value.shape[0]
    out_ref[0, :count, :] = value.astype(BF16)
    line = lax.broadcasted_iota(jnp.int32, (HALO, CHUNK), 0)
    packed = jnp.zeros((HALO, CHUNK), F32)
    for chunk in range(chunks):
        row = cross_ref[0:1, chunk * CHUNK : (chunk + 1) * CHUNK]
        high = row.astype(BF16).astype(F32)
        packed = jnp.where(line == chunk, high, packed)
        packed = jnp.where(line == chunks + chunk, row - high, packed)
    out_ref[0, count:, :] = jnp.zeros((HALO, value.shape[1]), BF16)
    out_ref[0, count:, :CHUNK] = packed.astype(BF16)


def last_kernel(full_width, parts_ref, tokens_ref, scale_ref, gain_ref, cotangent_ref, out_ref):
    count = tokens_ref.shape[0]
    chunks = count // CHUNK
    size = parts_ref.shape[0]
    crossed = sum(parts_ref[i, count:, :CHUNK].astype(F32) for i in range(size))
    crossed = crossed[:chunks] + crossed[chunks : 2 * chunks]
    for chunk in range(chunks):
        rows = slice(chunk * CHUNK, (chunk + 1) * CHUNK)
        normed_grad = sum(parts_ref[i, rows, :].astype(F32) for i in range(size))
        scale = scale_ref[HALO + chunk * CHUNK : HALO + (chunk + 1) * CHUNK, 0:1]
        total = column(jnp.broadcast_to(crossed[chunk : chunk + 1], (8, CHUNK)))[:, 0:1]
        out_ref[rows, :] = (
            scale * gain_ref[...].astype(F32) * normed_grad
            - tokens_ref[rows, :].astype(F32) * (scale * scale * total / full_width)
            + cotangent_ref[rows, :].astype(F32)
        ).astype(BF16)


def store_piece(core_ref, kept_ref, given_ref, place, begin, piece):
    chips = kept_ref.shape[0]
    core, chip = place // chips, lax.rem(place, chips)
    rows = slice(begin, begin + piece.shape[0])
    piece = piece.astype(BF16)

    @pl.when(core_ref[0] == core)
    def _():
        kept_ref[chip, rows, :] = piece

    @pl.when(core_ref[0] != core)
    def _():
        given_ref[chip, rows, :] = piece


def gain_row(weight, block):
    sums = jnp.sum(weight.astype(F32) * block, axis=1, keepdims=True)
    lane = lax.broadcasted_iota(jnp.int32, (CHUNK, CHUNK), 1)
    rows = [
        jnp.where(lane == 0, sums[i : i + CHUNK], 0.0).T[0:1] for i in range(0, BLOCK, CHUNK)
    ]
    return jnp.concatenate(rows, axis=1)


def early_kernel(
    loose_ref, core_ref, normed_ref, gate_ref, mixed_ref, grad_ref, weight_ref,
    kept_ref, given_ref, gain_ref, held_ref
):
    chips, rows, channels = kept_ref.shape
    at = pl.program_id(0)
    count, width = grad_ref.shape
    pieces = 2 * chips
    step = width // pieces
    out_rows = channels // pieces
    out_blocks = channels // BLOCK
    every = width // BLOCK // out_blocks

    @pl.when(lax.rem(at, every) == 0)
    def _():
        held_ref[...] = dot_tn(mixed_ref[...], grad_ref[...])

    block = dot_tn(normed_ref[HALO : HALO + count, :], gate_ref[...])
    gain_ref[...] = gain_row(weight_ref[...], block)
    for i in range(BLOCK // step):
        place = at * (BLOCK // step) + i
        begin = lax.rem(at, every) * (BLOCK // step * out_rows) + i * out_rows
        own = held_ref[pl.ds(pl.multiple_of(begin, 8), out_rows), :]
        parts = [block[i * step : (i + 1) * step]]
        parts += [own[:, j : j + channels] for j in range(0, width, channels)]
        store_piece(core_ref, kept_ref, given_ref, place, 0, jnp.concatenate(parts, axis=0))


def late_kernel(
    early_ref, core_ref, normed_ref, value_ref, state_ref, value_small_ref, gate_small_ref, gain_ref,
    state_small_ref, value_weight_ref, state_weight_ref, gain_full_ref,
    kept_ref, given_ref, own_ref, shared_ref, gains_ref,
):
    chips, rows, channels = kept_ref.shape
    at = pl.program_id(0)
    count, maps_width = state_ref.shape
    width = gains_ref.shape[1]
    pieces = 2 * chips
    step = width // pieces
    lanes = channels // 128
    part = 2 * step // lanes
    columns = normed_ref[HALO : HALO + count, :]
    value = dot_tn(columns, value_ref[...])
    state = dot_tn(columns, state_ref[...])
    gain = (
        gain_ref[...] + gain_row(value_weight_ref[...], value) + gain_row(state_weight_ref[...], state)
    ) / gain_full_ref[0:1, :]
    gains_ref[0:1, pl.ds(pl.multiple_of(at * BLOCK, 128), BLOCK)] = gain
    for i in range(BLOCK // step):
        piece = slice(i * step, (i + 1) * step)
        stacked = jnp.concatenate([state[piece, :128], state[piece, 128:]], axis=0)
        stacked = jnp.concatenate(
            [stacked[j * part : (j + 1) * part] for j in range(lanes)], axis=1
        )
        store_piece(
            core_ref, kept_ref, given_ref, at * (BLOCK // step) + i, 0,
            jnp.concatenate([value[piece], stacked], axis=0),
        )

    @pl.when(at == width // BLOCK - 1)
    def _():
        own_ref[...] = jnp.zeros_like(own_ref)
        own_ref[: KERNEL + 1, :] = value_small_ref[: KERNEL + 1, :]
        own_ref[KERNEL + 1 : KERNEL + 3, :] = gate_small_ref[:2, :]
        shared_ref[...] = jnp.zeros_like(shared_ref)
        begin = width // channels
        for i in range(begin):
            shared_ref[i : i + 1, :] = gains_ref[0:1, i * channels : (i + 1) * channels]
        for i in range(0, (KERNEL + 1) * maps_width, 128):
            tap, column_from = divmod(i, maps_width)
            row, column_to = divmod(i, channels)
            shared_ref[begin + row : begin + row + 1, column_to : column_to + 128] = state_small_ref[
                tap : tap + 1, column_from : column_from + 128
            ]
        line = lax.broadcasted_iota(jnp.int32, (HALO, channels), 0)
        for place in range(pieces):
            own, shared = own_ref[place : place + 1, :], shared_ref[place : place + 1, :]
            own_high, shared_high = (v.astype(BF16).astype(F32) for v in (own, shared))
            small = jnp.zeros((HALO, channels), F32)
            for to, value in enumerate((own_high, own - own_high, shared_high, shared - shared_high)):
                small = jnp.where(line == to, value, small)
            store_piece(core_ref, kept_ref, given_ref, place, step + part, small)


def merge_pairs(block):
    tail = block[-HALO:]
    line = lax.broadcasted_iota(jnp.int32, tail.shape, 0)
    own, shared = tail[0:1] + tail[1:2], tail[2:3] + tail[3:4]
    own_high, shared_high = own.astype(BF16).astype(F32), shared.astype(BF16).astype(F32)
    new = jnp.zeros_like(tail)
    for at, value in enumerate((own_high, own - own_high, shared_high, shared - shared_high)):
        new = jnp.where(line == at, value, new)
    return jnp.concatenate([block[:-HALO], new], axis=0)


def heads_kernel(piece_ref, total_ref, arrived_ref, out_ref, low_ref):
    total = merge_pairs(total_ref[...] + arrived_ref[...].astype(F32))
    line = lax.broadcasted_iota(jnp.int32, total.shape, 0)
    first = total.shape[0] - HALO
    own = (line >= first) & (line < first + 2)
    out_ref[...] = total
    low_ref[...] = jnp.where(own, piece_ref[...], total).astype(BF16)


def half_kernel(paired, chips, chip_ref, kept_ref, arrived_ref, *refs):
    outs = refs[-chips:]
    for bits in range(chips):
        place = lax.bitwise_xor(chip_ref[0], bits)
        value = kept_ref[place].astype(F32) + arrived_ref[place].astype(F32)
        if paired:
            value = merge_pairs(value)
        outs[bits][...] = value.astype(outs[bits].dtype)


def piece_kernel(parts, paired, cut, *refs):
    total = sum(ref[...].astype(F32) for ref in refs[:parts])
    if not paired:
        refs[-1][...] = total.astype(BF16)
        return
    first_ref, last_ref = refs[-2:]
    first_ref[...] = total[:cut].astype(BF16)
    last_ref[...] = merge_pairs(total[cut:])


def square_half_kernel(
    chip_ref, kept_ref, arrived_ref, loose_ref, first_ref, first_give_ref, last_ref, last_give_ref
):
    cut = first_ref.shape[1]
    for bits in range(4):
        place = lax.bitwise_xor(chip_ref[0], bits)
        value = kept_ref[place].astype(F32) + arrived_ref[place].astype(F32)
        low, high = bits & 1, bits >> 1
        ref = first_give_ref if low else first_ref
        ref[high] = value[:cut].astype(ref.dtype)
        ref = last_give_ref if high else last_ref
        ref[low] = value[cut:].astype(ref.dtype)


def square_next_kernel(
    first_ref, first_got_ref, last_ref, last_got_ref, loose_ref,
    first_out_ref, first_give_ref, last_out_ref, last_give_ref,
):
    first_out_ref[...] = first_ref[0] + first_got_ref[0].astype(F32)
    first_give_ref[...] = (first_ref[1] + first_got_ref[1].astype(F32)).astype(BF16)
    last_out_ref[...] = last_ref[0] + last_got_ref[0].astype(F32)
    last_give_ref[...] = (last_ref[1] + last_got_ref[1].astype(F32)).astype(BF16)


def square_last_kernel(first_ref, first_got_ref, last_ref, last_got_ref, loose_ref, *outs):
    outs[0][...] = (first_ref[...] + first_got_ref[...].astype(F32)).astype(BF16)
    outs[1][...] = (last_ref[...] + last_got_ref[...].astype(F32)).astype(BF16)


def each_piece(core_ref, chip_ref, chips, groups, refs):
    refs = iter(refs)
    for part, bits_lists in enumerate(groups):
        number = 0
        for bits_list in bits_lists:
            for core, ref in ((core_ref[0], next(refs)), (1 - core_ref[0], next(refs))):
                for at, bits in enumerate(bits_list):
                    place = core * chips + lax.bitwise_xor(chip_ref[0], bits)
                    yield part, number, place, ref[at].astype(F32)
                    number += 1


def send_rows(buffer_ref, number, target_ref, place, sem_ref):
    rows = buffer_ref.shape[1]
    copy = pltpu.make_async_copy(
        buffer_ref.at[number],
        target_ref.at[pl.ds(pl.multiple_of(place * rows, 8), rows), :],
        sem_ref.at[number],
    )
    copy.start()
    return copy


def early_out_kernel(chips, groups, core_ref, chip_ref, *refs):
    gate_ref, output_ref, gate_buffer, output_buffer, gate_sems, output_sems = refs[-6:]
    out_rows, width = output_buffer.shape[1:]
    channels = gate_buffer.shape[2]
    copies = []
    for part, number, place, value in each_piece(core_ref, chip_ref, chips, groups, refs[:-6]):
        if part == 0:
            gate_buffer[number] = value
            copies.append(send_rows(gate_buffer, number, gate_ref, place, gate_sems))
        else:
            output_buffer[number] = jnp.concatenate(
                [value[i * out_rows : (i + 1) * out_rows] for i in range(width // channels)], axis=1
            )
            copies.append(send_rows(output_buffer, number, output_ref, place, output_sems))
    for copy in copies:
        copy.wait()


def late_out_kernel(chips, groups, core_ref, chip_ref, *refs):
    value_ref, buffer, sems = refs[-3:]
    copies = []
    for _, number, place, value in each_piece(core_ref, chip_ref, chips, groups, refs[:-3]):
        buffer[number] = value
        copies.append(send_rows(buffer, number, value_ref, place, sems))
    for copy in copies:
        copy.wait()


def shared_out_kernel(chips, groups, size, core_ref, chip_ref, head_ref, *refs):
    (
        state_ref, value_kernel_ref, value_bias_ref, state_kernel_ref, state_bias_ref, skip_ref,
        gated_ref, gain_ref, buffer, sems, own_ref, shared_ref,
    ) = refs[-12:]
    step, maps_width = buffer.shape[1:]
    channels = own_ref.shape[1]
    lanes = channels // 128
    rows = 2 * step // lanes
    copies = []
    for _, number, place, piece in each_piece(core_ref, chip_ref, chips, groups, refs[:-12]):
        stacked = jnp.concatenate(
            [piece[:rows, i * 128 : (i + 1) * 128] for i in range(lanes)], axis=0
        )
        buffer[number] = jnp.concatenate([stacked[:step], stacked[step:]], axis=1)
        copies.append(send_rows(buffer, number, state_ref, place, sems))
        own_ref[pl.ds(place, 1), :] = piece[rows : rows + 1] + piece[rows + 1 : rows + 2]
        shared_ref[pl.ds(place, 1), :] = piece[rows + 2 : rows + 3] + piece[rows + 3 : rows + 4]
    value_kernel_ref[...] = own_ref[:KERNEL, :]
    value_bias_ref[...] = own_ref[KERNEL, :]
    gated_ref[...] = own_ref[KERNEL + 1, :]
    heads = skip_ref.shape[0]
    at = lax.broadcasted_iota(jnp.int32, (heads, channels), 1)
    row = lax.broadcasted_iota(jnp.int32, (heads, channels), 0) * HEAD_DIM
    inside = (at >= row) & (at < row + HEAD_DIM)
    skip_ref[...] = jnp.sum(jnp.where(inside, own_ref[KERNEL + 2 : KERNEL + 3, :], 0.0), axis=1)
    own_width = gain_ref.shape[0]
    gain_rows = -(-own_width * size // channels)
    for head in range(size):
        row, begin = divmod(head * own_width, channels)

        @pl.when(head_ref[0] == head)
        def _(row=row, begin=begin):
            gain_ref[...] = shared_ref[row, begin : begin + own_width]

    for i in range(0, (KERNEL + 1) * maps_width, 128):
        tap, column_to = divmod(i, maps_width)
        row, column_from = divmod(i, channels)
        value = shared_ref[gain_rows + row : gain_rows + row + 1, column_from : column_from + 128]
        if tap < KERNEL:
            state_kernel_ref[tap : tap + 1, column_to : column_to + 128] = value
        else:
            state_bias_ref[column_to : column_to + 128] = value[0]
    for copy in copies:
        copy.wait()


SCALAR = "scalar"
WHOLE = "whole"
BLOCKED = "blocked"
LANES = "lanes"
LEADING = "leading"
FAR = "far"
LOOSE = "loose"


def run(kernel, name, flops, args, outs, steps=None, backward=False, scratch=()):
    at = (lambda i: steps - 1 - i) if backward else (lambda i: i)

    def spec(kind, shape):
        if isinstance(kind, int):
            return pl.BlockSpec((kind,) + shape[1:], lambda i: (at(i), 0))
        if kind == SCALAR:
            return pl.BlockSpec(memory_space=pltpu.SMEM)
        if kind == LOOSE:
            return pl.BlockSpec(memory_space=pl.ANY)
        if kind == FAR:
            return pl.BlockSpec(memory_space=pltpu.HBM)
        if isinstance(kind, tuple):
            return pl.BlockSpec(*kind)
        if steps is None:
            return pl.BlockSpec(memory_space=pltpu.VMEM)
        if kind == BLOCKED:
            return pl.BlockSpec((CHUNK, shape[1]), lambda i: (at(i), 0))
        if kind == LANES:
            return pl.BlockSpec((shape[0], CHUNK), lambda i: (0, at(i)))
        if kind == LEADING:
            return pl.BlockSpec((1,) + shape[1:], lambda i: (at(i),) + (0,) * (len(shape) - 1))
        return pl.BlockSpec(shape, lambda i: (0,) * len(shape))

    moved = sum(a.size * a.dtype.itemsize for kind, a in args if kind != LOOSE)
    shapes = [jax.ShapeDtypeStruct(shape, dtype) for _, shape, dtype in outs]
    moved += sum(a.size * a.dtype.itemsize for a in shapes)
    return pl.pallas_call(
        kernel,
        out_shape=shapes,
        in_specs=[spec(kind, a.shape) for kind, a in args],
        out_specs=[spec(kind, shape) for kind, shape, _ in outs],
        scratch_shapes=list(scratch),
        compiler_params=pltpu.CompilerParams(vmem_limit_bytes=VMEM_LIMIT),
        cost_estimate=pl.CostEstimate(flops=flops, bytes_accessed=moved, transcendentals=0),
        name=name,
        **({} if steps is None else {"grid": (steps,)}),
    )(*(a for _, a in args))


def per_device(
    tokens, decay_codes, norm_gain, gate_weight, value_weight, state_weight, value_kernel, value_bias,
    state_kernel, state_bias, skip_scale, gated_gain, output_weight, cotangent,
):
    tokens, decay_codes, cotangent = tokens[0], decay_codes[0], cotangent[0]
    count, own_width = tokens.shape
    heads = skip_scale.shape[0]
    channels = heads * HEAD_DIM
    head_size, chips = lax.axis_size("head"), lax.axis_size("chip")
    seq_size = 2 * chips
    width = own_width * head_size
    maps_width = 2 * NSTATE
    chunks = count // CHUNK
    core = (SCALAR, lax.axis_index("core").astype(jnp.int32)[None])
    chip = (SCALAR, lax.axis_index("chip").astype(jnp.int32)[None])
    head = (SCALAR, lax.axis_index("head").astype(jnp.int32)[None])

    rows = count + MARGIN
    packed = jnp.concatenate(
        [
            from_behind(tokens[-HALO:], 1),
            tokens,
            jnp.broadcast_to(norm_gain[None], (MARGIN - HALO, own_width)),
        ],
        axis=0,
    )
    logs = decay_codes.astype(F32) * (-DECAY_STEP)
    input_weight = jnp.sqrt(-jnp.expm1(2.0 * logs))
    e_full, f_full, factors = run(
        decay_kernel, "decays", count * channels * 200,
        [(WHOLE, decay_codes), (WHOLE, input_weight)],
        [
            (WHOLE, (count, heads), F32),
            (WHOLE, (count, heads), F32),
            (WHOLE, (8, channels), F32),
        ],
    )
    parts, passed = line_parts(packed, "head")
    skip_full = jnp.repeat(skip_scale, HEAD_DIM)[None]

    half = rows // 2
    gain_rows = ((MARGIN - HALO, own_width), lambda i: ((HALO + count) // (MARGIN - HALO), 0))
    normed, scale_in, gain_full, copies = run(
        functools.partial(norm_kernel, head_size), "norm", count * width * 10,
        [head, (half, passed)] + [(half, part) for part in parts]
        + [(gain_rows, part) for part in parts] + [(gain_rows, passed), (count // 2, cotangent)],
        [
            (half, (rows, width), BF16),
            (half, (rows, 128), F32),
            (WHOLE, (8, width), F32),
            (
                ((head_size, count // 2, own_width), lambda i: (0, i, 0)),
                (head_size, count, own_width), BF16,
            ),
        ],
        steps=2,
    )
    cotangent_parts = deal(copies, "head")
    value_raw = dot(normed, value_weight).astype(BF16)
    state_raw = dot(normed, state_weight).astype(BF16)
    conv, weighted, value_slope, maps, map_slope, local_end = run(
        conv_kernel, "conv", count * channels * 400,
        [
            (WHOLE, value_raw), (WHOLE, state_raw), (WHOLE, value_kernel), (WHOLE, value_bias[None]),
            (WHOLE, state_kernel), (WHOLE, state_bias[None]), (BLOCKED, f_full), (WHOLE, factors),
        ],
        [
            (BLOCKED, (count, channels), BF16),
            (BLOCKED, (count, channels), BF16),
            (BLOCKED, (count, channels), F32),
            (BLOCKED, (count, maps_width), BF16),
            (BLOCKED, (count, maps_width), F32),
            (WHOLE, (NSTATE + 8, channels), F32),
        ],
        steps=chunks,
    )
    gate_pre = dot(normed, gate_weight)[HALO : HALO + count]
    state_in, _, _ = entering(core, chip, local_end, False, (gate_pre,))
    mixed_grad, full_cotangent = run(
        mixed_grad_kernel, "mixed_grad", 2 * count * width * channels,
        [(WHOLE, cotangent_parts), (WHOLE, output_weight)],
        [(WHOLE, (count, channels), F32), (WHOLE, (count, width), BF16)],
    )
    mixer, stats, high, low = run(
        mixer_kernel, "mixer", count * channels * 1000,
        [
            (WHOLE, state_in), (BLOCKED, maps), (BLOCKED, weighted), (BLOCKED, conv),
            (BLOCKED, e_full), (WHOLE, factors), (WHOLE, skip_full), (BLOCKED, gate_pre),
            (BLOCKED, mixed_grad), (WHOLE, gated_gain[None]),
        ],
        [
            (BLOCKED, (count, channels), F32),
            (LANES, (8, count), F32),
            (LEADING, (chunks, NSTATE, channels), BF16),
            (LEADING, (chunks, NSTATE, channels), BF16),
        ],
        steps=chunks,
        scratch=[pltpu.VMEM((NSTATE, channels), F32)],
    )
    mixed, gate_grad, mixer_grad, gate_small, start_grad, gate_cross = run(
        functools.partial(gate_kernel, float(channels * head_size), chunks, head_size),
        "gate", count * channels * 600,
        [(LANES, part) for part in turn_all(stats, "head")]
        + [
            (BLOCKED, mixer), (BLOCKED, gate_pre), (BLOCKED, mixed_grad), (WHOLE, gated_gain[None]),
            (BLOCKED, conv), (BLOCKED, e_full), (WHOLE, factors), (BLOCKED, maps),
        ],
        [
            (BLOCKED, (count, channels), BF16),
            (BLOCKED, (count, channels), BF16),
            (BLOCKED, (count, channels), F32),
            (WHOLE, (8, channels), F32),
            (WHOLE, (NSTATE + 8, channels), F32),
            (LANES, (8, count), F32),
        ],
        steps=chunks,
        backward=True,
    )
    step, out_rows = width // seq_size, channels // seq_size
    early_rows = step + out_rows * (width // channels)
    features = width // BLOCK
    feature_block = ((rows, BLOCK), lambda i: (0, i))
    every = features // (channels // BLOCK)
    out_parts = run(
        out_kernel, "out", 2 * count * channels * width,
        [(LOOSE, start_grad), (WHOLE, mixed), (WHOLE, output_weight)],
        [(WHOLE, (head_size, count, own_width), BF16)],
    )[0]
    early_made = []

    def make_early(pair):
        early_made.extend(
            run(
                early_kernel, "early", 4 * count * channels * width,
                [
                    (LOOSE, pair), core, (feature_block, normed), (WHOLE, gate_grad),
                    (((count, BLOCK), lambda i: (0, i // every)), mixed), (WHOLE, full_cotangent),
                    (BLOCK, gate_weight),
                ],
                [(WHOLE, (chips, early_rows, channels), BF16)] * 2
                + [(((1, BLOCK), lambda i: (0, i)), (1, width), F32)],
                steps=features,
                scratch=[pltpu.VMEM((BLOCK, width), F32)],
            )
        )
        return early_made[1:2]

    grad_after, after_prefix, after_first = entering(
        core, chip, start_grad, True, (out_parts,), make_early
    )
    early_kept, early_given, early_gain = early_made
    early_state, half_mark = sum_pieces(
        chip, early_kept, early_given, "early", True, step, False, (after_prefix,)
    )
    out_arrived = deal(tie(out_parts, after_first), "head")
    branch = jnp.sum(out_arrived.astype(F32), axis=0)
    block_out = (tokens.astype(F32) + branch).astype(BF16)

    value_grads, map_grads = run(
        functools.partial(back_kernel, chunks), "back", count * channels * 2000,
        [
            (LOOSE, half_mark), (WHOLE, grad_after), (BLOCKED, mixer_grad), (BLOCKED, e_full),
            (BLOCKED, f_full), (WHOLE, factors), (BLOCKED, weighted), (LEADING, high),
            (LEADING, low), (BLOCKED, maps), (BLOCKED, value_slope), (BLOCKED, map_slope),
            (WHOLE, skip_full),
        ],
        [(BLOCKED, (count, channels), F32), (BLOCKED, (count, maps_width), F32)],
        steps=chunks,
        backward=True,
        scratch=[pltpu.VMEM((NSTATE, channels), F32)],
    )
    after = from_behind(jnp.concatenate([value_grads[:8], map_grads[:8]], axis=1), -1)
    value_raw_grad, state_raw_grad, value_small, state_small, crossed = run(
        functools.partial(conv_back_kernel, chunks), "conv_back", count * channels * 100,
        [
            (BLOCKED, value_grads), (BLOCKED, map_grads), (WHOLE, after),
            (WHOLE, value_raw), (WHOLE, state_raw), (WHOLE, value_kernel), (WHOLE, state_kernel),
            (LANES, gate_cross),
        ],
        [
            (BLOCKED, (count, channels), BF16),
            (BLOCKED, (count, maps_width), BF16),
            (WHOLE, (8, channels), F32),
            (WHOLE, (8, maps_width), F32),
            (LANES, (8, count), F32),
        ],
        steps=chunks,
        backward=True,
        scratch=[pltpu.VMEM((8, channels), F32), pltpu.VMEM((8, maps_width), F32)],
    )
    next_mark = early_state[0]
    if chips == 4:
        early_state = square_next("early", early_state, early_rows * channels, crossed)
        next_mark = early_state[0]
    normed_parts = run(
        functools.partial(normed_kernel, chunks), "normed", 4 * count * channels * width,
        [
            (LOOSE, next_mark), (LOOSE, out_arrived), (WHOLE, gate_grad), (WHOLE, value_raw_grad),
            (WHOLE, state_raw_grad), (own_width, gate_weight), (own_width, value_weight),
            (own_width, state_weight), (WHOLE, crossed),
        ],
        [(LEADING, (head_size, count + HALO, own_width), BF16)],
        steps=head_size,
    )[0]
    if chips == 4:
        early_gate, early_out = square_end(
            "early", early_state,
            [(WHOLE, (step, channels), BF16), (WHOLE, (early_rows - step, channels), BF16)],
            early_rows * channels, normed_parts,
        )
    else:
        early_gate, early_out = early_state[0][:step], early_state[0][step:]
    lanes = channels // 128
    state_rows = 2 * step // lanes
    late_rows = step + state_rows + HALO
    late_kept, late_given = run(
        late_kernel, "late", 3 * count * channels * width,
        [
            (LOOSE, early_gate), core, (feature_block, normed), (WHOLE, value_raw_grad),
            (WHOLE, state_raw_grad),
            (WHOLE, value_small), (WHOLE, gate_small), (((1, BLOCK), lambda i: (0, i)), early_gain),
            (WHOLE, state_small), (BLOCK, value_weight), (BLOCK, state_weight),
            (((8, BLOCK), lambda i: (0, i)), gain_full),
        ],
        [(WHOLE, (chips, late_rows, channels), BF16)] * 2,
        steps=features,
        scratch=[
            pltpu.VMEM((HALO, channels), F32),
            pltpu.VMEM((HALO, channels), F32),
            pltpu.VMEM((8, width), F32),
        ],
    )
    (late_piece, shared_piece), late_mark = sum_pieces(
        chip, late_kept, late_given, "late", False, step, True
    )
    normed_parts = deal(normed_parts, "head")
    shared_piece = heads_sum(shared_piece)

    def unpack(kernel, name, pieces, outs, flops, scratch, extra=(), args=()):
        groups = [collect(*piece) for piece in pieces]
        bits = [[found[2] for found in group] for group in groups]
        arrays = [(WHOLE, value) for group in groups for found in group for value in found[:2]]
        return run(
            functools.partial(kernel, chips, bits, *extra), name, flops,
            [core, chip, *args] + arrays, outs, scratch=scratch,
        )

    sems = pltpu.SemaphoreType.DMA((seq_size,))
    gate_weight_gradient, output_weight_gradient = unpack(
        early_out_kernel, "early_out",
        [(early_gate, (2, 1), late_mark), (early_out, (1, 2), late_mark)],
        [(FAR, (width, channels), F32), (FAR, (channels, width), F32)], 4 * channels * width,
        [
            pltpu.VMEM((seq_size, step, channels), F32),
            pltpu.VMEM((seq_size, out_rows, width), F32),
            sems,
            sems,
        ],
    )
    value_weight_gradient = unpack(
        late_out_kernel, "late_out", [(late_piece, None)],
        [(FAR, (width, channels), F32)], 2 * channels * width,
        [pltpu.VMEM((seq_size, step, channels), F32), sems],
    )[0]
    (
        state_weight_gradient, value_kernel_gradient, value_bias_gradient, state_kernel_gradient,
        state_bias_gradient, skip_scale_gradient, gated_gain_gradient, norm_gain_gradient,
    ) = unpack(
        shared_out_kernel, "shared_out", [(shared_piece, (2, 1))],
        [
            (FAR, (width, maps_width), F32),
            (WHOLE, (KERNEL, channels), F32),
            (WHOLE, (channels,), F32),
            (WHOLE, (KERNEL, maps_width), F32),
            (WHOLE, (maps_width,), F32),
            (WHOLE, (heads,), F32),
            (WHOLE, (channels,), F32),
            (WHOLE, (own_width,), F32),
        ],
        2 * maps_width * width,
        [
            pltpu.VMEM((seq_size, step, maps_width), F32),
            sems,
            pltpu.VMEM((HALO, channels), F32),
            pltpu.VMEM((HALO, channels), F32),
        ],
        extra=(head_size,),
        args=[head],
    )
    tokens_gradient = run(
        functools.partial(last_kernel, float(width)), "last", count * own_width * 20,
        [
            (WHOLE, normed_parts), (WHOLE, tokens), (WHOLE, scale_in),
            (WHOLE, norm_gain[None]), (WHOLE, cotangent),
        ],
        [(WHOLE, (count, own_width), BF16)],
    )[0]
    return (
        block_out[None],
        tokens_gradient[None],
        norm_gain_gradient,
        gate_weight_gradient,
        value_weight_gradient,
        state_weight_gradient,
        value_kernel_gradient,
        value_bias_gradient,
        state_kernel_gradient,
        state_bias_gradient,
        skip_scale_gradient,
        gated_gain_gradient,
        output_weight_gradient,
    )


def solution(mesh):
    seq_size, head_size = mesh.shape["seq"], mesh.shape["head"]
    mesh = Mesh(mesh.devices.reshape(seq_size // 2, 2, head_size), ("chip", "core", "head"))
    seq = ("chip", "core")
    in_specs = (
        P(None, seq, "head"),
        P(None, seq, "head"),
        P("head"),
        P(None, "head"),
        P(None, "head"),
        P(),
        P(None, "head"),
        P("head"),
        P(),
        P(),
        P("head"),
        P("head"),
        P("head", None),
        P(None, seq, "head"),
    )
    out_specs = (
        P(None, seq, "head"),
        P(None, seq, "head"),
        P("head"),
        P(None, "head"),
        P(None, "head"),
        P(),
        P(None, "head"),
        P("head"),
        P(),
        P(),
        P("head"),
        P("head"),
        P("head", None),
    )
    return jax.shard_map(
        per_device, mesh=mesh, in_specs=in_specs, out_specs=out_specs, check_vma=False
    )
```

```python
import functools

import jax
import jax.numpy as jnp
from jax import lax
from jax.experimental import pallas as pl
from jax.experimental.pallas import tpu as pltpu
from jax.sharding import Mesh
from jax.sharding import PartitionSpec as P

HEAD_DIM = 64
NSTATE = 128
KERNEL = 4
CHUNK = 128
BLOCK = 384
VMEM_LIMIT = 20 * 1024 * 1024
MARGIN = 32
HALO = 16


DECAY_STEP = 1.0 / 1048576.0
EPSILON = 1e-05
BF16 = jnp.bfloat16
F32 = jnp.float32


def tie_kernel(*refs):
    del refs


def tie(value, *others):
    return pl.pallas_call(
        tie_kernel,
        out_shape=jax.ShapeDtypeStruct(value.shape, value.dtype),
        in_specs=[pl.BlockSpec(memory_space=pl.ANY)] * (1 + len(others)),
        out_specs=pl.BlockSpec(memory_space=pl.ANY),
        input_output_aliases={0: 0},
        name="tie",
    )(value, *others)


def from_behind(value, by):
    axis = ("chip", "core")
    size = lax.axis_size("chip") * 2
    pairs = [(i, i + by) for i in range(size) if 0 <= i + by < size]
    return lax.ppermute(value, axis, pairs)


def beside(value):
    return lax.ppermute(value, "core", [(0, 1), (1, 0)])


def turn(value, axis, by):
    size = lax.axis_size(axis)
    return lax.ppermute(value, axis, [(i, (i + by) % size) for i in range(size)])


def turn_all(value, axis):
    return [value] + [turn(value, axis, by) for by in range(1, lax.axis_size(axis))]


def line_parts(value, axis):
    if lax.axis_size(axis) != 4:
        parts = turn_all(value, axis)
        return parts, value
    two = turn(value, axis, 2)
    one = lax.ppermute(value, axis, [(0, 1), (1, 2), (2, 3)])
    three = lax.ppermute(value, axis, [(1, 0), (2, 1), (3, 2)])
    passed = lax.ppermute(two, axis, [(2, 3), (1, 0)])
    return [value, one, two, three], passed


def deal(parts, axis):
    return lax.all_to_all(parts, axis, 0, 0)


def cross(value, bits):
    return lax.ppermute(value, "chip", [(i, i ^ bits) for i in range(lax.axis_size("chip"))])


def cross_all(value):
    return [value] + [cross(value, bits) for bits in range(1, lax.axis_size("chip"))]


def heads_sum(piece):
    total, low, first = piece, piece.astype(BF16), None
    bits, size = 1, lax.axis_size("head")
    while bits < size:
        arrived = lax.ppermute(low, "head", [(i, i ^ bits) for i in range(size)])
        total, low = run(
            heads_kernel, "heads", piece.size,
            [(WHOLE, piece), (WHOLE, total), (WHOLE, arrived)],
            [(WHOLE, piece.shape, F32), (WHOLE, piece.shape, BF16)],
        )
        first = low if first is None else first
        bits *= 2
    return low, first


def entering(core, chip, total, backward, meanwhile, later=lambda pair: ()):
    name = "after" if backward else "before"
    chips = lax.axis_size("chip")
    channels = total.shape[1]
    half = NSTATE // 2
    partner = beside(total)
    pair = run(
        functools.partial(pair_kernel, backward), name + "_pair", total.size,
        [core, (WHOLE, total), (WHOLE, partner)] + [(LOOSE, value) for value in meanwhile],
        [(WHOLE, (half + 8, channels), F32)],
    )[0]
    prefix = run(
        functools.partial(prefix_kernel, backward, chips), name + "_prefix", chips * pair.size,
        [chip] + [(WHOLE, value) for value in cross_all(pair)]
        + [(LOOSE, value) for value in later(pair)],
        [(WHOLE, (half, channels), F32)],
    )[0]
    return run(
        functools.partial(enter_kernel, backward), name + "_enter", total.size,
        [core, (WHOLE, partner), (WHOLE, prefix), (WHOLE, beside(prefix))],
        [(WHOLE, (NSTATE, channels), F32)],
    )[0], prefix


def sum_pieces(chip, kept, given, name, square, cut, paired, before_half=(), meanwhile=lambda mark: ()):
    chips, rows, channels = kept.shape
    arrived = beside(given)
    size = chips * rows * channels
    if paired:
        outs = [(WHOLE, (cut, channels), BF16), (WHOLE, (rows - cut, channels), F32)]
    else:
        outs = [(WHOLE, (rows, channels), BF16)]
    if chips != 4 or not square:
        halves = run(
            functools.partial(half_kernel, paired, chips), name + "_half", size,
            [chip, (WHOLE, kept), (WHOLE, arrived)] + [(LOOSE, mark) for mark in before_half],
            [(WHOLE, (rows, channels), F32)] + [(WHOLE, (rows, channels), BF16)] * (chips - 1),
        )
        parts = [halves[0]] + [cross(halves[bits], bits) for bits in range(1, chips)]
        found = run(
            functools.partial(piece_kernel, chips, paired, cut), name + "_piece", size,
            [(WHOLE, part) for part in parts] + [(LOOSE, mark) for mark in meanwhile(halves[0])],
            outs,
        )
        return found, halves[0]
    rest = rows - cut
    state = run(
        square_half_kernel, name + "_half", size,
        [chip, (WHOLE, kept), (WHOLE, arrived)] + [(LOOSE, mark) for mark in before_half],
        [
            (WHOLE, (2, cut, channels), F32), (WHOLE, (2, cut, channels), BF16),
            (WHOLE, (2, rest, channels), F32), (WHOLE, (2, rest, channels), BF16),
        ],
    )
    return state, state[0]


def square_next(name, state, size, mark):
    first, first_give, last, last_give = state
    _, cut, channels = first.shape
    rest = last.shape[1]
    return run(
        square_next_kernel, name + "_next", size,
        [
            (WHOLE, first), (WHOLE, cross(first_give, 1)),
            (WHOLE, last), (WHOLE, cross(last_give, 2)), (LOOSE, mark),
        ],
        [
            (WHOLE, (cut, channels), F32), (WHOLE, (cut, channels), BF16),
            (WHOLE, (rest, channels), F32), (WHOLE, (rest, channels), BF16),
        ],
    )


def square_end(name, state, outs, size, mark):
    first, first_give, last, last_give = state
    return run(
        square_last_kernel, name + "_piece", size,
        [
            (WHOLE, first), (WHOLE, cross(first_give, 2)),
            (WHOLE, last), (WHOLE, cross(last_give, 1)), (LOOSE, mark),
        ],
        outs,
    )


def collect(piece, order, mark=None):
    chips = lax.axis_size("chip")
    if chips != 4 or order is None:
        found = [(value[None], (bits,)) for bits, value in enumerate(cross_all(piece))]
    else:
        near, far = order
        both = jnp.stack([piece, cross(piece, near)])
        if mark is not None:
            both = tie(both, mark)
        found = [(both, (0, near)), (cross(both, far), (far, far ^ near))]
    return [(value, beside(value), bits) for value, bits in found]


def dot(left, right):
    return jnp.dot(left, right, preferred_element_type=F32)


def dot_nt(left, right):
    return lax.dot_general(left, right, (((1,), (1,)), ((), ())), preferred_element_type=F32)


def dot_tn(left, right):
    return lax.dot_general(left, right, (((0,), (0,)), ((), ())), preferred_element_type=F32)


def split(values):
    high = values.astype(BF16)
    return high, (values - high.astype(F32)).astype(BF16)


def lower_mask():
    row = lax.broadcasted_iota(jnp.int32, (CHUNK, CHUNK), 0)
    column = lax.broadcasted_iota(jnp.int32, (CHUNK, CHUNK), 1)
    return row >= column


def spread_heads(heads, channels):
    row = lax.broadcasted_iota(jnp.int32, (heads, channels), 0) * HEAD_DIM
    place = lax.broadcasted_iota(jnp.int32, (heads, channels), 1)
    return jnp.where((place >= row) & (place < row + HEAD_DIM), 1.0, 0.0).astype(BF16)


def expand(values, channels):
    high, low = split(values)
    spread = spread_heads(values.shape[1], channels)
    return dot(high, spread) + dot(low, spread)


def decay_kernel(codes_ref, weight_ref, e_ref, f_ref, k_ref):
    heads, channels = codes_ref.shape[1], k_ref.shape[1]
    lower = jnp.where(lower_mask(), 1.0, 0.0).astype(F32)
    count = codes_ref.shape[0] // CHUNK
    line = lax.broadcasted_iota(jnp.int32, (8, heads), 0)
    marks = jnp.zeros((8, heads), F32)
    total = jnp.zeros((1, heads), F32)
    for chunk in range(count):
        rows = pl.ds(chunk * CHUNK, CHUNK)
        logs = codes_ref[rows, :].astype(F32) * (-DECAY_STEP)
        cumulative = jnp.dot(
            lower, logs, precision=lax.Precision.HIGHEST, preferred_element_type=F32
        )
        last = cumulative[CHUNK - 1 :]
        middle = 0.5 * last
        e_ref[rows, :] = jnp.exp(cumulative - middle)
        f_ref[rows, :] = weight_ref[rows, :] * jnp.exp(middle - cumulative)
        marks = jnp.where(line == chunk, jnp.exp(middle), marks)
        total = total + last
    marks = jnp.where(line == 7, total, marks)
    high, low = split(marks)
    lowest = (marks - high.astype(F32) - low.astype(F32)).astype(BF16)
    spread = spread_heads(heads, channels)
    factors = dot(high, spread) + dot(low, spread) + dot(lowest, spread)
    k_ref[...] = factors


def pair_kernel(backward, core_ref, own_ref, other_ref, *refs):
    out_ref = refs[-1]
    half = NSTATE // 2
    logs, other_logs = own_ref[NSTATE:, :], other_ref[NSTATE:, :]
    for core in range(2):

        @pl.when(core_ref[0] == core)
        def _():
            rows = slice(core * half, (core + 1) * half)
            if core == (0 if backward else 1):
                out_ref[:half, :] = jnp.exp(logs[0:1]) * other_ref[rows, :] + own_ref[rows, :]
            else:
                out_ref[:half, :] = jnp.exp(other_logs[0:1]) * own_ref[rows, :] + other_ref[rows, :]

    out_ref[half:, :] = logs + other_logs


def prefix_kernel(backward, chips, chip_ref, *refs):
    parts, out_ref = refs[:chips], refs[-1]
    half = out_ref.shape[0]
    mine = chip_ref[0]
    total = jnp.zeros(out_ref.shape, F32)
    for bits in range(1, chips):
        source = lax.bitwise_xor(mine, bits)
        span = jnp.zeros((1, out_ref.shape[1]), F32)
        for other in range(1, chips):
            middle = lax.bitwise_xor(mine, other)
            if backward:
                between = (middle < source) & (middle > mine)
            else:
                between = (middle > source) & (middle < mine)
            span = span + jnp.where(between, parts[other][half : half + 1, :], 0.0)
        passes = source > mine if backward else source < mine
        total = total + jnp.where(passes, jnp.exp(span), 0.0) * parts[bits][:half, :]
    out_ref[...] = total


def enter_kernel(backward, core_ref, partner_ref, prefix_ref, other_ref, out_ref):
    half = prefix_ref.shape[0]
    decay = jnp.exp(partner_ref[NSTATE : NSTATE + 1, :])
    for core in range(2):

        @pl.when(core_ref[0] == core)
        def _():
            for place, ref in ((core, prefix_ref), (1 - core, other_ref)):
                rows = slice(place * half, (place + 1) * half)
                if core == (0 if backward else 1):
                    out_ref[rows, :] = decay * ref[...] + partner_ref[rows, :]
                else:
                    out_ref[rows, :] = ref[...]


def taps(window, kernel, bias, begin):
    summed = bias
    for offset in range(KERNEL):
        summed = summed + kernel[offset : offset + 1] * window[begin + offset : begin + offset + CHUNK]
    return summed


def silu_parts(values):
    sigmoid = jax.nn.sigmoid(values)
    return values * sigmoid, sigmoid * (1.0 + values * (1.0 - sigmoid))


def first_step(action):
    pl.when(pl.program_id(0) == 0)(action)


def clear(*refs):
    def action():
        for ref in refs:
            ref[...] = jnp.zeros_like(ref)

    first_step(action)


def place_parts(mine, parts, target, width, value):
    size = len(parts)
    if width % 128 == 0:
        for i in range(size):
            owner = lax.rem(mine + size - i, size)
            target[:, pl.ds(pl.multiple_of(owner * width, 128), width)] = value(i)
        return

    def write(me):
        for i in range(size):
            owner = (me + size - i) % size
            target[:, owner * width : (owner + 1) * width] = value(i)

    for me in range(size):
        pl.when(mine == me)(functools.partial(write, me))


def copies_kernel(loose_ref, own_ref, out_ref):
    for i in range(out_ref.shape[0]):
        out_ref[i] = own_ref[...]


def norm_kernel(size, head_ref, passed_ref, *refs):
    parts, gains = refs[:size], refs[size : 2 * size]
    passed_gain_ref, normed_ref, scale_ref, gain_ref = refs[2 * size :]
    width = parts[0].shape[1]
    mine = head_ref[0]

    def pick(i, refs, passed):
        if size == 4 and i == 1:
            return jnp.where(mine == 0, passed[...], refs[i][...])
        if size == 4 and i == 3:
            return jnp.where(mine == 3, passed[...], refs[i][...])
        return refs[i][...]

    part = lambda i: pick(i, parts, passed_ref).astype(F32)
    gain = lambda i: pick(i, gains, passed_gain_ref)[0:1].astype(F32)
    squares = sum(jnp.sum(part(i) ** 2, axis=1, keepdims=True) for i in range(size))
    scale = lax.rsqrt(squares / (size * width) + EPSILON)
    scale_ref[...] = jnp.broadcast_to(scale, scale_ref.shape)
    place_parts(
        mine, parts, normed_ref, width,
        lambda i: (part(i) * scale_ref[:, 0:1] * gain(i)).astype(BF16),
    )
    place_parts(mine, parts, gain_ref, width, lambda i: jnp.broadcast_to(gain(i), (8, width)))


def mixed_grad_kernel(parts_ref, weight_ref, out_ref, full_ref):
    size, _, width = parts_ref.shape
    for i in range(size):
        full_ref[:, i * width : (i + 1) * width] = parts_ref[i]
    out_ref[...] = dot_nt(full_ref[...], weight_ref[...])


def out_kernel(loose_ref, mixed_ref, weight_ref, out_ref):
    width = out_ref.shape[2]
    for owner in range(out_ref.shape[0]):
        value = dot(mixed_ref[...], weight_ref[:, owner * width : (owner + 1) * width])
        out_ref[owner] = value.astype(BF16)


def conv_kernel(
    value_ref, state_ref, value_kernel_ref, value_bias_ref, state_kernel_ref, state_bias_ref,
    f_ref, k_ref, conv_ref, weighted_ref, value_slope_ref, maps_ref, state_slope_ref, total_ref,
):
    chunk = pl.program_id(0)
    clear(total_ref)
    around = pl.ds(pl.multiple_of(chunk * CHUNK, CHUNK), CHUNK + HALO)
    pre = taps(
        state_ref[around, :].astype(F32), state_kernel_ref[...].astype(F32),
        state_bias_ref[...].astype(F32), HALO - KERNEL + 1,
    )
    conv, slope = silu_parts(pre)
    maps = conv.astype(BF16)
    maps_ref[...] = maps
    state_slope_ref[...] = slope
    pre = taps(
        value_ref[around, :].astype(F32), value_kernel_ref[...].astype(F32),
        value_bias_ref[...].astype(F32), HALO - KERNEL + 1,
    )
    conv, slope = silu_parts(pre)
    conv = conv.astype(BF16)
    conv_ref[...] = conv
    value_slope_ref[...] = slope
    weighted = (conv.astype(F32) * expand(f_ref[...], conv.shape[1])).astype(BF16)
    weighted_ref[...] = weighted
    factor = k_ref[pl.ds(chunk, 1), :]
    total_ref[:NSTATE, :] = factor * (
        factor * total_ref[:NSTATE, :] + dot_tn(maps[:, :NSTATE], weighted)
    )
    total_ref[NSTATE:, :] = jnp.broadcast_to(k_ref[7:8, :], (8, k_ref.shape[1]))


def mixer_kernel(
    state_in_ref, maps_ref, weighted_ref, conv_ref, e_ref, k_ref, skip_ref, gate_ref, grad_ref, gain_ref,
    mixer_ref, stats_ref, high_ref, low_ref, state_ref,
):
    chunk = pl.program_id(0)

    def start():
        state_ref[...] = state_in_ref[...]

    first_step(start)
    lane = lax.broadcasted_iota(jnp.int32, (CHUNK, CHUNK), 1)
    factor = k_ref[pl.ds(chunk, 1), :]
    input_map, output_map = maps_ref[:, :NSTATE], maps_ref[:, NSTATE:]
    weighted = weighted_ref[...]
    scaled = factor * state_ref[...]
    high, low = split(scaled)
    high_ref[0], low_ref[0] = high, low
    scores = jnp.where(lower_mask(), dot_nt(output_map, input_map), 0.0).astype(BF16)
    mixed = dot(
        jnp.concatenate([scores, output_map], axis=1), jnp.concatenate([weighted, high], axis=0)
    )
    mixed = mixed + dot(output_map, low)
    mixer = expand(e_ref[...], weighted.shape[1]) * mixed + skip_ref[...] * conv_ref[...].astype(F32)
    mixer_ref[...] = mixer
    gate = gate_ref[...]
    gated = mixer * (gate * jax.nn.sigmoid(gate))
    squares = jnp.sum(gated * gated, axis=1, keepdims=True)
    products = jnp.sum(gated * (grad_ref[...] * gain_ref[...].astype(F32)), axis=1, keepdims=True)
    sums = jnp.where(lane == 0, squares, jnp.where(lane == 1, products, 0.0))
    stats_ref[...] = sums.T[:8]
    state_ref[...] = factor * (scaled + dot_tn(input_map, weighted))


def column(row_block):
    rest = jnp.zeros((CHUNK - row_block.shape[0], CHUNK), F32)
    return jnp.concatenate([row_block, rest], axis=0).T


def row_of(sums):
    lane = lax.broadcasted_iota(jnp.int32, (CHUNK, CHUNK), 1)
    return jnp.where(lane == 0, sums, 0.0).T[:8]


def gate_kernel(
    inner, chunks, size, *refs
):
    stats_refs = refs[:size]
    (
        mixer_ref, gate_ref, grad_ref, gain_ref, conv_ref, e_ref, k_ref, maps_ref,
        mixed_ref, gate_grad_ref, mixer_grad_ref, small_ref, total_ref, cross_ref,
    ) = refs[size:]
    chunk = chunks - 1 - pl.program_id(0)
    clear(small_ref, total_ref)
    gain = gain_ref[...].astype(F32)
    stats = column(sum(ref[...] for ref in stats_refs))
    scale = lax.rsqrt(stats[:, 0:1] / inner + EPSILON)
    cross_term = stats[:, 1:2] * (scale * scale * scale) / inner
    gate = gate_ref[...]
    silu, slope = silu_parts(gate)
    mixer = mixer_ref[...]
    gated = mixer * silu
    normed = gated * scale
    mixed_ref[...] = (normed * gain).astype(BF16)
    grad = grad_ref[...]
    gated_grad = scale * (grad * gain) - gated * cross_term
    gate_grad = (gated_grad * mixer * slope).astype(BF16)
    gate_grad_ref[...] = gate_grad
    cross_ref[...] = row_of(jnp.sum(gate_grad.astype(F32) * gate, axis=1, keepdims=True))
    mixer_grad = gated_grad * silu
    mixer_grad_ref[...] = mixer_grad
    small_ref[0:1, :] += jnp.sum(grad * normed, axis=0, keepdims=True)
    small_ref[1:2, :] += jnp.sum(mixer_grad * conv_ref[...].astype(F32), axis=0, keepdims=True)
    high, low = split(expand(e_ref[...], grad.shape[1]) * mixer_grad)
    output_map = maps_ref[:, NSTATE:]
    factor = k_ref[pl.ds(chunk, 1), :]
    total_ref[:NSTATE, :] = factor * (
        factor * total_ref[:NSTATE, :] + (dot_tn(output_map, high) + dot_tn(output_map, low))
    )
    total_ref[NSTATE:, :] = jnp.broadcast_to(k_ref[7:8, :], (8, k_ref.shape[1]))


def back_kernel(
    chunks, state_in_ref, mixer_grad_ref, e_ref, f_ref, k_ref, weighted_ref, high_ref, low_ref,
    maps_ref, value_slope_ref, state_slope_ref, skip_ref,
    value_ref, map_ref, state_ref,
):
    chunk = chunks - 1 - pl.program_id(0)

    def start():
        state_ref[...] = state_in_ref[...]

    first_step(start)
    lower = lower_mask()
    row = lax.broadcasted_iota(jnp.int32, (CHUNK, CHUNK), 0)
    upper = row <= lax.broadcasted_iota(jnp.int32, (CHUNK, CHUNK), 1)
    factor = k_ref[pl.ds(chunk, 1), :]
    input_map, output_map = maps_ref[:, :NSTATE], maps_ref[:, NSTATE:]
    weighted = weighted_ref[...]
    mixer_grad = mixer_grad_ref[...]
    high, low = split(expand(e_ref[...], weighted.shape[1]) * mixer_grad)
    scaled = factor * state_ref[...]
    state_high, state_low = split(scaled)
    both = jnp.concatenate([weighted, high_ref[0]], axis=0)
    sums = dot_nt(high, both) + dot_nt(low, both)
    score_grad = jnp.where(lower, sums[:, :CHUNK], 0.0).astype(BF16)
    output_grad = sums[:, CHUNK:] + dot_nt(high, low_ref[0]) + dot(score_grad, input_map)
    sums = dot_nt(weighted, jnp.concatenate([state_high, state_low], axis=0))
    input_grad = sums[:, :NSTATE] + sums[:, NSTATE:] + dot_tn(score_grad, output_map)
    scores = jnp.where(upper, dot_nt(input_map, output_map), 0.0).astype(BF16)
    grads = dot(
        jnp.concatenate([scores, input_map], axis=1), jnp.concatenate([high, state_high], axis=0)
    )
    decayed = expand(f_ref[...], weighted.shape[1]) * grads
    value_ref[...] = (decayed + skip_ref[...] * mixer_grad) * value_slope_ref[...]
    slope = state_slope_ref[...]
    map_ref[:, :NSTATE] = input_grad * slope[:, :NSTATE]
    map_ref[:, NSTATE:] = output_grad * slope[:, NSTATE:]
    state_ref[...] = factor * (scaled + (dot_tn(output_map, high) + dot_tn(output_map, low)))


def conv_back_kernel(
    chunks, early_ref, value_ref, map_ref, after_ref, value_raw_ref, state_raw_ref, value_kernel_ref,
    state_kernel_ref, cross_in_ref,
    value_grad_ref, state_grad_ref, value_small_ref, state_small_ref, cross_ref, value_next_ref,
    state_next_ref,
):
    chunk = chunks - 1 - pl.program_id(0)
    channels = value_ref.shape[1]
    clear(value_small_ref, state_small_ref)

    def start():
        value_next_ref[...] = after_ref[:, :channels]
        state_next_ref[...] = after_ref[:, channels:]

    first_step(start)

    def back(slope_ref, next_ref, raw_ref, kernel_ref, grad_ref, small_ref):
        kernel = kernel_ref[...].astype(F32)
        slope = slope_ref[...]
        window = jnp.concatenate([slope, next_ref[...]], axis=0)
        around = pl.ds(pl.multiple_of(chunk * CHUNK, CHUNK), CHUNK + HALO)
        raw = raw_ref[around, :].astype(F32)
        grad = jnp.zeros_like(slope)
        for offset in range(KERNEL):
            back_by = KERNEL - 1 - offset
            grad = grad + kernel[offset : offset + 1] * window[back_by : back_by + CHUNK]
            begin = HALO - KERNEL + 1 + offset
            small_ref[offset : offset + 1, :] += jnp.sum(
                slope * raw[begin : begin + CHUNK], axis=0, keepdims=True
            )
        small_ref[KERNEL : KERNEL + 1, :] += jnp.sum(slope, axis=0, keepdims=True)
        grad = grad.astype(BF16)
        grad_ref[...] = grad
        next_ref[...] = slope[:8]
        return jnp.sum(grad.astype(F32) * raw[HALO:], axis=1, keepdims=True)

    crossed = back(map_ref, state_next_ref, state_raw_ref, state_kernel_ref, state_grad_ref, state_small_ref)
    crossed = crossed + back(
        value_ref, value_next_ref, value_raw_ref, value_kernel_ref, value_grad_ref, value_small_ref
    )
    cross_ref[...] = cross_in_ref[...] + row_of(crossed)


def normed_kernel(
    chunks, late_ref, gate_grad_ref, value_grad_ref, state_grad_ref, gate_weight_ref, value_weight_ref,
    state_weight_ref, cross_ref, out_ref
):
    value = (
        dot_nt(gate_grad_ref[...], gate_weight_ref[...])
        + dot_nt(value_grad_ref[...], value_weight_ref[...])
        + dot_nt(state_grad_ref[...], state_weight_ref[...])
    )
    count = value.shape[0]
    out_ref[0, :count, :] = value.astype(BF16)
    line = lax.broadcasted_iota(jnp.int32, (HALO, CHUNK), 0)
    packed = jnp.zeros((HALO, CHUNK), F32)
    for chunk in range(chunks):
        row = cross_ref[0:1, chunk * CHUNK : (chunk + 1) * CHUNK]
        high = row.astype(BF16).astype(F32)
        packed = jnp.where(line == chunk, high, packed)
        packed = jnp.where(line == chunks + chunk, row - high, packed)
    out_ref[0, count:, :] = jnp.zeros((HALO, value.shape[1]), BF16)
    out_ref[0, count:, :CHUNK] = packed.astype(BF16)


def last_kernel(full_width, parts_ref, tokens_ref, scale_ref, gain_ref, cotangent_ref, out_ref):
    count = tokens_ref.shape[0]
    chunks = count // CHUNK
    size = parts_ref.shape[0]
    crossed = sum(parts_ref[i, count:, :CHUNK].astype(F32) for i in range(size))
    crossed = crossed[:chunks] + crossed[chunks : 2 * chunks]
    for chunk in range(chunks):
        rows = slice(chunk * CHUNK, (chunk + 1) * CHUNK)
        normed_grad = sum(parts_ref[i, rows, :].astype(F32) for i in range(size))
        scale = scale_ref[HALO + chunk * CHUNK : HALO + (chunk + 1) * CHUNK, 0:1]
        total = column(jnp.broadcast_to(crossed[chunk : chunk + 1], (8, CHUNK)))[:, 0:1]
        out_ref[rows, :] = (
            scale * gain_ref[...].astype(F32) * normed_grad
            - tokens_ref[rows, :].astype(F32) * (scale * scale * total / full_width)
            + cotangent_ref[rows, :].astype(F32)
        ).astype(BF16)


def store_piece(core_ref, kept_ref, given_ref, place, begin, piece):
    chips = kept_ref.shape[0]
    core, chip = place // chips, lax.rem(place, chips)
    rows = slice(begin, begin + piece.shape[0])
    piece = piece.astype(BF16)

    @pl.when(core_ref[0] == core)
    def _():
        kept_ref[chip, rows, :] = piece

    @pl.when(core_ref[0] != core)
    def _():
        given_ref[chip, rows, :] = piece


def gain_row(weight, block):
    sums = jnp.sum(weight.astype(F32) * block, axis=1, keepdims=True)
    lane = lax.broadcasted_iota(jnp.int32, (CHUNK, CHUNK), 1)
    rows = [
        jnp.where(lane == 0, sums[i : i + CHUNK], 0.0).T[0:1] for i in range(0, BLOCK, CHUNK)
    ]
    return jnp.concatenate(rows, axis=1)


def early_kernel(
    loose_ref, core_ref, normed_ref, gate_ref, mixed_ref, grad_ref, weight_ref,
    kept_ref, given_ref, gain_ref, held_ref
):
    chips, rows, channels = kept_ref.shape
    at = pl.program_id(0)
    count, width = grad_ref.shape
    pieces = 2 * chips
    step = width // pieces
    out_rows = channels // pieces
    out_blocks = channels // BLOCK
    every = width // BLOCK // out_blocks

    @pl.when(lax.rem(at, every) == 0)
    def _():
        held_ref[...] = dot_tn(mixed_ref[...], grad_ref[...])

    block = dot_tn(normed_ref[HALO : HALO + count, :], gate_ref[...])
    gain_ref[...] = gain_row(weight_ref[...], block)
    for i in range(BLOCK // step):
        place = at * (BLOCK // step) + i
        begin = lax.rem(at, every) * (BLOCK // step * out_rows) + i * out_rows
        own = held_ref[pl.ds(pl.multiple_of(begin, 8), out_rows), :]
        parts = [block[i * step : (i + 1) * step]]
        parts += [own[:, j : j + channels] for j in range(0, width, channels)]
        store_piece(core_ref, kept_ref, given_ref, place, 0, jnp.concatenate(parts, axis=0))


def late_kernel(
    early_ref, core_ref, normed_ref, value_ref, state_ref, value_small_ref, gate_small_ref, gain_ref,
    state_small_ref, value_weight_ref, state_weight_ref, gain_full_ref,
    kept_ref, given_ref, own_ref, shared_ref, gains_ref,
):
    chips, rows, channels = kept_ref.shape
    at = pl.program_id(0)
    count, maps_width = state_ref.shape
    width = gains_ref.shape[1]
    pieces = 2 * chips
    step = width // pieces
    lanes = channels // 128
    part = 2 * step // lanes
    columns = normed_ref[HALO : HALO + count, :]
    value = dot_tn(columns, value_ref[...])
    state = dot_tn(columns, state_ref[...])
    gain = (
        gain_ref[...] + gain_row(value_weight_ref[...], value) + gain_row(state_weight_ref[...], state)
    ) / gain_full_ref[0:1, :]
    gains_ref[0:1, pl.ds(pl.multiple_of(at * BLOCK, 128), BLOCK)] = gain
    for i in range(BLOCK // step):
        piece = slice(i * step, (i + 1) * step)
        stacked = jnp.concatenate([state[piece, :128], state[piece, 128:]], axis=0)
        stacked = jnp.concatenate(
            [stacked[j * part : (j + 1) * part] for j in range(lanes)], axis=1
        )
        store_piece(
            core_ref, kept_ref, given_ref, at * (BLOCK // step) + i, 0,
            jnp.concatenate([value[piece], stacked], axis=0),
        )

    @pl.when(at == width // BLOCK - 1)
    def _():
        own_ref[...] = jnp.zeros_like(own_ref)
        own_ref[: KERNEL + 1, :] = value_small_ref[: KERNEL + 1, :]
        own_ref[KERNEL + 1 : KERNEL + 3, :] = gate_small_ref[:2, :]
        shared_ref[...] = jnp.zeros_like(shared_ref)
        begin = width // channels
        for i in range(begin):
            shared_ref[i : i + 1, :] = gains_ref[0:1, i * channels : (i + 1) * channels]
        for i in range(0, (KERNEL + 1) * maps_width, 128):
            tap, column_from = divmod(i, maps_width)
            row, column_to = divmod(i, channels)
            shared_ref[begin + row : begin + row + 1, column_to : column_to + 128] = state_small_ref[
                tap : tap + 1, column_from : column_from + 128
            ]
        line = lax.broadcasted_iota(jnp.int32, (HALO, channels), 0)
        for place in range(pieces):
            own, shared = own_ref[place : place + 1, :], shared_ref[place : place + 1, :]
            own_high, shared_high = (v.astype(BF16).astype(F32) for v in (own, shared))
            small = jnp.zeros((HALO, channels), F32)
            for to, value in enumerate((own_high, own - own_high, shared_high, shared - shared_high)):
                small = jnp.where(line == to, value, small)
            store_piece(core_ref, kept_ref, given_ref, place, step + part, small)


def merge_pairs(block):
    tail = block[-HALO:]
    line = lax.broadcasted_iota(jnp.int32, tail.shape, 0)
    own, shared = tail[0:1] + tail[1:2], tail[2:3] + tail[3:4]
    own_high, shared_high = own.astype(BF16).astype(F32), shared.astype(BF16).astype(F32)
    new = jnp.zeros_like(tail)
    for at, value in enumerate((own_high, own - own_high, shared_high, shared - shared_high)):
        new = jnp.where(line == at, value, new)
    return jnp.concatenate([block[:-HALO], new], axis=0)


def heads_kernel(piece_ref, total_ref, arrived_ref, out_ref, low_ref):
    total = merge_pairs(total_ref[...] + arrived_ref[...].astype(F32))
    line = lax.broadcasted_iota(jnp.int32, total.shape, 0)
    first = total.shape[0] - HALO
    own = (line >= first) & (line < first + 2)
    out_ref[...] = total
    low_ref[...] = jnp.where(own, piece_ref[...], total).astype(BF16)


def half_kernel(paired, chips, chip_ref, kept_ref, arrived_ref, *refs):
    outs = refs[-chips:]
    for bits in range(chips):
        place = lax.bitwise_xor(chip_ref[0], bits)
        value = kept_ref[place].astype(F32) + arrived_ref[place].astype(F32)
        if paired:
            value = merge_pairs(value)
        outs[bits][...] = value.astype(outs[bits].dtype)


def piece_kernel(parts, paired, cut, *refs):
    total = sum(ref[...].astype(F32) for ref in refs[:parts])
    if not paired:
        refs[-1][...] = total.astype(BF16)
        return
    first_ref, last_ref = refs[-2:]
    first_ref[...] = total[:cut].astype(BF16)
    last_ref[...] = merge_pairs(total[cut:])


def square_half_kernel(
    chip_ref, kept_ref, arrived_ref, loose_ref, first_ref, first_give_ref, last_ref, last_give_ref
):
    cut = first_ref.shape[1]
    for bits in range(4):
        place = lax.bitwise_xor(chip_ref[0], bits)
        value = kept_ref[place].astype(F32) + arrived_ref[place].astype(F32)
        low, high = bits & 1, bits >> 1
        ref = first_give_ref if low else first_ref
        ref[high] = value[:cut].astype(ref.dtype)
        ref = last_give_ref if high else last_ref
        ref[low] = value[cut:].astype(ref.dtype)


def square_next_kernel(
    first_ref, first_got_ref, last_ref, last_got_ref, loose_ref,
    first_out_ref, first_give_ref, last_out_ref, last_give_ref,
):
    first_out_ref[...] = first_ref[0] + first_got_ref[0].astype(F32)
    first_give_ref[...] = (first_ref[1] + first_got_ref[1].astype(F32)).astype(BF16)
    last_out_ref[...] = last_ref[0] + last_got_ref[0].astype(F32)
    last_give_ref[...] = (last_ref[1] + last_got_ref[1].astype(F32)).astype(BF16)


def square_last_kernel(first_ref, first_got_ref, last_ref, last_got_ref, loose_ref, *outs):
    outs[0][...] = (first_ref[...] + first_got_ref[...].astype(F32)).astype(BF16)
    outs[1][...] = (last_ref[...] + last_got_ref[...].astype(F32)).astype(BF16)


def each_piece(core_ref, chip_ref, chips, groups, refs):
    refs = iter(refs)
    for part, bits_lists in enumerate(groups):
        number = 0
        for bits_list in bits_lists:
            for core, ref in ((core_ref[0], next(refs)), (1 - core_ref[0], next(refs))):
                for at, bits in enumerate(bits_list):
                    place = core * chips + lax.bitwise_xor(chip_ref[0], bits)
                    yield part, number, place, ref[at].astype(F32)
                    number += 1


def send_rows(buffer_ref, number, target_ref, place, sem_ref):
    rows = buffer_ref.shape[1]
    copy = pltpu.make_async_copy(
        buffer_ref.at[number],
        target_ref.at[pl.ds(pl.multiple_of(place * rows, 8), rows), :],
        sem_ref.at[number],
    )
    copy.start()
    return copy


def early_out_kernel(chips, groups, core_ref, chip_ref, *refs):
    gate_ref, output_ref, gate_buffer, output_buffer, gate_sems, output_sems = refs[-6:]
    out_rows, width = output_buffer.shape[1:]
    channels = gate_buffer.shape[2]
    copies = []
    for part, number, place, value in each_piece(core_ref, chip_ref, chips, groups, refs[:-6]):
        if part == 0:
            gate_buffer[number] = value
            copies.append(send_rows(gate_buffer, number, gate_ref, place, gate_sems))
        else:
            output_buffer[number] = jnp.concatenate(
                [value[i * out_rows : (i + 1) * out_rows] for i in range(width // channels)], axis=1
            )
            copies.append(send_rows(output_buffer, number, output_ref, place, output_sems))
    for copy in copies:
        copy.wait()


def late_out_kernel(chips, groups, core_ref, chip_ref, *refs):
    value_ref, buffer, sems = refs[-3:]
    copies = []
    for _, number, place, value in each_piece(core_ref, chip_ref, chips, groups, refs[:-3]):
        buffer[number] = value
        copies.append(send_rows(buffer, number, value_ref, place, sems))
    for copy in copies:
        copy.wait()


def shared_out_kernel(chips, groups, size, core_ref, chip_ref, head_ref, *refs):
    (
        state_ref, value_kernel_ref, value_bias_ref, state_kernel_ref, state_bias_ref, skip_ref,
        gated_ref, gain_ref, buffer, sems, own_ref, shared_ref,
    ) = refs[-12:]
    step, maps_width = buffer.shape[1:]
    channels = own_ref.shape[1]
    lanes = channels // 128
    rows = 2 * step // lanes
    copies = []
    for _, number, place, piece in each_piece(core_ref, chip_ref, chips, groups, refs[:-12]):
        stacked = jnp.concatenate(
            [piece[:rows, i * 128 : (i + 1) * 128] for i in range(lanes)], axis=0
        )
        buffer[number] = jnp.concatenate([stacked[:step], stacked[step:]], axis=1)
        copies.append(send_rows(buffer, number, state_ref, place, sems))
        own_ref[pl.ds(place, 1), :] = piece[rows : rows + 1] + piece[rows + 1 : rows + 2]
        shared_ref[pl.ds(place, 1), :] = piece[rows + 2 : rows + 3] + piece[rows + 3 : rows + 4]
    value_kernel_ref[...] = own_ref[:KERNEL, :]
    value_bias_ref[...] = own_ref[KERNEL, :]
    gated_ref[...] = own_ref[KERNEL + 1, :]
    heads = skip_ref.shape[0]
    at = lax.broadcasted_iota(jnp.int32, (heads, channels), 1)
    row = lax.broadcasted_iota(jnp.int32, (heads, channels), 0) * HEAD_DIM
    inside = (at >= row) & (at < row + HEAD_DIM)
    skip_ref[...] = jnp.sum(jnp.where(inside, own_ref[KERNEL + 2 : KERNEL + 3, :], 0.0), axis=1)
    own_width = gain_ref.shape[0]
    gain_rows = -(-own_width * size // channels)
    for head in range(size):
        row, begin = divmod(head * own_width, channels)

        @pl.when(head_ref[0] == head)
        def _(row=row, begin=begin):
            gain_ref[...] = shared_ref[row, begin : begin + own_width]

    for i in range(0, (KERNEL + 1) * maps_width, 128):
        tap, column_to = divmod(i, maps_width)
        row, column_from = divmod(i, channels)
        value = shared_ref[gain_rows + row : gain_rows + row + 1, column_from : column_from + 128]
        if tap < KERNEL:
            state_kernel_ref[tap : tap + 1, column_to : column_to + 128] = value
        else:
            state_bias_ref[column_to : column_to + 128] = value[0]
    for copy in copies:
        copy.wait()


SCALAR = "scalar"
WHOLE = "whole"
BLOCKED = "blocked"
LANES = "lanes"
LEADING = "leading"
FAR = "far"
LOOSE = "loose"


def run(kernel, name, flops, args, outs, steps=None, backward=False, scratch=()):
    at = (lambda i: steps - 1 - i) if backward else (lambda i: i)

    def spec(kind, shape):
        if isinstance(kind, int):
            return pl.BlockSpec((kind,) + shape[1:], lambda i: (at(i), 0))
        if kind == SCALAR:
            return pl.BlockSpec(memory_space=pltpu.SMEM)
        if kind == LOOSE:
            return pl.BlockSpec(memory_space=pl.ANY)
        if kind == FAR:
            return pl.BlockSpec(memory_space=pltpu.HBM)
        if isinstance(kind, tuple):
            return pl.BlockSpec(*kind)
        if steps is None:
            return pl.BlockSpec(memory_space=pltpu.VMEM)
        if kind == BLOCKED:
            return pl.BlockSpec((CHUNK, shape[1]), lambda i: (at(i), 0))
        if kind == LANES:
            return pl.BlockSpec((shape[0], CHUNK), lambda i: (0, at(i)))
        if kind == LEADING:
            return pl.BlockSpec((1,) + shape[1:], lambda i: (at(i),) + (0,) * (len(shape) - 1))
        return pl.BlockSpec(shape, lambda i: (0,) * len(shape))

    moved = sum(a.size * a.dtype.itemsize for kind, a in args if kind != LOOSE)
    shapes = [jax.ShapeDtypeStruct(shape, dtype) for _, shape, dtype in outs]
    moved += sum(a.size * a.dtype.itemsize for a in shapes)
    return pl.pallas_call(
        kernel,
        out_shape=shapes,
        in_specs=[spec(kind, a.shape) for kind, a in args],
        out_specs=[spec(kind, shape) for kind, shape, _ in outs],
        scratch_shapes=list(scratch),
        compiler_params=pltpu.CompilerParams(vmem_limit_bytes=VMEM_LIMIT),
        cost_estimate=pl.CostEstimate(flops=flops, bytes_accessed=moved, transcendentals=0),
        name=name,
        **({} if steps is None else {"grid": (steps,)}),
    )(*(a for _, a in args))


def per_device(
    tokens, decay_codes, norm_gain, gate_weight, value_weight, state_weight, value_kernel, value_bias,
    state_kernel, state_bias, skip_scale, gated_gain, output_weight, cotangent,
):
    tokens, decay_codes, cotangent = tokens[0], decay_codes[0], cotangent[0]
    count, own_width = tokens.shape
    heads = skip_scale.shape[0]
    channels = heads * HEAD_DIM
    head_size, chips = lax.axis_size("head"), lax.axis_size("chip")
    seq_size = 2 * chips
    width = own_width * head_size
    maps_width = 2 * NSTATE
    chunks = count // CHUNK
    core = (SCALAR, lax.axis_index("core").astype(jnp.int32)[None])
    chip = (SCALAR, lax.axis_index("chip").astype(jnp.int32)[None])
    head = (SCALAR, lax.axis_index("head").astype(jnp.int32)[None])

    rows = count + MARGIN
    packed = jnp.concatenate(
        [
            from_behind(tokens[-HALO:], 1),
            tokens,
            jnp.broadcast_to(norm_gain[None], (MARGIN - HALO, own_width)),
        ],
        axis=0,
    )
    logs = decay_codes.astype(F32) * (-DECAY_STEP)
    input_weight = jnp.sqrt(-jnp.expm1(2.0 * logs))
    e_full, f_full, factors = run(
        decay_kernel, "decays", count * channels * 200,
        [(WHOLE, decay_codes), (WHOLE, input_weight)],
        [
            (WHOLE, (count, heads), F32),
            (WHOLE, (count, heads), F32),
            (WHOLE, (8, channels), F32),
        ],
    )
    parts, passed = line_parts(packed, "head")
    skip_full = jnp.repeat(skip_scale, HEAD_DIM)[None]

    half = rows // 2
    gain_rows = ((MARGIN - HALO, own_width), lambda i: ((HALO + count) // (MARGIN - HALO), 0))
    normed, scale_in, gain_full = run(
        functools.partial(norm_kernel, head_size), "norm", count * width * 10,
        [head, (half, passed)] + [(half, part) for part in parts]
        + [(gain_rows, part) for part in parts] + [(gain_rows, passed)],
        [(half, (rows, width), BF16), (half, (rows, 128), F32), (WHOLE, (8, width), F32)],
        steps=2,
    )
    cotangent_parts = deal(
        run(
            copies_kernel, "copies", 1, [(LOOSE, normed), (WHOLE, cotangent)],
            [(WHOLE, (head_size, count, own_width), BF16)],
        )[0],
        "head",
    )
    value_raw = dot(normed, value_weight).astype(BF16)
    state_raw = dot(normed, state_weight).astype(BF16)
    conv, weighted, value_slope, maps, map_slope, local_end = run(
        conv_kernel, "conv", count * channels * 400,
        [
            (WHOLE, value_raw), (WHOLE, state_raw), (WHOLE, value_kernel), (WHOLE, value_bias[None]),
            (WHOLE, state_kernel), (WHOLE, state_bias[None]), (BLOCKED, f_full), (WHOLE, factors),
        ],
        [
            (BLOCKED, (count, channels), BF16),
            (BLOCKED, (count, channels), BF16),
            (BLOCKED, (count, channels), F32),
            (BLOCKED, (count, maps_width), BF16),
            (BLOCKED, (count, maps_width), F32),
            (WHOLE, (NSTATE + 8, channels), F32),
        ],
        steps=chunks,
    )
    gate_pre = dot(normed, gate_weight)[HALO : HALO + count]
    state_in, _ = entering(core, chip, local_end, False, (gate_pre,))
    mixed_grad, full_cotangent = run(
        mixed_grad_kernel, "mixed_grad", 2 * count * width * channels,
        [(WHOLE, cotangent_parts), (WHOLE, output_weight)],
        [(WHOLE, (count, channels), F32), (WHOLE, (count, width), BF16)],
    )
    mixer, stats, high, low = run(
        mixer_kernel, "mixer", count * channels * 1000,
        [
            (WHOLE, state_in), (BLOCKED, maps), (BLOCKED, weighted), (BLOCKED, conv),
            (BLOCKED, e_full), (WHOLE, factors), (WHOLE, skip_full), (BLOCKED, gate_pre),
            (BLOCKED, mixed_grad), (WHOLE, gated_gain[None]),
        ],
        [
            (BLOCKED, (count, channels), F32),
            (LANES, (8, count), F32),
            (LEADING, (chunks, NSTATE, channels), BF16),
            (LEADING, (chunks, NSTATE, channels), BF16),
        ],
        steps=chunks,
        scratch=[pltpu.VMEM((NSTATE, channels), F32)],
    )
    mixed, gate_grad, mixer_grad, gate_small, start_grad, gate_cross = run(
        functools.partial(gate_kernel, float(channels * head_size), chunks, head_size),
        "gate", count * channels * 600,
        [(LANES, part) for part in turn_all(stats, "head")]
        + [
            (BLOCKED, mixer), (BLOCKED, gate_pre), (BLOCKED, mixed_grad), (WHOLE, gated_gain[None]),
            (BLOCKED, conv), (BLOCKED, e_full), (WHOLE, factors), (BLOCKED, maps),
        ],
        [
            (BLOCKED, (count, channels), BF16),
            (BLOCKED, (count, channels), BF16),
            (BLOCKED, (count, channels), F32),
            (WHOLE, (8, channels), F32),
            (WHOLE, (NSTATE + 8, channels), F32),
            (LANES, (8, count), F32),
        ],
        steps=chunks,
        backward=True,
    )
    step, out_rows = width // seq_size, channels // seq_size
    early_rows = step + out_rows * (width // channels)
    features = width // BLOCK
    feature_block = ((rows, BLOCK), lambda i: (0, i))
    every = features // (channels // BLOCK)
    out_parts = run(
        out_kernel, "out", 2 * count * channels * width,
        [(LOOSE, start_grad), (WHOLE, mixed), (WHOLE, output_weight)],
        [(WHOLE, (head_size, count, own_width), BF16)],
    )[0]
    grad_after, _ = entering(core, chip, start_grad, True, (out_parts,))
    branch = jnp.sum(deal(out_parts, "head").astype(F32), axis=0)
    block_out = (tokens.astype(F32) + branch).astype(BF16)

    value_grads, map_grads = run(
        functools.partial(back_kernel, chunks), "back", count * channels * 2000,
        [
            (WHOLE, grad_after), (BLOCKED, mixer_grad), (BLOCKED, e_full),
            (BLOCKED, f_full), (WHOLE, factors), (BLOCKED, weighted), (LEADING, high),
            (LEADING, low), (BLOCKED, maps), (BLOCKED, value_slope), (BLOCKED, map_slope),
            (WHOLE, skip_full),
        ],
        [(BLOCKED, (count, channels), F32), (BLOCKED, (count, maps_width), F32)],
        steps=chunks,
        backward=True,
        scratch=[pltpu.VMEM((NSTATE, channels), F32)],
    )
    early_kept, early_given, early_gain = run(
        early_kernel, "early", 4 * count * channels * width,
        [
            (LOOSE, value_grads), core, (feature_block, normed), (WHOLE, gate_grad),
            (((count, BLOCK), lambda i: (0, i // every)), mixed), (WHOLE, full_cotangent),
            (BLOCK, gate_weight),
        ],
        [(WHOLE, (chips, early_rows, channels), BF16)] * 2
        + [(((1, BLOCK), lambda i: (0, i)), (1, width), F32)],
        steps=features,
        scratch=[pltpu.VMEM((BLOCK, width), F32)],
    )
    after = from_behind(jnp.concatenate([value_grads[:8], map_grads[:8]], axis=1), -1)
    value_raw_grad, state_raw_grad, value_small, state_small, crossed = run(
        functools.partial(conv_back_kernel, chunks), "conv_back", count * channels * 100,
        [
            (LOOSE, early_given), (BLOCKED, value_grads), (BLOCKED, map_grads), (WHOLE, after),
            (WHOLE, value_raw), (WHOLE, state_raw), (WHOLE, value_kernel), (WHOLE, state_kernel),
            (LANES, gate_cross),
        ],
        [
            (BLOCKED, (count, channels), BF16),
            (BLOCKED, (count, maps_width), BF16),
            (WHOLE, (8, channels), F32),
            (WHOLE, (8, maps_width), F32),
            (LANES, (8, count), F32),
        ],
        steps=chunks,
        backward=True,
        scratch=[pltpu.VMEM((8, channels), F32), pltpu.VMEM((8, maps_width), F32)],
    )
    early_state, half_mark = sum_pieces(
        chip, early_kept, early_given, "early", True, step, False, (crossed,)
    )
    lanes = channels // 128
    state_rows = 2 * step // lanes
    late_rows = step + state_rows + HALO
    late_kept, late_given = run(
        late_kernel, "late", 3 * count * channels * width,
        [
            (LOOSE, half_mark), core, (feature_block, normed), (WHOLE, value_raw_grad),
            (WHOLE, state_raw_grad),
            (WHOLE, value_small), (WHOLE, gate_small), (((1, BLOCK), lambda i: (0, i)), early_gain),
            (WHOLE, state_small), (BLOCK, value_weight), (BLOCK, state_weight),
            (((8, BLOCK), lambda i: (0, i)), gain_full),
        ],
        [(WHOLE, (chips, late_rows, channels), BF16)] * 2,
        steps=features,
        scratch=[
            pltpu.VMEM((HALO, channels), F32),
            pltpu.VMEM((HALO, channels), F32),
            pltpu.VMEM((8, width), F32),
        ],
    )
    made = []

    def make_normed(mark):
        made.extend(
            run(
                functools.partial(normed_kernel, chunks), "normed", 4 * count * channels * width,
                [
                    (LOOSE, mark), (WHOLE, gate_grad), (WHOLE, value_raw_grad),
                    (WHOLE, state_raw_grad), (own_width, gate_weight), (own_width, value_weight),
                    (own_width, state_weight), (WHOLE, crossed),
                ],
                [(LEADING, (head_size, count + HALO, own_width), BF16)],
                steps=head_size,
            )
        )
        return made

    (late_piece, shared_piece), late_mark = sum_pieces(
        chip, late_kept, late_given, "late", False, step, True, meanwhile=make_normed
    )
    normed_parts = made[0]
    shared_piece, heads_mark = heads_sum(shared_piece)
    if chips == 4:
        early_state = square_next("early", early_state, early_rows * channels, late_piece)
    if chips == 4:
        early_gate, early_out = square_end(
            "early", early_state,
            [(WHOLE, (step, channels), BF16), (WHOLE, (early_rows - step, channels), BF16)],
            early_rows * channels, heads_mark,
        )
    else:
        early_gate, early_out = early_state[0][:step], early_state[0][step:]
    normed_parts = deal(normed_parts, "head")
    def unpack(kernel, name, pieces, outs, flops, scratch, extra=(), args=()):
        groups = [collect(*piece) for piece in pieces]
        bits = [[found[2] for found in group] for group in groups]
        arrays = [(WHOLE, value) for group in groups for found in group for value in found[:2]]
        return run(
            functools.partial(kernel, chips, bits, *extra), name, flops,
            [core, chip, *args] + arrays, outs, scratch=scratch,
        )

    sems = pltpu.SemaphoreType.DMA((seq_size,))
    gate_weight_gradient, output_weight_gradient = unpack(
        early_out_kernel, "early_out",
        [(early_gate, (2, 1), late_mark), (early_out, (1, 2), late_mark)],
        [(FAR, (width, channels), F32), (FAR, (channels, width), F32)], 4 * channels * width,
        [
            pltpu.VMEM((seq_size, step, channels), F32),
            pltpu.VMEM((seq_size, out_rows, width), F32),
            sems,
            sems,
        ],
    )
    value_weight_gradient = unpack(
        late_out_kernel, "late_out", [(late_piece, None)],
        [(FAR, (width, channels), F32)], 2 * channels * width,
        [pltpu.VMEM((seq_size, step, channels), F32), sems],
    )[0]
    (
        state_weight_gradient, value_kernel_gradient, value_bias_gradient, state_kernel_gradient,
        state_bias_gradient, skip_scale_gradient, gated_gain_gradient, norm_gain_gradient,
    ) = unpack(
        shared_out_kernel, "shared_out", [(shared_piece, (2, 1))],
        [
            (FAR, (width, maps_width), F32),
            (WHOLE, (KERNEL, channels), F32),
            (WHOLE, (channels,), F32),
            (WHOLE, (KERNEL, maps_width), F32),
            (WHOLE, (maps_width,), F32),
            (WHOLE, (heads,), F32),
            (WHOLE, (channels,), F32),
            (WHOLE, (own_width,), F32),
        ],
        2 * maps_width * width,
        [
            pltpu.VMEM((seq_size, step, maps_width), F32),
            sems,
            pltpu.VMEM((HALO, channels), F32),
            pltpu.VMEM((HALO, channels), F32),
        ],
        extra=(head_size,),
        args=[head],
    )
    tokens_gradient = run(
        functools.partial(last_kernel, float(width)), "last", count * own_width * 20,
        [
            (WHOLE, normed_parts), (WHOLE, tokens), (WHOLE, scale_in),
            (WHOLE, norm_gain[None]), (WHOLE, cotangent),
        ],
        [(WHOLE, (count, own_width), BF16)],
    )[0]
    return (
        block_out[None],
        tokens_gradient[None],
        norm_gain_gradient,
        gate_weight_gradient,
        value_weight_gradient,
        state_weight_gradient,
        value_kernel_gradient,
        value_bias_gradient,
        state_kernel_gradient,
        state_bias_gradient,
        skip_scale_gradient,
        gated_gain_gradient,
        output_weight_gradient,
    )


def solution(mesh):
    seq_size, head_size = mesh.shape["seq"], mesh.shape["head"]
    mesh = Mesh(mesh.devices.reshape(seq_size // 2, 2, head_size), ("chip", "core", "head"))
    seq = ("chip", "core")
    in_specs = (
        P(None, seq, "head"),
        P(None, seq, "head"),
        P("head"),
        P(None, "head"),
        P(None, "head"),
        P(),
        P(None, "head"),
        P("head"),
        P(),
        P(),
        P("head"),
        P("head"),
        P("head", None),
        P(None, seq, "head"),
    )
    out_specs = (
        P(None, seq, "head"),
        P(None, seq, "head"),
        P("head"),
        P(None, "head"),
        P(None, "head"),
        P(),
        P(None, "head"),
        P("head"),
        P(),
        P(),
        P("head"),
        P("head"),
        P("head", None),
    )
    return jax.shard_map(
        per_device, mesh=mesh, in_specs=in_specs, out_specs=out_specs, check_vma=False
    )
```

```python
import functools

import jax
import jax.numpy as jnp
from jax import lax
from jax.experimental import pallas as pl
from jax.experimental.pallas import tpu as pltpu
from jax.sharding import Mesh
from jax.sharding import PartitionSpec as P

HEAD_DIM = 64
NSTATE = 128
KERNEL = 4
CHUNK = 128
BLOCK = 384
VMEM_LIMIT = 20 * 1024 * 1024
MARGIN = 32
HALO = 16


DECAY_STEP = 1.0 / 1048576.0
EPSILON = 1e-05
BF16 = jnp.bfloat16
F32 = jnp.float32


def tie_kernel(*refs):
    del refs


def tie(value, *others):
    return pl.pallas_call(
        tie_kernel,
        out_shape=jax.ShapeDtypeStruct(value.shape, value.dtype),
        in_specs=[pl.BlockSpec(memory_space=pl.ANY)] * (1 + len(others)),
        out_specs=pl.BlockSpec(memory_space=pl.ANY),
        input_output_aliases={0: 0},
        name="tie",
    )(value, *others)


def from_behind(value, by):
    axis = ("chip", "core")
    size = lax.axis_size("chip") * 2
    pairs = [(i, i + by) for i in range(size) if 0 <= i + by < size]
    return lax.ppermute(value, axis, pairs)


def beside(value):
    return lax.ppermute(value, "core", [(0, 1), (1, 0)])


def turn(value, axis, by):
    size = lax.axis_size(axis)
    return lax.ppermute(value, axis, [(i, (i + by) % size) for i in range(size)])


def turn_all(value, axis):
    return [value] + [turn(value, axis, by) for by in range(1, lax.axis_size(axis))]


def line_parts(value, axis):
    if lax.axis_size(axis) != 4:
        parts = turn_all(value, axis)
        return parts, value
    two = turn(value, axis, 2)
    one = lax.ppermute(value, axis, [(0, 1), (1, 2), (2, 3)])
    three = lax.ppermute(value, axis, [(1, 0), (2, 1), (3, 2)])
    passed = lax.ppermute(two, axis, [(2, 3), (1, 0)])
    return [value, one, two, three], passed


def deal(parts, axis):
    return lax.all_to_all(parts, axis, 0, 0)


def cross(value, bits):
    return lax.ppermute(value, "chip", [(i, i ^ bits) for i in range(lax.axis_size("chip"))])


def cross_all(value):
    return [value] + [cross(value, bits) for bits in range(1, lax.axis_size("chip"))]


def heads_sum(piece):
    total, low, first = piece, piece.astype(BF16), None
    bits, size = 1, lax.axis_size("head")
    while bits < size:
        arrived = lax.ppermute(low, "head", [(i, i ^ bits) for i in range(size)])
        total, low = run(
            heads_kernel, "heads", piece.size,
            [(WHOLE, piece), (WHOLE, total), (WHOLE, arrived)],
            [(WHOLE, piece.shape, F32), (WHOLE, piece.shape, BF16)],
        )
        first = low if first is None else first
        bits *= 2
    return low, first


def entering(core, chip, total, backward, meanwhile, later=lambda pair: ()):
    name = "after" if backward else "before"
    chips = lax.axis_size("chip")
    channels = total.shape[1]
    half = NSTATE // 2
    partner = beside(total)
    pair = run(
        functools.partial(pair_kernel, backward), name + "_pair", total.size,
        [core, (WHOLE, total), (WHOLE, partner)] + [(LOOSE, value) for value in meanwhile],
        [(WHOLE, (half + 8, channels), F32)],
    )[0]
    prefix = run(
        functools.partial(prefix_kernel, backward, chips), name + "_prefix", chips * pair.size,
        [chip] + [(WHOLE, value) for value in cross_all(pair)]
        + [(LOOSE, value) for value in later(pair)],
        [(WHOLE, (half, channels), F32)],
    )[0]
    return run(
        functools.partial(enter_kernel, backward), name + "_enter", total.size,
        [core, (WHOLE, partner), (WHOLE, prefix), (WHOLE, beside(prefix))],
        [(WHOLE, (NSTATE, channels), F32)],
    )[0], prefix


def sum_pieces(chip, kept, given, name, square, cut, paired, before_half=(), meanwhile=lambda mark: ()):
    chips, rows, channels = kept.shape
    arrived = beside(given)
    size = chips * rows * channels
    if paired:
        outs = [(WHOLE, (cut, channels), BF16), (WHOLE, (rows - cut, channels), F32)]
    else:
        outs = [(WHOLE, (rows, channels), BF16)]
    if chips != 4 or not square:
        halves = run(
            functools.partial(half_kernel, paired, chips), name + "_half", size,
            [chip, (WHOLE, kept), (WHOLE, arrived)] + [(LOOSE, mark) for mark in before_half],
            [(WHOLE, (rows, channels), F32)] + [(WHOLE, (rows, channels), BF16)] * (chips - 1),
        )
        parts = [halves[0]] + [cross(halves[bits], bits) for bits in range(1, chips)]
        found = run(
            functools.partial(piece_kernel, chips, paired, cut), name + "_piece", size,
            [(WHOLE, part) for part in parts] + [(LOOSE, mark) for mark in meanwhile(halves[0])],
            outs,
        )
        return found, halves[0]
    rest = rows - cut
    state = run(
        square_half_kernel, name + "_half", size,
        [chip, (WHOLE, kept), (WHOLE, arrived)] + [(LOOSE, mark) for mark in before_half],
        [
            (WHOLE, (2, cut, channels), F32), (WHOLE, (2, cut, channels), BF16),
            (WHOLE, (2, rest, channels), F32), (WHOLE, (2, rest, channels), BF16),
        ],
    )
    return state, state[0]


def square_next(name, state, size, mark):
    first, first_give, last, last_give = state
    _, cut, channels = first.shape
    rest = last.shape[1]
    return run(
        square_next_kernel, name + "_next", size,
        [
            (WHOLE, first), (WHOLE, cross(first_give, 1)),
            (WHOLE, last), (WHOLE, cross(last_give, 2)), (LOOSE, mark),
        ],
        [
            (WHOLE, (cut, channels), F32), (WHOLE, (cut, channels), BF16),
            (WHOLE, (rest, channels), F32), (WHOLE, (rest, channels), BF16),
        ],
    )


def square_end(name, state, outs, size, mark):
    first, first_give, last, last_give = state
    return run(
        square_last_kernel, name + "_piece", size,
        [
            (WHOLE, first), (WHOLE, cross(first_give, 2)),
            (WHOLE, last), (WHOLE, cross(last_give, 1)),
        ]
        + [(LOOSE, value) for value in mark],
        outs,
    )


def collect(piece, order, mark=None):
    chips = lax.axis_size("chip")
    if chips != 4 or order is None:
        found = [(value[None], (bits,)) for bits, value in enumerate(cross_all(piece))]
    else:
        near, far = order
        both = jnp.stack([piece, cross(piece, near)])
        if mark is not None:
            both = tie(both, mark)
        found = [(both, (0, near)), (cross(both, far), (far, far ^ near))]
    return [(value, beside(value), bits) for value, bits in found]


def dot(left, right):
    return jnp.dot(left, right, preferred_element_type=F32)


def dot_nt(left, right):
    return lax.dot_general(left, right, (((1,), (1,)), ((), ())), preferred_element_type=F32)


def dot_tn(left, right):
    return lax.dot_general(left, right, (((0,), (0,)), ((), ())), preferred_element_type=F32)


def split(values):
    high = values.astype(BF16)
    return high, (values - high.astype(F32)).astype(BF16)


def lower_mask():
    row = lax.broadcasted_iota(jnp.int32, (CHUNK, CHUNK), 0)
    column = lax.broadcasted_iota(jnp.int32, (CHUNK, CHUNK), 1)
    return row >= column


def spread_heads(heads, channels):
    row = lax.broadcasted_iota(jnp.int32, (heads, channels), 0) * HEAD_DIM
    place = lax.broadcasted_iota(jnp.int32, (heads, channels), 1)
    return jnp.where((place >= row) & (place < row + HEAD_DIM), 1.0, 0.0).astype(BF16)


def expand(values, channels):
    high, low = split(values)
    spread = spread_heads(values.shape[1], channels)
    return dot(high, spread) + dot(low, spread)


def decay_kernel(codes_ref, weight_ref, e_ref, f_ref, k_ref):
    heads, channels = codes_ref.shape[1], k_ref.shape[1]
    lower = jnp.where(lower_mask(), 1.0, 0.0).astype(F32)
    count = codes_ref.shape[0] // CHUNK
    line = lax.broadcasted_iota(jnp.int32, (8, heads), 0)
    marks = jnp.zeros((8, heads), F32)
    total = jnp.zeros((1, heads), F32)
    for chunk in range(count):
        rows = pl.ds(chunk * CHUNK, CHUNK)
        logs = codes_ref[rows, :].astype(F32) * (-DECAY_STEP)
        cumulative = jnp.dot(
            lower, logs, precision=lax.Precision.HIGHEST, preferred_element_type=F32
        )
        last = cumulative[CHUNK - 1 :]
        middle = 0.5 * last
        e_ref[rows, :] = jnp.exp(cumulative - middle)
        f_ref[rows, :] = weight_ref[rows, :] * jnp.exp(middle - cumulative)
        marks = jnp.where(line == chunk, jnp.exp(middle), marks)
        total = total + last
    marks = jnp.where(line == 7, total, marks)
    high, low = split(marks)
    lowest = (marks - high.astype(F32) - low.astype(F32)).astype(BF16)
    spread = spread_heads(heads, channels)
    factors = dot(high, spread) + dot(low, spread) + dot(lowest, spread)
    k_ref[...] = factors


def pair_kernel(backward, core_ref, own_ref, other_ref, *refs):
    out_ref = refs[-1]
    half = NSTATE // 2
    logs, other_logs = own_ref[NSTATE:, :], other_ref[NSTATE:, :]
    for core in range(2):

        @pl.when(core_ref[0] == core)
        def _():
            rows = slice(core * half, (core + 1) * half)
            if core == (0 if backward else 1):
                out_ref[:half, :] = jnp.exp(logs[0:1]) * other_ref[rows, :] + own_ref[rows, :]
            else:
                out_ref[:half, :] = jnp.exp(other_logs[0:1]) * own_ref[rows, :] + other_ref[rows, :]

    out_ref[half:, :] = logs + other_logs


def prefix_kernel(backward, chips, chip_ref, *refs):
    parts, out_ref = refs[:chips], refs[-1]
    half = out_ref.shape[0]
    mine = chip_ref[0]
    total = jnp.zeros(out_ref.shape, F32)
    for bits in range(1, chips):
        source = lax.bitwise_xor(mine, bits)
        span = jnp.zeros((1, out_ref.shape[1]), F32)
        for other in range(1, chips):
            middle = lax.bitwise_xor(mine, other)
            if backward:
                between = (middle < source) & (middle > mine)
            else:
                between = (middle > source) & (middle < mine)
            span = span + jnp.where(between, parts[other][half : half + 1, :], 0.0)
        passes = source > mine if backward else source < mine
        total = total + jnp.where(passes, jnp.exp(span), 0.0) * parts[bits][:half, :]
    out_ref[...] = total


def enter_kernel(backward, core_ref, partner_ref, prefix_ref, other_ref, out_ref):
    half = prefix_ref.shape[0]
    decay = jnp.exp(partner_ref[NSTATE : NSTATE + 1, :])
    for core in range(2):

        @pl.when(core_ref[0] == core)
        def _():
            for place, ref in ((core, prefix_ref), (1 - core, other_ref)):
                rows = slice(place * half, (place + 1) * half)
                if core == (0 if backward else 1):
                    out_ref[rows, :] = decay * ref[...] + partner_ref[rows, :]
                else:
                    out_ref[rows, :] = ref[...]


def taps(window, kernel, bias, begin):
    summed = bias
    for offset in range(KERNEL):
        summed = summed + kernel[offset : offset + 1] * window[begin + offset : begin + offset + CHUNK]
    return summed


def silu_parts(values):
    sigmoid = jax.nn.sigmoid(values)
    return values * sigmoid, sigmoid * (1.0 + values * (1.0 - sigmoid))


def first_step(action):
    pl.when(pl.program_id(0) == 0)(action)


def clear(*refs):
    def action():
        for ref in refs:
            ref[...] = jnp.zeros_like(ref)

    first_step(action)


def place_parts(mine, parts, target, width, value):
    size = len(parts)
    if width % 128 == 0:
        for i in range(size):
            owner = lax.rem(mine + size - i, size)
            target[:, pl.ds(pl.multiple_of(owner * width, 128), width)] = value(i)
        return

    def write(me):
        for i in range(size):
            owner = (me + size - i) % size
            target[:, owner * width : (owner + 1) * width] = value(i)

    for me in range(size):
        pl.when(mine == me)(functools.partial(write, me))


def copies_kernel(loose_ref, own_ref, out_ref):
    for i in range(out_ref.shape[0]):
        out_ref[i] = own_ref[...]


def norm_kernel(size, head_ref, passed_ref, *refs):
    parts, gains = refs[:size], refs[size : 2 * size]
    passed_gain_ref, normed_ref, scale_ref, gain_ref = refs[2 * size :]
    width = parts[0].shape[1]
    mine = head_ref[0]

    def pick(i, refs, passed):
        if size == 4 and i == 1:
            return jnp.where(mine == 0, passed[...], refs[i][...])
        if size == 4 and i == 3:
            return jnp.where(mine == 3, passed[...], refs[i][...])
        return refs[i][...]

    part = lambda i: pick(i, parts, passed_ref).astype(F32)
    gain = lambda i: pick(i, gains, passed_gain_ref)[0:1].astype(F32)
    squares = sum(jnp.sum(part(i) ** 2, axis=1, keepdims=True) for i in range(size))
    scale = lax.rsqrt(squares / (size * width) + EPSILON)
    scale_ref[...] = jnp.broadcast_to(scale, scale_ref.shape)
    place_parts(
        mine, parts, normed_ref, width,
        lambda i: (part(i) * scale_ref[:, 0:1] * gain(i)).astype(BF16),
    )
    place_parts(mine, parts, gain_ref, width, lambda i: jnp.broadcast_to(gain(i), (8, width)))


def mixed_grad_kernel(parts_ref, weight_ref, out_ref, full_ref):
    size, _, width = parts_ref.shape
    for i in range(size):
        full_ref[:, i * width : (i + 1) * width] = parts_ref[i]
    out_ref[...] = dot_nt(full_ref[...], weight_ref[...])


def out_kernel(loose_ref, mixed_ref, weight_ref, out_ref):
    width = out_ref.shape[2]
    for owner in range(out_ref.shape[0]):
        value = dot(mixed_ref[...], weight_ref[:, owner * width : (owner + 1) * width])
        out_ref[owner] = value.astype(BF16)


def conv_kernel(
    value_ref, state_ref, value_kernel_ref, value_bias_ref, state_kernel_ref, state_bias_ref,
    f_ref, k_ref, conv_ref, weighted_ref, value_slope_ref, maps_ref, state_slope_ref, total_ref,
):
    chunk = pl.program_id(0)
    clear(total_ref)
    around = pl.ds(pl.multiple_of(chunk * CHUNK, CHUNK), CHUNK + HALO)
    pre = taps(
        state_ref[around, :].astype(F32), state_kernel_ref[...].astype(F32),
        state_bias_ref[...].astype(F32), HALO - KERNEL + 1,
    )
    conv, slope = silu_parts(pre)
    maps = conv.astype(BF16)
    maps_ref[...] = maps
    state_slope_ref[...] = slope
    pre = taps(
        value_ref[around, :].astype(F32), value_kernel_ref[...].astype(F32),
        value_bias_ref[...].astype(F32), HALO - KERNEL + 1,
    )
    conv, slope = silu_parts(pre)
    conv = conv.astype(BF16)
    conv_ref[...] = conv
    value_slope_ref[...] = slope
    weighted = (conv.astype(F32) * expand(f_ref[...], conv.shape[1])).astype(BF16)
    weighted_ref[...] = weighted
    factor = k_ref[pl.ds(chunk, 1), :]
    total_ref[:NSTATE, :] = factor * (
        factor * total_ref[:NSTATE, :] + dot_tn(maps[:, :NSTATE], weighted)
    )
    total_ref[NSTATE:, :] = jnp.broadcast_to(k_ref[7:8, :], (8, k_ref.shape[1]))


def mixer_kernel(
    state_in_ref, maps_ref, weighted_ref, conv_ref, e_ref, k_ref, skip_ref, gate_ref, grad_ref, gain_ref,
    mixer_ref, stats_ref, high_ref, low_ref, state_ref,
):
    chunk = pl.program_id(0)

    def start():
        state_ref[...] = state_in_ref[...]

    first_step(start)
    lane = lax.broadcasted_iota(jnp.int32, (CHUNK, CHUNK), 1)
    factor = k_ref[pl.ds(chunk, 1), :]
    input_map, output_map = maps_ref[:, :NSTATE], maps_ref[:, NSTATE:]
    weighted = weighted_ref[...]
    scaled = factor * state_ref[...]
    high, low = split(scaled)
    high_ref[0], low_ref[0] = high, low
    scores = jnp.where(lower_mask(), dot_nt(output_map, input_map), 0.0).astype(BF16)
    mixed = dot(
        jnp.concatenate([scores, output_map], axis=1), jnp.concatenate([weighted, high], axis=0)
    )
    mixed = mixed + dot(output_map, low)
    mixer = expand(e_ref[...], weighted.shape[1]) * mixed + skip_ref[...] * conv_ref[...].astype(F32)
    mixer_ref[...] = mixer
    gate = gate_ref[...]
    gated = mixer * (gate * jax.nn.sigmoid(gate))
    squares = jnp.sum(gated * gated, axis=1, keepdims=True)
    products = jnp.sum(gated * (grad_ref[...] * gain_ref[...].astype(F32)), axis=1, keepdims=True)
    sums = jnp.where(lane == 0, squares, jnp.where(lane == 1, products, 0.0))
    stats_ref[...] = sums.T[:8]
    state_ref[...] = factor * (scaled + dot_tn(input_map, weighted))


def column(row_block):
    rest = jnp.zeros((CHUNK - row_block.shape[0], CHUNK), F32)
    return jnp.concatenate([row_block, rest], axis=0).T


def row_of(sums):
    lane = lax.broadcasted_iota(jnp.int32, (CHUNK, CHUNK), 1)
    return jnp.where(lane == 0, sums, 0.0).T[:8]


def gate_kernel(
    inner, chunks, size, *refs
):
    stats_refs = refs[:size]
    (
        mixer_ref, gate_ref, grad_ref, gain_ref, conv_ref, e_ref, k_ref, maps_ref,
        mixed_ref, gate_grad_ref, mixer_grad_ref, small_ref, total_ref, cross_ref,
    ) = refs[size:]
    chunk = chunks - 1 - pl.program_id(0)
    clear(small_ref, total_ref)
    gain = gain_ref[...].astype(F32)
    stats = column(sum(ref[...] for ref in stats_refs))
    scale = lax.rsqrt(stats[:, 0:1] / inner + EPSILON)
    cross_term = stats[:, 1:2] * (scale * scale * scale) / inner
    gate = gate_ref[...]
    silu, slope = silu_parts(gate)
    mixer = mixer_ref[...]
    gated = mixer * silu
    normed = gated * scale
    mixed_ref[...] = (normed * gain).astype(BF16)
    grad = grad_ref[...]
    gated_grad = scale * (grad * gain) - gated * cross_term
    gate_grad = (gated_grad * mixer * slope).astype(BF16)
    gate_grad_ref[...] = gate_grad
    cross_ref[...] = row_of(jnp.sum(gate_grad.astype(F32) * gate, axis=1, keepdims=True))
    mixer_grad = gated_grad * silu
    mixer_grad_ref[...] = mixer_grad
    small_ref[0:1, :] += jnp.sum(grad * normed, axis=0, keepdims=True)
    small_ref[1:2, :] += jnp.sum(mixer_grad * conv_ref[...].astype(F32), axis=0, keepdims=True)
    high, low = split(expand(e_ref[...], grad.shape[1]) * mixer_grad)
    output_map = maps_ref[:, NSTATE:]
    factor = k_ref[pl.ds(chunk, 1), :]
    total_ref[:NSTATE, :] = factor * (
        factor * total_ref[:NSTATE, :] + (dot_tn(output_map, high) + dot_tn(output_map, low))
    )
    total_ref[NSTATE:, :] = jnp.broadcast_to(k_ref[7:8, :], (8, k_ref.shape[1]))


def back_kernel(
    chunks, state_in_ref, mixer_grad_ref, e_ref, f_ref, k_ref, weighted_ref, high_ref, low_ref,
    maps_ref, value_slope_ref, state_slope_ref, skip_ref,
    value_ref, map_ref, state_ref,
):
    chunk = chunks - 1 - pl.program_id(0)

    def start():
        state_ref[...] = state_in_ref[...]

    first_step(start)
    lower = lower_mask()
    row = lax.broadcasted_iota(jnp.int32, (CHUNK, CHUNK), 0)
    upper = row <= lax.broadcasted_iota(jnp.int32, (CHUNK, CHUNK), 1)
    factor = k_ref[pl.ds(chunk, 1), :]
    input_map, output_map = maps_ref[:, :NSTATE], maps_ref[:, NSTATE:]
    weighted = weighted_ref[...]
    mixer_grad = mixer_grad_ref[...]
    high, low = split(expand(e_ref[...], weighted.shape[1]) * mixer_grad)
    scaled = factor * state_ref[...]
    state_high, state_low = split(scaled)
    both = jnp.concatenate([weighted, high_ref[0]], axis=0)
    sums = dot_nt(high, both) + dot_nt(low, both)
    score_grad = jnp.where(lower, sums[:, :CHUNK], 0.0).astype(BF16)
    output_grad = sums[:, CHUNK:] + dot_nt(high, low_ref[0]) + dot(score_grad, input_map)
    sums = dot_nt(weighted, jnp.concatenate([state_high, state_low], axis=0))
    input_grad = sums[:, :NSTATE] + sums[:, NSTATE:] + dot_tn(score_grad, output_map)
    scores = jnp.where(upper, dot_nt(input_map, output_map), 0.0).astype(BF16)
    grads = dot(
        jnp.concatenate([scores, input_map], axis=1), jnp.concatenate([high, state_high], axis=0)
    )
    decayed = expand(f_ref[...], weighted.shape[1]) * grads
    value_ref[...] = (decayed + skip_ref[...] * mixer_grad) * value_slope_ref[...]
    slope = state_slope_ref[...]
    map_ref[:, :NSTATE] = input_grad * slope[:, :NSTATE]
    map_ref[:, NSTATE:] = output_grad * slope[:, NSTATE:]
    state_ref[...] = factor * (scaled + (dot_tn(output_map, high) + dot_tn(output_map, low)))


def conv_back_kernel(
    chunks, early_ref, value_ref, map_ref, after_ref, value_raw_ref, state_raw_ref, value_kernel_ref,
    state_kernel_ref, cross_in_ref,
    value_grad_ref, state_grad_ref, value_small_ref, state_small_ref, cross_ref, value_next_ref,
    state_next_ref,
):
    chunk = chunks - 1 - pl.program_id(0)
    channels = value_ref.shape[1]
    clear(value_small_ref, state_small_ref)

    def start():
        value_next_ref[...] = after_ref[:, :channels]
        state_next_ref[...] = after_ref[:, channels:]

    first_step(start)

    def back(slope_ref, next_ref, raw_ref, kernel_ref, grad_ref, small_ref):
        kernel = kernel_ref[...].astype(F32)
        slope = slope_ref[...]
        window = jnp.concatenate([slope, next_ref[...]], axis=0)
        around = pl.ds(pl.multiple_of(chunk * CHUNK, CHUNK), CHUNK + HALO)
        raw = raw_ref[around, :].astype(F32)
        grad = jnp.zeros_like(slope)
        for offset in range(KERNEL):
            back_by = KERNEL - 1 - offset
            grad = grad + kernel[offset : offset + 1] * window[back_by : back_by + CHUNK]
            begin = HALO - KERNEL + 1 + offset
            small_ref[offset : offset + 1, :] += jnp.sum(
                slope * raw[begin : begin + CHUNK], axis=0, keepdims=True
            )
        small_ref[KERNEL : KERNEL + 1, :] += jnp.sum(slope, axis=0, keepdims=True)
        grad = grad.astype(BF16)
        grad_ref[...] = grad
        next_ref[...] = slope[:8]
        return jnp.sum(grad.astype(F32) * raw[HALO:], axis=1, keepdims=True)

    crossed = back(map_ref, state_next_ref, state_raw_ref, state_kernel_ref, state_grad_ref, state_small_ref)
    crossed = crossed + back(
        value_ref, value_next_ref, value_raw_ref, value_kernel_ref, value_grad_ref, value_small_ref
    )
    cross_ref[...] = cross_in_ref[...] + row_of(crossed)


def normed_kernel(
    chunks, late_ref, gate_grad_ref, value_grad_ref, state_grad_ref, gate_weight_ref, value_weight_ref,
    state_weight_ref, cross_ref, out_ref
):
    value = (
        dot_nt(gate_grad_ref[...], gate_weight_ref[...])
        + dot_nt(value_grad_ref[...], value_weight_ref[...])
        + dot_nt(state_grad_ref[...], state_weight_ref[...])
    )
    count = value.shape[0]
    out_ref[0, :count, :] = value.astype(BF16)
    line = lax.broadcasted_iota(jnp.int32, (HALO, CHUNK), 0)
    packed = jnp.zeros((HALO, CHUNK), F32)
    for chunk in range(chunks):
        row = cross_ref[0:1, chunk * CHUNK : (chunk + 1) * CHUNK]
        high = row.astype(BF16).astype(F32)
        packed = jnp.where(line == chunk, high, packed)
        packed = jnp.where(line == chunks + chunk, row - high, packed)
    out_ref[0, count:, :] = jnp.zeros((HALO, value.shape[1]), BF16)
    out_ref[0, count:, :CHUNK] = packed.astype(BF16)


def last_kernel(full_width, parts_ref, tokens_ref, scale_ref, gain_ref, cotangent_ref, out_ref):
    count = tokens_ref.shape[0]
    chunks = count // CHUNK
    size = parts_ref.shape[0]
    crossed = sum(parts_ref[i, count:, :CHUNK].astype(F32) for i in range(size))
    crossed = crossed[:chunks] + crossed[chunks : 2 * chunks]
    for chunk in range(chunks):
        rows = slice(chunk * CHUNK, (chunk + 1) * CHUNK)
        normed_grad = sum(parts_ref[i, rows, :].astype(F32) for i in range(size))
        scale = scale_ref[HALO + chunk * CHUNK : HALO + (chunk + 1) * CHUNK, 0:1]
        total = column(jnp.broadcast_to(crossed[chunk : chunk + 1], (8, CHUNK)))[:, 0:1]
        out_ref[rows, :] = (
            scale * gain_ref[...].astype(F32) * normed_grad
            - tokens_ref[rows, :].astype(F32) * (scale * scale * total / full_width)
            + cotangent_ref[rows, :].astype(F32)
        ).astype(BF16)


def store_piece(core_ref, kept_ref, given_ref, place, begin, piece):
    chips = kept_ref.shape[0]
    core, chip = place // chips, lax.rem(place, chips)
    rows = slice(begin, begin + piece.shape[0])
    piece = piece.astype(BF16)

    @pl.when(core_ref[0] == core)
    def _():
        kept_ref[chip, rows, :] = piece

    @pl.when(core_ref[0] != core)
    def _():
        given_ref[chip, rows, :] = piece


def gain_row(weight, block):
    sums = jnp.sum(weight.astype(F32) * block, axis=1, keepdims=True)
    lane = lax.broadcasted_iota(jnp.int32, (CHUNK, CHUNK), 1)
    rows = [
        jnp.where(lane == 0, sums[i : i + CHUNK], 0.0).T[0:1] for i in range(0, BLOCK, CHUNK)
    ]
    return jnp.concatenate(rows, axis=1)


def early_kernel(
    loose_ref, core_ref, normed_ref, gate_ref, mixed_ref, grad_ref, weight_ref,
    kept_ref, given_ref, gain_ref, held_ref
):
    chips, rows, channels = kept_ref.shape
    at = pl.program_id(0)
    count, width = grad_ref.shape
    pieces = 2 * chips
    step = width // pieces
    out_rows = channels // pieces
    out_blocks = channels // BLOCK
    every = width // BLOCK // out_blocks

    @pl.when(lax.rem(at, every) == 0)
    def _():
        held_ref[...] = dot_tn(mixed_ref[...], grad_ref[...])

    block = dot_tn(normed_ref[HALO : HALO + count, :], gate_ref[...])
    gain_ref[...] = gain_row(weight_ref[...], block)
    for i in range(BLOCK // step):
        place = at * (BLOCK // step) + i
        begin = lax.rem(at, every) * (BLOCK // step * out_rows) + i * out_rows
        own = held_ref[pl.ds(pl.multiple_of(begin, 8), out_rows), :]
        parts = [block[i * step : (i + 1) * step]]
        parts += [own[:, j : j + channels] for j in range(0, width, channels)]
        store_piece(core_ref, kept_ref, given_ref, place, 0, jnp.concatenate(parts, axis=0))


def late_kernel(
    core_ref, normed_ref, value_ref, state_ref, value_small_ref, gate_small_ref, gain_ref,
    state_small_ref, value_weight_ref, state_weight_ref, gain_full_ref,
    kept_ref, given_ref, own_ref, shared_ref, gains_ref,
):
    chips, rows, channels = kept_ref.shape
    at = pl.program_id(0)
    count, maps_width = state_ref.shape
    width = gains_ref.shape[1]
    pieces = 2 * chips
    step = width // pieces
    lanes = channels // 128
    part = 2 * step // lanes
    columns = normed_ref[HALO : HALO + count, :]
    value = dot_tn(columns, value_ref[...])
    state = dot_tn(columns, state_ref[...])
    gain = (
        gain_ref[...] + gain_row(value_weight_ref[...], value) + gain_row(state_weight_ref[...], state)
    ) / gain_full_ref[0:1, :]
    gains_ref[0:1, pl.ds(pl.multiple_of(at * BLOCK, 128), BLOCK)] = gain
    for i in range(BLOCK // step):
        piece = slice(i * step, (i + 1) * step)
        stacked = jnp.concatenate([state[piece, :128], state[piece, 128:]], axis=0)
        stacked = jnp.concatenate(
            [stacked[j * part : (j + 1) * part] for j in range(lanes)], axis=1
        )
        store_piece(
            core_ref, kept_ref, given_ref, at * (BLOCK // step) + i, 0,
            jnp.concatenate([value[piece], stacked], axis=0),
        )

    @pl.when(at == width // BLOCK - 1)
    def _():
        own_ref[...] = jnp.zeros_like(own_ref)
        own_ref[: KERNEL + 1, :] = value_small_ref[: KERNEL + 1, :]
        own_ref[KERNEL + 1 : KERNEL + 3, :] = gate_small_ref[:2, :]
        shared_ref[...] = jnp.zeros_like(shared_ref)
        begin = width // channels
        for i in range(begin):
            shared_ref[i : i + 1, :] = gains_ref[0:1, i * channels : (i + 1) * channels]
        for i in range(0, (KERNEL + 1) * maps_width, 128):
            tap, column_from = divmod(i, maps_width)
            row, column_to = divmod(i, channels)
            shared_ref[begin + row : begin + row + 1, column_to : column_to + 128] = state_small_ref[
                tap : tap + 1, column_from : column_from + 128
            ]
        line = lax.broadcasted_iota(jnp.int32, (HALO, channels), 0)
        for place in range(pieces):
            own, shared = own_ref[place : place + 1, :], shared_ref[place : place + 1, :]
            own_high, shared_high = (v.astype(BF16).astype(F32) for v in (own, shared))
            small = jnp.zeros((HALO, channels), F32)
            for to, value in enumerate((own_high, own - own_high, shared_high, shared - shared_high)):
                small = jnp.where(line == to, value, small)
            store_piece(core_ref, kept_ref, given_ref, place, step + part, small)


def merge_pairs(block):
    tail = block[-HALO:]
    line = lax.broadcasted_iota(jnp.int32, tail.shape, 0)
    own, shared = tail[0:1] + tail[1:2], tail[2:3] + tail[3:4]
    own_high, shared_high = own.astype(BF16).astype(F32), shared.astype(BF16).astype(F32)
    new = jnp.zeros_like(tail)
    for at, value in enumerate((own_high, own - own_high, shared_high, shared - shared_high)):
        new = jnp.where(line == at, value, new)
    return jnp.concatenate([block[:-HALO], new], axis=0)


def heads_kernel(piece_ref, total_ref, arrived_ref, out_ref, low_ref):
    total = merge_pairs(total_ref[...] + arrived_ref[...].astype(F32))
    line = lax.broadcasted_iota(jnp.int32, total.shape, 0)
    first = total.shape[0] - HALO
    own = (line >= first) & (line < first + 2)
    out_ref[...] = total
    low_ref[...] = jnp.where(own, piece_ref[...], total).astype(BF16)


def half_kernel(paired, chips, chip_ref, kept_ref, arrived_ref, *refs):
    outs = refs[-chips:]
    for bits in range(chips):
        place = lax.bitwise_xor(chip_ref[0], bits)
        value = kept_ref[place].astype(F32) + arrived_ref[place].astype(F32)
        if paired:
            value = merge_pairs(value)
        outs[bits][...] = value.astype(outs[bits].dtype)


def piece_kernel(parts, paired, cut, *refs):
    total = sum(ref[...].astype(F32) for ref in refs[:parts])
    if not paired:
        refs[-1][...] = total.astype(BF16)
        return
    first_ref, last_ref = refs[-2:]
    first_ref[...] = total[:cut].astype(BF16)
    last_ref[...] = merge_pairs(total[cut:])


def square_half_kernel(
    chip_ref, kept_ref, arrived_ref, loose_ref, first_ref, first_give_ref, last_ref, last_give_ref
):
    cut = first_ref.shape[1]
    for bits in range(4):
        place = lax.bitwise_xor(chip_ref[0], bits)
        value = kept_ref[place].astype(F32) + arrived_ref[place].astype(F32)
        low, high = bits & 1, bits >> 1
        ref = first_give_ref if low else first_ref
        ref[high] = value[:cut].astype(ref.dtype)
        ref = last_give_ref if high else last_ref
        ref[low] = value[cut:].astype(ref.dtype)


def square_next_kernel(
    first_ref, first_got_ref, last_ref, last_got_ref, loose_ref,
    first_out_ref, first_give_ref, last_out_ref, last_give_ref,
):
    first_out_ref[...] = first_ref[0] + first_got_ref[0].astype(F32)
    first_give_ref[...] = (first_ref[1] + first_got_ref[1].astype(F32)).astype(BF16)
    last_out_ref[...] = last_ref[0] + last_got_ref[0].astype(F32)
    last_give_ref[...] = (last_ref[1] + last_got_ref[1].astype(F32)).astype(BF16)


def square_last_kernel(first_ref, first_got_ref, last_ref, last_got_ref, *refs):
    outs = refs[-2:]
    outs[0][...] = (first_ref[...] + first_got_ref[...].astype(F32)).astype(BF16)
    outs[1][...] = (last_ref[...] + last_got_ref[...].astype(F32)).astype(BF16)


def each_piece(core_ref, chip_ref, chips, groups, refs):
    refs = iter(refs)
    for part, bits_lists in enumerate(groups):
        number = 0
        for bits_list in bits_lists:
            for core, ref in ((core_ref[0], next(refs)), (1 - core_ref[0], next(refs))):
                for at, bits in enumerate(bits_list):
                    place = core * chips + lax.bitwise_xor(chip_ref[0], bits)
                    yield part, number, place, ref[at].astype(F32)
                    number += 1


def send_rows(buffer_ref, number, target_ref, place, sem_ref):
    rows = buffer_ref.shape[1]
    copy = pltpu.make_async_copy(
        buffer_ref.at[number],
        target_ref.at[pl.ds(pl.multiple_of(place * rows, 8), rows), :],
        sem_ref.at[number],
    )
    copy.start()
    return copy


def early_out_kernel(chips, groups, core_ref, chip_ref, *refs):
    gate_ref, output_ref, gate_buffer, output_buffer, gate_sems, output_sems = refs[-6:]
    out_rows, width = output_buffer.shape[1:]
    channels = gate_buffer.shape[2]
    copies = []
    for part, number, place, value in each_piece(core_ref, chip_ref, chips, groups, refs[:-6]):
        if part == 0:
            gate_buffer[number] = value
            copies.append(send_rows(gate_buffer, number, gate_ref, place, gate_sems))
        else:
            output_buffer[number] = jnp.concatenate(
                [value[i * out_rows : (i + 1) * out_rows] for i in range(width // channels)], axis=1
            )
            copies.append(send_rows(output_buffer, number, output_ref, place, output_sems))
    for copy in copies:
        copy.wait()


def late_out_kernel(chips, groups, core_ref, chip_ref, *refs):
    value_ref, buffer, sems = refs[-3:]
    copies = []
    for _, number, place, value in each_piece(core_ref, chip_ref, chips, groups, refs[:-3]):
        buffer[number] = value
        copies.append(send_rows(buffer, number, value_ref, place, sems))
    for copy in copies:
        copy.wait()


def shared_out_kernel(chips, groups, size, core_ref, chip_ref, head_ref, *refs):
    (
        state_ref, value_kernel_ref, value_bias_ref, state_kernel_ref, state_bias_ref, skip_ref,
        gated_ref, gain_ref, buffer, sems, own_ref, shared_ref,
    ) = refs[-12:]
    step, maps_width = buffer.shape[1:]
    channels = own_ref.shape[1]
    lanes = channels // 128
    rows = 2 * step // lanes
    copies = []
    for _, number, place, piece in each_piece(core_ref, chip_ref, chips, groups, refs[:-12]):
        stacked = jnp.concatenate(
            [piece[:rows, i * 128 : (i + 1) * 128] for i in range(lanes)], axis=0
        )
        buffer[number] = jnp.concatenate([stacked[:step], stacked[step:]], axis=1)
        copies.append(send_rows(buffer, number, state_ref, place, sems))
        own_ref[pl.ds(place, 1), :] = piece[rows : rows + 1] + piece[rows + 1 : rows + 2]
        shared_ref[pl.ds(place, 1), :] = piece[rows + 2 : rows + 3] + piece[rows + 3 : rows + 4]
    value_kernel_ref[...] = own_ref[:KERNEL, :]
    value_bias_ref[...] = own_ref[KERNEL, :]
    gated_ref[...] = own_ref[KERNEL + 1, :]
    heads = skip_ref.shape[0]
    at = lax.broadcasted_iota(jnp.int32, (heads, channels), 1)
    row = lax.broadcasted_iota(jnp.int32, (heads, channels), 0) * HEAD_DIM
    inside = (at >= row) & (at < row + HEAD_DIM)
    skip_ref[...] = jnp.sum(jnp.where(inside, own_ref[KERNEL + 2 : KERNEL + 3, :], 0.0), axis=1)
    own_width = gain_ref.shape[0]
    gain_rows = -(-own_width * size // channels)
    for head in range(size):
        row, begin = divmod(head * own_width, channels)

        @pl.when(head_ref[0] == head)
        def _(row=row, begin=begin):
            gain_ref[...] = shared_ref[row, begin : begin + own_width]

    for i in range(0, (KERNEL + 1) * maps_width, 128):
        tap, column_to = divmod(i, maps_width)
        row, column_from = divmod(i, channels)
        value = shared_ref[gain_rows + row : gain_rows + row + 1, column_from : column_from + 128]
        if tap < KERNEL:
            state_kernel_ref[tap : tap + 1, column_to : column_to + 128] = value
        else:
            state_bias_ref[column_to : column_to + 128] = value[0]
    for copy in copies:
        copy.wait()


SCALAR = "scalar"
WHOLE = "whole"
BLOCKED = "blocked"
LANES = "lanes"
LEADING = "leading"
FAR = "far"
LOOSE = "loose"


def run(kernel, name, flops, args, outs, steps=None, backward=False, scratch=()):
    at = (lambda i: steps - 1 - i) if backward else (lambda i: i)

    def spec(kind, shape):
        if isinstance(kind, int):
            return pl.BlockSpec((kind,) + shape[1:], lambda i: (at(i), 0))
        if kind == SCALAR:
            return pl.BlockSpec(memory_space=pltpu.SMEM)
        if kind == LOOSE:
            return pl.BlockSpec(memory_space=pl.ANY)
        if kind == FAR:
            return pl.BlockSpec(memory_space=pltpu.HBM)
        if isinstance(kind, tuple):
            return pl.BlockSpec(*kind)
        if steps is None:
            return pl.BlockSpec(memory_space=pltpu.VMEM)
        if kind == BLOCKED:
            return pl.BlockSpec((CHUNK, shape[1]), lambda i: (at(i), 0))
        if kind == LANES:
            return pl.BlockSpec((shape[0], CHUNK), lambda i: (0, at(i)))
        if kind == LEADING:
            return pl.BlockSpec((1,) + shape[1:], lambda i: (at(i),) + (0,) * (len(shape) - 1))
        return pl.BlockSpec(shape, lambda i: (0,) * len(shape))

    moved = sum(a.size * a.dtype.itemsize for kind, a in args if kind != LOOSE)
    shapes = [jax.ShapeDtypeStruct(shape, dtype) for _, shape, dtype in outs]
    moved += sum(a.size * a.dtype.itemsize for a in shapes)
    return pl.pallas_call(
        kernel,
        out_shape=shapes,
        in_specs=[spec(kind, a.shape) for kind, a in args],
        out_specs=[spec(kind, shape) for kind, shape, _ in outs],
        scratch_shapes=list(scratch),
        compiler_params=pltpu.CompilerParams(vmem_limit_bytes=VMEM_LIMIT),
        cost_estimate=pl.CostEstimate(flops=flops, bytes_accessed=moved, transcendentals=0),
        name=name,
        **({} if steps is None else {"grid": (steps,)}),
    )(*(a for _, a in args))


def per_device(
    tokens, decay_codes, norm_gain, gate_weight, value_weight, state_weight, value_kernel, value_bias,
    state_kernel, state_bias, skip_scale, gated_gain, output_weight, cotangent,
):
    tokens, decay_codes, cotangent = tokens[0], decay_codes[0], cotangent[0]
    count, own_width = tokens.shape
    heads = skip_scale.shape[0]
    channels = heads * HEAD_DIM
    head_size, chips = lax.axis_size("head"), lax.axis_size("chip")
    seq_size = 2 * chips
    width = own_width * head_size
    maps_width = 2 * NSTATE
    chunks = count // CHUNK
    core = (SCALAR, lax.axis_index("core").astype(jnp.int32)[None])
    chip = (SCALAR, lax.axis_index("chip").astype(jnp.int32)[None])
    head = (SCALAR, lax.axis_index("head").astype(jnp.int32)[None])

    rows = count + MARGIN
    packed = jnp.concatenate(
        [
            from_behind(tokens[-HALO:], 1),
            tokens,
            jnp.broadcast_to(norm_gain[None], (MARGIN - HALO, own_width)),
        ],
        axis=0,
    )
    logs = decay_codes.astype(F32) * (-DECAY_STEP)
    input_weight = jnp.sqrt(-jnp.expm1(2.0 * logs))
    e_full, f_full, factors = run(
        decay_kernel, "decays", count * channels * 200,
        [(WHOLE, decay_codes), (WHOLE, input_weight)],
        [
            (WHOLE, (count, heads), F32),
            (WHOLE, (count, heads), F32),
            (WHOLE, (8, channels), F32),
        ],
    )
    parts, passed = line_parts(packed, "head")
    skip_full = jnp.repeat(skip_scale, HEAD_DIM)[None]

    half = rows // 2
    gain_rows = ((MARGIN - HALO, own_width), lambda i: ((HALO + count) // (MARGIN - HALO), 0))
    normed, scale_in, gain_full = run(
        functools.partial(norm_kernel, head_size), "norm", count * width * 10,
        [head, (half, passed)] + [(half, part) for part in parts]
        + [(gain_rows, part) for part in parts] + [(gain_rows, passed)],
        [(half, (rows, width), BF16), (half, (rows, 128), F32), (WHOLE, (8, width), F32)],
        steps=2,
    )
    cotangent_parts = deal(
        run(
            copies_kernel, "copies", 1, [(LOOSE, normed), (WHOLE, cotangent)],
            [(WHOLE, (head_size, count, own_width), BF16)],
        )[0],
        "head",
    )
    value_raw = dot(normed, value_weight).astype(BF16)
    state_raw = dot(normed, state_weight).astype(BF16)
    conv, weighted, value_slope, maps, map_slope, local_end = run(
        conv_kernel, "conv", count * channels * 400,
        [
            (WHOLE, value_raw), (WHOLE, state_raw), (WHOLE, value_kernel), (WHOLE, value_bias[None]),
            (WHOLE, state_kernel), (WHOLE, state_bias[None]), (BLOCKED, f_full), (WHOLE, factors),
        ],
        [
            (BLOCKED, (count, channels), BF16),
            (BLOCKED, (count, channels), BF16),
            (BLOCKED, (count, channels), F32),
            (BLOCKED, (count, maps_width), BF16),
            (BLOCKED, (count, maps_width), F32),
            (WHOLE, (NSTATE + 8, channels), F32),
        ],
        steps=chunks,
    )
    gate_pre = dot(normed, gate_weight)[HALO : HALO + count]
    state_in, _ = entering(core, chip, local_end, False, (gate_pre,))
    mixed_grad, full_cotangent = run(
        mixed_grad_kernel, "mixed_grad", 2 * count * width * channels,
        [(WHOLE, cotangent_parts), (WHOLE, output_weight)],
        [(WHOLE, (count, channels), F32), (WHOLE, (count, width), BF16)],
    )
    mixer, stats, high, low = run(
        mixer_kernel, "mixer", count * channels * 1000,
        [
            (WHOLE, state_in), (BLOCKED, maps), (BLOCKED, weighted), (BLOCKED, conv),
            (BLOCKED, e_full), (WHOLE, factors), (WHOLE, skip_full), (BLOCKED, gate_pre),
            (BLOCKED, mixed_grad), (WHOLE, gated_gain[None]),
        ],
        [
            (BLOCKED, (count, channels), F32),
            (LANES, (8, count), F32),
            (LEADING, (chunks, NSTATE, channels), BF16),
            (LEADING, (chunks, NSTATE, channels), BF16),
        ],
        steps=chunks,
        scratch=[pltpu.VMEM((NSTATE, channels), F32)],
    )
    mixed, gate_grad, mixer_grad, gate_small, start_grad, gate_cross = run(
        functools.partial(gate_kernel, float(channels * head_size), chunks, head_size),
        "gate", count * channels * 600,
        [(LANES, part) for part in turn_all(stats, "head")]
        + [
            (BLOCKED, mixer), (BLOCKED, gate_pre), (BLOCKED, mixed_grad), (WHOLE, gated_gain[None]),
            (BLOCKED, conv), (BLOCKED, e_full), (WHOLE, factors), (BLOCKED, maps),
        ],
        [
            (BLOCKED, (count, channels), BF16),
            (BLOCKED, (count, channels), BF16),
            (BLOCKED, (count, channels), F32),
            (WHOLE, (8, channels), F32),
            (WHOLE, (NSTATE + 8, channels), F32),
            (LANES, (8, count), F32),
        ],
        steps=chunks,
        backward=True,
    )
    step, out_rows = width // seq_size, channels // seq_size
    early_rows = step + out_rows * (width // channels)
    features = width // BLOCK
    feature_block = ((rows, BLOCK), lambda i: (0, i))
    every = features // (channels // BLOCK)
    out_parts = run(
        out_kernel, "out", 2 * count * channels * width,
        [(LOOSE, start_grad), (WHOLE, mixed), (WHOLE, output_weight)],
        [(WHOLE, (head_size, count, own_width), BF16)],
    )[0]
    grad_after, _ = entering(core, chip, start_grad, True, (out_parts,))
    branch = jnp.sum(deal(out_parts, "head").astype(F32), axis=0)
    block_out = (tokens.astype(F32) + branch).astype(BF16)

    value_grads, map_grads = run(
        functools.partial(back_kernel, chunks), "back", count * channels * 2000,
        [
            (WHOLE, grad_after), (BLOCKED, mixer_grad), (BLOCKED, e_full),
            (BLOCKED, f_full), (WHOLE, factors), (BLOCKED, weighted), (LEADING, high),
            (LEADING, low), (BLOCKED, maps), (BLOCKED, value_slope), (BLOCKED, map_slope),
            (WHOLE, skip_full),
        ],
        [(BLOCKED, (count, channels), F32), (BLOCKED, (count, maps_width), F32)],
        steps=chunks,
        backward=True,
        scratch=[pltpu.VMEM((NSTATE, channels), F32)],
    )
    early_kept, early_given, early_gain = run(
        early_kernel, "early", 4 * count * channels * width,
        [
            (LOOSE, value_grads), core, (feature_block, normed), (WHOLE, gate_grad),
            (((count, BLOCK), lambda i: (0, i // every)), mixed), (WHOLE, full_cotangent),
            (BLOCK, gate_weight),
        ],
        [(WHOLE, (chips, early_rows, channels), BF16)] * 2
        + [(((1, BLOCK), lambda i: (0, i)), (1, width), F32)],
        steps=features,
        scratch=[pltpu.VMEM((BLOCK, width), F32)],
    )
    after = from_behind(jnp.concatenate([value_grads[:8], map_grads[:8]], axis=1), -1)
    value_raw_grad, state_raw_grad, value_small, state_small, crossed = run(
        functools.partial(conv_back_kernel, chunks), "conv_back", count * channels * 100,
        [
            (LOOSE, early_given), (BLOCKED, value_grads), (BLOCKED, map_grads), (WHOLE, after),
            (WHOLE, value_raw), (WHOLE, state_raw), (WHOLE, value_kernel), (WHOLE, state_kernel),
            (LANES, gate_cross),
        ],
        [
            (BLOCKED, (count, channels), BF16),
            (BLOCKED, (count, maps_width), BF16),
            (WHOLE, (8, channels), F32),
            (WHOLE, (8, maps_width), F32),
            (LANES, (8, count), F32),
        ],
        steps=chunks,
        backward=True,
        scratch=[pltpu.VMEM((8, channels), F32), pltpu.VMEM((8, maps_width), F32)],
    )
    lanes = channels // 128
    state_rows = 2 * step // lanes
    late_rows = step + state_rows + HALO
    late_kept, late_given = run(
        late_kernel, "late", 3 * count * channels * width,
        [
            core, (feature_block, normed), (WHOLE, value_raw_grad),
            (WHOLE, state_raw_grad),
            (WHOLE, value_small), (WHOLE, gate_small), (((1, BLOCK), lambda i: (0, i)), early_gain),
            (WHOLE, state_small), (BLOCK, value_weight), (BLOCK, state_weight),
            (((8, BLOCK), lambda i: (0, i)), gain_full),
        ],
        [(WHOLE, (chips, late_rows, channels), BF16)] * 2,
        steps=features,
        scratch=[
            pltpu.VMEM((HALO, channels), F32),
            pltpu.VMEM((HALO, channels), F32),
            pltpu.VMEM((8, width), F32),
        ],
    )
    made = []

    def make_normed(mark):
        made.extend(
            run(
                functools.partial(normed_kernel, chunks), "normed", 4 * count * channels * width,
                [
                    (LOOSE, mark), (WHOLE, gate_grad), (WHOLE, value_raw_grad),
                    (WHOLE, state_raw_grad), (own_width, gate_weight), (own_width, value_weight),
                    (own_width, state_weight), (WHOLE, crossed),
                ],
                [(LEADING, (head_size, count + HALO, own_width), BF16)],
                steps=head_size,
            )
        )
        return made

    (late_piece, shared_piece), late_mark = sum_pieces(
        chip, late_kept, late_given, "late", False, step, True, meanwhile=make_normed
    )
    normed_parts = made[0]
    shared_piece, heads_mark = heads_sum(shared_piece)
    late_found, shared_found = collect(late_piece, None), collect(shared_piece, (2, 1))
    early_state, _ = sum_pieces(
        chip, early_kept, early_given, "early", True, step, False, (late_piece,)
    )
    if chips == 4:
        early_state = square_next("early", early_state, early_rows * channels, shared_piece)
    if chips == 4:
        early_gate, early_out = square_end(
            "early", early_state,
            [(WHOLE, (step, channels), BF16), (WHOLE, (early_rows - step, channels), BF16)],
            early_rows * channels, [found[0] for found in late_found[1:] + shared_found[:1]],
        )
    else:
        early_gate, early_out = early_state[0][:step], early_state[0][step:]
    normed_parts = deal(normed_parts, "head")
    def unpack(kernel, name, pieces, outs, flops, scratch, extra=(), args=()):
        groups = [piece if isinstance(piece, list) else collect(*piece) for piece in pieces]
        bits = [[found[2] for found in group] for group in groups]
        arrays = [(WHOLE, value) for group in groups for found in group for value in found[:2]]
        return run(
            functools.partial(kernel, chips, bits, *extra), name, flops,
            [core, chip, *args] + arrays, outs, scratch=scratch,
        )

    sems = pltpu.SemaphoreType.DMA((seq_size,))
    gate_weight_gradient, output_weight_gradient = unpack(
        early_out_kernel, "early_out",
        [(early_gate, (2, 1), late_mark), (early_out, (1, 2), late_mark)],
        [(FAR, (width, channels), F32), (FAR, (channels, width), F32)], 4 * channels * width,
        [
            pltpu.VMEM((seq_size, step, channels), F32),
            pltpu.VMEM((seq_size, out_rows, width), F32),
            sems,
            sems,
        ],
    )
    value_weight_gradient = unpack(
        late_out_kernel, "late_out", [late_found],
        [(FAR, (width, channels), F32)], 2 * channels * width,
        [pltpu.VMEM((seq_size, step, channels), F32), sems],
    )[0]
    (
        state_weight_gradient, value_kernel_gradient, value_bias_gradient, state_kernel_gradient,
        state_bias_gradient, skip_scale_gradient, gated_gain_gradient, norm_gain_gradient,
    ) = unpack(
        shared_out_kernel, "shared_out", [shared_found],
        [
            (FAR, (width, maps_width), F32),
            (WHOLE, (KERNEL, channels), F32),
            (WHOLE, (channels,), F32),
            (WHOLE, (KERNEL, maps_width), F32),
            (WHOLE, (maps_width,), F32),
            (WHOLE, (heads,), F32),
            (WHOLE, (channels,), F32),
            (WHOLE, (own_width,), F32),
        ],
        2 * maps_width * width,
        [
            pltpu.VMEM((seq_size, step, maps_width), F32),
            sems,
            pltpu.VMEM((HALO, channels), F32),
            pltpu.VMEM((HALO, channels), F32),
        ],
        extra=(head_size,),
        args=[head],
    )
    tokens_gradient = run(
        functools.partial(last_kernel, float(width)), "last", count * own_width * 20,
        [
            (WHOLE, normed_parts), (WHOLE, tokens), (WHOLE, scale_in),
            (WHOLE, norm_gain[None]), (WHOLE, cotangent),
        ],
        [(WHOLE, (count, own_width), BF16)],
    )[0]
    return (
        block_out[None],
        tokens_gradient[None],
        norm_gain_gradient,
        gate_weight_gradient,
        value_weight_gradient,
        state_weight_gradient,
        value_kernel_gradient,
        value_bias_gradient,
        state_kernel_gradient,
        state_bias_gradient,
        skip_scale_gradient,
        gated_gain_gradient,
        output_weight_gradient,
    )


def solution(mesh):
    seq_size, head_size = mesh.shape["seq"], mesh.shape["head"]
    mesh = Mesh(mesh.devices.reshape(seq_size // 2, 2, head_size), ("chip", "core", "head"))
    seq = ("chip", "core")
    in_specs = (
        P(None, seq, "head"),
        P(None, seq, "head"),
        P("head"),
        P(None, "head"),
        P(None, "head"),
        P(),
        P(None, "head"),
        P("head"),
        P(),
        P(),
        P("head"),
        P("head"),
        P("head", None),
        P(None, seq, "head"),
    )
    out_specs = (
        P(None, seq, "head"),
        P(None, seq, "head"),
        P("head"),
        P(None, "head"),
        P(None, "head"),
        P(),
        P(None, "head"),
        P("head"),
        P(),
        P(),
        P("head"),
        P("head"),
        P("head", None),
    )
    return jax.shard_map(
        per_device, mesh=mesh, in_specs=in_specs, out_specs=out_specs, check_vma=False
    )
```

```python
import functools

import jax
import jax.numpy as jnp
from jax import lax
from jax.experimental import pallas as pl
from jax.experimental.pallas import tpu as pltpu
from jax.sharding import Mesh
from jax.sharding import PartitionSpec as P

HEAD_DIM = 64
NSTATE = 128
KERNEL = 4
CHUNK = 128
BLOCK = 384
VMEM_LIMIT = 20 * 1024 * 1024
MARGIN = 32
HALO = 16


DECAY_STEP = 1.0 / 1048576.0
EPSILON = 1e-05
BF16 = jnp.bfloat16
F32 = jnp.float32


def tie_kernel(*refs):
    del refs


def tie(value, *others):
    return pl.pallas_call(
        tie_kernel,
        out_shape=jax.ShapeDtypeStruct(value.shape, value.dtype),
        in_specs=[pl.BlockSpec(memory_space=pl.ANY)] * (1 + len(others)),
        out_specs=pl.BlockSpec(memory_space=pl.ANY),
        input_output_aliases={0: 0},
        name="tie",
    )(value, *others)


def from_behind(value, by):
    axis = ("chip", "core")
    size = lax.axis_size("chip") * 2
    pairs = [(i, i + by) for i in range(size) if 0 <= i + by < size]
    return lax.ppermute(value, axis, pairs)


def beside(value):
    return lax.ppermute(value, "core", [(0, 1), (1, 0)])


def turn(value, axis, by):
    size = lax.axis_size(axis)
    return lax.ppermute(value, axis, [(i, (i + by) % size) for i in range(size)])


def turn_all(value, axis):
    return [value] + [turn(value, axis, by) for by in range(1, lax.axis_size(axis))]


def line_parts(value, axis):
    if lax.axis_size(axis) != 4:
        parts = turn_all(value, axis)
        return parts, value
    two = turn(value, axis, 2)
    one = lax.ppermute(value, axis, [(0, 1), (1, 2), (2, 3)])
    three = lax.ppermute(value, axis, [(1, 0), (2, 1), (3, 2)])
    passed = lax.ppermute(two, axis, [(2, 3), (1, 0)])
    return [value, one, two, three], passed


def deal(parts, axis):
    return lax.all_to_all(parts, axis, 0, 0)


def cross(value, bits):
    return lax.ppermute(value, "chip", [(i, i ^ bits) for i in range(lax.axis_size("chip"))])


def cross_all(value):
    return [value] + [cross(value, bits) for bits in range(1, lax.axis_size("chip"))]


def heads_sum(piece):
    total, low = piece, piece.astype(BF16)
    bits, size = 1, lax.axis_size("head")
    while bits < size:
        arrived = lax.ppermute(low, "head", [(i, i ^ bits) for i in range(size)])
        total, low = run(
            heads_kernel, "heads", piece.size,
            [(WHOLE, piece), (WHOLE, total), (WHOLE, arrived)],
            [(WHOLE, piece.shape, F32), (WHOLE, piece.shape, BF16)],
        )
        bits *= 2
    return low


def entering(core, chip, total, backward, meanwhile, later=lambda pair: ()):
    name = "after" if backward else "before"
    chips = lax.axis_size("chip")
    channels = total.shape[1]
    half = NSTATE // 2
    partner = beside(total)
    pair = run(
        functools.partial(pair_kernel, backward), name + "_pair", total.size,
        [core, (WHOLE, total), (WHOLE, partner)] + [(LOOSE, value) for value in meanwhile],
        [(WHOLE, (half + 8, channels), F32)],
    )[0]
    prefix = run(
        functools.partial(prefix_kernel, backward, chips), name + "_prefix", chips * pair.size,
        [chip] + [(WHOLE, value) for value in cross_all(pair)]
        + [(LOOSE, value) for value in later(pair)],
        [(WHOLE, (half, channels), F32)],
    )[0]
    return run(
        functools.partial(enter_kernel, backward), name + "_enter", total.size,
        [core, (WHOLE, partner), (WHOLE, prefix), (WHOLE, beside(prefix))],
        [(WHOLE, (NSTATE, channels), F32)],
    )[0], prefix


def sum_pieces(chip, kept, given, name, square, cut, paired, before_half=()):
    chips, rows, channels = kept.shape
    arrived = beside(given)
    size = chips * rows * channels
    if paired:
        outs = [(WHOLE, (cut, channels), BF16), (WHOLE, (rows - cut, channels), F32)]
    else:
        outs = [(WHOLE, (rows, channels), BF16)]
    if chips != 4 or not square:
        halves = run(
            functools.partial(half_kernel, paired, chips), name + "_half", size,
            [chip, (WHOLE, kept), (WHOLE, arrived)] + [(LOOSE, mark) for mark in before_half],
            [(WHOLE, (rows, channels), F32)] + [(WHOLE, (rows, channels), BF16)] * (chips - 1),
        )
        parts = [halves[0]] + [cross(halves[bits], bits) for bits in range(1, chips)]
        found = run(
            functools.partial(piece_kernel, chips, paired, cut), name + "_piece", size,
            [(WHOLE, part) for part in parts], outs,
        )
        return found, halves[0]
    rest = rows - cut
    state = run(
        square_half_kernel, name + "_half", size,
        [chip, (WHOLE, kept), (WHOLE, arrived)] + [(LOOSE, mark) for mark in before_half],
        [
            (WHOLE, (2, cut, channels), F32), (WHOLE, (2, cut, channels), BF16),
            (WHOLE, (2, rest, channels), F32), (WHOLE, (2, rest, channels), BF16),
        ],
    )
    return state, state[0]


def square_next(name, state, size, mark):
    first, first_give, last, last_give = state
    _, cut, channels = first.shape
    rest = last.shape[1]
    return run(
        square_next_kernel, name + "_next", size,
        [
            (WHOLE, first), (WHOLE, cross(first_give, 1)),
            (WHOLE, last), (WHOLE, cross(last_give, 2)), (LOOSE, mark),
        ],
        [
            (WHOLE, (cut, channels), F32), (WHOLE, (cut, channels), BF16),
            (WHOLE, (rest, channels), F32), (WHOLE, (rest, channels), BF16),
        ],
    )


def square_end(name, state, outs, size, mark):
    first, first_give, last, last_give = state
    return run(
        square_last_kernel, name + "_piece", size,
        [
            (WHOLE, first), (WHOLE, cross(first_give, 2)),
            (WHOLE, last), (WHOLE, cross(last_give, 1)), (LOOSE, mark),
        ],
        outs,
    )


def collect(piece, order, mark=None):
    chips = lax.axis_size("chip")
    if chips != 4 or order is None:
        found = [(value[None], (bits,)) for bits, value in enumerate(cross_all(piece))]
    else:
        near, far = order
        both = jnp.stack([piece, cross(piece, near)])
        if mark is not None:
            both = tie(both, mark)
        found = [(both, (0, near)), (cross(both, far), (far, far ^ near))]
    return [(value, beside(value), bits) for value, bits in found]


def dot(left, right):
    return jnp.dot(left, right, preferred_element_type=F32)


def dot_nt(left, right):
    return lax.dot_general(left, right, (((1,), (1,)), ((), ())), preferred_element_type=F32)


def dot_tn(left, right):
    return lax.dot_general(left, right, (((0,), (0,)), ((), ())), preferred_element_type=F32)


def split(values):
    high = values.astype(BF16)
    return high, (values - high.astype(F32)).astype(BF16)


def lower_mask():
    row = lax.broadcasted_iota(jnp.int32, (CHUNK, CHUNK), 0)
    column = lax.broadcasted_iota(jnp.int32, (CHUNK, CHUNK), 1)
    return row >= column


def spread_heads(heads, channels):
    row = lax.broadcasted_iota(jnp.int32, (heads, channels), 0) * HEAD_DIM
    place = lax.broadcasted_iota(jnp.int32, (heads, channels), 1)
    return jnp.where((place >= row) & (place < row + HEAD_DIM), 1.0, 0.0).astype(BF16)


def expand(values, channels):
    high, low = split(values)
    spread = spread_heads(values.shape[1], channels)
    return dot(high, spread) + dot(low, spread)


def decay_kernel(codes_ref, weight_ref, e_ref, f_ref, k_ref):
    heads, channels = codes_ref.shape[1], k_ref.shape[1]
    lower = jnp.where(lower_mask(), 1.0, 0.0).astype(F32)
    count = codes_ref.shape[0] // CHUNK
    line = lax.broadcasted_iota(jnp.int32, (8, heads), 0)
    marks = jnp.zeros((8, heads), F32)
    total = jnp.zeros((1, heads), F32)
    for chunk in range(count):
        rows = pl.ds(chunk * CHUNK, CHUNK)
        logs = codes_ref[rows, :].astype(F32) * (-DECAY_STEP)
        cumulative = jnp.dot(
            lower, logs, precision=lax.Precision.HIGHEST, preferred_element_type=F32
        )
        last = cumulative[CHUNK - 1 :]
        middle = 0.5 * last
        e_ref[rows, :] = jnp.exp(cumulative - middle)
        f_ref[rows, :] = weight_ref[rows, :] * jnp.exp(middle - cumulative)
        marks = jnp.where(line == chunk, jnp.exp(middle), marks)
        total = total + last
    marks = jnp.where(line == 7, total, marks)
    high, low = split(marks)
    lowest = (marks - high.astype(F32) - low.astype(F32)).astype(BF16)
    spread = spread_heads(heads, channels)
    factors = dot(high, spread) + dot(low, spread) + dot(lowest, spread)
    k_ref[...] = factors


def pair_kernel(backward, core_ref, own_ref, other_ref, *refs):
    out_ref = refs[-1]
    half = NSTATE // 2
    logs, other_logs = own_ref[NSTATE:, :], other_ref[NSTATE:, :]
    for core in range(2):

        @pl.when(core_ref[0] == core)
        def _():
            rows = slice(core * half, (core + 1) * half)
            if core == (0 if backward else 1):
                out_ref[:half, :] = jnp.exp(logs[0:1]) * other_ref[rows, :] + own_ref[rows, :]
            else:
                out_ref[:half, :] = jnp.exp(other_logs[0:1]) * own_ref[rows, :] + other_ref[rows, :]

    out_ref[half:, :] = logs + other_logs


def prefix_kernel(backward, chips, chip_ref, *refs):
    parts, out_ref = refs[:chips], refs[-1]
    half = out_ref.shape[0]
    mine = chip_ref[0]
    total = jnp.zeros(out_ref.shape, F32)
    for bits in range(1, chips):
        source = lax.bitwise_xor(mine, bits)
        span = jnp.zeros((1, out_ref.shape[1]), F32)
        for other in range(1, chips):
            middle = lax.bitwise_xor(mine, other)
            if backward:
                between = (middle < source) & (middle > mine)
            else:
                between = (middle > source) & (middle < mine)
            span = span + jnp.where(between, parts[other][half : half + 1, :], 0.0)
        passes = source > mine if backward else source < mine
        total = total + jnp.where(passes, jnp.exp(span), 0.0) * parts[bits][:half, :]
    out_ref[...] = total


def enter_kernel(backward, core_ref, partner_ref, prefix_ref, other_ref, out_ref):
    half = prefix_ref.shape[0]
    decay = jnp.exp(partner_ref[NSTATE : NSTATE + 1, :])
    for core in range(2):

        @pl.when(core_ref[0] == core)
        def _():
            for place, ref in ((core, prefix_ref), (1 - core, other_ref)):
                rows = slice(place * half, (place + 1) * half)
                if core == (0 if backward else 1):
                    out_ref[rows, :] = decay * ref[...] + partner_ref[rows, :]
                else:
                    out_ref[rows, :] = ref[...]


def taps(window, kernel, bias, begin):
    summed = bias
    for offset in range(KERNEL):
        summed = summed + kernel[offset : offset + 1] * window[begin + offset : begin + offset + CHUNK]
    return summed


def silu_parts(values):
    sigmoid = jax.nn.sigmoid(values)
    return values * sigmoid, sigmoid * (1.0 + values * (1.0 - sigmoid))


def first_step(action):
    pl.when(pl.program_id(0) == 0)(action)


def clear(*refs):
    def action():
        for ref in refs:
            ref[...] = jnp.zeros_like(ref)

    first_step(action)


def place_parts(mine, parts, target, width, value):
    size = len(parts)
    if width % 128 == 0:
        for i in range(size):
            owner = lax.rem(mine + size - i, size)
            target[:, pl.ds(pl.multiple_of(owner * width, 128), width)] = value(i)
        return

    def write(me):
        for i in range(size):
            owner = (me + size - i) % size
            target[:, owner * width : (owner + 1) * width] = value(i)

    for me in range(size):
        pl.when(mine == me)(functools.partial(write, me))


def copies_kernel(loose_ref, own_ref, out_ref):
    for i in range(out_ref.shape[0]):
        out_ref[i] = own_ref[...]


def norm_kernel(size, head_ref, passed_ref, *refs):
    parts, gains = refs[:size], refs[size : 2 * size]
    passed_gain_ref, normed_ref, scale_ref, gain_ref = refs[2 * size :]
    width = parts[0].shape[1]
    mine = head_ref[0]

    def pick(i, refs, passed):
        if size == 4 and i == 1:
            return jnp.where(mine == 0, passed[...], refs[i][...])
        if size == 4 and i == 3:
            return jnp.where(mine == 3, passed[...], refs[i][...])
        return refs[i][...]

    part = lambda i: pick(i, parts, passed_ref).astype(F32)
    gain = lambda i: pick(i, gains, passed_gain_ref)[0:1].astype(F32)
    squares = sum(jnp.sum(part(i) ** 2, axis=1, keepdims=True) for i in range(size))
    scale = lax.rsqrt(squares / (size * width) + EPSILON)
    scale_ref[...] = jnp.broadcast_to(scale, scale_ref.shape)
    place_parts(
        mine, parts, normed_ref, width,
        lambda i: (part(i) * scale_ref[:, 0:1] * gain(i)).astype(BF16),
    )
    place_parts(mine, parts, gain_ref, width, lambda i: jnp.broadcast_to(gain(i), (8, width)))


def mixed_grad_kernel(parts_ref, weight_ref, out_ref, full_ref):
    size, _, width = parts_ref.shape
    for i in range(size):
        full_ref[:, i * width : (i + 1) * width] = parts_ref[i]
    out_ref[...] = dot_nt(full_ref[...], weight_ref[...])


def out_kernel(loose_ref, mixed_ref, weight_ref, out_ref):
    width = out_ref.shape[2]
    for owner in range(out_ref.shape[0]):
        value = dot(mixed_ref[...], weight_ref[:, owner * width : (owner + 1) * width])
        out_ref[owner] = value.astype(BF16)


def conv_kernel(
    value_ref, state_ref, value_kernel_ref, value_bias_ref, state_kernel_ref, state_bias_ref,
    f_ref, k_ref, conv_ref, weighted_ref, value_slope_ref, maps_ref, state_slope_ref, total_ref,
):
    chunk = pl.program_id(0)
    clear(total_ref)
    around = pl.ds(pl.multiple_of(chunk * CHUNK, CHUNK), CHUNK + HALO)
    pre = taps(
        state_ref[around, :].astype(F32), state_kernel_ref[...].astype(F32),
        state_bias_ref[...].astype(F32), HALO - KERNEL + 1,
    )
    conv, slope = silu_parts(pre)
    maps = conv.astype(BF16)
    maps_ref[...] = maps
    state_slope_ref[...] = slope
    pre = taps(
        value_ref[around, :].astype(F32), value_kernel_ref[...].astype(F32),
        value_bias_ref[...].astype(F32), HALO - KERNEL + 1,
    )
    conv, slope = silu_parts(pre)
    conv = conv.astype(BF16)
    conv_ref[...] = conv
    value_slope_ref[...] = slope
    weighted = (conv.astype(F32) * expand(f_ref[...], conv.shape[1])).astype(BF16)
    weighted_ref[...] = weighted
    factor = k_ref[pl.ds(chunk, 1), :]
    total_ref[:NSTATE, :] = factor * (
        factor * total_ref[:NSTATE, :] + dot_tn(maps[:, :NSTATE], weighted)
    )
    total_ref[NSTATE:, :] = jnp.broadcast_to(k_ref[7:8, :], (8, k_ref.shape[1]))


def mixer_kernel(
    state_in_ref, maps_ref, weighted_ref, conv_ref, e_ref, k_ref, skip_ref, gate_ref, grad_ref, gain_ref,
    mixer_ref, stats_ref, high_ref, low_ref, state_ref,
):
    chunk = pl.program_id(0)

    def start():
        state_ref[...] = state_in_ref[...]

    first_step(start)
    lane = lax.broadcasted_iota(jnp.int32, (CHUNK, CHUNK), 1)
    factor = k_ref[pl.ds(chunk, 1), :]
    input_map, output_map = maps_ref[:, :NSTATE], maps_ref[:, NSTATE:]
    weighted = weighted_ref[...]
    scaled = factor * state_ref[...]
    high, low = split(scaled)
    high_ref[0], low_ref[0] = high, low
    scores = jnp.where(lower_mask(), dot_nt(output_map, input_map), 0.0).astype(BF16)
    mixed = dot(
        jnp.concatenate([scores, output_map], axis=1), jnp.concatenate([weighted, high], axis=0)
    )
    mixed = mixed + dot(output_map, low)
    mixer = expand(e_ref[...], weighted.shape[1]) * mixed + skip_ref[...] * conv_ref[...].astype(F32)
    mixer_ref[...] = mixer
    gate = gate_ref[...]
    gated = mixer * (gate * jax.nn.sigmoid(gate))
    squares = jnp.sum(gated * gated, axis=1, keepdims=True)
    products = jnp.sum(gated * (grad_ref[...] * gain_ref[...].astype(F32)), axis=1, keepdims=True)
    sums = jnp.where(lane == 0, squares, jnp.where(lane == 1, products, 0.0))
    stats_ref[...] = sums.T[:8]
    state_ref[...] = factor * (scaled + dot_tn(input_map, weighted))


def column(row_block):
    rest = jnp.zeros((CHUNK - row_block.shape[0], CHUNK), F32)
    return jnp.concatenate([row_block, rest], axis=0).T


def row_of(sums):
    lane = lax.broadcasted_iota(jnp.int32, (CHUNK, CHUNK), 1)
    return jnp.where(lane == 0, sums, 0.0).T[:8]


def gate_kernel(
    inner, chunks, size, *refs
):
    stats_refs = refs[:size]
    (
        mixer_ref, gate_ref, grad_ref, gain_ref, conv_ref, e_ref, k_ref, maps_ref,
        mixed_ref, gate_grad_ref, mixer_grad_ref, small_ref, total_ref, cross_ref,
    ) = refs[size:]
    chunk = chunks - 1 - pl.program_id(0)
    clear(small_ref, total_ref)
    gain = gain_ref[...].astype(F32)
    stats = column(sum(ref[...] for ref in stats_refs))
    scale = lax.rsqrt(stats[:, 0:1] / inner + EPSILON)
    cross_term = stats[:, 1:2] * (scale * scale * scale) / inner
    gate = gate_ref[...]
    silu, slope = silu_parts(gate)
    mixer = mixer_ref[...]
    gated = mixer * silu
    normed = gated * scale
    mixed_ref[...] = (normed * gain).astype(BF16)
    grad = grad_ref[...]
    gated_grad = scale * (grad * gain) - gated * cross_term
    gate_grad = (gated_grad * mixer * slope).astype(BF16)
    gate_grad_ref[...] = gate_grad
    cross_ref[...] = row_of(jnp.sum(gate_grad.astype(F32) * gate, axis=1, keepdims=True))
    mixer_grad = gated_grad * silu
    mixer_grad_ref[...] = mixer_grad
    small_ref[0:1, :] += jnp.sum(grad * normed, axis=0, keepdims=True)
    small_ref[1:2, :] += jnp.sum(mixer_grad * conv_ref[...].astype(F32), axis=0, keepdims=True)
    high, low = split(expand(e_ref[...], grad.shape[1]) * mixer_grad)
    output_map = maps_ref[:, NSTATE:]
    factor = k_ref[pl.ds(chunk, 1), :]
    total_ref[:NSTATE, :] = factor * (
        factor * total_ref[:NSTATE, :] + (dot_tn(output_map, high) + dot_tn(output_map, low))
    )
    total_ref[NSTATE:, :] = jnp.broadcast_to(k_ref[7:8, :], (8, k_ref.shape[1]))


def back_kernel(
    chunks, early_ref, state_in_ref, mixer_grad_ref, e_ref, f_ref, k_ref, weighted_ref, high_ref, low_ref,
    maps_ref, value_slope_ref, state_slope_ref, skip_ref,
    value_ref, map_ref, state_ref,
):
    chunk = chunks - 1 - pl.program_id(0)

    def start():
        state_ref[...] = state_in_ref[...]

    first_step(start)
    lower = lower_mask()
    row = lax.broadcasted_iota(jnp.int32, (CHUNK, CHUNK), 0)
    upper = row <= lax.broadcasted_iota(jnp.int32, (CHUNK, CHUNK), 1)
    factor = k_ref[pl.ds(chunk, 1), :]
    input_map, output_map = maps_ref[:, :NSTATE], maps_ref[:, NSTATE:]
    weighted = weighted_ref[...]
    mixer_grad = mixer_grad_ref[...]
    high, low = split(expand(e_ref[...], weighted.shape[1]) * mixer_grad)
    scaled = factor * state_ref[...]
    state_high, state_low = split(scaled)
    both = jnp.concatenate([weighted, high_ref[0]], axis=0)
    sums = dot_nt(high, both) + dot_nt(low, both)
    score_grad = jnp.where(lower, sums[:, :CHUNK], 0.0).astype(BF16)
    output_grad = sums[:, CHUNK:] + dot_nt(high, low_ref[0]) + dot(score_grad, input_map)
    sums = dot_nt(weighted, jnp.concatenate([state_high, state_low], axis=0))
    input_grad = sums[:, :NSTATE] + sums[:, NSTATE:] + dot_tn(score_grad, output_map)
    scores = jnp.where(upper, dot_nt(input_map, output_map), 0.0).astype(BF16)
    grads = dot(
        jnp.concatenate([scores, input_map], axis=1), jnp.concatenate([high, state_high], axis=0)
    )
    decayed = expand(f_ref[...], weighted.shape[1]) * grads
    value_ref[...] = (decayed + skip_ref[...] * mixer_grad) * value_slope_ref[...]
    slope = state_slope_ref[...]
    map_ref[:, :NSTATE] = input_grad * slope[:, :NSTATE]
    map_ref[:, NSTATE:] = output_grad * slope[:, NSTATE:]
    state_ref[...] = factor * (scaled + (dot_tn(output_map, high) + dot_tn(output_map, low)))


def conv_back_kernel(
    chunks, value_ref, map_ref, after_ref, value_raw_ref, state_raw_ref, value_kernel_ref,
    state_kernel_ref, cross_in_ref,
    value_grad_ref, state_grad_ref, value_small_ref, state_small_ref, cross_ref, value_next_ref,
    state_next_ref,
):
    chunk = chunks - 1 - pl.program_id(0)
    channels = value_ref.shape[1]
    clear(value_small_ref, state_small_ref)

    def start():
        value_next_ref[...] = after_ref[:, :channels]
        state_next_ref[...] = after_ref[:, channels:]

    first_step(start)

    def back(slope_ref, next_ref, raw_ref, kernel_ref, grad_ref, small_ref):
        kernel = kernel_ref[...].astype(F32)
        slope = slope_ref[...]
        window = jnp.concatenate([slope, next_ref[...]], axis=0)
        around = pl.ds(pl.multiple_of(chunk * CHUNK, CHUNK), CHUNK + HALO)
        raw = raw_ref[around, :].astype(F32)
        grad = jnp.zeros_like(slope)
        for offset in range(KERNEL):
            back_by = KERNEL - 1 - offset
            grad = grad + kernel[offset : offset + 1] * window[back_by : back_by + CHUNK]
            begin = HALO - KERNEL + 1 + offset
            small_ref[offset : offset + 1, :] += jnp.sum(
                slope * raw[begin : begin + CHUNK], axis=0, keepdims=True
            )
        small_ref[KERNEL : KERNEL + 1, :] += jnp.sum(slope, axis=0, keepdims=True)
        grad = grad.astype(BF16)
        grad_ref[...] = grad
        next_ref[...] = slope[:8]
        return jnp.sum(grad.astype(F32) * raw[HALO:], axis=1, keepdims=True)

    crossed = back(map_ref, state_next_ref, state_raw_ref, state_kernel_ref, state_grad_ref, state_small_ref)
    crossed = crossed + back(
        value_ref, value_next_ref, value_raw_ref, value_kernel_ref, value_grad_ref, value_small_ref
    )
    cross_ref[...] = cross_in_ref[...] + row_of(crossed)


def normed_kernel(
    chunks, late_ref, gate_grad_ref, value_grad_ref, state_grad_ref, gate_weight_ref, value_weight_ref,
    state_weight_ref, cross_ref, out_ref
):
    value = (
        dot_nt(gate_grad_ref[...], gate_weight_ref[...])
        + dot_nt(value_grad_ref[...], value_weight_ref[...])
        + dot_nt(state_grad_ref[...], state_weight_ref[...])
    )
    count = value.shape[0]
    out_ref[0, :count, :] = value.astype(BF16)
    line = lax.broadcasted_iota(jnp.int32, (HALO, CHUNK), 0)
    packed = jnp.zeros((HALO, CHUNK), F32)
    for chunk in range(chunks):
        row = cross_ref[0:1, chunk * CHUNK : (chunk + 1) * CHUNK]
        high = row.astype(BF16).astype(F32)
        packed = jnp.where(line == chunk, high, packed)
        packed = jnp.where(line == chunks + chunk, row - high, packed)
    out_ref[0, count:, :] = jnp.zeros((HALO, value.shape[1]), BF16)
    out_ref[0, count:, :CHUNK] = packed.astype(BF16)


def last_kernel(full_width, parts_ref, tokens_ref, scale_ref, gain_ref, cotangent_ref, out_ref):
    count = tokens_ref.shape[0]
    chunks = count // CHUNK
    size = parts_ref.shape[0]
    crossed = sum(parts_ref[i, count:, :CHUNK].astype(F32) for i in range(size))
    crossed = crossed[:chunks] + crossed[chunks : 2 * chunks]
    for chunk in range(chunks):
        rows = slice(chunk * CHUNK, (chunk + 1) * CHUNK)
        normed_grad = sum(parts_ref[i, rows, :].astype(F32) for i in range(size))
        scale = scale_ref[HALO + chunk * CHUNK : HALO + (chunk + 1) * CHUNK, 0:1]
        total = column(jnp.broadcast_to(crossed[chunk : chunk + 1], (8, CHUNK)))[:, 0:1]
        out_ref[rows, :] = (
            scale * gain_ref[...].astype(F32) * normed_grad
            - tokens_ref[rows, :].astype(F32) * (scale * scale * total / full_width)
            + cotangent_ref[rows, :].astype(F32)
        ).astype(BF16)


def store_piece(core_ref, kept_ref, given_ref, place, begin, piece):
    chips = kept_ref.shape[0]
    core, chip = place // chips, lax.rem(place, chips)
    rows = slice(begin, begin + piece.shape[0])
    piece = piece.astype(BF16)

    @pl.when(core_ref[0] == core)
    def _():
        kept_ref[chip, rows, :] = piece

    @pl.when(core_ref[0] != core)
    def _():
        given_ref[chip, rows, :] = piece


def gain_row(weight, block):
    sums = jnp.sum(weight.astype(F32) * block, axis=1, keepdims=True)
    lane = lax.broadcasted_iota(jnp.int32, (CHUNK, CHUNK), 1)
    rows = [
        jnp.where(lane == 0, sums[i : i + CHUNK], 0.0).T[0:1] for i in range(0, BLOCK, CHUNK)
    ]
    return jnp.concatenate(rows, axis=1)


def early_kernel(
    loose_ref, core_ref, normed_ref, gate_ref, mixed_ref, grad_ref, weight_ref,
    kept_ref, given_ref, gain_ref, held_ref
):
    chips, rows, channels = kept_ref.shape
    at = pl.program_id(0)
    count, width = grad_ref.shape
    pieces = 2 * chips
    step = width // pieces
    out_rows = channels // pieces
    out_blocks = channels // BLOCK
    every = width // BLOCK // out_blocks

    @pl.when(lax.rem(at, every) == 0)
    def _():
        held_ref[...] = dot_tn(mixed_ref[...], grad_ref[...])

    block = dot_tn(normed_ref[HALO : HALO + count, :], gate_ref[...])
    gain_ref[...] = gain_row(weight_ref[...], block)
    for i in range(BLOCK // step):
        place = at * (BLOCK // step) + i
        begin = lax.rem(at, every) * (BLOCK // step * out_rows) + i * out_rows
        own = held_ref[pl.ds(pl.multiple_of(begin, 8), out_rows), :]
        parts = [block[i * step : (i + 1) * step]]
        parts += [own[:, j : j + channels] for j in range(0, width, channels)]
        store_piece(core_ref, kept_ref, given_ref, place, 0, jnp.concatenate(parts, axis=0))


def late_kernel(
    early_ref, core_ref, normed_ref, value_ref, state_ref, value_small_ref, gate_small_ref, gain_ref,
    state_small_ref, value_weight_ref, state_weight_ref, gain_full_ref,
    kept_ref, given_ref, own_ref, shared_ref, gains_ref,
):
    chips, rows, channels = kept_ref.shape
    at = pl.program_id(0)
    count, maps_width = state_ref.shape
    width = gains_ref.shape[1]
    pieces = 2 * chips
    step = width // pieces
    lanes = channels // 128
    part = 2 * step // lanes
    columns = normed_ref[HALO : HALO + count, :]
    value = dot_tn(columns, value_ref[...])
    state = dot_tn(columns, state_ref[...])
    gain = (
        gain_ref[...] + gain_row(value_weight_ref[...], value) + gain_row(state_weight_ref[...], state)
    ) / gain_full_ref[0:1, :]
    gains_ref[0:1, pl.ds(pl.multiple_of(at * BLOCK, 128), BLOCK)] = gain
    for i in range(BLOCK // step):
        piece = slice(i * step, (i + 1) * step)
        stacked = jnp.concatenate([state[piece, :128], state[piece, 128:]], axis=0)
        stacked = jnp.concatenate(
            [stacked[j * part : (j + 1) * part] for j in range(lanes)], axis=1
        )
        store_piece(
            core_ref, kept_ref, given_ref, at * (BLOCK // step) + i, 0,
            jnp.concatenate([value[piece], stacked], axis=0),
        )

    @pl.when(at == width // BLOCK - 1)
    def _():
        own_ref[...] = jnp.zeros_like(own_ref)
        own_ref[: KERNEL + 1, :] = value_small_ref[: KERNEL + 1, :]
        own_ref[KERNEL + 1 : KERNEL + 3, :] = gate_small_ref[:2, :]
        shared_ref[...] = jnp.zeros_like(shared_ref)
        begin = width // channels
        for i in range(begin):
            shared_ref[i : i + 1, :] = gains_ref[0:1, i * channels : (i + 1) * channels]
        for i in range(0, (KERNEL + 1) * maps_width, 128):
            tap, column_from = divmod(i, maps_width)
            row, column_to = divmod(i, channels)
            shared_ref[begin + row : begin + row + 1, column_to : column_to + 128] = state_small_ref[
                tap : tap + 1, column_from : column_from + 128
            ]
        line = lax.broadcasted_iota(jnp.int32, (HALO, channels), 0)
        for place in range(pieces):
            own, shared = own_ref[place : place + 1, :], shared_ref[place : place + 1, :]
            own_high, shared_high = (v.astype(BF16).astype(F32) for v in (own, shared))
            small = jnp.zeros((HALO, channels), F32)
            for to, value in enumerate((own_high, own - own_high, shared_high, shared - shared_high)):
                small = jnp.where(line == to, value, small)
            store_piece(core_ref, kept_ref, given_ref, place, step + part, small)


def merge_pairs(block):
    tail = block[-HALO:]
    line = lax.broadcasted_iota(jnp.int32, tail.shape, 0)
    own, shared = tail[0:1] + tail[1:2], tail[2:3] + tail[3:4]
    own_high, shared_high = own.astype(BF16).astype(F32), shared.astype(BF16).astype(F32)
    new = jnp.zeros_like(tail)
    for at, value in enumerate((own_high, own - own_high, shared_high, shared - shared_high)):
        new = jnp.where(line == at, value, new)
    return jnp.concatenate([block[:-HALO], new], axis=0)


def heads_kernel(piece_ref, total_ref, arrived_ref, out_ref, low_ref):
    total = merge_pairs(total_ref[...] + arrived_ref[...].astype(F32))
    line = lax.broadcasted_iota(jnp.int32, total.shape, 0)
    first = total.shape[0] - HALO
    own = (line >= first) & (line < first + 2)
    out_ref[...] = total
    low_ref[...] = jnp.where(own, piece_ref[...], total).astype(BF16)


def half_kernel(paired, chips, chip_ref, kept_ref, arrived_ref, *refs):
    outs = refs[-chips:]
    for bits in range(chips):
        place = lax.bitwise_xor(chip_ref[0], bits)
        value = kept_ref[place].astype(F32) + arrived_ref[place].astype(F32)
        if paired:
            value = merge_pairs(value)
        outs[bits][...] = value.astype(outs[bits].dtype)


def piece_kernel(parts, paired, cut, *refs):
    total = sum(ref[...].astype(F32) for ref in refs[:parts])
    if not paired:
        refs[-1][...] = total.astype(BF16)
        return
    first_ref, last_ref = refs[-2:]
    first_ref[...] = total[:cut].astype(BF16)
    last_ref[...] = merge_pairs(total[cut:])


def square_half_kernel(
    chip_ref, kept_ref, arrived_ref, loose_ref, first_ref, first_give_ref, last_ref, last_give_ref
):
    cut = first_ref.shape[1]
    for bits in range(4):
        place = lax.bitwise_xor(chip_ref[0], bits)
        value = kept_ref[place].astype(F32) + arrived_ref[place].astype(F32)
        low, high = bits & 1, bits >> 1
        ref = first_give_ref if low else first_ref
        ref[high] = value[:cut].astype(ref.dtype)
        ref = last_give_ref if high else last_ref
        ref[low] = value[cut:].astype(ref.dtype)


def square_next_kernel(
    first_ref, first_got_ref, last_ref, last_got_ref, loose_ref,
    first_out_ref, first_give_ref, last_out_ref, last_give_ref,
):
    first_out_ref[...] = first_ref[0] + first_got_ref[0].astype(F32)
    first_give_ref[...] = (first_ref[1] + first_got_ref[1].astype(F32)).astype(BF16)
    last_out_ref[...] = last_ref[0] + last_got_ref[0].astype(F32)
    last_give_ref[...] = (last_ref[1] + last_got_ref[1].astype(F32)).astype(BF16)


def square_last_kernel(first_ref, first_got_ref, last_ref, last_got_ref, loose_ref, *outs):
    outs[0][...] = (first_ref[...] + first_got_ref[...].astype(F32)).astype(BF16)
    outs[1][...] = (last_ref[...] + last_got_ref[...].astype(F32)).astype(BF16)


def each_piece(core_ref, chip_ref, chips, groups, refs):
    refs = iter(refs)
    for part, bits_lists in enumerate(groups):
        number = 0
        for bits_list in bits_lists:
            for core, ref in ((core_ref[0], next(refs)), (1 - core_ref[0], next(refs))):
                for at, bits in enumerate(bits_list):
                    place = core * chips + lax.bitwise_xor(chip_ref[0], bits)
                    yield part, number, place, ref[at].astype(F32)
                    number += 1


def send_rows(buffer_ref, number, target_ref, place, sem_ref):
    rows = buffer_ref.shape[1]
    copy = pltpu.make_async_copy(
        buffer_ref.at[number],
        target_ref.at[pl.ds(pl.multiple_of(place * rows, 8), rows), :],
        sem_ref.at[number],
    )
    copy.start()
    return copy


def early_out_kernel(chips, groups, core_ref, chip_ref, *refs):
    gate_ref, output_ref, gate_buffer, output_buffer, gate_sems, output_sems = refs[-6:]
    out_rows, width = output_buffer.shape[1:]
    channels = gate_buffer.shape[2]
    copies = []
    for part, number, place, value in each_piece(core_ref, chip_ref, chips, groups, refs[:-6]):
        if part == 0:
            gate_buffer[number] = value
            copies.append(send_rows(gate_buffer, number, gate_ref, place, gate_sems))
        else:
            output_buffer[number] = jnp.concatenate(
                [value[i * out_rows : (i + 1) * out_rows] for i in range(width // channels)], axis=1
            )
            copies.append(send_rows(output_buffer, number, output_ref, place, output_sems))
    for copy in copies:
        copy.wait()


def late_out_kernel(chips, groups, core_ref, chip_ref, *refs):
    value_ref, buffer, sems = refs[-3:]
    copies = []
    for _, number, place, value in each_piece(core_ref, chip_ref, chips, groups, refs[:-3]):
        buffer[number] = value
        copies.append(send_rows(buffer, number, value_ref, place, sems))
    for copy in copies:
        copy.wait()


def shared_out_kernel(chips, groups, size, core_ref, chip_ref, head_ref, *refs):
    (
        state_ref, value_kernel_ref, value_bias_ref, state_kernel_ref, state_bias_ref, skip_ref,
        gated_ref, gain_ref, buffer, sems, own_ref, shared_ref,
    ) = refs[-12:]
    step, maps_width = buffer.shape[1:]
    channels = own_ref.shape[1]
    lanes = channels // 128
    rows = 2 * step // lanes
    copies = []
    for _, number, place, piece in each_piece(core_ref, chip_ref, chips, groups, refs[:-12]):
        stacked = jnp.concatenate(
            [piece[:rows, i * 128 : (i + 1) * 128] for i in range(lanes)], axis=0
        )
        buffer[number] = jnp.concatenate([stacked[:step], stacked[step:]], axis=1)
        copies.append(send_rows(buffer, number, state_ref, place, sems))
        own_ref[pl.ds(place, 1), :] = piece[rows : rows + 1] + piece[rows + 1 : rows + 2]
        shared_ref[pl.ds(place, 1), :] = piece[rows + 2 : rows + 3] + piece[rows + 3 : rows + 4]
    value_kernel_ref[...] = own_ref[:KERNEL, :]
    value_bias_ref[...] = own_ref[KERNEL, :]
    gated_ref[...] = own_ref[KERNEL + 1, :]
    heads = skip_ref.shape[0]
    at = lax.broadcasted_iota(jnp.int32, (heads, channels), 1)
    row = lax.broadcasted_iota(jnp.int32, (heads, channels), 0) * HEAD_DIM
    inside = (at >= row) & (at < row + HEAD_DIM)
    skip_ref[...] = jnp.sum(jnp.where(inside, own_ref[KERNEL + 2 : KERNEL + 3, :], 0.0), axis=1)
    own_width = gain_ref.shape[0]
    gain_rows = -(-own_width * size // channels)
    for head in range(size):
        row, begin = divmod(head * own_width, channels)

        @pl.when(head_ref[0] == head)
        def _(row=row, begin=begin):
            gain_ref[...] = shared_ref[row, begin : begin + own_width]

    for i in range(0, (KERNEL + 1) * maps_width, 128):
        tap, column_to = divmod(i, maps_width)
        row, column_from = divmod(i, channels)
        value = shared_ref[gain_rows + row : gain_rows + row + 1, column_from : column_from + 128]
        if tap < KERNEL:
            state_kernel_ref[tap : tap + 1, column_to : column_to + 128] = value
        else:
            state_bias_ref[column_to : column_to + 128] = value[0]
    for copy in copies:
        copy.wait()


SCALAR = "scalar"
WHOLE = "whole"
BLOCKED = "blocked"
LANES = "lanes"
LEADING = "leading"
FAR = "far"
LOOSE = "loose"


def run(kernel, name, flops, args, outs, steps=None, backward=False, scratch=()):
    at = (lambda i: steps - 1 - i) if backward else (lambda i: i)

    def spec(kind, shape):
        if isinstance(kind, int):
            return pl.BlockSpec((kind,) + shape[1:], lambda i: (at(i), 0))
        if kind == SCALAR:
            return pl.BlockSpec(memory_space=pltpu.SMEM)
        if kind == LOOSE:
            return pl.BlockSpec(memory_space=pl.ANY)
        if kind == FAR:
            return pl.BlockSpec(memory_space=pltpu.HBM)
        if isinstance(kind, tuple):
            return pl.BlockSpec(*kind)
        if steps is None:
            return pl.BlockSpec(memory_space=pltpu.VMEM)
        if kind == BLOCKED:
            return pl.BlockSpec((CHUNK, shape[1]), lambda i: (at(i), 0))
        if kind == LANES:
            return pl.BlockSpec((shape[0], CHUNK), lambda i: (0, at(i)))
        if kind == LEADING:
            return pl.BlockSpec((1,) + shape[1:], lambda i: (at(i),) + (0,) * (len(shape) - 1))
        return pl.BlockSpec(shape, lambda i: (0,) * len(shape))

    moved = sum(a.size * a.dtype.itemsize for kind, a in args if kind != LOOSE)
    shapes = [jax.ShapeDtypeStruct(shape, dtype) for _, shape, dtype in outs]
    moved += sum(a.size * a.dtype.itemsize for a in shapes)
    return pl.pallas_call(
        kernel,
        out_shape=shapes,
        in_specs=[spec(kind, a.shape) for kind, a in args],
        out_specs=[spec(kind, shape) for kind, shape, _ in outs],
        scratch_shapes=list(scratch),
        compiler_params=pltpu.CompilerParams(vmem_limit_bytes=VMEM_LIMIT),
        cost_estimate=pl.CostEstimate(flops=flops, bytes_accessed=moved, transcendentals=0),
        name=name,
        **({} if steps is None else {"grid": (steps,)}),
    )(*(a for _, a in args))


def per_device(
    tokens, decay_codes, norm_gain, gate_weight, value_weight, state_weight, value_kernel, value_bias,
    state_kernel, state_bias, skip_scale, gated_gain, output_weight, cotangent,
):
    tokens, decay_codes, cotangent = tokens[0], decay_codes[0], cotangent[0]
    count, own_width = tokens.shape
    heads = skip_scale.shape[0]
    channels = heads * HEAD_DIM
    head_size, chips = lax.axis_size("head"), lax.axis_size("chip")
    seq_size = 2 * chips
    width = own_width * head_size
    maps_width = 2 * NSTATE
    chunks = count // CHUNK
    core = (SCALAR, lax.axis_index("core").astype(jnp.int32)[None])
    chip = (SCALAR, lax.axis_index("chip").astype(jnp.int32)[None])
    head = (SCALAR, lax.axis_index("head").astype(jnp.int32)[None])

    rows = count + MARGIN
    packed = jnp.concatenate(
        [
            from_behind(tokens[-HALO:], 1),
            tokens,
            jnp.broadcast_to(norm_gain[None], (MARGIN - HALO, own_width)),
        ],
        axis=0,
    )
    logs = decay_codes.astype(F32) * (-DECAY_STEP)
    input_weight = jnp.sqrt(-jnp.expm1(2.0 * logs))
    e_full, f_full, factors = run(
        decay_kernel, "decays", count * channels * 200,
        [(WHOLE, decay_codes), (WHOLE, input_weight)],
        [
            (WHOLE, (count, heads), F32),
            (WHOLE, (count, heads), F32),
            (WHOLE, (8, channels), F32),
        ],
    )
    parts, passed = line_parts(packed, "head")
    skip_full = jnp.repeat(skip_scale, HEAD_DIM)[None]

    half = rows // 2
    gain_rows = ((MARGIN - HALO, own_width), lambda i: ((HALO + count) // (MARGIN - HALO), 0))
    normed, scale_in, gain_full = run(
        functools.partial(norm_kernel, head_size), "norm", count * width * 10,
        [head, (half, passed)] + [(half, part) for part in parts]
        + [(gain_rows, part) for part in parts] + [(gain_rows, passed)],
        [(half, (rows, width), BF16), (half, (rows, 128), F32), (WHOLE, (8, width), F32)],
        steps=2,
    )
    cotangent_parts = deal(
        run(
            copies_kernel, "copies", 1, [(LOOSE, normed), (WHOLE, cotangent)],
            [(WHOLE, (head_size, count, own_width), BF16)],
        )[0],
        "head",
    )
    value_raw = dot(normed, value_weight).astype(BF16)
    state_raw = dot(normed, state_weight).astype(BF16)
    conv, weighted, value_slope, maps, map_slope, local_end = run(
        conv_kernel, "conv", count * channels * 400,
        [
            (WHOLE, value_raw), (WHOLE, state_raw), (WHOLE, value_kernel), (WHOLE, value_bias[None]),
            (WHOLE, state_kernel), (WHOLE, state_bias[None]), (BLOCKED, f_full), (WHOLE, factors),
        ],
        [
            (BLOCKED, (count, channels), BF16),
            (BLOCKED, (count, channels), BF16),
            (BLOCKED, (count, channels), F32),
            (BLOCKED, (count, maps_width), BF16),
            (BLOCKED, (count, maps_width), F32),
            (WHOLE, (NSTATE + 8, channels), F32),
        ],
        steps=chunks,
    )
    gate_pre = dot(normed, gate_weight)[HALO : HALO + count]
    state_in, _ = entering(core, chip, local_end, False, (gate_pre,))
    mixed_grad, full_cotangent = run(
        mixed_grad_kernel, "mixed_grad", 2 * count * width * channels,
        [(WHOLE, cotangent_parts), (WHOLE, output_weight)],
        [(WHOLE, (count, channels), F32), (WHOLE, (count, width), BF16)],
    )
    mixer, stats, high, low = run(
        mixer_kernel, "mixer", count * channels * 1000,
        [
            (WHOLE, state_in), (BLOCKED, maps), (BLOCKED, weighted), (BLOCKED, conv),
            (BLOCKED, e_full), (WHOLE, factors), (WHOLE, skip_full), (BLOCKED, gate_pre),
            (BLOCKED, mixed_grad), (WHOLE, gated_gain[None]),
        ],
        [
            (BLOCKED, (count, channels), F32),
            (LANES, (8, count), F32),
            (LEADING, (chunks, NSTATE, channels), BF16),
            (LEADING, (chunks, NSTATE, channels), BF16),
        ],
        steps=chunks,
        scratch=[pltpu.VMEM((NSTATE, channels), F32)],
    )
    mixed, gate_grad, mixer_grad, gate_small, start_grad, gate_cross = run(
        functools.partial(gate_kernel, float(channels * head_size), chunks, head_size),
        "gate", count * channels * 600,
        [(LANES, part) for part in turn_all(stats, "head")]
        + [
            (BLOCKED, mixer), (BLOCKED, gate_pre), (BLOCKED, mixed_grad), (WHOLE, gated_gain[None]),
            (BLOCKED, conv), (BLOCKED, e_full), (WHOLE, factors), (BLOCKED, maps),
        ],
        [
            (BLOCKED, (count, channels), BF16),
            (BLOCKED, (count, channels), BF16),
            (BLOCKED, (count, channels), F32),
            (WHOLE, (8, channels), F32),
            (WHOLE, (NSTATE + 8, channels), F32),
            (LANES, (8, count), F32),
        ],
        steps=chunks,
        backward=True,
    )
    step, out_rows = width // seq_size, channels // seq_size
    early_rows = step + out_rows * (width // channels)
    features = width // BLOCK
    feature_block = ((rows, BLOCK), lambda i: (0, i))
    every = features // (channels // BLOCK)
    out_parts = run(
        out_kernel, "out", 2 * count * channels * width,
        [(LOOSE, start_grad), (WHOLE, mixed), (WHOLE, output_weight)],
        [(WHOLE, (head_size, count, own_width), BF16)],
    )[0]
    early_made = []

    def make_early(pair):
        early_made.extend(
            run(
                early_kernel, "early", 4 * count * channels * width,
                [
                    (LOOSE, pair), core, (feature_block, normed), (WHOLE, gate_grad),
                    (((count, BLOCK), lambda i: (0, i // every)), mixed), (WHOLE, full_cotangent),
                    (BLOCK, gate_weight),
                ],
                [(WHOLE, (chips, early_rows, channels), BF16)] * 2
                + [(((1, BLOCK), lambda i: (0, i)), (1, width), F32)],
                steps=features,
                scratch=[pltpu.VMEM((BLOCK, width), F32)],
            )
        )
        return early_made[1:2]

    grad_after, after_prefix = entering(core, chip, start_grad, True, (out_parts,), make_early)
    early_kept, early_given, early_gain = early_made
    early_state, half_mark = sum_pieces(
        chip, early_kept, early_given, "early", True, step, False, (after_prefix,)
    )
    branch = jnp.sum(deal(out_parts, "head").astype(F32), axis=0)
    block_out = (tokens.astype(F32) + branch).astype(BF16)

    value_grads, map_grads = run(
        functools.partial(back_kernel, chunks), "back", count * channels * 2000,
        [
            (LOOSE, half_mark), (WHOLE, grad_after), (BLOCKED, mixer_grad), (BLOCKED, e_full),
            (BLOCKED, f_full), (WHOLE, factors), (BLOCKED, weighted), (LEADING, high),
            (LEADING, low), (BLOCKED, maps), (BLOCKED, value_slope), (BLOCKED, map_slope),
            (WHOLE, skip_full),
        ],
        [(BLOCKED, (count, channels), F32), (BLOCKED, (count, maps_width), F32)],
        steps=chunks,
        backward=True,
        scratch=[pltpu.VMEM((NSTATE, channels), F32)],
    )
    after = from_behind(jnp.concatenate([value_grads[:8], map_grads[:8]], axis=1), -1)
    value_raw_grad, state_raw_grad, value_small, state_small, crossed = run(
        functools.partial(conv_back_kernel, chunks), "conv_back", count * channels * 100,
        [
            (BLOCKED, value_grads), (BLOCKED, map_grads), (WHOLE, after),
            (WHOLE, value_raw), (WHOLE, state_raw), (WHOLE, value_kernel), (WHOLE, state_kernel),
            (LANES, gate_cross),
        ],
        [
            (BLOCKED, (count, channels), BF16),
            (BLOCKED, (count, maps_width), BF16),
            (WHOLE, (8, channels), F32),
            (WHOLE, (8, maps_width), F32),
            (LANES, (8, count), F32),
        ],
        steps=chunks,
        backward=True,
        scratch=[pltpu.VMEM((8, channels), F32), pltpu.VMEM((8, maps_width), F32)],
    )
    next_mark = early_state[0]
    if chips == 4:
        early_state = square_next("early", early_state, early_rows * channels, crossed)
        next_mark = early_state[0]
    normed_parts = run(
        functools.partial(normed_kernel, chunks), "normed", 4 * count * channels * width,
        [
            (LOOSE, next_mark), (WHOLE, gate_grad), (WHOLE, value_raw_grad),
            (WHOLE, state_raw_grad), (own_width, gate_weight), (own_width, value_weight),
            (own_width, state_weight), (WHOLE, crossed),
        ],
        [(LEADING, (head_size, count + HALO, own_width), BF16)],
        steps=head_size,
    )[0]
    if chips == 4:
        early_gate, early_out = square_end(
            "early", early_state,
            [(WHOLE, (step, channels), BF16), (WHOLE, (early_rows - step, channels), BF16)],
            early_rows * channels, normed_parts,
        )
    else:
        early_gate, early_out = early_state[0][:step], early_state[0][step:]
    lanes = channels // 128
    state_rows = 2 * step // lanes
    late_rows = step + state_rows + HALO
    late_kept, late_given = run(
        late_kernel, "late", 3 * count * channels * width,
        [
            (LOOSE, early_gate), core, (feature_block, normed), (WHOLE, value_raw_grad),
            (WHOLE, state_raw_grad),
            (WHOLE, value_small), (WHOLE, gate_small), (((1, BLOCK), lambda i: (0, i)), early_gain),
            (WHOLE, state_small), (BLOCK, value_weight), (BLOCK, state_weight),
            (((8, BLOCK), lambda i: (0, i)), gain_full),
        ],
        [(WHOLE, (chips, late_rows, channels), BF16)] * 2,
        steps=features,
        scratch=[
            pltpu.VMEM((HALO, channels), F32),
            pltpu.VMEM((HALO, channels), F32),
            pltpu.VMEM((8, width), F32),
        ],
    )
    (late_piece, shared_piece), late_mark = sum_pieces(
        chip, late_kept, late_given, "late", False, step, True
    )
    normed_parts = deal(normed_parts, "head")
    shared_piece = heads_sum(shared_piece)

    def unpack(kernel, name, pieces, outs, flops, scratch, extra=(), args=()):
        groups = [collect(*piece) for piece in pieces]
        bits = [[found[2] for found in group] for group in groups]
        arrays = [(WHOLE, value) for group in groups for found in group for value in found[:2]]
        return run(
            functools.partial(kernel, chips, bits, *extra), name, flops,
            [core, chip, *args] + arrays, outs, scratch=scratch,
        )

    sems = pltpu.SemaphoreType.DMA((seq_size,))
    gate_weight_gradient, output_weight_gradient = unpack(
        early_out_kernel, "early_out",
        [(early_gate, (2, 1), late_mark), (early_out, (1, 2), late_mark)],
        [(FAR, (width, channels), F32), (FAR, (channels, width), F32)], 4 * channels * width,
        [
            pltpu.VMEM((seq_size, step, channels), F32),
            pltpu.VMEM((seq_size, out_rows, width), F32),
            sems,
            sems,
        ],
    )
    value_weight_gradient = unpack(
        late_out_kernel, "late_out", [(late_piece, None)],
        [(FAR, (width, channels), F32)], 2 * channels * width,
        [pltpu.VMEM((seq_size, step, channels), F32), sems],
    )[0]
    (
        state_weight_gradient, value_kernel_gradient, value_bias_gradient, state_kernel_gradient,
        state_bias_gradient, skip_scale_gradient, gated_gain_gradient, norm_gain_gradient,
    ) = unpack(
        shared_out_kernel, "shared_out", [(shared_piece, (2, 1))],
        [
            (FAR, (width, maps_width), F32),
            (WHOLE, (KERNEL, channels), F32),
            (WHOLE, (channels,), F32),
            (WHOLE, (KERNEL, maps_width), F32),
            (WHOLE, (maps_width,), F32),
            (WHOLE, (heads,), F32),
            (WHOLE, (channels,), F32),
            (WHOLE, (own_width,), F32),
        ],
        2 * maps_width * width,
        [
            pltpu.VMEM((seq_size, step, maps_width), F32),
            sems,
            pltpu.VMEM((HALO, channels), F32),
            pltpu.VMEM((HALO, channels), F32),
        ],
        extra=(head_size,),
        args=[head],
    )
    tokens_gradient = run(
        functools.partial(last_kernel, float(width)), "last", count * own_width * 20,
        [
            (WHOLE, normed_parts), (WHOLE, tokens), (WHOLE, scale_in),
            (WHOLE, norm_gain[None]), (WHOLE, cotangent),
        ],
        [(WHOLE, (count, own_width), BF16)],
    )[0]
    return (
        block_out[None],
        tokens_gradient[None],
        norm_gain_gradient,
        gate_weight_gradient,
        value_weight_gradient,
        state_weight_gradient,
        value_kernel_gradient,
        value_bias_gradient,
        state_kernel_gradient,
        state_bias_gradient,
        skip_scale_gradient,
        gated_gain_gradient,
        output_weight_gradient,
    )


def solution(mesh):
    seq_size, head_size = mesh.shape["seq"], mesh.shape["head"]
    mesh = Mesh(mesh.devices.reshape(seq_size // 2, 2, head_size), ("chip", "core", "head"))
    seq = ("chip", "core")
    in_specs = (
        P(None, seq, "head"),
        P(None, seq, "head"),
        P("head"),
        P(None, "head"),
        P(None, "head"),
        P(),
        P(None, "head"),
        P("head"),
        P(),
        P(),
        P("head"),
        P("head"),
        P("head", None),
        P(None, seq, "head"),
    )
    out_specs = (
        P(None, seq, "head"),
        P(None, seq, "head"),
        P("head"),
        P(None, "head"),
        P(None, "head"),
        P(),
        P(None, "head"),
        P("head"),
        P(),
        P(),
        P("head"),
        P("head"),
        P("head", None),
    )
    return jax.shard_map(
        per_device, mesh=mesh, in_specs=in_specs, out_specs=out_specs, check_vma=False
    )
```
